32 devices in a mesh: dp: 16 (over z, y, x), seq: 2 (over core).
Axes of the slice: x: 2, y: 2, z: 4, core: 2. Of those that a mesh axis runs over, the one named last changes fastest.
Arguments:
- hidden: bfloat16 [48, 512, 768], P('dp', 'seq'), may hold values from -6 to 6
- span_mask: int32 [48, 512], P('dp', 'seq'), may hold values 0 or 1
- replace_kind: int32 [48, 512], P('dp', 'seq'), may hold values from 0 to 9
- replace_from: int32 [48, 512], P('dp', 'seq'), may hold values from 0 to 255
- weights: float32 [9216, 768], P('dp'), may hold values from -0.48549177 to 0.48549177
- vectors: float32 [13, 768], P(None, 'dp'), may hold values from -4 to 4
- weight_first: float32 [9216, 768], P('dp'), may hold values from -0.00061035156 to 0.00061035156
- weight_second: float32 [9216, 768], P('dp'), may hold values from 7.054304e-11 to 1.1286886e-09
- vector_first: float32 [13, 768], P(None, 'dp'), may hold values from -0.00061035156 to 0.00061035156
- vector_second: float32 [13, 768], P(None, 'dp'), may hold values from 7.054304e-11 to 1.1286886e-09
- cotangent: bfloat16 [48, 512, 768], P('dp', 'seq'), may hold values from -6 to 6
Outputs:
- layer_out: float32 [48, 512, 768], P('dp', 'seq')
- input_grad: float32 [48, 512, 768], P('dp', 'seq')
- grad_norm: float32 [], replicated
- weights_new: float32 [9216, 768], P('dp')
- weight_first_new: float32 [9216, 768], P('dp')
- weight_second_new: float32 [9216, 768], P('dp')
- vectors_new: float32 [13, 768], P(None, 'dp')
- vector_first_new: float32 [13, 768], P(None, 'dp')
- vector_second_new: float32 [13, 768], P(None, 'dp')
- weights_low: bfloat16 [9216, 768], P('dp')
- vectors_low: bfloat16 [13, 768], P(None, 'dp')
The draws below stay inside these ranges and needn't reach their ends.
All inputs are finite; a program needn't handle non-finite values. No bound on the sum of `span_mask` on one device may be relied on, other than what follows from the above.
Results may differ from the reference program's by a relative error of at most 0.015.
The reference program's roundings to bfloat16 on the way count: a program that leaves them out, or rounds other values in their place, can miss the bound.
Values may be sent and summed in bfloat16 or wider, within the bound.
No kernel may reach another device: no remote copies, remote signals or barrier semaphores. Data moves between devices by JAX's collectives and lax.ppermute only.
A program may use at most 192 MiB of HBM per device.

```python
import math
import jax
import jax.numpy as jnp
from jax import lax

D = 768
HEADS = 12
HEAD_DIM = 64
FF = 3072
LEN = 512
STEP = 10
SEQS = 48
HALF = 256
WROWS = 9216
VROWS = 13


def draw_weights(key, part):
    key = jax.random.fold_in(key, 11)
    row_ids = jnp.arange(WROWS)[:, None]
    base_scale = D ** (-0.5)
    mixed_scale = 0.5 ** 0.5 * LEN ** 0.25 * base_scale
    scales = jnp.where(row_ids < 2 * D, 1.2 * base_scale, base_scale)
    scales = jnp.where((row_ids >= 2 * D) & (row_ids < 4 * D), mixed_scale, scales)
    scales = jnp.where(row_ids >= 4 * D + FF, 1.5 * FF ** (-0.5), scales)
    spread_draw = jax.random.truncated_normal(key, -4.0, 4.0, (WROWS, D), jnp.float32)
    return (spread_draw * scales).astype(jnp.float32)


def draw_vectors(key, part):
    key = jax.random.fold_in(key, 23)
    row_ids = jnp.arange(VROWS)[:, None]
    columns = jnp.arange(D)[None, :].astype(jnp.float32) / D
    spread_draw = jax.random.truncated_normal(key, -4.0, 4.0, (VROWS, D), jnp.float32)
    is_gain = (row_ids == 3) | (row_ids == 6)
    gains = (0.6 + 1.2 * columns) * (1.0 + 0.1 * spread_draw)
    biases = 0.2 * spread_draw
    result = jnp.where(is_gain, gains, jnp.where(row_ids == 8, spread_draw, biases))
    return result.astype(jnp.float32)


def touch_ends(values, own_key, smallest, top_value):
    index_at = [jax.random.randint(jax.random.fold_in(own_key, axis), (), 0, length) for axis, length in enumerate(values.shape)]
    widest = values.shape.index(max(values.shape))
    next_to = index_at[:widest] + [(index_at[widest] + 1) % values.shape[widest]] + index_at[widest + 1:]
    return values.at[tuple(index_at)].set(smallest).at[tuple(next_to)].set(top_value)


def shard_levels(rng, extent, shards, least, high):
    level = 1.0
    for dim, parts in shards:
        heights = jax.random.uniform(jax.random.fold_in(jax.random.fold_in(rng, 6), dim), (parts,), jnp.float32, least / len(shards), high / len(shards))
        level = level * jnp.repeat(jnp.exp(heights), extent[dim] // parts).reshape((-1,) + (1,) * (len(extent) - 1 - dim))
    return level


def noise(key, dims, width, most, split=(), kind=jnp.bfloat16):
    loudness = shard_levels(key, dims, split, -0.22, 0.18) if split else 1.0
    entries = jax.random.normal(key, dims, jnp.float32) * width * loudness
    return jnp.minimum(jnp.maximum(entries, -most), most).astype(kind)


def setup_inputs(seed: int = 0) -> dict:
    key_of = jax.random.split(jax.random.key(seed), 12)
    return {
        "hidden": noise(key_of[0], (SEQS, LEN, D), 1.0, 6.0, ((0, 16), (1, 2))),
        "span_mask": touch_ends((jax.random.randint(key_of[1], (SEQS, LEN), 0, 100) < 15).astype(jnp.int32), jax.random.fold_in(key_of[1], 1), 0, 1),
        "replace_kind": touch_ends(jax.random.randint(key_of[2], (SEQS, LEN), 0, 10), jax.random.fold_in(key_of[2], 1), 0, 9).astype(jnp.int32),
        "replace_from": touch_ends(jax.random.randint(key_of[3], (SEQS, LEN), 0, HALF), jax.random.fold_in(key_of[3], 1), 0, HALF - 1).astype(jnp.int32),
        "weights": draw_weights(jax.random.fold_in(key_of[11], 71), 0),
        "vectors": draw_vectors(jax.random.fold_in(key_of[11], 71), 0),
        "weight_first": noise(key_of[6], (WROWS, D), (0.11 * ((WROWS + VROWS) * D) ** -0.5), 0.00061035156, ((0, 16),), jnp.float32),
        "weight_second": jnp.clip(jnp.exp(math.log(1.1286885870376295e-09) - 2.7725887 * jax.random.uniform(key_of[7], (WROWS, D), jnp.float32) ** shard_levels(key_of[7], (WROWS, D), ((0, 16),), -0.2, 0.2)), 7.054303668985185e-11, 1.1286885870376295e-09),
        "vector_first": noise(key_of[8], (VROWS, D), (0.11 * ((WROWS + VROWS) * D) ** -0.5), 0.00061035156, ((1, 16),), jnp.float32),
        "vector_second": jnp.clip(jnp.exp(math.log(1.1286885870376295e-09) - 2.7725887 * jax.random.uniform(key_of[9], (VROWS, D), jnp.float32) ** shard_levels(key_of[9], (VROWS, D), ((1, 16),), -0.2, 0.2)), 7.054303668985185e-11, 1.1286885870376295e-09),
        "cotangent": noise(key_of[10], (SEQS, LEN, D), 1.0, 6.0, ((0, 16), (1, 2))),
    }


@jax.custom_vjp
def low(v):
    return lax.optimization_barrier(v.astype(jnp.bfloat16)).astype(jnp.float32)

@jax.custom_vjp
def low_back(v):
    return v

def low_keep(v):
    return (low(v), None)

def low_pass(kept, grad):
    return (grad,)

def back_keep(v):
    return (v, None)

def back_low(kept, grad):
    return (low(grad),)
low.defvjp(low_keep, low_pass)
low_back.defvjp(back_keep, back_low)
ln_eps = 1e-12
beta_one = 0.9
beta_two = 0.999
adam_eps = 1e-08
learn_rate = 0.05
vector_rate = 0.3
decay_rate = 0.01
highest = lax.Precision.HIGHEST

def matmul(left, right):
    return jnp.dot(left, right, precision=highest, preferred_element_type=jnp.float32)

def layer_norm(values, gain, shift):
    center = values - lax.optimization_barrier(jnp.mean(values, axis=-1, keepdims=True))
    inv_std = lax.rsqrt(lax.optimization_barrier(jnp.mean(center * center, axis=-1, keepdims=True)) + ln_eps)
    return center * inv_std * gain + shift

def corrupt(initial, mask_row, span_mask, replace_kind, source):
    picked = jax.vmap(lambda seq_rows, where_from: seq_rows[where_from])(initial, source)
    chosen = span_mask == 1
    masked = (chosen & (replace_kind < 8))[..., None]
    swapped = (chosen & (replace_kind == 8))[..., None]
    return jnp.where(masked, mask_row, jnp.where(swapped, picked, initial))

def group_layer(low_w, low_v, initial, span_group, kind_group, source_group):
    group_count = initial.shape[0]
    w_qkv = low_w[:3 * D]
    w_out = low_w[3 * D:4 * D]
    w_in = low_w[4 * D:4 * D + FF]
    w_back = low_w[4 * D + FF:]
    inputs = corrupt(initial, low_v[8], span_group, kind_group, source_group).reshape(-1, D)
    bias_qkv = jnp.concatenate([low_v[0], jnp.zeros((D,), jnp.float32), low_v[1]])
    projected = low_back(low(matmul(inputs, w_qkv.T) + bias_qkv))
    heads = projected.reshape(group_count, LEN, 3, HEADS, HEAD_DIM)
    queries = heads[:, :, 0]
    keys = heads[:, :, 1]
    values = heads[:, :, 2]
    scores = low_back(jnp.einsum('bqhd,bkhd->bhqk', queries, keys, precision=highest) * HEAD_DIM ** (-0.5))
    probabilities = jax.nn.softmax(scores, axis=-1)
    attended = jnp.einsum('bhqk,bkhd->bqhd', low(probabilities), values, precision=highest).reshape(-1, D)
    attended = low_back(low(attended))
    branch = low_back(matmul(attended, w_out.T) + low_v[2])
    hidden_one = layer_norm(inputs + branch, low_v[3], low_v[4])
    preact = low_back(matmul(low(hidden_one), w_in.T) + low_v[9:].reshape(FF))
    gelu_low = low(jax.nn.gelu(preact, approximate=False))
    feed_out = low_back(matmul(gelu_low, w_back) + low_v[5])
    finished = layer_norm(hidden_one + feed_out, low_v[6], low_v[7])
    return finished.reshape(group_count, LEN, D)

def adam_step(master, first_old, second, gradient, decay_on, step_rate):
    first_new = beta_one * first_old + (1.0 - beta_one) * gradient
    second_new = beta_two * second + (1.0 - beta_two) * gradient * gradient
    fix_one = 1.0 - beta_one ** STEP
    fix_two = 1.0 - beta_two ** STEP
    update = first_new / fix_one / (jnp.sqrt(second_new / fix_two) + adam_eps)
    return (master - step_rate * (update + decay_on * master), first_new, second_new)

def reference(hidden, span_mask, replace_kind, replace_from, weights, vectors, weight_first, weight_second, vector_first, vector_second, cotangent):
    positions = jnp.arange(LEN, dtype=jnp.int32)
    source = (positions // HALF * HALF)[None, :] + replace_from

    def grouped(array):
        return array.reshape((-1, 8) + array.shape[1:])
    checked = jax.checkpoint(group_layer)

    def forward(master_w, master_v, initial):
        low_w = low(master_w)
        low_v = low(master_v)

        def scan_step(unused_carry, slices):
            return (unused_carry, checked(low_w, low_v, slices[0], slices[1], slices[2], slices[3]))
        start = jnp.zeros((), jnp.float32)
        _, results = lax.scan(scan_step, start, (grouped(initial), grouped(span_mask), grouped(replace_kind), grouped(source)))
        return results.reshape(initial.shape)
    layer_out, pullback = jax.vjp(forward, weights, vectors, hidden.astype(jnp.float32))
    wgrad, vgrad, input_grad = pullback(cotangent.astype(jnp.float32))
    grad_norm = jnp.sqrt(jnp.sum(wgrad * wgrad) + jnp.sum(vgrad * vgrad))
    clip = 1.0 / jnp.maximum(grad_norm, 1.0)
    weights_new, weight_first_new, weight_second_new = adam_step(weights, weight_first, weight_second, wgrad * clip, decay_rate, learn_rate)
    vectors_new, vector_first_new, vector_second_new = adam_step(vectors, vector_first, vector_second, vgrad * clip, 0.0, vector_rate)
    return (layer_out, input_grad, grad_norm, weights_new, weight_first_new, weight_second_new, vectors_new, vector_first_new, vector_second_new, weights_new.astype(jnp.bfloat16), vectors_new.astype(jnp.bfloat16))
```

```python
import functools

import jax
import jax.numpy as jnp
from jax import lax
from jax.experimental import pallas as pl
from jax.experimental.pallas import tpu as pltpu
from jax.sharding import PartitionSpec as P

D = 768
HEADS = 12
HEAD_DIM = 64
FF = 3072
STEP = 10
CHUNK = 96
OWN = D // 2
UNITS = FF // 2

ln_eps = 1e-12
beta_one = 0.9
beta_two = 0.999
adam_eps = 1e-08
learn_rate = 0.05
vector_rate = 0.3
decay_rate = 0.01

bf16 = jnp.bfloat16
f32 = jnp.float32
SWAP = [(0, 1), (1, 0)]


def params(limit=48):
    return pltpu.CompilerParams(vmem_limit_bytes=limit * 2**20)


def dot(left, right, over):
    return lax.dot_general(left, right, (over, ((), ())), preferred_element_type=f32)


NT = ((1,), (1,))
NN = ((1,), (0,))
TN = ((0,), (0,))


def swap(value):
    return lax.ppermute(value, "seq", SWAP)


def other_half(array, axis=0):
    half = array.shape[axis] // 2
    return lax.slice_in_dim(array, half, 2 * half, axis=axis)


def pack(rows, index):
    core = lax.axis_index("seq")
    chunks = rows.shape[0] // (2 * CHUNK)
    plain = lax.dynamic_index_in_dim(rows.reshape(chunks, 2, CHUNK, D), core, 1, keepdims=False)
    columns = lax.dynamic_slice_in_dim(rows, core * OWN, OWN, axis=1).reshape(chunks, 2, CHUNK, OWN)
    wide = jnp.concatenate([columns[:, 0], columns[:, 1]], axis=-1)
    where = index * chunks + jnp.arange(chunks)
    is_out = ((where >= 12) & (where < 16))[:, None, None]
    return jnp.where(is_out, wide, plain).reshape(chunks * CHUNK, D)


def unpack(mine, theirs, index):
    core = lax.axis_index("seq")
    chunks = mine.shape[0] // CHUNK
    first = jnp.where(core == 0, mine, theirs).reshape(chunks, CHUNK, D)
    second = jnp.where(core == 0, theirs, mine).reshape(chunks, CHUNK, D)
    plain = jnp.stack([first, second], axis=1)
    upper = jnp.concatenate([first[..., :OWN], second[..., :OWN]], axis=-1)
    lower = jnp.concatenate([first[..., OWN:], second[..., OWN:]], axis=-1)
    wide = jnp.stack([upper, lower], axis=1)
    where = index * chunks + jnp.arange(chunks)
    is_out = ((where >= 12) & (where < 16))[:, None, None, None]
    return jnp.where(is_out, wide, plain).reshape(chunks * 2 * CHUNK, D)


SIDE_X = [(i, i ^ 1) for i in range(16)]
SIDE_Y = [(i, i ^ 2) for i in range(16)]


def up(first, last):
    return [(i, i + 4) for i in range(16) if first <= i // 4 <= last]


def down(first, last):
    return [(i, i - 4) for i in range(16) if first <= i // 4 <= last]


def send(value, pairs):
    return lax.ppermute(value, "dp", pairs)


def pick(plane, *options):
    result = options[-1]
    for i in range(len(options) - 2, -1, -1):
        result = jnp.where(plane == i, options[i], result)
    return result


def in_plane(block):
    half = block.shape[0] // 2
    over_x = send(block, SIDE_X)
    over_y = send(block, SIDE_Y)
    over_xy = jnp.concatenate([send(over_x[:half], SIDE_Y), send(over_y[half:], SIDE_X)], axis=0)
    return (block, over_x, over_y, over_xy)


def place_kernel(piece, me_ref, *refs):
    out_ref, sems = refs[-2], refs[-1]
    slots = [refs[4 * i : 4 * i + 4] for i in range((len(refs) - 2) // 4)]
    me = me_ref[0]
    plane = me // 4
    spot = me % 4
    for z in range(4):
        order = [z] + [i for i in range(4) if i != z]
        slot = order.index(piece)
        if slot >= len(slots):
            continue

        @pl.when(plane == z)
        def _():
            copies = []
            for side in range(4):
                place = side + spot - 2 * (side & spot)
                copies.append(
                    pltpu.make_async_copy(slots[slot][side], out_ref.at[place], sems.at[side])
                )
            for copy in copies:
                copy.start()
            for copy in copies:
                copy.wait()


def place(piece, me, slots):
    flat = [block for slot in slots for block in slot]
    rows = flat[0].shape[0]
    return pl.pallas_call(
        functools.partial(place_kernel, piece),
        in_specs=[pl.BlockSpec(memory_space=pltpu.SMEM)]
        + [pl.BlockSpec(memory_space=pl.ANY)] * len(flat),
        out_specs=pl.BlockSpec(memory_space=pl.ANY),
        out_shape=jax.ShapeDtypeStruct((4, rows, D), bf16),
        scratch_shapes=[pltpu.SemaphoreType.DMA((4,))],
        cost_estimate=pl.CostEstimate(flops=0, bytes_accessed=8 * rows * D * 2, transcendentals=0),
        name="place",
    )(me, *flat).reshape(4 * rows, D)


def gather_pieces(block):
    index = lax.axis_index("dp")
    plane = index // 4
    me = index.reshape(1)
    rise1 = send(block, up(0, 2))
    fall1 = send(block, down(1, 3))
    slot0 = in_plane(block)
    rise2 = send(rise1, up(1, 2))
    fall2 = send(fall1, down(1, 2))
    rise3 = send(rise2, up(2, 2))
    fall3 = send(fall2, down(1, 1))
    slot1 = in_plane(pick(plane, fall1, rise1, rise2, rise3))
    slot2 = in_plane(pick(plane, fall2, fall1, rise1, rise2))
    slot3 = in_plane(pick(plane, fall3, fall2, fall1, rise1))
    return [
        place(0, me, (slot0, slot1)),
        place(1, me, (slot0, slot1, slot2)),
        place(2, me, (slot0, slot1, slot2, slot3)),
        place(3, me, (slot0, slot1, slot2, slot3)),
    ]


def plus(*values):
    total = values[0].astype(f32)
    for value in values[1:]:
        total = total + value.astype(f32)
    return total.astype(bf16)


def reduce_in_plane(piece, spot):
    blocks = piece.reshape(4, -1, D)
    own, side_x, side_y, side_xy = (
        lax.dynamic_index_in_dim(blocks, spot ^ i, 0, keepdims=False) for i in range(4)
    )
    half = own.shape[0] // 2
    from_y = send(side_xy[:half], SIDE_Y)
    from_x = send(side_xy[half:], SIDE_X)
    side_x = jnp.concatenate([plus(side_x[:half], from_y), side_x[half:]], axis=0)
    side_y = jnp.concatenate([side_y[:half], plus(side_y[half:], from_x)], axis=0)
    return plus(own, send(side_x, SIDE_X), send(side_y, SIDE_Y))


def reduce_pieces(pieces, index):
    plane, spot = index // 4, index % 4
    three, two, one, zero = (reduce_in_plane(piece, spot) for piece in pieces)
    three = plus(three, send(three, up(0, 0)))
    three = plus(three, send(three, up(1, 1)))
    three = plus(three, send(three, up(2, 2)))
    two = plus(two, send(two, up(0, 0) + down(3, 3)))
    two = plus(two, send(two, up(1, 1)))
    one = plus(one, send(one, down(3, 3) + up(0, 0)))
    one = plus(one, send(one, down(2, 2)))
    zero = plus(zero, send(zero, down(3, 3)))
    zero = plus(zero, send(zero, down(2, 2)))
    zero = plus(zero, send(zero, down(1, 1)))
    return pick(plane, zero, one, two, three)


def sum_ranks(value, ranks):
    if ranks & (ranks - 1):
        return lax.psum(value, ("dp", "seq"))
    value = value + swap(value)
    step = 1
    while step < ranks:
        value = value + lax.ppermute(value, "dp", [(i, i ^ step) for i in range(ranks)])
        step *= 2
    return value


def gather_vectors(low_vectors, ranks):
    if ranks & (ranks - 1):
        return lax.all_gather(low_vectors, "dp", axis=1, tiled=True).astype(f32)
    count, width = low_vectors.shape
    index = lax.axis_index("dp")
    spread = jnp.zeros((ranks, count, width), bf16)
    spread = lax.dynamic_update_slice(spread, low_vectors[None], (index, 0, 0))
    spread = spread.transpose(1, 0, 2).reshape(count, ranks * width)
    step = 1
    while step < ranks:
        spread = spread + lax.ppermute(spread, "dp", [(i, i ^ step) for i in range(ranks)])
        step *= 2
    return spread.astype(f32)


def selection(span, kind, source, half_len):
    chosen = span == 1
    masked = chosen & (kind < 8)
    swapped = chosen & (kind == 8)
    here = lax.broadcasted_iota(jnp.int32, (1, half_len), 1)
    origin = jnp.where(masked, -1, jnp.where(swapped, source, here))
    rows = lax.broadcasted_iota(jnp.int32, (half_len, half_len), 0)
    one_hot = (rows == origin).astype(f32).astype(bf16)
    first = lax.broadcasted_iota(jnp.int32, (16, half_len), 0) == 0
    mask_rows = jnp.where(first & masked, 1.0, 0.0).astype(bf16)
    return one_hot, mask_rows


def corrupt_kernel(span_ref, kind_ref, from_ref, hidden_ref, mask_ref, out_ref):
    seqs, half_len = span_ref.shape
    for s in range(seqs):
        rows = slice(s, s + 1)
        one_hot, mask_rows = selection(
            span_ref[rows, :], kind_ref[rows, :], from_ref[rows, :], half_len
        )
        picked = dot(one_hot, hidden_ref[s], TN) + dot(mask_rows, mask_ref[...], TN)
        out_ref[s] = picked.astype(bf16)


def corrupt(span, kind, source, hidden, mask_row):
    mask = jnp.broadcast_to(mask_row.astype(bf16)[None], (16, D))
    return pl.pallas_call(
        corrupt_kernel,
        out_shape=jax.ShapeDtypeStruct(hidden.shape, bf16),
        compiler_params=params(),
        name="corrupt",
    )(span, kind, source, hidden, mask)


def corrupt_back_kernel(span_ref, kind_ref, from_ref, grad_ref, partial_ref, out_ref, mask_ref):
    seqs, half_len = span_ref.shape
    mask_sum = jnp.zeros((16, D), f32)
    for s in range(seqs):
        rows = slice(s, s + 1)
        one_hot, mask_rows = selection(
            span_ref[rows, :], kind_ref[rows, :], from_ref[rows, :], half_len
        )
        grad = grad_ref[s] + partial_ref[s].astype(f32)
        high = grad.astype(bf16)
        low = (grad - high.astype(f32)).astype(bf16)
        out_ref[s] = dot(one_hot, high, NN) + dot(one_hot, low, NN)
        mask_sum = mask_sum + dot(mask_rows, high, NN) + dot(mask_rows, low, NN)
    mask_ref[...] = mask_sum


def corrupt_back(span, kind, source, grad, partial):
    return pl.pallas_call(
        corrupt_back_kernel,
        out_shape=[
            jax.ShapeDtypeStruct(grad.shape, f32),
            jax.ShapeDtypeStruct((16, D), f32),
        ],
        compiler_params=params(),
        name="corrupt_back",
    )(span, kind, source, grad, partial)


def attend_kernel(u_ref, w_ref, bias_ref, qkv_ref, low_ref, wide_ref, lse_ref):
    half_len = u_ref.shape[2]
    rows = u_ref[:, 0].reshape(2 * half_len, D)
    projected = (dot(rows, w_ref[...], NT) + bias_ref[...]).astype(bf16)
    qkv_ref[:, 0] = projected.reshape(2, half_len, 3 * OWN)
    wide, totals = [], []
    for h in range(OWN // HEAD_DIM):
        columns = slice(h * HEAD_DIM, (h + 1) * HEAD_DIM)
        query = projected[:, :OWN][:, columns] * bf16(HEAD_DIM**-0.5)
        key = projected[:, OWN : 2 * OWN][:, columns]
        value = projected[:, 2 * OWN :][:, columns]
        scores = dot(query, key, NT)
        top = jnp.max(scores, axis=-1, keepdims=True)
        exponents = jnp.exp(scores - top)
        total = jnp.sum(exponents, axis=-1, keepdims=True)
        probabilities = (exponents / total).astype(bf16)
        wide.append(dot(probabilities, value, NN))
        totals.append(top + jnp.log(total))
    attended = jnp.concatenate(wide, axis=-1)
    wide_ref[:, 0] = attended.reshape(2, half_len, OWN)
    low_ref[:, 0] = attended.astype(bf16).reshape(2, half_len, OWN)
    fill = jnp.zeros((2 * half_len, 128 - len(totals)), f32)
    lse_ref[0] = jnp.concatenate(totals + [fill], axis=-1).T[:8]


def attend(u_all, w_own, bias):
    _, seqs, half_len, _ = u_all.shape
    block = lambda width: pl.BlockSpec((2, 1, half_len, width), lambda s: (0, s, 0, 0))
    flops = seqs * (2 * 512 * D * 3 * OWN + 4 * 6 * 512 * 512 * 256)
    return pl.pallas_call(
        attend_kernel,
        grid=(seqs,),
        in_specs=[
            block(D),
            pl.BlockSpec((3 * OWN, D), lambda s: (0, 0)),
            pl.BlockSpec((1, 3 * OWN), lambda s: (0, 0)),
        ],
        out_specs=[
            block(3 * OWN),
            block(OWN),
            block(OWN),
            pl.BlockSpec((1, 8, 2 * half_len), lambda s: (s, 0, 0)),
        ],
        out_shape=[
            jax.ShapeDtypeStruct((2, seqs, half_len, 3 * OWN), bf16),
            jax.ShapeDtypeStruct((2, seqs, half_len, OWN), bf16),
            jax.ShapeDtypeStruct((2, seqs, half_len, OWN), f32),
            jax.ShapeDtypeStruct((seqs, 8, 2 * half_len), f32),
        ],
        cost_estimate=pl.CostEstimate(
            flops=flops, bytes_accessed=12 * 2**20, transcendentals=seqs * 6 * 512 * 512
        ),
        compiler_params=params(),
        name="attend",
    )(u_all, w_own, bias)


def attend_back_kernel(qkv_ref, grad_ref, wo_ref, wide_ref, lse_ref, out_ref, sums_ref):
    half_len = qkv_ref.shape[2]
    length = 2 * half_len
    projected = qkv_ref[:, 0].reshape(length, 3 * OWN)
    grad = dot(grad_ref[:, 0].reshape(length, D), wo_ref[...], NN).astype(bf16)
    product = grad.astype(f32) * wide_ref[:, 0].reshape(length, OWN)
    heads = OWN // HEAD_DIM
    deltas = [
        jnp.sum(product[:, h * HEAD_DIM : (h + 1) * HEAD_DIM], axis=-1, keepdims=True)
        for h in range(heads)
    ]
    fill = jnp.zeros((length, 128 - heads), f32)
    delta_rows = jnp.concatenate(deltas + [fill], axis=-1).T
    parts = [[], [], []]
    for h in range(heads):
        columns = slice(h * HEAD_DIM, (h + 1) * HEAD_DIM)
        query = projected[:, :OWN][:, columns] * bf16(HEAD_DIM**-0.5)
        key = projected[:, OWN : 2 * OWN][:, columns]
        value = projected[:, 2 * OWN :][:, columns]
        grad_head = grad[:, columns]
        weights = jnp.exp(dot(key, query, NT) - lse_ref[0, h : h + 1, :])
        grad_weights = dot(value, grad_head, NT)
        grad_scores = (weights * (grad_weights - delta_rows[h : h + 1, :])).astype(bf16)
        parts[0].append(dot(grad_scores, key, TN) * HEAD_DIM**-0.5)
        parts[1].append(dot(grad_scores, query, NN))
        parts[2].append(dot(weights.astype(bf16), grad_head, NN))
    result = jnp.concatenate(parts[0] + parts[1] + parts[2], axis=-1).astype(bf16)
    out_ref[:, 0] = result.reshape(2, half_len, 3 * OWN)
    sums = jnp.sum(result.astype(f32), axis=0, keepdims=True)

    @pl.when(pl.program_id(0) == 0)
    def _():
        sums_ref[...] = jnp.zeros_like(sums_ref)

    sums_ref[...] += sums


def attend_back(qkv, grad_all, wo_own, wide, lse):
    _, seqs, half_len, _ = qkv.shape
    block = lambda width: pl.BlockSpec((2, 1, half_len, width), lambda s: (0, s, 0, 0))
    flops = seqs * (2 * 512 * D * OWN + 10 * 6 * 512 * 512 * 256)
    return pl.pallas_call(
        attend_back_kernel,
        grid=(seqs,),
        in_specs=[
            block(3 * OWN),
            block(D),
            pl.BlockSpec((D, OWN), lambda s: (0, 0)),
            block(OWN),
            pl.BlockSpec((1, 8, 2 * half_len), lambda s: (s, 0, 0)),
        ],
        out_specs=[block(3 * OWN), pl.BlockSpec((1, 3 * OWN), lambda s: (0, 0))],
        out_shape=[
            jax.ShapeDtypeStruct((2, seqs, half_len, 3 * OWN), bf16),
            jax.ShapeDtypeStruct((1, 3 * OWN), f32),
        ],
        cost_estimate=pl.CostEstimate(
            flops=flops, bytes_accessed=12 * 2**20, transcendentals=seqs * 6 * 512 * 512
        ),
        compiler_params=params(),
        name="attend_back",
    )(qkv, grad_all, wo_own, wide, lse)


def hidden_kernel(h_ref, w_ref, bias_ref, gelu_ref, slope_ref):
    points = dot(h_ref[...], w_ref[...], NT) + bias_ref[...]
    below = 0.5 * (1.0 + lax.erf(points * 2**-0.5))
    density = jnp.exp(-0.5 * points * points) * 0.3989422804014327
    gelu_ref[...] = (points * below).astype(bf16)
    slope_ref[...] = (below + points * density).astype(bf16)


def hidden_units(h_rows, w_in, bias):
    rows = h_rows.shape[0]
    units = w_in.shape[0]
    width = 256
    block = pl.BlockSpec((rows, width), lambda i: (0, i))
    return pl.pallas_call(
        hidden_kernel,
        grid=(units // width,),
        in_specs=[
            pl.BlockSpec((rows, D), lambda i: (0, 0)),
            pl.BlockSpec((width, D), lambda i: (i, 0)),
            pl.BlockSpec((1, width), lambda i: (0, i)),
        ],
        out_specs=[block, block],
        out_shape=[jax.ShapeDtypeStruct((rows, units), bf16)] * 2,
        cost_estimate=pl.CostEstimate(
            flops=2 * rows * units * D,
            bytes_accessed=4 * rows * units + 2 * rows * D,
            transcendentals=2 * rows * units,
        ),
        compiler_params=params(),
        name="hidden_units",
    )(h_rows, w_in, bias)


def norm(values):
    center = values - jnp.mean(values, axis=-1, keepdims=True)
    inv_std = lax.rsqrt(jnp.mean(center * center, axis=-1, keepdims=True) + ln_eps)
    return center * inv_std, inv_std


def norm_backward(upstream, normed, inv_std, gain):
    scaled = upstream * gain
    return inv_std * (
        scaled
        - jnp.mean(scaled, axis=-1, keepdims=True)
        - normed * jnp.mean(scaled * normed, axis=-1, keepdims=True)
    )


def adam_step(master, first_old, second, gradient, decay_on, step_rate):
    first_new = beta_one * first_old + (1.0 - beta_one) * gradient
    second_new = beta_two * second + (1.0 - beta_two) * gradient * gradient
    fix_one = 1.0 - beta_one**STEP
    fix_two = 1.0 - beta_two**STEP
    update = first_new / fix_one / (jnp.sqrt(second_new / fix_two) + adam_eps)
    return (master - step_rate * (update + decay_on * master), first_new, second_new)


def own_columns(value):
    return lax.dynamic_slice_in_dim(value, lax.axis_index("seq") * OWN, OWN, axis=value.ndim - 1)


def shards(
    ranks,
    hidden,
    span_mask,
    replace_kind,
    replace_from,
    weights,
    vectors,
    weight_first,
    weight_second,
    vector_first,
    vector_second,
    cotangent,
):
    seqs, half_len, _ = hidden.shape
    rows = seqs * half_len
    index = lax.axis_index("dp")
    core = lax.axis_index("seq")

    low_weights = weights.astype(bf16)
    vals = gather_vectors(vectors.astype(bf16), ranks)
    if ranks == 16:
        pieces = gather_pieces(pack(low_weights, index))
    else:
        whole = pack(lax.all_gather(low_weights, "dp", axis=0, tiled=True), 0)
        pieces = [whole[i * 12 * CHUNK : (i + 1) * 12 * CHUNK] for i in range(4)]
    piece0, piece1, piece2, piece3 = pieces

    u_own = corrupt(span_mask, replace_kind, replace_from, hidden, vals[8])
    u_all = jnp.stack([u_own, swap(u_own)])

    halves = piece0.reshape(3, 2, 2, CHUNK, D)
    mine = lax.dynamic_index_in_dim(halves, core, 1, keepdims=False)
    theirs = swap(lax.dynamic_index_in_dim(halves, 1 - core, 1, keepdims=False))
    w_qkv = jnp.where(
        core == 0, jnp.stack([mine, theirs], axis=2), jnp.stack([theirs, mine], axis=2)
    ).reshape(3 * OWN, D)
    bias = jnp.concatenate(
        [own_columns(vals[0:1]), jnp.zeros((1, OWN), f32), own_columns(vals[1:2])], axis=-1
    )
    qkv, attended, attended_wide, lse = attend(u_all, w_qkv, bias)

    out_pack = piece1[: 4 * CHUNK].reshape(4, CHUNK, 2, OWN)
    wo_own = out_pack.transpose(0, 2, 1, 3).reshape(D, OWN)
    wo_other = swap(wo_own)
    from_other = swap(attended[1]).reshape(rows, OWN)
    branch = (
        dot(attended[0].reshape(rows, OWN), wo_own, NT) + dot(from_other, wo_other, NT) + vals[2]
    )
    normed_one, inv_one = norm(u_own.reshape(rows, D).astype(f32) + branch)
    hidden_one = normed_one * vals[3] + vals[4]
    h_low = hidden_one.astype(bf16)
    h_all = jnp.concatenate([h_low, swap(h_low)], axis=0)

    bias_in = lax.dynamic_index_in_dim(
        vals[9:].reshape(FF // (2 * CHUNK), 2, CHUNK), core, 1, keepdims=False
    ).reshape(1, UNITS)
    half_units = UNITS // 2
    w_in = jnp.concatenate([piece1[4 * CHUNK :], piece2[: 8 * CHUNK]], axis=0)
    gelu_a, slope_a = hidden_units(h_all, piece1[4 * CHUNK :], bias_in[:, :half_units])
    gelu_b, slope_b = hidden_units(h_all, piece2[: 8 * CHUNK], bias_in[:, half_units:])
    gelu = jnp.concatenate([gelu_a, gelu_b], axis=1)
    slope = jnp.concatenate([slope_a, slope_b], axis=1)
    w_down = jnp.concatenate([piece2[8 * CHUNK :], piece3], axis=0)
    feed_other = swap(dot(gelu[rows:], w_down, NN).astype(bf16))
    feed = dot(gelu[:rows], w_down, NN) + feed_other.astype(f32) + vals[5]
    normed_two, inv_two = norm(hidden_one + feed)
    layer_out = normed_two * vals[6] + vals[7]

    grad_out = cotangent.astype(f32).reshape(rows, D)
    grad_two = norm_backward(grad_out, normed_two, inv_two, vals[6])
    grad_feed = grad_two.astype(bf16)
    grad_feed_all = jnp.concatenate([grad_feed, swap(grad_feed)], axis=0)
    grad_down = dot(gelu, grad_feed_all, TN).astype(bf16)
    grad_pre = (dot(grad_feed_all, w_down, NT) * slope.astype(f32)).astype(bf16)
    grad_in = dot(grad_pre, h_all, TN).astype(bf16)
    sent_hidden = swap(dot(grad_pre[rows:], w_in, NN).astype(bf16))
    grad_hidden = grad_two + dot(grad_pre[:rows], w_in, NN) + sent_hidden.astype(f32)
    grad_one = norm_backward(grad_hidden, normed_one, inv_one, vals[3])
    grad_branch = grad_one.astype(bf16)
    grad_branch_all = jnp.concatenate([grad_branch, swap(grad_branch)], axis=0)
    grad_wo = dot(grad_branch_all, attended.reshape(2 * rows, OWN), TN).astype(bf16)
    grad_out_pack = (
        grad_wo.reshape(4, 2, CHUNK, OWN).transpose(0, 2, 1, 3).reshape(4 * CHUNK, D)
    )
    grad_qkv, qkv_sums = attend_back(
        qkv, grad_branch_all.reshape(2, seqs, half_len, D), wo_own, attended_wide, lse
    )
    grad_rows = grad_qkv.reshape(2 * rows, 3 * OWN)
    grad_proj = dot(grad_rows, u_all.reshape(2 * rows, D), TN).astype(bf16)
    sent_inputs = swap(dot(grad_rows[rows:], w_qkv, NN).astype(bf16))
    grad_inputs = grad_one + dot(grad_rows[:rows], w_qkv, NN)
    input_grad, grad_mask = corrupt_back(
        span_mask,
        replace_kind,
        replace_from,
        grad_inputs.reshape(seqs, half_len, D),
        sent_inputs.reshape(seqs, half_len, D),
    )

    halves = grad_proj.reshape(3, 2, 2, CHUNK, D)
    keep = lax.dynamic_index_in_dim(halves, core, 2, keepdims=False)
    give = swap(lax.dynamic_index_in_dim(halves, 1 - core, 2, keepdims=False))
    grad_zero = jnp.where(
        core == 0, jnp.stack([keep, give], axis=1), jnp.stack([give, keep], axis=1)
    ).reshape(12 * CHUNK, D)
    grad_pieces = [
        grad_down[4 * CHUNK :],
        jnp.concatenate([grad_in[8 * CHUNK :], grad_down[: 4 * CHUNK]], axis=0),
        jnp.concatenate([grad_out_pack, grad_in[: 8 * CHUNK]], axis=0),
        grad_zero,
    ]
    if ranks == 16:
        shard_half = reduce_pieces(grad_pieces, index)
        shard_w = unpack(shard_half, swap(shard_half), index).astype(f32)
    else:
        core_rows = jnp.concatenate(grad_pieces[::-1], axis=0)
        whole = unpack(core_rows, swap(core_rows), 0).astype(f32)
        shard_w = lax.psum_scatter(whole, "dp", scatter_dimension=0, tiled=True)
        shard_half = lax.dynamic_slice_in_dim(shard_w, core * OWN, OWN, axis=1)

    def at_own(value, width, step):
        spread = jnp.zeros((1, width), f32)
        return lax.dynamic_update_slice(spread, value, (0, core * step))

    bias_rows = jnp.zeros((FF // (2 * CHUNK), 2, CHUNK), f32)
    bias_rows = lax.dynamic_update_slice(
        bias_rows,
        jnp.sum(grad_pre.astype(f32), axis=0).reshape(FF // (2 * CHUNK), 1, CHUNK),
        (0, core, 0),
    ).reshape(FF // D, D)
    vector_rows = jnp.concatenate(
        [
            at_own(qkv_sums[:, :OWN], D, OWN),
            at_own(qkv_sums[:, 2 * OWN :], D, OWN),
            jnp.stack(
                [
                    jnp.sum(grad_branch.astype(f32), axis=0),
                    jnp.sum(grad_hidden * normed_one, axis=0),
                    jnp.sum(grad_hidden, axis=0),
                    jnp.sum(grad_feed.astype(f32), axis=0),
                    jnp.sum(grad_out * normed_two, axis=0),
                    jnp.sum(grad_out, axis=0),
                ]
            ),
            grad_mask[:1],
            bias_rows,
        ],
        axis=0,
    )
    vector_grad = sum_ranks(vector_rows, ranks)
    width = vectors.shape[1]
    shard_v = lax.dynamic_slice_in_dim(vector_grad, index * width, width, axis=1)

    half32 = shard_half.astype(f32)
    squares = sum_ranks(jnp.sum(half32 * half32).reshape(1, 1), ranks)[0, 0]
    grad_norm = jnp.sqrt(squares + jnp.sum(vector_grad * vector_grad))
    clip = 1.0 / jnp.maximum(grad_norm, 1.0)
    weights_new, weight_first_new, weight_second_new = adam_step(
        weights, weight_first, weight_second, shard_w * clip, decay_rate, learn_rate
    )
    vectors_new, vector_first_new, vector_second_new = adam_step(
        vectors, vector_first, vector_second, shard_v * clip, 0.0, vector_rate
    )
    return (
        layer_out.reshape(seqs, half_len, D),
        input_grad,
        grad_norm,
        weights_new,
        weight_first_new,
        weight_second_new,
        vectors_new,
        vector_first_new,
        vector_second_new,
        weights_new.astype(bf16),
        vectors_new.astype(bf16),
    )


def solution(mesh):
    token = P("dp", "seq", None)
    by_row = P("dp", None)
    by_column = P(None, "dp")
    position = P("dp", "seq")
    in_specs = (
        (token,) + (position,) * 3 + (by_row, by_column, by_row, by_row, by_column, by_column, token)
    )
    out_specs = (token, token, P()) + (by_row,) * 3 + (by_column,) * 3 + (by_row, by_column)
    return jax.shard_map(
        functools.partial(shards, mesh.shape["dp"]),
        mesh=mesh,
        in_specs=in_specs,
        out_specs=out_specs,
        check_vma=False,
    )
```

```python
import functools

import jax
import jax.numpy as jnp
from jax import lax
from jax.experimental import pallas as pl
from jax.experimental.pallas import tpu as pltpu
from jax.sharding import PartitionSpec as P

D = 768
HEAD_DIM = 64
FF = 3072
STEP = 10
CHUNK = 96
OWN = D // 2
UNITS = FF // 2

ln_eps = 1e-12
beta_one = 0.9
beta_two = 0.999
adam_eps = 1e-08
learn_rate = 0.05
vector_rate = 0.3
decay_rate = 0.01

bf16 = jnp.bfloat16
f32 = jnp.float32
SWAP = [(0, 1), (1, 0)]


def params(limit=24):
    return pltpu.CompilerParams(vmem_limit_bytes=limit * 2**20)


def cost(micros):
    return pl.CostEstimate(flops=int(micros), bytes_accessed=0, transcendentals=0)


def dot(left, right, over):
    return lax.dot_general(left, right, (over, ((), ())), preferred_element_type=f32)


NT = ((1,), (1,))
NN = ((1,), (0,))
TN = ((0,), (0,))


def swap(value):
    return lax.ppermute(value, "seq", SWAP)


def pack(rows, index):
    core = lax.axis_index("seq")
    chunks = rows.shape[0] // (2 * CHUNK)
    plain = lax.dynamic_index_in_dim(rows.reshape(chunks, 2, CHUNK, D), core, 1, keepdims=False)
    columns = lax.dynamic_slice_in_dim(rows, core * OWN, OWN, axis=1).reshape(chunks, 2, CHUNK, OWN)
    wide = jnp.concatenate([columns[:, 0], columns[:, 1]], axis=-1)
    where = index * chunks + jnp.arange(chunks)
    is_out = ((where >= 12) & (where < 16))[:, None, None]
    return jnp.where(is_out, wide, plain).reshape(chunks * CHUNK, D)


def unpack(mine, theirs, index):
    core = lax.axis_index("seq")
    chunks = mine.shape[0] // CHUNK
    first = jnp.where(core == 0, mine, theirs).reshape(chunks, CHUNK, D)
    second = jnp.where(core == 0, theirs, mine).reshape(chunks, CHUNK, D)
    plain = jnp.stack([first, second], axis=1)
    upper = jnp.concatenate([first[..., :OWN], second[..., :OWN]], axis=-1)
    lower = jnp.concatenate([first[..., OWN:], second[..., OWN:]], axis=-1)
    wide = jnp.stack([upper, lower], axis=1)
    where = index * chunks + jnp.arange(chunks)
    is_out = ((where >= 12) & (where < 16))[:, None, None, None]
    return jnp.where(is_out, wide, plain).reshape(chunks * 2 * CHUNK, D)


SIDE_X = [(i, i ^ 1) for i in range(16)]
SIDE_Y = [(i, i ^ 2) for i in range(16)]


def up(first, last):
    return [(i, i + 4) for i in range(16) if first <= i // 4 <= last]


def down(first, last):
    return [(i, i - 4) for i in range(16) if first <= i // 4 <= last]


def send(value, pairs):
    return lax.ppermute(value, "dp", pairs)


def pick(plane, *options):
    result = options[-1]
    for i in range(len(options) - 2, -1, -1):
        result = jnp.where(plane == i, options[i], result)
    return result


def barrier(*values):
    return lax.optimization_barrier(values)


HALF = 3 * CHUNK // 2


def top(block):
    return block[:HALF]


def bottom(block):
    return block[HALF:]


def join(first, second):
    return jnp.concatenate([first, second], axis=0)


def planes(step, *targets):
    pairs = [(i, i ^ (4 * step)) for i in range(16)]
    return [pair for pair in pairs if not targets or pair[1] // 4 in targets]


PIECES = ((0, 1, 2, 3), (1, 0, 3, 2), (2, 2, 0, 0), (3, 3, 1, 1))


def gather_steps(block, slots):
    odd = lax.axis_index("dp") // 4 % 2 == 1
    x0, y0 = send(block, SIDE_X), send(block, SIDE_Y)
    s1 = send(block, planes(1))
    x0, y0, s1 = yield x0, y0, s1

    x1, y1 = send(s1, SIDE_X), send(s1, SIDE_Y)
    c0 = send(x0, SIDE_Y)
    s2 = send(jnp.where(odd, s1, block), planes(2))
    x1, y1, c0, s2 = yield x1, y1, c0, s2
    slots.append(((block, 0), (x0, 0), (y0, 0), (c0, 0)))

    x2, y2 = send(s2, SIDE_X), send(s2, SIDE_Y)
    c1 = send(top(x1), SIDE_Y), send(bottom(y1), SIDE_X)
    s3 = send(jnp.where(odd, block, s1), planes(2))
    x2, y2, *c1 = yield x2, y2, *c1
    slots.append(((s1, 0), (x1, 0), (y1, 0), tuple(c1)))

    c2 = send(top(x2), SIDE_Y), send(bottom(y2), SIDE_X)
    *c2, s3 = yield *c2, s3
    slots.append(((s2, 0), (x2, 0), (y2, 0), tuple(c2)))

    x3, y3 = send(s3, SIDE_X), send(s3, SIDE_Y)
    x3, y3 = yield x3, y3
    c3 = send(top(x3), SIDE_Y), send(bottom(y3), SIDE_X)
    slots.append(((s3, 0), (x3, 0), (y3, 0), None))
    c3 = yield c3
    slots[3] = (*slots[3][:3], tuple(c3))


def reduce_steps(grads, plane, result):
    odd = plane % 2 == 1
    own3, x3, y3, c3 = grads[3]
    (got,) = yield (send(c3, SIDE_X),)
    y3 = plus(y3, got)
    (got,) = yield (send(x3, SIDE_X),)
    own3 = plus(own3, got)
    got = yield cross(grads[2])
    x2, y2 = yield across(grads[2], got)
    own2 = plus(grads[2][0], x2, y2)
    own1, x1, y1, c1 = grads[1]
    got3, got1 = yield send(y3, SIDE_Y), send(c1, SIDE_X)
    own3, y1 = plus(own3, got3), plus(y1, got1)
    high = send(jnp.where(odd, own2, own3), planes(1))
    high, got_x, got_y = yield high, send(x1, SIDE_X), send(y1, SIDE_Y)
    high = plus(jnp.where(odd, own3, own2), high)
    own1 = plus(own1, got_x, got_y)
    (got,) = yield (send(own1, up(0, 0) + down(3, 3)),)
    own1 = plus(own1, got)
    yield ()
    got = yield cross(grads[0])
    x0, y0, got = yield *across(grads[0], got), send(own1, down(2, 2))
    own1 = plus(own1, got)
    own0 = plus(grads[0][0], x0, y0)
    got, two = yield send(own0, down(1, 1) + down(3, 3)), send(high, planes(2, 2))
    own0 = plus(own0, got)
    zero, three = yield send(own0, planes(2, 0)), send(high, planes(2, 3))
    result.append(pick(plane, plus(own0, zero), own1, plus(high, two), plus(high, three)))


class Steps:
    def __init__(self, steps):
        self.steps = steps
        self.arrays = next(steps) if steps else ()

    def __call__(self, *values):
        count = len(self.arrays)
        passed = barrier(*self.arrays, *values) if count or values else ()
        if self.steps:
            try:
                self.arrays = self.steps.send(passed[:count])
            except StopIteration:
                self.steps, self.arrays = None, ()
        return passed[count:]


def parts_of(side):
    if side is None:
        return []
    first, second = side
    if isinstance(second, int):
        rows = 3 * CHUNK
        return [(first, second * rows, rows, 0)]
    return [(first, 0, HALF, 0), (second, 0, HALF, HALF)]


def slot_arrays(slots):
    arrays, known = [], {}
    shape = []
    for slot in slots:
        sides = []
        for side in slot:
            parts = []
            for array, start, rows, place in parts_of(side):
                if id(array) not in known:
                    known[id(array)] = len(arrays)
                    arrays.append(array)
                parts.append((known[id(array)], start, rows, place))
            sides.append(tuple(parts))
        shape.append(tuple(sides))
    return arrays, tuple(shape)


def run_copies(pairs, sems):
    copies = [
        pltpu.make_async_copy(source, target, sems.at[i])
        for i, (source, target) in enumerate(pairs)
    ]
    for copy in copies:
        copy.start()
    for copy in copies:
        copy.wait()


def place_heads_kernel(shape, me_ref, *refs):
    mine_ref, give_ref, whole_ref, sems = refs[-4:]
    spot, core, plane = me_ref[0], me_ref[1], me_ref[2]
    for z in range(4):

        @pl.when(plane == z)
        def _():
            pairs = []
            for side in range(4):
                start = 3 * CHUNK * (side + spot - 2 * (side & spot))
                for number, first, rows, place in shape[min(z, 2)][side]:
                    where = pl.ds(pl.multiple_of(start + place, 16), rows)
                    pairs.append((refs[number].at[pl.ds(first, rows)], whole_ref.at[where]))
            run_copies(pairs, sems)

    for ref, who in ((mine_ref, core), (give_ref, 1 - core)):
        for j in range(6):
            chunk = 4 * (j // 2) + 2 * who + j % 2
            ref[j] = whole_ref[pl.ds(pl.multiple_of(chunk * CHUNK, 16), CHUNK)]


def place_heads(me, slots):
    arrays, shape = slot_arrays(slots)
    half = jax.ShapeDtypeStruct((6, CHUNK, D), bf16)
    return pl.pallas_call(
        functools.partial(place_heads_kernel, shape),
        in_specs=[pl.BlockSpec(memory_space=pltpu.SMEM)]
        + [pl.BlockSpec(memory_space=pl.ANY)] * len(arrays),
        out_shape=[half, half],
        scratch_shapes=[pltpu.VMEM((12 * CHUNK, D), bf16), pltpu.SemaphoreType.DMA((8,))],
        compiler_params=params(),
        cost_estimate=cost(1),
        name="place_heads",
    )(me, *arrays)


def place_rest_kernel(shape, held, me_ref, *refs):
    out_ref, in_ref, down_ref, stage_ref, load_sems, store_sems = refs[-6:]
    spot, plane = me_ref[0], me_ref[2]

    def part(pairs, source, first, rows, row):
        while rows:
            if row < 4 * CHUNK:
                chunk, offset = divmod(row, CHUNK)
                count = min(rows, CHUNK - offset)
                targets = []
                for h in range(2):
                    target = 2 * CHUNK * chunk + CHUNK * h + offset
                    targets.append((pl.ds(OWN * h, OWN), out_ref.at[pl.ds(target, count)]))
            else:
                ref, start = (in_ref, 4 * CHUNK) if row < 20 * CHUNK else (down_ref, 20 * CHUNK)
                count = min(rows, start + 16 * CHUNK - row)
                targets = [(slice(None), ref.at[pl.ds(row - start, count)])]
            pairs.append((source.at[pl.ds(first, count)], count, targets))
            row, first, rows = row + count, first + count, rows - count

    for z in range(4):
        for s in range(4):
            pairs = []
            for slot, (number, sides) in zip(shape, held, strict=True):
                piece = PIECES[number][z]
                for side in sides if piece else ():
                    base = 3 * CHUNK * (4 * (piece - 1) + (side ^ s))
                    for array, first, rows, place in slot[side]:
                        part(pairs, refs[array], first, rows, base + place)

            @pl.when((plane == z) & (spot == s))
            def _():
                loads, stores, row = [], [], 0
                for i, (source, count, targets) in enumerate(pairs):
                    spot_rows = pl.ds(row, count)
                    loads.append(
                        pltpu.make_async_copy(source, stage_ref.at[spot_rows], load_sems.at[i])
                    )
                    stores.append([])
                    for columns, target in targets:
                        stores[-1].append(
                            pltpu.make_async_copy(
                                stage_ref.at[spot_rows, columns],
                                target,
                                store_sems.at[2 * i + len(stores[-1])],
                            )
                        )
                    row += count
                for load in loads:
                    load.start()
                for load, store in zip(loads, stores, strict=True):
                    load.wait()
                    for copy in store:
                        copy.start()
                for store in stores:
                    for copy in store:
                        copy.wait()


def place_rest(me, slots, held, state):
    arrays, shape = slot_arrays(
        [[slots[i][side] if side in sides else None for side in range(4)] for i, sides in held]
    )
    units = jax.ShapeDtypeStruct((UNITS, D), bf16)
    anywhere = pl.BlockSpec(memory_space=pl.ANY)
    return pl.pallas_call(
        functools.partial(place_rest_kernel, shape, held),
        in_specs=[pl.BlockSpec(memory_space=pltpu.SMEM)] + [anywhere] * (len(arrays) + len(state)),
        out_specs=[anywhere] * 3,
        out_shape=[jax.ShapeDtypeStruct((D, OWN), bf16), units, units],
        input_output_aliases={1 + len(arrays) + i: i for i in range(len(state))},
        scratch_shapes=[
            pltpu.VMEM((24 * CHUNK, D), bf16),
            pltpu.SemaphoreType.DMA((32,)),
            pltpu.SemaphoreType.DMA((64,)),
        ],
        compiler_params=params(),
        cost_estimate=cost(1),
        name="place_rest",
    )(me, *arrays, *state)


def plus(*values):
    total = values[0].astype(f32)
    for value in values[1:]:
        total = total + value.astype(f32)
    return total.astype(bf16)


def cross(sides):
    return send(sides[3], SIDE_Y), send(sides[4], SIDE_X)


def across(sides, crossed):
    over_x = join(plus(top(sides[1]), crossed[0]), bottom(sides[1]))
    over_y = join(top(sides[2]), plus(bottom(sides[2]), crossed[1]))
    return send(over_x, SIDE_X), send(over_y, SIDE_Y)


def gather_vectors(low_vectors, ranks):
    count, width = low_vectors.shape
    block = jnp.pad(low_vectors, ((0, 16 - count), (0, 128 - width)))
    blocks = lax.all_to_all(jnp.broadcast_to(block, (ranks, 16, 128)), "dp", 0, 0, tiled=True)
    return blocks[:, :count, :width].transpose(1, 0, 2).reshape(count, ranks * width).astype(f32)


def scatter_vectors(rows, ranks, count):
    width = D // ranks
    blocks = rows.reshape(16, ranks, width).transpose(1, 0, 2)
    blocks = jnp.pad(blocks, ((0, 0), (0, 0), (0, 128 - width)))
    blocks = jnp.repeat(blocks, 2, axis=0)
    blocks = lax.all_to_all(blocks, ("dp", "seq"), 0, 0, tiled=True)
    return jnp.sum(blocks, axis=0)[:count, :width]


def sum_everywhere(value, ranks):
    blocks = lax.all_to_all(
        jnp.full((2 * ranks, 8, 128), value), ("dp", "seq"), 0, 0, tiled=True
    )
    return jnp.sum(blocks[:, 0, 0])


def selection(span, kind, source, half_len):
    chosen = span == 1
    masked = chosen & (kind < 8)
    swapped = chosen & (kind == 8)
    here = lax.broadcasted_iota(jnp.int32, (1, half_len), 1)
    origin = jnp.where(masked, -1, jnp.where(swapped, source, here))
    rows = lax.broadcasted_iota(jnp.int32, (half_len, half_len), 0)
    one_hot = (rows == origin).astype(f32).astype(bf16)
    first = lax.broadcasted_iota(jnp.int32, (16, half_len), 0) == 0
    mask_rows = jnp.where(first & masked, 1.0, 0.0).astype(bf16)
    return one_hot, mask_rows


def corrupt_kernel(span_ref, kind_ref, from_ref, hidden_ref, mask_ref, out_ref):
    seqs, half_len = span_ref.shape
    for s in range(seqs):
        rows = slice(s, s + 1)
        one_hot, mask_rows = selection(
            span_ref[rows, :], kind_ref[rows, :], from_ref[rows, :], half_len
        )
        picked = dot(one_hot, hidden_ref[s], TN) + dot(mask_rows, mask_ref[...], TN)
        out_ref[s] = picked.astype(bf16)


def corrupt(span, kind, source, hidden, mask_row):
    mask = jnp.broadcast_to(mask_row.astype(bf16)[None], (16, D))
    return pl.pallas_call(
        corrupt_kernel,
        out_shape=jax.ShapeDtypeStruct(hidden.shape, bf16),
        compiler_params=params(),
        name="corrupt",
    )(span, kind, source, hidden, mask)


def corrupt_back_kernel(
    span_ref, kind_ref, from_ref, grad_ref, own_ref, partial_ref, out_ref, mask_ref
):
    seqs, half_len = span_ref.shape
    mask_sum = jnp.zeros((16, D), f32)
    for s in range(seqs):
        rows = slice(s, s + 1)
        block = pl.ds(s * half_len, half_len)
        one_hot, mask_rows = selection(
            span_ref[rows, :], kind_ref[rows, :], from_ref[rows, :], half_len
        )
        grad = grad_ref[block] + own_ref[block] + partial_ref[block].astype(f32)
        high = grad.astype(bf16)
        low = (grad - high.astype(f32)).astype(bf16)
        out_ref[s] = dot(one_hot, high, NN) + dot(one_hot, low, NN)
        mask_sum = mask_sum + dot(mask_rows, high, NN) + dot(mask_rows, low, NN)
    mask_ref[...] = mask_sum


def corrupt_back(span, kind, source, grad, own, partial):
    seqs, half_len = span.shape
    return pl.pallas_call(
        corrupt_back_kernel,
        out_shape=[
            jax.ShapeDtypeStruct((seqs, half_len, D), f32),
            jax.ShapeDtypeStruct((16, D), f32),
        ],
        compiler_params=params(),
        cost_estimate=cost(1),
        name="corrupt_back",
    )(span, kind, source, grad, own, partial)


def attend_kernel(
    me_ref, own_ref, other_ref, mine_ref, theirs_ref, vals_ref, w_ref, qkv_ref, low_ref, wide_ref, lse_ref
):
    half_len = own_ref.shape[1]
    core = me_ref[1]

    @pl.when(pl.program_id(0) == 0)
    def _():
        for j in range(6):
            for ref, which in ((mine_ref, core), (theirs_ref, 1 - core)):
                where = pl.ds(pl.multiple_of((2 * j + which) * CHUNK, 16), CHUNK)
                w_ref[where] = ref[j]

    rows = jnp.concatenate([own_ref[0], other_ref[0]], axis=0)
    columns = pl.ds(pl.multiple_of(core * OWN, 128), OWN)
    bias = jnp.concatenate(
        [vals_ref[0:1, columns], jnp.zeros((1, OWN), f32), vals_ref[1:2, columns]], axis=-1
    )
    projected = (dot(rows, w_ref[...], NT) + bias).astype(bf16)
    qkv_ref[:, 0] = projected.reshape(2, half_len, 3 * OWN)
    wide, totals = [], []
    for h in range(OWN // HEAD_DIM):
        columns = slice(h * HEAD_DIM, (h + 1) * HEAD_DIM)
        query = projected[:, :OWN][:, columns] * bf16(HEAD_DIM**-0.5)
        key = projected[:, OWN : 2 * OWN][:, columns]
        value = projected[:, 2 * OWN :][:, columns]
        scores = dot(query, key, NT)
        highest = jnp.max(scores, axis=-1, keepdims=True)
        exponents = jnp.exp(scores - highest)
        total = jnp.sum(exponents, axis=-1, keepdims=True)
        probabilities = (exponents / total).astype(bf16)
        wide.append(dot(probabilities, value, NN))
        totals.append(highest + jnp.log(total))
    attended = jnp.concatenate(wide, axis=-1)
    wide_ref[:, 0] = attended.reshape(2, half_len, OWN)
    low_ref[:, 0] = attended.astype(bf16).reshape(2, half_len, OWN)
    fill = jnp.zeros((2 * half_len, 128 - len(totals)), f32)
    lse_ref[0] = jnp.concatenate(totals + [fill], axis=-1).T[:8]


def whole(*shape):
    return pl.BlockSpec(shape, lambda *_: (0,) * len(shape))


def attend(me, u_own, u_other, mine, theirs, vals):
    seqs, half_len, _ = u_own.shape
    block = lambda width: pl.BlockSpec((2, 1, half_len, width), lambda s: (0, s, 0, 0))
    token = pl.BlockSpec((1, half_len, D), lambda s: (s, 0, 0))
    return pl.pallas_call(
        attend_kernel,
        grid=(seqs,),
        in_specs=[
            pl.BlockSpec(memory_space=pltpu.SMEM),
            token,
            token,
            whole(6, CHUNK, D),
            whole(6, CHUNK, D),
            whole(*vals.shape),
        ],
        out_specs=[
            whole(3 * OWN, D),
            block(3 * OWN),
            block(OWN),
            block(OWN),
            pl.BlockSpec((1, 8, 2 * half_len), lambda s: (s, 0, 0)),
        ],
        out_shape=[
            jax.ShapeDtypeStruct((3 * OWN, D), bf16),
            jax.ShapeDtypeStruct((2, seqs, half_len, 3 * OWN), bf16),
            jax.ShapeDtypeStruct((2, seqs, half_len, OWN), bf16),
            jax.ShapeDtypeStruct((2, seqs, half_len, OWN), f32),
            jax.ShapeDtypeStruct((seqs, 8, 2 * half_len), f32),
        ],
        cost_estimate=cost(3),
        compiler_params=params(),
        name="attend",
    )(me, u_own, u_other, mine, theirs, vals)


def attend_back_kernel(
    skip, qkv_ref, own_ref, other_ref, wo_ref, wide_ref, lse_ref, *refs
):
    out_ref, sums_ref = refs[skip:]
    half_len = qkv_ref.shape[2]
    length = 2 * half_len
    projected = qkv_ref[:, 0].reshape(length, 3 * OWN)
    rows = jnp.concatenate([own_ref[0], other_ref[0]], axis=0)
    grad = dot(rows, wo_ref[...], NN).astype(bf16)
    product = grad.astype(f32) * wide_ref[:, 0].reshape(length, OWN)
    heads = OWN // HEAD_DIM
    deltas = [
        jnp.sum(product[:, h * HEAD_DIM : (h + 1) * HEAD_DIM], axis=-1, keepdims=True)
        for h in range(heads)
    ]
    fill = jnp.zeros((length, 128 - heads), f32)
    delta_rows = jnp.concatenate(deltas + [fill], axis=-1).T
    parts = [[], [], []]
    for h in range(heads):
        columns = slice(h * HEAD_DIM, (h + 1) * HEAD_DIM)
        query = projected[:, :OWN][:, columns] * bf16(HEAD_DIM**-0.5)
        key = projected[:, OWN : 2 * OWN][:, columns]
        value = projected[:, 2 * OWN :][:, columns]
        grad_head = grad[:, columns]
        weights = jnp.exp(dot(key, query, NT) - lse_ref[0, h : h + 1, :])
        grad_weights = dot(value, grad_head, NT)
        grad_scores = (weights * (grad_weights - delta_rows[h : h + 1, :])).astype(bf16)
        parts[0].append(dot(grad_scores, key, TN) * HEAD_DIM**-0.5)
        parts[1].append(dot(grad_scores, query, NN))
        parts[2].append(dot(weights.astype(bf16), grad_head, NN))
    result = jnp.concatenate(parts[0] + parts[1] + parts[2], axis=-1).astype(bf16)
    out_ref[:, 0] = result.reshape(2, half_len, 3 * OWN)
    sums = jnp.sum(result.astype(f32), axis=0, keepdims=True)

    @pl.when(pl.program_id(0) == 0)
    def _():
        sums_ref[...] = refs[1][...] if skip else jnp.zeros_like(sums_ref)

    sums_ref[...] += sums


def attend_back(qkv, own, other, wo_own, wide, lse, first, count, state):
    _, seqs, half_len, _ = qkv.shape
    block = lambda width: pl.BlockSpec((2, 1, half_len, width), lambda s: (0, s + first, 0, 0))
    token = pl.BlockSpec((1, half_len, D), lambda s: (s + first, 0, 0))
    return pl.pallas_call(
        functools.partial(attend_back_kernel, len(state)),
        grid=(count,),
        in_specs=[
            block(3 * OWN),
            token,
            token,
            whole(D, OWN),
            block(OWN),
            pl.BlockSpec((1, 8, 2 * half_len), lambda s: (s + first, 0, 0)),
        ]
        + ([pl.BlockSpec(memory_space=pl.ANY), whole(1, 3 * OWN)] if state else []),
        out_specs=[block(3 * OWN), whole(1, 3 * OWN)],
        input_output_aliases={6: 0} if state else {},
        out_shape=[
            jax.ShapeDtypeStruct((2, seqs, half_len, 3 * OWN), bf16),
            jax.ShapeDtypeStruct((1, 3 * OWN), f32),
        ],
        cost_estimate=cost(2 * count),
        compiler_params=params(),
        name="attend_back",
    )(qkv, own, other, wo_own, wide, lse, *state)


def norm(values):
    center = values - jnp.mean(values, axis=-1, keepdims=True)
    inv_std = lax.rsqrt(jnp.mean(center * center, axis=-1, keepdims=True) + ln_eps)
    return center * inv_std, inv_std


def norm_backward(upstream, normed, inv_std, gain):
    scaled = upstream * gain
    return inv_std * (
        scaled
        - jnp.mean(scaled, axis=-1, keepdims=True)
        - normed * jnp.mean(scaled * normed, axis=-1, keepdims=True)
    )


def row(ref, i):
    return ref[i : i + 1, :]


def branch_kernel(own_ref, other_ref, u_ref, wo_ref, wo_other_ref, vals_ref, normed_ref, inv_ref, low_ref):
    branch = dot(own_ref[0, 0], wo_ref[...], NT) + dot(other_ref[0], wo_other_ref[...], NT)
    normed, inv = norm(u_ref[0].astype(f32) + branch + row(vals_ref, 2))
    normed_ref[...] = normed
    inv_ref[...] = jnp.broadcast_to(inv, inv_ref.shape)
    low_ref[...] = (normed * row(vals_ref, 3) + row(vals_ref, 4)).astype(bf16)


def attention_branch(attended, from_other, u_own, wo_own, wo_other, vals):
    seqs, half_len, _ = u_own.shape
    rows = pl.BlockSpec((half_len, D), lambda s: (s, 0))
    return pl.pallas_call(
        branch_kernel,
        grid=(seqs,),
        in_specs=[
            pl.BlockSpec((1, 1, half_len, OWN), lambda s: (0, s, 0, 0)),
            pl.BlockSpec((1, half_len, OWN), lambda s: (s, 0, 0)),
            pl.BlockSpec((1, half_len, D), lambda s: (s, 0, 0)),
            whole(D, OWN),
            whole(D, OWN),
            whole(*vals.shape),
        ],
        out_specs=[rows, pl.BlockSpec((half_len, 128), lambda s: (s, 0)), rows],
        out_shape=[
            jax.ShapeDtypeStruct((seqs * half_len, D), f32),
            jax.ShapeDtypeStruct((seqs * half_len, 128), f32),
            jax.ShapeDtypeStruct((seqs * half_len, D), bf16),
        ],
        cost_estimate=cost(1),
        compiler_params=params(),
        name="attention_branch",
    )(attended, from_other, u_own, wo_own, wo_other, vals)


def hidden_kernel(own_ref, other_ref, w_ref, bias_ref, gelu_ref, slope_ref):
    for half, ref in enumerate((own_ref, other_ref)):
        points = dot(ref[...], w_ref[...], NT) + bias_ref[...]
        below = 0.5 * (1.0 + lax.erf(points * 2**-0.5))
        density = jnp.exp(-0.5 * points * points) * 0.3989422804014327
        gelu_ref[half] = (points * below).astype(bf16)
        slope_ref[half] = (below + points * density).astype(bf16)


def hidden_units(h_own, h_other, w_in, bias):
    rows = h_own.shape[0]
    width = 256
    block = pl.BlockSpec((2, rows, width), lambda i: (0, 0, i))
    return pl.pallas_call(
        hidden_kernel,
        grid=(UNITS // width,),
        in_specs=[
            whole(rows, D),
            whole(rows, D),
            pl.BlockSpec((width, D), lambda i: (i, 0)),
            pl.BlockSpec((1, width), lambda i: (0, i)),
        ],
        out_specs=[block, block],
        out_shape=[jax.ShapeDtypeStruct((2, rows, UNITS), bf16)] * 2,
        cost_estimate=cost(3),
        compiler_params=params(),
        name="hidden_units",
    )(h_own, h_other, w_in, bias)


def rows_kernel(left_ref, right_ref, out_ref):
    out_ref[...] = dot(left_ref[0], right_ref[...], NN).astype(out_ref.dtype)


def rows_times(left, half, right, dtype, name):
    _, rows, depth = left.shape
    tile = rows // 3
    return pl.pallas_call(
        rows_kernel,
        grid=(3,),
        in_specs=[pl.BlockSpec((1, tile, depth), lambda i: (half, i, 0)), whole(*right.shape)],
        out_specs=pl.BlockSpec((tile, D), lambda i: (i, 0)),
        out_shape=jax.ShapeDtypeStruct((rows, D), dtype),
        cost_estimate=cost(1),
        compiler_params=params(),
        name=name,
    )(left, right)


def add_sums(sums_ref, *values):
    @pl.when(pl.program_id(0) == 0)
    def _():
        sums_ref[...] = jnp.zeros_like(sums_ref)

    for i, value in enumerate(values):
        sums_ref[i : i + 1, :] += jnp.sum(value, axis=0, keepdims=True)


def finish_kernel(own_ref, other_ref, normed_ref, grad_ref, vals_ref, out_ref, wide_ref, low_ref, sums_ref):
    hidden_one = normed_ref[...] * row(vals_ref, 3) + row(vals_ref, 4)
    feed = own_ref[...] + other_ref[...].astype(f32) + row(vals_ref, 5)
    normed, inv = norm(hidden_one + feed)
    out_ref[...] = normed * row(vals_ref, 6) + row(vals_ref, 7)
    grad = grad_ref[...].astype(f32)
    wide = norm_backward(grad, normed, inv, row(vals_ref, 6))
    low = wide.astype(bf16)
    wide_ref[...] = wide
    low_ref[...] = low
    add_sums(sums_ref, low.astype(f32), grad * normed, grad)


def finish(own, other, normed, grad, vals):
    rows = own.shape[0]
    tile = rows // 3
    block = pl.BlockSpec((tile, D), lambda i: (i, 0))
    return pl.pallas_call(
        finish_kernel,
        grid=(3,),
        in_specs=[block] * 4 + [whole(*vals.shape)],
        out_specs=[block] * 3 + [whole(8, D)],
        out_shape=[
            jax.ShapeDtypeStruct((rows, D), f32),
            jax.ShapeDtypeStruct((rows, D), f32),
            jax.ShapeDtypeStruct((rows, D), bf16),
            jax.ShapeDtypeStruct((8, D), f32),
        ],
        cost_estimate=cost(1),
        compiler_params=params(),
        name="finish",
    )(own, other, normed, grad, vals)


def norm_one_kernel(two_ref, own_ref, other_ref, normed_ref, inv_ref, vals_ref, wide_ref, low_ref, sums_ref):
    grad = two_ref[...] + own_ref[...] + other_ref[...].astype(f32)
    normed = normed_ref[...]
    wide = norm_backward(grad, normed, inv_ref[:, 0:1], row(vals_ref, 3))
    low = wide.astype(bf16)
    wide_ref[...] = wide
    low_ref[...] = low
    add_sums(sums_ref, low.astype(f32), grad * normed, grad)


def norm_one_back(two, own, other, normed, inv, vals):
    rows = own.shape[0]
    tile = rows // 3
    block = pl.BlockSpec((tile, D), lambda i: (i, 0))
    return pl.pallas_call(
        norm_one_kernel,
        grid=(3,),
        in_specs=[block] * 4 + [pl.BlockSpec((tile, 128), lambda i: (i, 0)), whole(*vals.shape)],
        out_specs=[block] * 2 + [whole(8, D)],
        out_shape=[
            jax.ShapeDtypeStruct((rows, D), f32),
            jax.ShapeDtypeStruct((rows, D), bf16),
            jax.ShapeDtypeStruct((8, D), f32),
        ],
        cost_estimate=cost(1),
        compiler_params=params(),
        name="norm_one_back",
    )(two, own, other, normed, inv, vals)


def slope_kernel(grad_ref, w_ref, slope_ref, out_ref, sums_ref):
    low = (dot(grad_ref[...], w_ref[...], NT) * slope_ref[0].astype(f32)).astype(bf16)
    out_ref[0] = low
    sums_ref[...] = jnp.sum(low.astype(f32), axis=0, keepdims=True)


def before_gelu(grad, w_down, slope, half):
    rows = grad.shape[0]
    width = 384
    return pl.pallas_call(
        slope_kernel,
        grid=(UNITS // width,),
        in_specs=[
            whole(rows, D),
            pl.BlockSpec((width, D), lambda i: (i, 0)),
            pl.BlockSpec((1, rows, width), lambda i: (half, 0, i)),
        ],
        out_specs=[
            pl.BlockSpec((1, rows, width), lambda i: (0, 0, i)),
            pl.BlockSpec((1, width), lambda i: (0, i)),
        ],
        out_shape=[
            jax.ShapeDtypeStruct((1, rows, UNITS), bf16),
            jax.ShapeDtypeStruct((1, UNITS), f32),
        ],
        cost_estimate=cost(1),
        compiler_params=params(),
        name="before_gelu",
    )(grad, w_down, slope)


def rows_of(count):
    return jax.ShapeDtypeStruct((count, D), bf16)


CROSS = ((0, 0, 288), (1, 0, 288), (2, 0, 288), (3, 0, 144), (3, 144, 144))
PLAIN = ((0, 0, 288), (1, 0, 288), (2, 0, 288), (3, 0, 288))


def side_rows(spot, side, first, rows):
    start = 3 * CHUNK * (side + spot - 2 * (side & spot)) + first
    return pl.ds(pl.multiple_of(start, 16), rows)


def write_sides(order, spot, piece_ref, outs):
    for out, (side, first, rows) in zip(outs, order, strict=True):
        out[...] = piece_ref[side_rows(spot, side, first, rows)]


def rows_at(step):
    return pl.ds(pl.multiple_of(step * OWN, 16), OWN)


def two_halves(left, left_other, right, right_other):
    return dot(left, right, TN) + dot(left_other, right_other, TN)


def grads3_kernel(me_ref, g_ref, d_ref, d_other_ref, *refs):
    piece_ref = refs[-1]
    step = pl.program_id(0)
    piece_ref[rows_at(step)] = two_halves(
        g_ref[0], g_ref[1], d_ref[...], d_other_ref[...]
    ).astype(bf16)

    @pl.when(step == 2)
    def _():
        write_sides(PLAIN, me_ref[0], piece_ref, refs[:-1])


def grads2_kernel(me_ref, z_ref, z_other_ref, h_ref, h_other_ref, g_ref, d_ref, d_other_ref, *refs):
    piece_ref = refs[-1]
    step = pl.program_id(0)

    @pl.when(step < 2)
    def _():
        piece_ref[rows_at(step)] = two_halves(
            z_ref[0], z_other_ref[0], h_ref[...], h_other_ref[...]
        ).astype(bf16)

    @pl.when(step == 2)
    def _():
        piece_ref[rows_at(step)] = two_halves(
            g_ref[0], g_ref[1], d_ref[...], d_other_ref[...]
        ).astype(bf16)
        write_sides(CROSS, me_ref[0], piece_ref, refs[:-1])


def grads1_kernel(me_ref, z_ref, z_other_ref, h_ref, h_other_ref, a_ref, a_other_ref, att_ref, *refs):
    piece_ref = refs[-1]
    step = pl.program_id(0)

    @pl.when(step < 2)
    def _():
        piece_ref[rows_at(step + 1)] = two_halves(
            z_ref[0], z_other_ref[0], h_ref[...], h_other_ref[...]
        ).astype(bf16)

    @pl.when(step == 2)
    def _():
        wo = two_halves(a_ref[...], a_other_ref[...], att_ref[0], att_ref[1]).astype(bf16)
        for j in range(4):
            upper = wo[2 * CHUNK * j : 2 * CHUNK * j + CHUNK]
            lower = wo[2 * CHUNK * j + CHUNK : 2 * CHUNK * (j + 1)]
            piece_ref[CHUNK * j : CHUNK * (j + 1)] = jnp.concatenate([upper, lower], axis=-1)
        write_sides(PLAIN, me_ref[0], piece_ref, refs[:-1])


def grads_call(kernel, order, specs, arrays, name):
    return pl.pallas_call(
        kernel,
        grid=(3,),
        in_specs=[pl.BlockSpec(memory_space=pltpu.SMEM)] + specs,
        out_specs=[whole(count, D) for _, _, count in order],
        out_shape=[rows_of(count) for _, _, count in order],
        scratch_shapes=[pltpu.VMEM((12 * CHUNK, D), bf16)],
        cost_estimate=cost(2),
        compiler_params=params(),
        name=name,
    )(*arrays)


def grads0_kernel(me_ref, g_ref, u_ref, u_other_ref, keep_ref, give_ref, piece_ref):
    core = me_ref[1]
    step = pl.program_id(0)
    piece_ref[rows_at(step)] = two_halves(
        g_ref[0], g_ref[1], u_ref[...], u_other_ref[...]
    ).astype(bf16)

    @pl.when(step == 2)
    def _():
        for j in range(6):
            for ref, which in ((keep_ref, core), (give_ref, 1 - core)):
                where = pl.ds(pl.multiple_of((2 * j + which) * CHUNK, 16), CHUNK)
                ref[j] = piece_ref[where]


def grads0(me, grad, u_own, u_other):
    rows = grad.shape[1]
    half = jax.ShapeDtypeStruct((6, CHUNK, D), bf16)
    return pl.pallas_call(
        grads0_kernel,
        grid=(3,),
        in_specs=[
            pl.BlockSpec(memory_space=pltpu.SMEM),
            pl.BlockSpec((2, rows, OWN), lambda i: (0, 0, i)),
            whole(rows, D),
            whole(rows, D),
        ],
        out_specs=[whole(6, CHUNK, D)] * 2,
        out_shape=[half, half],
        scratch_shapes=[pltpu.VMEM((12 * CHUNK, D), bf16)],
        cost_estimate=cost(2),
        compiler_params=params(),
        name="grads0",
    )(me, grad, u_own, u_other)


def regroup_kernel(me_ref, keep_ref, take_ref, *refs):
    piece_ref = refs[-1]
    core = me_ref[1]
    for ref, who in ((keep_ref, core), (take_ref, 1 - core)):
        for j in range(6):
            chunk = 4 * (j // 2) + 2 * who + j % 2
            piece_ref[pl.ds(pl.multiple_of(chunk * CHUNK, 16), CHUNK)] = ref[j]
    write_sides(CROSS, me_ref[0], piece_ref, refs[:-1])


def regroup(me, keep, take):
    return pl.pallas_call(
        regroup_kernel,
        in_specs=[pl.BlockSpec(memory_space=pltpu.SMEM)]
        + [pl.BlockSpec(memory_space=pltpu.VMEM)] * 2,
        out_shape=[rows_of(count) for _, _, count in CROSS],
        scratch_shapes=[pltpu.VMEM((12 * CHUNK, D), bf16)],
        cost_estimate=cost(1),
        compiler_params=params(),
        name="regroup",
    )(me, keep, take)


def vector_kernel(me_ref, qkv_ref, one_ref, two_ref, mask_ref, bias_ref, out_ref):
    out_ref[...] = jnp.zeros_like(out_ref)
    columns = pl.ds(pl.multiple_of(me_ref[1] * OWN, 128), OWN)
    out_ref[0:1, columns] = qkv_ref[:, :OWN]
    out_ref[1:2, columns] = qkv_ref[:, 2 * OWN :]
    out_ref[2:5, :] = one_ref[0:3, :]
    out_ref[5:8, :] = two_ref[0:3, :]
    out_ref[8:9, :] = mask_ref[0:1, :]
    out_ref[9:13, :] = bias_ref[...]


def vector_rows(me, qkv_sums, one_sums, two_sums, mask_sums, bias_sums):
    return pl.pallas_call(
        vector_kernel,
        in_specs=[pl.BlockSpec(memory_space=pltpu.SMEM)]
        + [pl.BlockSpec(memory_space=pltpu.VMEM)] * 5,
        out_shape=jax.ShapeDtypeStruct((16, D), f32),
        cost_estimate=cost(1),
        name="vector_rows",
    )(me, qkv_sums, one_sums, two_sums, mask_sums, bias_sums)


def adam_step(master, first_old, second, gradient, decay_on, step_rate):
    first_new = beta_one * first_old + (1.0 - beta_one) * gradient
    second_new = beta_two * second + (1.0 - beta_two) * gradient * gradient
    fix_one = 1.0 - beta_one**STEP
    fix_two = 1.0 - beta_two**STEP
    update = first_new / fix_one / (jnp.sqrt(second_new / fix_two) + adam_eps)
    return (master - step_rate * (update + decay_on * master), first_new, second_new)


def shards(
    ranks,
    hidden,
    span_mask,
    replace_kind,
    replace_from,
    weights,
    vectors,
    weight_first,
    weight_second,
    vector_first,
    vector_second,
    cotangent,
):
    seqs, half_len, _ = hidden.shape
    rows = seqs * half_len
    index = lax.axis_index("dp")
    core = lax.axis_index("seq")
    staged = ranks == 16
    plane = index // 4
    spot = index % 4 if staged else jnp.zeros_like(index)
    me = jnp.stack([spot, core, plane]).astype(jnp.int32)
    low_weights = weights.astype(bf16)
    slots, grads, result = [], {}, []
    if staged:
        gather = Steps(gather_steps(pack(low_weights, index), slots))
    else:
        gather = Steps(None)
        stacked = pack(lax.all_gather(low_weights, "dp", axis=0, tiled=True), 0)

    vals = gather_vectors(vectors.astype(bf16), ranks)
    (vals,) = gather(vals)
    u_own = corrupt(span_mask, replace_kind, replace_from, hidden, vals[8])
    u_other = swap(u_own)
    bias_in = lax.dynamic_index_in_dim(
        vals[9:].reshape(FF // (2 * CHUNK), 2, CHUNK), core, 1, keepdims=False
    ).reshape(1, UNITS)
    u_own, u_other, vals, bias_in = gather(u_own, u_other, vals, bias_in)
    every, rest = (0, 1, 2, 3), ()
    if staged:
        rest = place_rest(me, slots, ((0, every),), ())
    rest = gather(*rest)
    if staged:
        rest = place_rest(me, slots, ((1, every),), rest)
    rest = gather(*rest)

    if staged:
        mine, give = place_heads(me, slots)
    else:
        halves = stacked[: 12 * CHUNK].reshape(3, 2, 2, CHUNK, D)
        mine = lax.dynamic_index_in_dim(halves, core, 1, keepdims=False).reshape(6, CHUNK, D)
        give = lax.dynamic_index_in_dim(halves, 1 - core, 1, keepdims=False).reshape(6, CHUNK, D)
    w_qkv, qkv, attended, attended_wide, lse = attend(
        me, u_own, u_other, mine, swap(give), vals
    )
    w_qkv, qkv, attended, attended_wide, lse, *rest = gather(
        w_qkv, qkv, attended, attended_wide, lse, *rest
    )
    from_other = swap(attended[1])
    if staged:
        rest = place_rest(me, slots, ((2, every), (3, (0, 1, 2))), rest)
    attended, from_other, *rest = gather(attended, from_other, *rest)

    if staged:
        wo_own, w_in, w_down = place_rest(me, slots, ((3, (3,)),), rest)
    else:
        rest = stacked[12 * CHUNK :]
        wo_own = (
            rest[: 4 * CHUNK].reshape(4, CHUNK, 2, OWN).transpose(0, 2, 1, 3).reshape(D, OWN)
        )
        w_in, w_down = rest[4 * CHUNK : 20 * CHUNK], rest[20 * CHUNK :]
    normed_one, inv_one, h_own = attention_branch(
        attended, from_other, u_own, wo_own, swap(wo_own), vals
    )
    h_other = swap(h_own)
    gelu, slope = hidden_units(h_own, h_other, w_in, bias_in)
    feed_other = swap(rows_times(gelu, 1, w_down, bf16, "feed_other"))
    feed_own = rows_times(gelu, 0, w_down, f32, "feed_own")
    layer_out, grad_two, d_own, two_sums = finish(
        feed_own, feed_other, normed_one, cotangent.reshape(rows, D), vals
    )

    d_other = swap(d_own)
    z_own, z_sums = before_gelu(d_own, w_down, slope, 0)
    d_other, z_own, z_sums = barrier(d_other, z_own, z_sums)
    unit = lambda first: pl.BlockSpec((2, rows, OWN), lambda i: (0, 0, i + first))
    one_unit = lambda first: pl.BlockSpec((1, rows, OWN), lambda i: (0, 0, jnp.minimum(i, 1) + first))
    tokens = whole(rows, D)
    grads[3] = grads_call(
        grads3_kernel, PLAIN, [unit(1), tokens, tokens], (me, gelu, d_own, d_other), "grads3"
    )
    *grads[3], d_other = barrier(*grads[3], d_other)
    reduce = Steps(reduce_steps(grads, plane, result) if staged else None)
    z_other, z_other_sums = before_gelu(d_other, w_down, slope, 1)
    hidden_other = rows_times(z_other, 0, w_in, bf16, "hidden_other")
    z_other, z_other_sums, hidden_other, z_own = reduce(
        z_other, z_other_sums, hidden_other, z_own
    )
    sent_hidden = swap(hidden_other)
    hidden_own = rows_times(z_own, 0, w_in, f32, "hidden_own")
    first_unit = pl.BlockSpec((2, rows, OWN), lambda i: (0, 0, 0))
    grads[2] = grads_call(
        grads2_kernel,
        CROSS,
        [one_unit(2), one_unit(2), tokens, tokens, first_unit, tokens, tokens],
        (me, z_own, z_other, h_own, h_other, gelu, d_own, d_other),
        "grads2",
    )
    *grads[2], sent_hidden, hidden_own, grad_two = reduce(
        *grads[2], sent_hidden, hidden_own, grad_two
    )
    grad_one, a_own, one_sums = norm_one_back(
        grad_two, hidden_own, sent_hidden, normed_one, inv_one, vals
    )
    grad_one, a_own, one_sums = reduce(grad_one, a_own, one_sums)
    a_other = swap(a_own)
    grads[1] = grads_call(
        grads1_kernel,
        PLAIN,
        [one_unit(0), one_unit(0), tokens, tokens, tokens, tokens, whole(2, rows, OWN)],
        (me, z_own, z_other, h_own, h_other, a_own, a_other, attended.reshape(2, rows, OWN)),
        "grads1",
    )
    *grads[1], a_own, a_other, qkv = reduce(*grads[1], a_own, a_other, qkv)
    back = (
        a_own.reshape(seqs, half_len, D),
        a_other.reshape(seqs, half_len, D),
        wo_own,
        attended_wide,
        lse,
    )
    state = attend_back(qkv, *back, 0, 1, ())
    a, b, qkv = reduce(*state, qkv)
    state = attend_back(qkv, *back, 1, 1, (a, b))
    a, b, qkv = reduce(*state, qkv)
    grad_qkv, qkv_sums = attend_back(qkv, *back, 2, seqs - 2, (a, b))
    grad_rows = grad_qkv.reshape(2, rows, 3 * OWN)
    keep, give = grads0(me, grad_rows, u_own.reshape(rows, D), u_other.reshape(rows, D))
    keep, give, grad_rows = reduce(keep, give, grad_rows)
    take = swap(give)
    inputs_other = rows_times(grad_rows, 1, w_qkv, bf16, "inputs_other")
    grads[0] = regroup(me, keep, take)
    *grads[0], grad_rows, inputs_other = reduce(*grads[0], grad_rows, inputs_other)
    sent_inputs = swap(inputs_other)
    inputs_own = rows_times(grad_rows, 0, w_qkv, f32, "inputs_own")
    sent_inputs, inputs_own, z_sums = reduce(sent_inputs, inputs_own, z_sums)
    input_grad, mask_sums = corrupt_back(
        span_mask, replace_kind, replace_from, grad_one, inputs_own, sent_inputs
    )
    bias_sums = jnp.zeros((FF // (2 * CHUNK), 2, CHUNK), f32)
    bias_sums = lax.dynamic_update_slice(
        bias_sums,
        (z_sums + z_other_sums).reshape(FF // (2 * CHUNK), 1, CHUNK),
        (0, core, 0),
    ).reshape(FF // D, D)
    vector_part = vector_rows(me, qkv_sums, one_sums, two_sums, mask_sums, bias_sums)
    input_grad, vector_part = reduce(input_grad, vector_part)
    shard_v = scatter_vectors(vector_part, ranks, vectors.shape[0])
    (shard_v,) = reduce(shard_v)
    reduce()

    if staged:
        shard_half = result[0]
        shard_w = unpack(shard_half, swap(shard_half), index).astype(f32)
    else:
        core_rows = [block for i in range(4) for block in grads[i]]
        core_rows = jnp.concatenate(core_rows, axis=0)
        stacked = unpack(core_rows, swap(core_rows), 0).astype(f32)
        shard_w = lax.psum_scatter(stacked, "dp", scatter_dimension=0, tiled=True)
        shard_half = lax.dynamic_slice_in_dim(shard_w, core * OWN, OWN, axis=1)

    half32 = shard_half.astype(f32)
    squares = jnp.sum(half32 * half32) + 0.5 * jnp.sum(shard_v * shard_v)
    grad_norm = jnp.sqrt(sum_everywhere(squares, ranks))
    clip = 1.0 / jnp.maximum(grad_norm, 1.0)
    weights_new, weight_first_new, weight_second_new = adam_step(
        weights, weight_first, weight_second, shard_w * clip, decay_rate, learn_rate
    )
    vectors_new, vector_first_new, vector_second_new = adam_step(
        vectors, vector_first, vector_second, shard_v * clip, 0.0, vector_rate
    )
    return (
        layer_out.reshape(seqs, half_len, D),
        input_grad,
        grad_norm,
        weights_new,
        weight_first_new,
        weight_second_new,
        vectors_new,
        vector_first_new,
        vector_second_new,
        weights_new.astype(bf16),
        vectors_new.astype(bf16),
    )


def solution(mesh):
    token = P("dp", "seq", None)
    by_row = P("dp", None)
    by_column = P(None, "dp")
    position = P("dp", "seq")
    in_specs = (
        (token,) + (position,) * 3 + (by_row, by_column, by_row, by_row, by_column, by_column, token)
    )
    out_specs = (token, token, P()) + (by_row,) * 3 + (by_column,) * 3 + (by_row, by_column)
    return jax.shard_map(
        functools.partial(shards, mesh.shape["dp"]),
        mesh=mesh,
        in_specs=in_specs,
        out_specs=out_specs,
        check_vma=False,
    )
```

```python
import functools

import jax
import jax.numpy as jnp
from jax import lax
from jax.experimental import pallas as pl
from jax.experimental.pallas import tpu as pltpu
from jax.sharding import PartitionSpec as P

D = 768
HEAD_DIM = 64
FF = 3072
STEP = 10
CHUNK = 96
OWN = D // 2
UNITS = FF // 2

ln_eps = 1e-12
beta_one = 0.9
beta_two = 0.999
adam_eps = 1e-08
learn_rate = 0.05
vector_rate = 0.3
decay_rate = 0.01

bf16 = jnp.bfloat16
f32 = jnp.float32
SWAP = [(0, 1), (1, 0)]


def params(limit=24):
    return pltpu.CompilerParams(vmem_limit_bytes=limit * 2**20)


def cost(micros):
    return pl.CostEstimate(flops=int(micros), bytes_accessed=0, transcendentals=0)


def dot(left, right, over):
    return lax.dot_general(left, right, (over, ((), ())), preferred_element_type=f32)


NT = ((1,), (1,))
NN = ((1,), (0,))
TN = ((0,), (0,))


def swap(value):
    return lax.ppermute(value, "seq", SWAP)


def pack(rows, index):
    core = lax.axis_index("seq")
    chunks = rows.shape[0] // (2 * CHUNK)
    plain = lax.dynamic_index_in_dim(rows.reshape(chunks, 2, CHUNK, D), core, 1, keepdims=False)
    columns = lax.dynamic_slice_in_dim(rows, core * OWN, OWN, axis=1).reshape(chunks, 2, CHUNK, OWN)
    wide = jnp.concatenate([columns[:, 0], columns[:, 1]], axis=-1)
    where = index * chunks + jnp.arange(chunks)
    is_out = ((where >= 12) & (where < 16))[:, None, None]
    return jnp.where(is_out, wide, plain).reshape(chunks * CHUNK, D)


def unpack(mine, theirs, index):
    core = lax.axis_index("seq")
    chunks = mine.shape[0] // CHUNK
    first = jnp.where(core == 0, mine, theirs).reshape(chunks, CHUNK, D)
    second = jnp.where(core == 0, theirs, mine).reshape(chunks, CHUNK, D)
    plain = jnp.stack([first, second], axis=1)
    upper = jnp.concatenate([first[..., :OWN], second[..., :OWN]], axis=-1)
    lower = jnp.concatenate([first[..., OWN:], second[..., OWN:]], axis=-1)
    wide = jnp.stack([upper, lower], axis=1)
    where = index * chunks + jnp.arange(chunks)
    is_out = ((where >= 12) & (where < 16))[:, None, None, None]
    return jnp.where(is_out, wide, plain).reshape(chunks * 2 * CHUNK, D)


SIDE_X = [(i, i ^ 1) for i in range(16)]
SIDE_Y = [(i, i ^ 2) for i in range(16)]


def up(first, last):
    return [(i, i + 4) for i in range(16) if first <= i // 4 <= last]


def down(first, last):
    return [(i, i - 4) for i in range(16) if first <= i // 4 <= last]


def send(value, pairs):
    return lax.ppermute(value, "dp", pairs)


def pick(plane, *options):
    result = options[-1]
    for i in range(len(options) - 2, -1, -1):
        result = jnp.where(plane == i, options[i], result)
    return result


def barrier(*values):
    return lax.optimization_barrier(values)


HALF = 3 * CHUNK // 2


def top(block):
    return block[:HALF]


def bottom(block):
    return block[HALF:]


def join(first, second):
    return jnp.concatenate([first, second], axis=0)


def planes(step, *targets):
    pairs = [(i, i ^ (4 * step)) for i in range(16)]
    return [pair for pair in pairs if not targets or pair[1] // 4 in targets]


PIECES = ((0, 1, 2, 3), (1, 0, 3, 2), (2, 2, 0, 0), (3, 3, 1, 1))


def gather_steps(block, slots):
    odd = lax.axis_index("dp") // 4 % 2 == 1
    x0, y0 = send(block, SIDE_X), send(block, SIDE_Y)
    s1 = send(block, planes(1))
    x0, y0, s1 = yield x0, y0, s1

    x1, y1 = send(s1, SIDE_X), send(s1, SIDE_Y)
    c0 = send(x0, SIDE_Y)
    s2 = send(jnp.where(odd, s1, block), planes(2))
    x1, y1, c0, s2 = yield x1, y1, c0, s2
    slots.append(((block, 0), (x0, 0), (y0, 0), (c0, 0)))

    x2, y2 = send(s2, SIDE_X), send(s2, SIDE_Y)
    c1 = send(top(x1), SIDE_Y), send(bottom(y1), SIDE_X)
    s3 = send(jnp.where(odd, block, s1), planes(2))
    x2, y2, *c1 = yield x2, y2, *c1
    slots.append(((s1, 0), (x1, 0), (y1, 0), tuple(c1)))

    c2 = send(top(x2), SIDE_Y), send(bottom(y2), SIDE_X)
    *c2, s3 = yield *c2, s3
    slots.append(((s2, 0), (x2, 0), (y2, 0), tuple(c2)))

    x3, y3 = send(s3, SIDE_X), send(s3, SIDE_Y)
    x3, y3 = yield x3, y3
    c3 = send(top(x3), SIDE_Y), send(bottom(y3), SIDE_X)
    slots.append(((s3, 0), (x3, 0), (y3, 0), None))
    c3 = yield c3
    slots[3] = (*slots[3][:3], tuple(c3))


def reduce_steps(grads, plane, result):
    odd = plane % 2 == 1
    got = yield cross(grads[3])
    x, y = yield across(grads[3], got)
    own3 = plus(grads[3][0], x, y)
    got = yield cross(grads[2])
    x, y = yield across(grads[2], got)
    own2 = plus(grads[2][0], x, y)
    got = yield cross(grads[1])
    high = send(jnp.where(odd, own2, own3), planes(1))
    x, y, high = yield *across(grads[1], got), high
    own1 = plus(grads[1][0], x, y)
    high = plus(jnp.where(odd, own3, own2), high)
    yield ()
    got = yield cross(grads[0])
    x, y, one = yield *across(grads[0], got), send(own1, up(0, 0) + down(3, 3))
    own0 = plus(grads[0][0], x, y)
    own1 = plus(own1, one)
    zero, one, two = yield (
        send(own0, down(1, 1) + down(3, 3)),
        send(own1, down(2, 2)),
        send(high, planes(2, 2)),
    )
    own0 = plus(own0, zero)
    zero, three = yield send(own0, planes(2, 0)), send(high, planes(2, 3))
    result.append(pick(plane, plus(own0, zero), plus(own1, one), plus(high, two), plus(high, three)))


class Steps:
    def __init__(self, steps):
        self.steps = steps
        self.arrays = next(steps) if steps else ()

    def __call__(self, *values):
        count = len(self.arrays)
        passed = barrier(*self.arrays, *values) if count or values else ()
        if self.steps:
            try:
                self.arrays = self.steps.send(passed[:count])
            except StopIteration:
                self.steps, self.arrays = None, ()
        return passed[count:]


def parts_of(side):
    if side is None:
        return []
    first, second = side
    if isinstance(second, int):
        rows = 3 * CHUNK
        return [(first, second * rows, rows, 0)]
    return [(first, 0, HALF, 0), (second, 0, HALF, HALF)]


def slot_arrays(slots):
    arrays, known = [], {}
    shape = []
    for slot in slots:
        sides = []
        for side in slot:
            parts = []
            for array, start, rows, place in parts_of(side):
                if id(array) not in known:
                    known[id(array)] = len(arrays)
                    arrays.append(array)
                parts.append((known[id(array)], start, rows, place))
            sides.append(tuple(parts))
        shape.append(tuple(sides))
    return arrays, tuple(shape)


def run_copies(pairs, sems):
    copies = [
        pltpu.make_async_copy(source, target, sems.at[i])
        for i, (source, target) in enumerate(pairs)
    ]
    for copy in copies:
        copy.start()
    for copy in copies:
        copy.wait()


def place_heads_kernel(shape, me_ref, *refs):
    mine_ref, give_ref, whole_ref, sems = refs[-4:]
    spot, core, plane = me_ref[0], me_ref[1], me_ref[2]
    for z in range(4):

        @pl.when(plane == z)
        def _():
            pairs = []
            for side in range(4):
                start = 3 * CHUNK * (side + spot - 2 * (side & spot))
                for number, first, rows, place in shape[min(z, 2)][side]:
                    where = pl.ds(pl.multiple_of(start + place, 16), rows)
                    pairs.append((refs[number].at[pl.ds(first, rows)], whole_ref.at[where]))
            run_copies(pairs, sems)

    for ref, who in ((mine_ref, core), (give_ref, 1 - core)):
        for j in range(6):
            chunk = 4 * (j // 2) + 2 * who + j % 2
            ref[j] = whole_ref[pl.ds(pl.multiple_of(chunk * CHUNK, 16), CHUNK)]


def place_heads(me, slots):
    arrays, shape = slot_arrays(slots)
    half = jax.ShapeDtypeStruct((6, CHUNK, D), bf16)
    return pl.pallas_call(
        functools.partial(place_heads_kernel, shape),
        in_specs=[pl.BlockSpec(memory_space=pltpu.SMEM)]
        + [pl.BlockSpec(memory_space=pl.ANY)] * len(arrays),
        out_shape=[half, half],
        scratch_shapes=[pltpu.VMEM((12 * CHUNK, D), bf16), pltpu.SemaphoreType.DMA((8,))],
        compiler_params=params(),
        cost_estimate=cost(1),
        name="place_heads",
    )(me, *arrays)


def place_rest_kernel(shape, held, me_ref, *refs):
    out_ref, in_ref, down_ref, stage_ref, load_sems, store_sems = refs[-6:]
    spot, plane = me_ref[0], me_ref[2]

    def part(pairs, source, first, rows, row):
        while rows:
            if row < 4 * CHUNK:
                chunk, offset = divmod(row, CHUNK)
                count = min(rows, CHUNK - offset)
                targets = []
                for h in range(2):
                    target = 2 * CHUNK * chunk + CHUNK * h + offset
                    targets.append((pl.ds(OWN * h, OWN), out_ref.at[pl.ds(target, count)]))
            else:
                ref, start = (in_ref, 4 * CHUNK) if row < 20 * CHUNK else (down_ref, 20 * CHUNK)
                count = min(rows, start + 16 * CHUNK - row)
                targets = [(slice(None), ref.at[pl.ds(row - start, count)])]
            pairs.append((source.at[pl.ds(first, count)], count, targets))
            row, first, rows = row + count, first + count, rows - count

    for z in range(4):
        for s in range(4):
            pairs = []
            for slot, (number, sides) in zip(shape, held, strict=True):
                piece = PIECES[number][z]
                for side in sides if piece else ():
                    base = 3 * CHUNK * (4 * (piece - 1) + (side ^ s))
                    for array, first, rows, place in slot[side]:
                        part(pairs, refs[array], first, rows, base + place)

            @pl.when((plane == z) & (spot == s))
            def _():
                loads, stores, row = [], [], 0
                for i, (source, count, targets) in enumerate(pairs):
                    spot_rows = pl.ds(row, count)
                    loads.append(
                        pltpu.make_async_copy(source, stage_ref.at[spot_rows], load_sems.at[i])
                    )
                    stores.append([])
                    for columns, target in targets:
                        stores[-1].append(
                            pltpu.make_async_copy(
                                stage_ref.at[spot_rows, columns],
                                target,
                                store_sems.at[2 * i + len(stores[-1])],
                            )
                        )
                    row += count
                for load in loads:
                    load.start()
                for load, store in zip(loads, stores, strict=True):
                    load.wait()
                    for copy in store:
                        copy.start()
                for store in stores:
                    for copy in store:
                        copy.wait()


def place_rest(me, slots, held, state):
    arrays, shape = slot_arrays(
        [[slots[i][side] if side in sides else None for side in range(4)] for i, sides in held]
    )
    units = jax.ShapeDtypeStruct((UNITS, D), bf16)
    anywhere = pl.BlockSpec(memory_space=pl.ANY)
    return pl.pallas_call(
        functools.partial(place_rest_kernel, shape, held),
        in_specs=[pl.BlockSpec(memory_space=pltpu.SMEM)] + [anywhere] * (len(arrays) + len(state)),
        out_specs=[anywhere] * 3,
        out_shape=[jax.ShapeDtypeStruct((D, OWN), bf16), units, units],
        input_output_aliases={1 + len(arrays) + i: i for i in range(len(state))},
        scratch_shapes=[
            pltpu.VMEM((24 * CHUNK, D), bf16),
            pltpu.SemaphoreType.DMA((32,)),
            pltpu.SemaphoreType.DMA((64,)),
        ],
        compiler_params=params(),
        cost_estimate=cost(1),
        name="place_rest",
    )(me, *arrays, *state)


def plus(*values):
    total = values[0].astype(f32)
    for value in values[1:]:
        total = total + value.astype(f32)
    return total.astype(bf16)


def cross(sides):
    return send(sides[3], SIDE_Y), send(sides[4], SIDE_X)


def across(sides, crossed):
    over_x = join(plus(top(sides[1]), crossed[0]), bottom(sides[1]))
    over_y = join(top(sides[2]), plus(bottom(sides[2]), crossed[1]))
    return send(over_x, SIDE_X), send(over_y, SIDE_Y)


def gather_vectors(low_vectors, ranks):
    count, width = low_vectors.shape
    block = jnp.pad(low_vectors, ((0, 16 - count), (0, 128 - width)))
    blocks = lax.all_to_all(jnp.broadcast_to(block, (ranks, 16, 128)), "dp", 0, 0, tiled=True)
    return blocks[:, :count, :width].transpose(1, 0, 2).reshape(count, ranks * width).astype(f32)


def scatter_vectors(rows, ranks, count):
    width = D // ranks
    blocks = (rows + swap(rows)).reshape(16, ranks, width).transpose(1, 0, 2)
    blocks = jnp.pad(blocks, ((0, 0), (0, 0), (0, 128 - width)))
    blocks = lax.all_to_all(blocks, "dp", 0, 0, tiled=True)
    return jnp.sum(blocks, axis=0)[:count, :width]


def sum_everywhere(value, ranks):
    blocks = lax.all_to_all(
        jnp.full((2 * ranks, 8, 128), value), ("dp", "seq"), 0, 0, tiled=True
    )
    return jnp.sum(blocks[:, 0, 0])


def selection(span, kind, source, half_len):
    chosen = span == 1
    masked = chosen & (kind < 8)
    swapped = chosen & (kind == 8)
    here = lax.broadcasted_iota(jnp.int32, (1, half_len), 1)
    origin = jnp.where(masked, -1, jnp.where(swapped, source, here))
    rows = lax.broadcasted_iota(jnp.int32, (half_len, half_len), 0)
    one_hot = (rows == origin).astype(f32).astype(bf16)
    first = lax.broadcasted_iota(jnp.int32, (16, half_len), 0) == 0
    mask_rows = jnp.where(first & masked, 1.0, 0.0).astype(bf16)
    return one_hot, mask_rows


def corrupt_kernel(span_ref, kind_ref, from_ref, hidden_ref, mask_ref, out_ref):
    seqs, half_len = span_ref.shape
    for s in range(seqs):
        rows = slice(s, s + 1)
        one_hot, mask_rows = selection(
            span_ref[rows, :], kind_ref[rows, :], from_ref[rows, :], half_len
        )
        picked = dot(one_hot, hidden_ref[s], TN) + dot(mask_rows, mask_ref[...], TN)
        out_ref[s] = picked.astype(bf16)


def corrupt(span, kind, source, hidden, mask_row):
    mask = jnp.broadcast_to(mask_row.astype(bf16)[None], (16, D))
    return pl.pallas_call(
        corrupt_kernel,
        out_shape=jax.ShapeDtypeStruct(hidden.shape, bf16),
        compiler_params=params(),
        name="corrupt",
    )(span, kind, source, hidden, mask)


def corrupt_back_kernel(
    span_ref, kind_ref, from_ref, grad_ref, own_ref, partial_ref, out_ref, mask_ref
):
    seqs, half_len = span_ref.shape
    mask_sum = jnp.zeros((16, D), f32)
    for s in range(seqs):
        rows = slice(s, s + 1)
        block = pl.ds(s * half_len, half_len)
        one_hot, mask_rows = selection(
            span_ref[rows, :], kind_ref[rows, :], from_ref[rows, :], half_len
        )
        grad = grad_ref[block] + own_ref[block] + partial_ref[block].astype(f32)
        high = grad.astype(bf16)
        low = (grad - high.astype(f32)).astype(bf16)
        out_ref[s] = dot(one_hot, high, NN) + dot(one_hot, low, NN)
        mask_sum = mask_sum + dot(mask_rows, high, NN) + dot(mask_rows, low, NN)
    mask_ref[...] = mask_sum


def corrupt_back(span, kind, source, grad, own, partial):
    seqs, half_len = span.shape
    return pl.pallas_call(
        corrupt_back_kernel,
        out_shape=[
            jax.ShapeDtypeStruct((seqs, half_len, D), f32),
            jax.ShapeDtypeStruct((16, D), f32),
        ],
        compiler_params=params(),
        cost_estimate=cost(1),
        name="corrupt_back",
    )(span, kind, source, grad, own, partial)


def attend_kernel(
    me_ref, own_ref, other_ref, mine_ref, theirs_ref, vals_ref, w_ref, qkv_ref, low_ref, wide_ref, lse_ref
):
    half_len = own_ref.shape[1]
    core = me_ref[1]

    @pl.when(pl.program_id(0) == 0)
    def _():
        for j in range(6):
            for ref, which in ((mine_ref, core), (theirs_ref, 1 - core)):
                where = pl.ds(pl.multiple_of((2 * j + which) * CHUNK, 16), CHUNK)
                w_ref[where] = ref[j]

    rows = jnp.concatenate([own_ref[0], other_ref[0]], axis=0)
    columns = pl.ds(pl.multiple_of(core * OWN, 128), OWN)
    bias = jnp.concatenate(
        [vals_ref[0:1, columns], jnp.zeros((1, OWN), f32), vals_ref[1:2, columns]], axis=-1
    )
    projected = (dot(rows, w_ref[...], NT) + bias).astype(bf16)
    qkv_ref[:, 0] = projected.reshape(2, half_len, 3 * OWN)
    wide, totals = [], []
    for h in range(OWN // HEAD_DIM):
        columns = slice(h * HEAD_DIM, (h + 1) * HEAD_DIM)
        query = projected[:, :OWN][:, columns] * bf16(HEAD_DIM**-0.5)
        key = projected[:, OWN : 2 * OWN][:, columns]
        value = projected[:, 2 * OWN :][:, columns]
        scores = dot(query, key, NT)
        highest = jnp.max(scores, axis=-1, keepdims=True)
        exponents = jnp.exp(scores - highest)
        total = jnp.sum(exponents, axis=-1, keepdims=True)
        probabilities = (exponents / total).astype(bf16)
        wide.append(dot(probabilities, value, NN))
        totals.append(highest + jnp.log(total))
    attended = jnp.concatenate(wide, axis=-1)
    wide_ref[:, 0] = attended.reshape(2, half_len, OWN)
    low_ref[:, 0] = attended.astype(bf16).reshape(2, half_len, OWN)
    fill = jnp.zeros((2 * half_len, 128 - len(totals)), f32)
    lse_ref[0] = jnp.concatenate(totals + [fill], axis=-1).T[:8]


def whole(*shape):
    return pl.BlockSpec(shape, lambda *_: (0,) * len(shape))


def attend(me, u_own, u_other, mine, theirs, vals):
    seqs, half_len, _ = u_own.shape
    block = lambda width: pl.BlockSpec((2, 1, half_len, width), lambda s: (0, s, 0, 0))
    token = pl.BlockSpec((1, half_len, D), lambda s: (s, 0, 0))
    return pl.pallas_call(
        attend_kernel,
        grid=(seqs,),
        in_specs=[
            pl.BlockSpec(memory_space=pltpu.SMEM),
            token,
            token,
            whole(6, CHUNK, D),
            whole(6, CHUNK, D),
            whole(*vals.shape),
        ],
        out_specs=[
            whole(3 * OWN, D),
            block(3 * OWN),
            block(OWN),
            block(OWN),
            pl.BlockSpec((1, 8, 2 * half_len), lambda s: (s, 0, 0)),
        ],
        out_shape=[
            jax.ShapeDtypeStruct((3 * OWN, D), bf16),
            jax.ShapeDtypeStruct((2, seqs, half_len, 3 * OWN), bf16),
            jax.ShapeDtypeStruct((2, seqs, half_len, OWN), bf16),
            jax.ShapeDtypeStruct((2, seqs, half_len, OWN), f32),
            jax.ShapeDtypeStruct((seqs, 8, 2 * half_len), f32),
        ],
        cost_estimate=cost(3),
        compiler_params=params(),
        name="attend",
    )(me, u_own, u_other, mine, theirs, vals)


def attend_back_kernel(
    skip, qkv_ref, own_ref, other_ref, wo_ref, wide_ref, lse_ref, *refs
):
    out_ref, sums_ref = refs[skip:]
    half_len = qkv_ref.shape[2]
    length = 2 * half_len
    projected = qkv_ref[:, 0].reshape(length, 3 * OWN)
    rows = jnp.concatenate([own_ref[0], other_ref[0]], axis=0)
    grad = dot(rows, wo_ref[...], NN).astype(bf16)
    product = grad.astype(f32) * wide_ref[:, 0].reshape(length, OWN)
    heads = OWN // HEAD_DIM
    deltas = [
        jnp.sum(product[:, h * HEAD_DIM : (h + 1) * HEAD_DIM], axis=-1, keepdims=True)
        for h in range(heads)
    ]
    fill = jnp.zeros((length, 128 - heads), f32)
    delta_rows = jnp.concatenate(deltas + [fill], axis=-1).T
    parts = [[], [], []]
    for h in range(heads):
        columns = slice(h * HEAD_DIM, (h + 1) * HEAD_DIM)
        query = projected[:, :OWN][:, columns] * bf16(HEAD_DIM**-0.5)
        key = projected[:, OWN : 2 * OWN][:, columns]
        value = projected[:, 2 * OWN :][:, columns]
        grad_head = grad[:, columns]
        weights = jnp.exp(dot(key, query, NT) - lse_ref[0, h : h + 1, :])
        grad_weights = dot(value, grad_head, NT)
        grad_scores = (weights * (grad_weights - delta_rows[h : h + 1, :])).astype(bf16)
        parts[0].append(dot(grad_scores, key, TN) * HEAD_DIM**-0.5)
        parts[1].append(dot(grad_scores, query, NN))
        parts[2].append(dot(weights.astype(bf16), grad_head, NN))
    result = jnp.concatenate(parts[0] + parts[1] + parts[2], axis=-1).astype(bf16)
    out_ref[:, 0] = result.reshape(2, half_len, 3 * OWN)
    sums = jnp.sum(result.astype(f32), axis=0, keepdims=True)

    @pl.when(pl.program_id(0) == 0)
    def _():
        sums_ref[...] = refs[1][...] if skip else jnp.zeros_like(sums_ref)

    sums_ref[...] += sums


def attend_back(qkv, own, other, wo_own, wide, lse, first, count, state):
    _, seqs, half_len, _ = qkv.shape
    block = lambda width: pl.BlockSpec((2, 1, half_len, width), lambda s: (0, s + first, 0, 0))
    token = pl.BlockSpec((1, half_len, D), lambda s: (s + first, 0, 0))
    return pl.pallas_call(
        functools.partial(attend_back_kernel, len(state)),
        grid=(count,),
        in_specs=[
            block(3 * OWN),
            token,
            token,
            whole(D, OWN),
            block(OWN),
            pl.BlockSpec((1, 8, 2 * half_len), lambda s: (s + first, 0, 0)),
        ]
        + ([pl.BlockSpec(memory_space=pl.ANY), whole(1, 3 * OWN)] if state else []),
        out_specs=[block(3 * OWN), whole(1, 3 * OWN)],
        input_output_aliases={6: 0} if state else {},
        out_shape=[
            jax.ShapeDtypeStruct((2, seqs, half_len, 3 * OWN), bf16),
            jax.ShapeDtypeStruct((1, 3 * OWN), f32),
        ],
        cost_estimate=cost(2 * count),
        compiler_params=params(),
        name="attend_back",
    )(qkv, own, other, wo_own, wide, lse, *state)


def norm(values):
    center = values - jnp.mean(values, axis=-1, keepdims=True)
    inv_std = lax.rsqrt(jnp.mean(center * center, axis=-1, keepdims=True) + ln_eps)
    return center * inv_std, inv_std


def norm_backward(upstream, normed, inv_std, gain):
    scaled = upstream * gain
    return inv_std * (
        scaled
        - jnp.mean(scaled, axis=-1, keepdims=True)
        - normed * jnp.mean(scaled * normed, axis=-1, keepdims=True)
    )


def row(ref, i):
    return ref[i : i + 1, :]


def branch_kernel(own_ref, other_ref, u_ref, wo_ref, wo_other_ref, vals_ref, normed_ref, inv_ref, low_ref):
    branch = dot(own_ref[0, 0], wo_ref[...], NT) + dot(other_ref[0], wo_other_ref[...], NT)
    normed, inv = norm(u_ref[0].astype(f32) + branch + row(vals_ref, 2))
    normed_ref[...] = normed
    inv_ref[...] = jnp.broadcast_to(inv, inv_ref.shape)
    low_ref[...] = (normed * row(vals_ref, 3) + row(vals_ref, 4)).astype(bf16)


def attention_branch(attended, from_other, u_own, wo_own, wo_other, vals):
    seqs, half_len, _ = u_own.shape
    rows = pl.BlockSpec((half_len, D), lambda s: (s, 0))
    return pl.pallas_call(
        branch_kernel,
        grid=(seqs,),
        in_specs=[
            pl.BlockSpec((1, 1, half_len, OWN), lambda s: (0, s, 0, 0)),
            pl.BlockSpec((1, half_len, OWN), lambda s: (s, 0, 0)),
            pl.BlockSpec((1, half_len, D), lambda s: (s, 0, 0)),
            whole(D, OWN),
            whole(D, OWN),
            whole(*vals.shape),
        ],
        out_specs=[rows, pl.BlockSpec((half_len, 128), lambda s: (s, 0)), rows],
        out_shape=[
            jax.ShapeDtypeStruct((seqs * half_len, D), f32),
            jax.ShapeDtypeStruct((seqs * half_len, 128), f32),
            jax.ShapeDtypeStruct((seqs * half_len, D), bf16),
        ],
        cost_estimate=cost(1),
        compiler_params=params(),
        name="attention_branch",
    )(attended, from_other, u_own, wo_own, wo_other, vals)


def hidden_kernel(own_ref, other_ref, w_ref, bias_ref, gelu_ref, slope_ref):
    for half, ref in enumerate((own_ref, other_ref)):
        points = dot(ref[...], w_ref[...], NT) + bias_ref[...]
        below = 0.5 * (1.0 + lax.erf(points * 2**-0.5))
        density = jnp.exp(-0.5 * points * points) * 0.3989422804014327
        gelu_ref[half] = (points * below).astype(bf16)
        slope_ref[half] = (below + points * density).astype(bf16)


def hidden_units(h_own, h_other, w_in, bias):
    rows = h_own.shape[0]
    width = 256
    block = pl.BlockSpec((2, rows, width), lambda i: (0, 0, i))
    return pl.pallas_call(
        hidden_kernel,
        grid=(UNITS // width,),
        in_specs=[
            whole(rows, D),
            whole(rows, D),
            pl.BlockSpec((width, D), lambda i: (i, 0)),
            pl.BlockSpec((1, width), lambda i: (0, i)),
        ],
        out_specs=[block, block],
        out_shape=[jax.ShapeDtypeStruct((2, rows, UNITS), bf16)] * 2,
        cost_estimate=cost(3),
        compiler_params=params(),
        name="hidden_units",
    )(h_own, h_other, w_in, bias)


def rows_kernel(left_ref, right_ref, out_ref):
    out_ref[...] = dot(left_ref[0], right_ref[...], NN).astype(out_ref.dtype)


def rows_times(left, half, right, dtype, name):
    _, rows, depth = left.shape
    tile = rows // 3
    return pl.pallas_call(
        rows_kernel,
        grid=(3,),
        in_specs=[pl.BlockSpec((1, tile, depth), lambda i: (half, i, 0)), whole(*right.shape)],
        out_specs=pl.BlockSpec((tile, D), lambda i: (i, 0)),
        out_shape=jax.ShapeDtypeStruct((rows, D), dtype),
        cost_estimate=cost(1),
        compiler_params=params(),
        name=name,
    )(left, right)


def add_sums(sums_ref, *values):
    @pl.when(pl.program_id(0) == 0)
    def _():
        sums_ref[...] = jnp.zeros_like(sums_ref)

    for i, value in enumerate(values):
        sums_ref[i : i + 1, :] += jnp.sum(value, axis=0, keepdims=True)


def finish_kernel(own_ref, other_ref, normed_ref, grad_ref, vals_ref, out_ref, wide_ref, low_ref, sums_ref):
    hidden_one = normed_ref[...] * row(vals_ref, 3) + row(vals_ref, 4)
    feed = own_ref[...] + other_ref[...].astype(f32) + row(vals_ref, 5)
    normed, inv = norm(hidden_one + feed)
    out_ref[...] = normed * row(vals_ref, 6) + row(vals_ref, 7)
    grad = grad_ref[...].astype(f32)
    wide = norm_backward(grad, normed, inv, row(vals_ref, 6))
    low = wide.astype(bf16)
    wide_ref[...] = wide
    low_ref[...] = low
    add_sums(sums_ref, low.astype(f32), grad * normed, grad)


def finish(own, other, normed, grad, vals):
    rows = own.shape[0]
    tile = rows // 3
    block = pl.BlockSpec((tile, D), lambda i: (i, 0))
    return pl.pallas_call(
        finish_kernel,
        grid=(3,),
        in_specs=[block] * 4 + [whole(*vals.shape)],
        out_specs=[block] * 3 + [whole(8, D)],
        out_shape=[
            jax.ShapeDtypeStruct((rows, D), f32),
            jax.ShapeDtypeStruct((rows, D), f32),
            jax.ShapeDtypeStruct((rows, D), bf16),
            jax.ShapeDtypeStruct((8, D), f32),
        ],
        cost_estimate=cost(1),
        compiler_params=params(),
        name="finish",
    )(own, other, normed, grad, vals)


def norm_one_kernel(two_ref, own_ref, other_ref, normed_ref, inv_ref, vals_ref, wide_ref, low_ref, sums_ref):
    grad = two_ref[...] + own_ref[...] + other_ref[...].astype(f32)
    normed = normed_ref[...]
    wide = norm_backward(grad, normed, inv_ref[:, 0:1], row(vals_ref, 3))
    low = wide.astype(bf16)
    wide_ref[...] = wide
    low_ref[...] = low
    add_sums(sums_ref, low.astype(f32), grad * normed, grad)


def norm_one_back(two, own, other, normed, inv, vals):
    rows = own.shape[0]
    tile = rows // 3
    block = pl.BlockSpec((tile, D), lambda i: (i, 0))
    return pl.pallas_call(
        norm_one_kernel,
        grid=(3,),
        in_specs=[block] * 4 + [pl.BlockSpec((tile, 128), lambda i: (i, 0)), whole(*vals.shape)],
        out_specs=[block] * 2 + [whole(8, D)],
        out_shape=[
            jax.ShapeDtypeStruct((rows, D), f32),
            jax.ShapeDtypeStruct((rows, D), bf16),
            jax.ShapeDtypeStruct((8, D), f32),
        ],
        cost_estimate=cost(1),
        compiler_params=params(),
        name="norm_one_back",
    )(two, own, other, normed, inv, vals)


def slope_kernel(grad_ref, w_ref, slope_ref, out_ref, sums_ref):
    low = (dot(grad_ref[...], w_ref[...], NT) * slope_ref[0].astype(f32)).astype(bf16)
    out_ref[0] = low
    sums_ref[...] = jnp.sum(low.astype(f32), axis=0, keepdims=True)


def before_gelu(grad, w_down, slope, half):
    rows = grad.shape[0]
    width = 384
    return pl.pallas_call(
        slope_kernel,
        grid=(UNITS // width,),
        in_specs=[
            whole(rows, D),
            pl.BlockSpec((width, D), lambda i: (i, 0)),
            pl.BlockSpec((1, rows, width), lambda i: (half, 0, i)),
        ],
        out_specs=[
            pl.BlockSpec((1, rows, width), lambda i: (0, 0, i)),
            pl.BlockSpec((1, width), lambda i: (0, i)),
        ],
        out_shape=[
            jax.ShapeDtypeStruct((1, rows, UNITS), bf16),
            jax.ShapeDtypeStruct((1, UNITS), f32),
        ],
        cost_estimate=cost(1),
        compiler_params=params(),
        name="before_gelu",
    )(grad, w_down, slope)


def rows_of(count):
    return jax.ShapeDtypeStruct((count, D), bf16)


CROSS = ((0, 0, 288), (1, 0, 288), (2, 0, 288), (3, 0, 144), (3, 144, 144))


def side_rows(spot, side, first, rows):
    start = 3 * CHUNK * (side + spot - 2 * (side & spot)) + first
    return pl.ds(pl.multiple_of(start, 16), rows)


def write_sides(spot, piece_ref, outs):
    for out, (side, first, rows) in zip(outs, CROSS, strict=True):
        out[...] = piece_ref[side_rows(spot, side, first, rows)]


def rows_at(step):
    return pl.ds(pl.multiple_of(step * OWN, 16), OWN)


def two_halves(left, left_other, right, right_other):
    return dot(left, right, TN) + dot(left_other, right_other, TN)


def grads3_kernel(me_ref, g_ref, d_ref, d_other_ref, *refs):
    piece_ref = refs[-1]
    step = pl.program_id(0)
    piece_ref[rows_at(step)] = two_halves(
        g_ref[0], g_ref[1], d_ref[...], d_other_ref[...]
    ).astype(bf16)

    @pl.when(step == 2)
    def _():
        write_sides(me_ref[0], piece_ref, refs[:-1])


def grads2_kernel(me_ref, z_ref, z_other_ref, h_ref, h_other_ref, g_ref, d_ref, d_other_ref, *refs):
    piece_ref = refs[-1]
    step = pl.program_id(0)

    @pl.when(step < 2)
    def _():
        piece_ref[rows_at(step)] = two_halves(
            z_ref[0], z_other_ref[0], h_ref[...], h_other_ref[...]
        ).astype(bf16)

    @pl.when(step == 2)
    def _():
        piece_ref[rows_at(step)] = two_halves(
            g_ref[0], g_ref[1], d_ref[...], d_other_ref[...]
        ).astype(bf16)
        write_sides(me_ref[0], piece_ref, refs[:-1])


def grads1_kernel(me_ref, z_ref, z_other_ref, h_ref, h_other_ref, a_ref, a_other_ref, att_ref, *refs):
    piece_ref = refs[-1]
    step = pl.program_id(0)

    @pl.when(step < 2)
    def _():
        piece_ref[rows_at(step + 1)] = two_halves(
            z_ref[0], z_other_ref[0], h_ref[...], h_other_ref[...]
        ).astype(bf16)

    @pl.when(step == 2)
    def _():
        wo = two_halves(a_ref[...], a_other_ref[...], att_ref[0], att_ref[1]).astype(bf16)
        for j in range(4):
            upper = wo[2 * CHUNK * j : 2 * CHUNK * j + CHUNK]
            lower = wo[2 * CHUNK * j + CHUNK : 2 * CHUNK * (j + 1)]
            piece_ref[CHUNK * j : CHUNK * (j + 1)] = jnp.concatenate([upper, lower], axis=-1)
        write_sides(me_ref[0], piece_ref, refs[:-1])


def grads_call(kernel, specs, arrays, name):
    return pl.pallas_call(
        kernel,
        grid=(3,),
        in_specs=[pl.BlockSpec(memory_space=pltpu.SMEM)] + specs,
        out_specs=[whole(count, D) for _, _, count in CROSS],
        out_shape=[rows_of(count) for _, _, count in CROSS],
        scratch_shapes=[pltpu.VMEM((12 * CHUNK, D), bf16)],
        cost_estimate=cost(2),
        compiler_params=params(),
        name=name,
    )(*arrays)


def grads0_kernel(me_ref, g_ref, u_ref, u_other_ref, keep_ref, give_ref, piece_ref):
    core = me_ref[1]
    step = pl.program_id(0)
    piece_ref[rows_at(step)] = two_halves(
        g_ref[0], g_ref[1], u_ref[...], u_other_ref[...]
    ).astype(bf16)

    @pl.when(step == 2)
    def _():
        for j in range(6):
            for ref, which in ((keep_ref, core), (give_ref, 1 - core)):
                where = pl.ds(pl.multiple_of((2 * j + which) * CHUNK, 16), CHUNK)
                ref[j] = piece_ref[where]


def grads0(me, grad, u_own, u_other):
    rows = grad.shape[1]
    half = jax.ShapeDtypeStruct((6, CHUNK, D), bf16)
    return pl.pallas_call(
        grads0_kernel,
        grid=(3,),
        in_specs=[
            pl.BlockSpec(memory_space=pltpu.SMEM),
            pl.BlockSpec((2, rows, OWN), lambda i: (0, 0, i)),
            whole(rows, D),
            whole(rows, D),
        ],
        out_specs=[whole(6, CHUNK, D)] * 2,
        out_shape=[half, half],
        scratch_shapes=[pltpu.VMEM((12 * CHUNK, D), bf16)],
        cost_estimate=cost(2),
        compiler_params=params(),
        name="grads0",
    )(me, grad, u_own, u_other)


def regroup_kernel(me_ref, keep_ref, take_ref, *refs):
    piece_ref = refs[-1]
    core = me_ref[1]
    for ref, who in ((keep_ref, core), (take_ref, 1 - core)):
        for j in range(6):
            chunk = 4 * (j // 2) + 2 * who + j % 2
            piece_ref[pl.ds(pl.multiple_of(chunk * CHUNK, 16), CHUNK)] = ref[j]
    write_sides(me_ref[0], piece_ref, refs[:-1])


def regroup(me, keep, take):
    return pl.pallas_call(
        regroup_kernel,
        in_specs=[pl.BlockSpec(memory_space=pltpu.SMEM)]
        + [pl.BlockSpec(memory_space=pltpu.VMEM)] * 2,
        out_shape=[rows_of(count) for _, _, count in CROSS],
        scratch_shapes=[pltpu.VMEM((12 * CHUNK, D), bf16)],
        cost_estimate=cost(1),
        compiler_params=params(),
        name="regroup",
    )(me, keep, take)


def vector_kernel(me_ref, qkv_ref, one_ref, two_ref, mask_ref, bias_ref, out_ref):
    out_ref[...] = jnp.zeros_like(out_ref)
    columns = pl.ds(pl.multiple_of(me_ref[1] * OWN, 128), OWN)
    out_ref[0:1, columns] = qkv_ref[:, :OWN]
    out_ref[1:2, columns] = qkv_ref[:, 2 * OWN :]
    out_ref[2:5, :] = one_ref[0:3, :]
    out_ref[5:8, :] = two_ref[0:3, :]
    out_ref[8:9, :] = mask_ref[0:1, :]
    out_ref[9:13, :] = bias_ref[...]


def vector_rows(me, qkv_sums, one_sums, two_sums, mask_sums, bias_sums):
    return pl.pallas_call(
        vector_kernel,
        in_specs=[pl.BlockSpec(memory_space=pltpu.SMEM)]
        + [pl.BlockSpec(memory_space=pltpu.VMEM)] * 5,
        out_shape=jax.ShapeDtypeStruct((16, D), f32),
        cost_estimate=cost(1),
        name="vector_rows",
    )(me, qkv_sums, one_sums, two_sums, mask_sums, bias_sums)


def adam_step(master, first_old, second, gradient, decay_on, step_rate):
    first_new = beta_one * first_old + (1.0 - beta_one) * gradient
    second_new = beta_two * second + (1.0 - beta_two) * gradient * gradient
    fix_one = 1.0 - beta_one**STEP
    fix_two = 1.0 - beta_two**STEP
    update = first_new / fix_one / (jnp.sqrt(second_new / fix_two) + adam_eps)
    return (master - step_rate * (update + decay_on * master), first_new, second_new)


def shards(
    ranks,
    hidden,
    span_mask,
    replace_kind,
    replace_from,
    weights,
    vectors,
    weight_first,
    weight_second,
    vector_first,
    vector_second,
    cotangent,
):
    seqs, half_len, _ = hidden.shape
    rows = seqs * half_len
    index = lax.axis_index("dp")
    core = lax.axis_index("seq")
    staged = ranks == 16
    plane = index // 4
    spot = index % 4 if staged else jnp.zeros_like(index)
    me = jnp.stack([spot, core, plane]).astype(jnp.int32)
    low_weights = weights.astype(bf16)
    slots, grads, result = [], {}, []
    if staged:
        gather = Steps(gather_steps(pack(low_weights, index), slots))
    else:
        gather = Steps(None)
        stacked = pack(lax.all_gather(low_weights, "dp", axis=0, tiled=True), 0)

    vals = gather_vectors(vectors.astype(bf16), ranks)
    (vals,) = gather(vals)
    u_own = corrupt(span_mask, replace_kind, replace_from, hidden, vals[8])
    u_other = swap(u_own)
    bias_in = lax.dynamic_index_in_dim(
        vals[9:].reshape(FF // (2 * CHUNK), 2, CHUNK), core, 1, keepdims=False
    ).reshape(1, UNITS)
    u_own, u_other, vals, bias_in = gather(u_own, u_other, vals, bias_in)
    every, rest = (0, 1, 2, 3), ()
    if staged:
        rest = place_rest(me, slots, ((0, every),), ())
    rest = gather(*rest)
    if staged:
        rest = place_rest(me, slots, ((1, every),), rest)
    rest = gather(*rest)

    if staged:
        mine, give = place_heads(me, slots)
    else:
        halves = stacked[: 12 * CHUNK].reshape(3, 2, 2, CHUNK, D)
        mine = lax.dynamic_index_in_dim(halves, core, 1, keepdims=False).reshape(6, CHUNK, D)
        give = lax.dynamic_index_in_dim(halves, 1 - core, 1, keepdims=False).reshape(6, CHUNK, D)
    w_qkv, qkv, attended, attended_wide, lse = attend(
        me, u_own, u_other, mine, swap(give), vals
    )
    w_qkv, qkv, attended, attended_wide, lse, *rest = gather(
        w_qkv, qkv, attended, attended_wide, lse, *rest
    )
    from_other = swap(attended[1])
    if staged:
        rest = place_rest(me, slots, ((2, every), (3, (0, 1, 2))), rest)
    attended, from_other, *rest = gather(attended, from_other, *rest)

    if staged:
        wo_own, w_in, w_down = place_rest(me, slots, ((3, (3,)),), rest)
    else:
        rest = stacked[12 * CHUNK :]
        wo_own = (
            rest[: 4 * CHUNK].reshape(4, CHUNK, 2, OWN).transpose(0, 2, 1, 3).reshape(D, OWN)
        )
        w_in, w_down = rest[4 * CHUNK : 20 * CHUNK], rest[20 * CHUNK :]
    normed_one, inv_one, h_own = attention_branch(
        attended, from_other, u_own, wo_own, swap(wo_own), vals
    )
    h_other = swap(h_own)
    gelu, slope = hidden_units(h_own, h_other, w_in, bias_in)
    feed_other = swap(rows_times(gelu, 1, w_down, bf16, "feed_other"))
    feed_own = rows_times(gelu, 0, w_down, f32, "feed_own")
    layer_out, grad_two, d_own, two_sums = finish(
        feed_own, feed_other, normed_one, cotangent.reshape(rows, D), vals
    )

    d_other = swap(d_own)
    z_own, z_sums = before_gelu(d_own, w_down, slope, 0)
    d_other, z_own, z_sums = barrier(d_other, z_own, z_sums)
    unit = lambda first: pl.BlockSpec((2, rows, OWN), lambda i: (0, 0, i + first))
    one_unit = lambda first: pl.BlockSpec((1, rows, OWN), lambda i: (0, 0, jnp.minimum(i, 1) + first))
    tokens = whole(rows, D)
    grads[3] = grads_call(
        grads3_kernel, [unit(1), tokens, tokens], (me, gelu, d_own, d_other), "grads3"
    )
    *grads[3], d_other = barrier(*grads[3], d_other)
    reduce = Steps(reduce_steps(grads, plane, result) if staged else None)
    z_other, z_other_sums = before_gelu(d_other, w_down, slope, 1)
    hidden_other = rows_times(z_other, 0, w_in, bf16, "hidden_other")
    z_other, z_other_sums, hidden_other, z_own = reduce(
        z_other, z_other_sums, hidden_other, z_own
    )
    sent_hidden = swap(hidden_other)
    hidden_own = rows_times(z_own, 0, w_in, f32, "hidden_own")
    grad_one, a_own, one_sums = norm_one_back(
        grad_two, hidden_own, sent_hidden, normed_one, inv_one, vals
    )
    first_unit = pl.BlockSpec((2, rows, OWN), lambda i: (0, 0, 0))
    grads[2] = grads_call(
        grads2_kernel,
        [one_unit(2), one_unit(2), tokens, tokens, first_unit, tokens, tokens],
        (me, z_own, z_other, h_own, h_other, gelu, d_own, d_other),
        "grads2",
    )
    *grads[2], grad_one, a_own, one_sums = reduce(*grads[2], grad_one, a_own, one_sums)
    a_other = swap(a_own)
    a_own, a_other, qkv = reduce(a_own, a_other, qkv)
    back = (
        a_own.reshape(seqs, half_len, D),
        a_other.reshape(seqs, half_len, D),
        wo_own,
        attended_wide,
        lse,
    )
    state = attend_back(qkv, *back, 0, 1, ())
    grads[1] = grads_call(
        grads1_kernel,
        [one_unit(0), one_unit(0), tokens, tokens, tokens, tokens, whole(2, rows, OWN)],
        (me, z_own, z_other, h_own, h_other, a_own, a_other, attended.reshape(2, rows, OWN)),
        "grads1",
    )
    *grads[1], a, b, qkv = reduce(*grads[1], *state, qkv)
    state = attend_back(qkv, *back, 1, 1, (a, b))
    a, b, qkv = reduce(*state, qkv)
    grad_qkv, qkv_sums = attend_back(qkv, *back, 2, seqs - 2, (a, b))
    grad_rows = grad_qkv.reshape(2, rows, 3 * OWN)
    keep, give = grads0(me, grad_rows, u_own.reshape(rows, D), u_other.reshape(rows, D))
    keep, give, grad_rows = reduce(keep, give, grad_rows)
    take = swap(give)
    inputs_other = rows_times(grad_rows, 1, w_qkv, bf16, "inputs_other")
    grads[0] = regroup(me, keep, take)
    *grads[0], grad_rows, inputs_other = reduce(*grads[0], grad_rows, inputs_other)
    sent_inputs = swap(inputs_other)
    inputs_own = rows_times(grad_rows, 0, w_qkv, f32, "inputs_own")
    sent_inputs, inputs_own, z_sums = reduce(sent_inputs, inputs_own, z_sums)
    input_grad, mask_sums = corrupt_back(
        span_mask, replace_kind, replace_from, grad_one, inputs_own, sent_inputs
    )
    bias_sums = jnp.zeros((FF // (2 * CHUNK), 2, CHUNK), f32)
    bias_sums = lax.dynamic_update_slice(
        bias_sums,
        (z_sums + z_other_sums).reshape(FF // (2 * CHUNK), 1, CHUNK),
        (0, core, 0),
    ).reshape(FF // D, D)
    vector_part = vector_rows(me, qkv_sums, one_sums, two_sums, mask_sums, bias_sums)
    input_grad, vector_part = reduce(input_grad, vector_part)
    shard_v = scatter_vectors(vector_part, ranks, vectors.shape[0])
    (shard_v,) = reduce(shard_v)
    reduce()

    if staged:
        shard_half = result[0]
        shard_w = unpack(shard_half, swap(shard_half), index).astype(f32)
    else:
        core_rows = [block for i in range(4) for block in grads[i]]
        core_rows = jnp.concatenate(core_rows, axis=0)
        stacked = unpack(core_rows, swap(core_rows), 0).astype(f32)
        shard_w = lax.psum_scatter(stacked, "dp", scatter_dimension=0, tiled=True)
        shard_half = lax.dynamic_slice_in_dim(shard_w, core * OWN, OWN, axis=1)

    half32 = shard_half.astype(f32)
    squares = jnp.sum(half32 * half32) + 0.5 * jnp.sum(shard_v * shard_v)
    grad_norm = jnp.sqrt(sum_everywhere(squares, ranks))
    clip = 1.0 / jnp.maximum(grad_norm, 1.0)
    weights_new, weight_first_new, weight_second_new = adam_step(
        weights, weight_first, weight_second, shard_w * clip, decay_rate, learn_rate
    )
    vectors_new, vector_first_new, vector_second_new = adam_step(
        vectors, vector_first, vector_second, shard_v * clip, 0.0, vector_rate
    )
    return (
        layer_out.reshape(seqs, half_len, D),
        input_grad,
        grad_norm,
        weights_new,
        weight_first_new,
        weight_second_new,
        vectors_new,
        vector_first_new,
        vector_second_new,
        weights_new.astype(bf16),
        vectors_new.astype(bf16),
    )


def solution(mesh):
    token = P("dp", "seq", None)
    by_row = P("dp", None)
    by_column = P(None, "dp")
    position = P("dp", "seq")
    in_specs = (
        (token,) + (position,) * 3 + (by_row, by_column, by_row, by_row, by_column, by_column, token)
    )
    out_specs = (token, token, P()) + (by_row,) * 3 + (by_column,) * 3 + (by_row, by_column)
    return jax.shard_map(
        functools.partial(shards, mesh.shape["dp"]),
        mesh=mesh,
        in_specs=in_specs,
        out_specs=out_specs,
        check_vma=False,
    )
```

```python
import functools

import jax
import jax.numpy as jnp
from jax import lax
from jax.experimental import pallas as pl
from jax.experimental.pallas import tpu as pltpu
from jax.sharding import PartitionSpec as P

D = 768
HEAD_DIM = 64
FF = 3072
STEP = 10
CHUNK = 96
OWN = D // 2
UNITS = FF // 2

ln_eps = 1e-12
beta_one = 0.9
beta_two = 0.999
adam_eps = 1e-08
learn_rate = 0.05
vector_rate = 0.3
decay_rate = 0.01

bf16 = jnp.bfloat16
f32 = jnp.float32
SWAP = [(0, 1), (1, 0)]


def params(limit=14):
    return pltpu.CompilerParams(vmem_limit_bytes=limit * 2**20)


def cost(micros):
    return pl.CostEstimate(flops=int(micros), bytes_accessed=0, transcendentals=0)


def dot(left, right, over):
    return lax.dot_general(left, right, (over, ((), ())), preferred_element_type=f32)


NT = ((1,), (1,))
NN = ((1,), (0,))
TN = ((0,), (0,))


def swap(value):
    return lax.ppermute(value, "seq", SWAP)


def pack(rows, index):
    core = lax.axis_index("seq")
    chunks = rows.shape[0] // (2 * CHUNK)
    plain = lax.dynamic_index_in_dim(rows.reshape(chunks, 2, CHUNK, D), core, 1, keepdims=False)
    columns = lax.dynamic_slice_in_dim(rows, core * OWN, OWN, axis=1).reshape(chunks, 2, CHUNK, OWN)
    wide = jnp.concatenate([columns[:, 0], columns[:, 1]], axis=-1)
    where = index * chunks + jnp.arange(chunks)
    is_out = ((where >= 12) & (where < 16))[:, None, None]
    return jnp.where(is_out, wide, plain).reshape(chunks * CHUNK, D)


def unpack(mine, theirs, index):
    core = lax.axis_index("seq")
    chunks = mine.shape[0] // CHUNK
    first = jnp.where(core == 0, mine, theirs).reshape(chunks, CHUNK, D)
    second = jnp.where(core == 0, theirs, mine).reshape(chunks, CHUNK, D)
    plain = jnp.stack([first, second], axis=1)
    upper = jnp.concatenate([first[..., :OWN], second[..., :OWN]], axis=-1)
    lower = jnp.concatenate([first[..., OWN:], second[..., OWN:]], axis=-1)
    wide = jnp.stack([upper, lower], axis=1)
    where = index * chunks + jnp.arange(chunks)
    is_out = ((where >= 12) & (where < 16))[:, None, None, None]
    return jnp.where(is_out, wide, plain).reshape(chunks * 2 * CHUNK, D)


SIDE_X = [(i, i ^ 1) for i in range(16)]
SIDE_Y = [(i, i ^ 2) for i in range(16)]


def up(first, last):
    return [(i, i + 4) for i in range(16) if first <= i // 4 <= last]


def down(first, last):
    return [(i, i - 4) for i in range(16) if first <= i // 4 <= last]


def send(value, pairs):
    return lax.ppermute(value, "dp", pairs)


def pick(plane, *options):
    result = options[-1]
    for i in range(len(options) - 2, -1, -1):
        result = jnp.where(plane == i, options[i], result)
    return result


def barrier(*values):
    return lax.optimization_barrier(values)


HALF = 3 * CHUNK // 2


def top(block):
    return block[:HALF]


def bottom(block):
    return block[HALF:]


def join(first, second):
    return jnp.concatenate([first, second], axis=0)


def planes(step, *targets):
    pairs = [(i, i ^ (4 * step)) for i in range(16)]
    return [pair for pair in pairs if not targets or pair[1] // 4 in targets]


PIECES = ((0, 1, 2, 3), (1, 0, 3, 2), (2, 2, 0, 0), (3, 3, 1, 1))


def gather_steps(block, slots):
    odd = lax.axis_index("dp") // 4 % 2 == 1
    x0, y0 = send(block, SIDE_X), send(block, SIDE_Y)
    s1, far = send(block, planes(1)), send(block, planes(2))
    c0 = send(top(x0), SIDE_Y), send(bottom(y0), SIDE_X)
    x0, y0, s1, far, *c0 = yield x0, y0, s1, far, *c0

    x1, y1 = send(s1, SIDE_X), send(s1, SIDE_Y)
    opposite = send(far, planes(1))
    x1, y1, opposite = yield x1, y1, opposite
    slots.append(((block, 0), (x0, 0), (y0, 0), tuple(c0)))

    s2 = jnp.where(odd, opposite, far)
    s3 = jnp.where(odd, far, opposite)
    x2, y2 = send(s2, SIDE_X), send(s2, SIDE_Y)
    c1 = send(top(x1), SIDE_Y), send(bottom(y1), SIDE_X)
    x2, y2, *c1 = yield x2, y2, *c1
    slots.append(((s1, 0), (x1, 0), (y1, 0), tuple(c1)))

    c2 = send(top(x2), SIDE_Y), send(bottom(y2), SIDE_X)
    c2 = yield c2
    slots.append(((s2, 0), (x2, 0), (y2, 0), tuple(c2)))

    x3, y3 = send(s3, SIDE_X), send(s3, SIDE_Y)
    x3, y3 = yield x3, y3
    c3 = send(top(x3), SIDE_Y), send(bottom(y3), SIDE_X)
    slots.append(((s3, 0), (x3, 0), (y3, 0), None))
    c3 = yield c3
    slots[3] = (*slots[3][:3], tuple(c3))


def reduce_steps(grads, plane, result):
    odd = plane % 2 == 1
    got = yield cross(grads[3])
    x, y = yield across(grads[3], got)
    own3 = plus(grads[3][0], x, y)
    got = yield cross(grads[2])
    x, y = yield across(grads[2], got)
    own2 = plus(grads[2][0], x, y)
    got = yield cross(grads[1])
    high = send(jnp.where(odd, own2, own3), planes(1))
    x, y, high = yield *across(grads[1], got), high
    own1 = plus(grads[1][0], x, y)
    high = plus(jnp.where(odd, own3, own2), high)
    yield ()
    got = yield cross(grads[0])
    x, y, one = yield *across(grads[0], got), send(own1, up(0, 0) + down(3, 3))
    own0 = plus(grads[0][0], x, y)
    own1 = plus(own1, one)
    zero, one, two = yield (
        send(own0, down(1, 1) + down(3, 3)),
        send(own1, down(2, 2)),
        send(high, planes(2, 2)),
    )
    own0 = plus(own0, zero)
    zero, three = yield send(own0, planes(2, 0)), send(high, planes(2, 3))
    result.append(pick(plane, plus(own0, zero), plus(own1, one), plus(high, two), plus(high, three)))


class Steps:
    def __init__(self, steps):
        self.steps = steps
        self.arrays = next(steps) if steps else ()

    def __call__(self, *values):
        count = len(self.arrays)
        passed = barrier(*self.arrays, *values) if count or values else ()
        if self.steps:
            try:
                self.arrays = self.steps.send(passed[:count])
            except StopIteration:
                self.steps, self.arrays = None, ()
        return passed[count:]


def parts_of(side):
    if side is None:
        return []
    first, second = side
    if isinstance(second, int):
        rows = 3 * CHUNK
        return [(first, second * rows, rows, 0)]
    return [(first, 0, HALF, 0), (second, 0, HALF, HALF)]


def slot_arrays(slots):
    arrays, known = [], {}
    shape = []
    for slot in slots:
        sides = []
        for side in slot:
            parts = []
            for array, start, rows, place in parts_of(side):
                if id(array) not in known:
                    known[id(array)] = len(arrays)
                    arrays.append(array)
                parts.append((known[id(array)], start, rows, place))
            sides.append(tuple(parts))
        shape.append(tuple(sides))
    return arrays, tuple(shape)


def run_copies(pairs, sems):
    copies = [
        pltpu.make_async_copy(source, target, sems.at[i])
        for i, (source, target) in enumerate(pairs)
    ]
    for copy in copies:
        copy.start()
    for copy in copies:
        copy.wait()


def place_heads_kernel(shape, me_ref, *refs):
    mine_ref, give_ref, whole_ref, sems = refs[-4:]
    spot, core, plane = me_ref[0], me_ref[1], me_ref[2]
    for z in range(4):

        @pl.when(plane == z)
        def _():
            pairs = []
            for side in range(4):
                start = 3 * CHUNK * (side + spot - 2 * (side & spot))
                for number, first, rows, place in shape[min(z, 2)][side]:
                    where = pl.ds(pl.multiple_of(start + place, 16), rows)
                    pairs.append((refs[number].at[pl.ds(first, rows)], whole_ref.at[where]))
            run_copies(pairs, sems)

    for ref, who in ((mine_ref, core), (give_ref, 1 - core)):
        for j in range(6):
            chunk = 4 * (j // 2) + 2 * who + j % 2
            ref[j] = whole_ref[pl.ds(pl.multiple_of(chunk * CHUNK, 16), CHUNK)]


def place_heads(me, slots):
    arrays, shape = slot_arrays(slots)
    half = jax.ShapeDtypeStruct((6, CHUNK, D), bf16)
    return pl.pallas_call(
        functools.partial(place_heads_kernel, shape),
        in_specs=[pl.BlockSpec(memory_space=pltpu.SMEM)]
        + [pl.BlockSpec(memory_space=pl.ANY)] * len(arrays),
        out_shape=[half, half],
        scratch_shapes=[pltpu.VMEM((12 * CHUNK, D), bf16), pltpu.SemaphoreType.DMA((8,))],
        compiler_params=params(),
        cost_estimate=cost(1),
        name="place_heads",
    )(me, *arrays)


def place_rest_kernel(shape, held, me_ref, *refs):
    out_ref, in_ref, down_ref, stage_ref, load_sems, store_sems = refs[-6:]
    spot, plane = me_ref[0], me_ref[2]

    def part(pairs, source, first, rows, row):
        while rows:
            if row < 4 * CHUNK:
                chunk, offset = divmod(row, CHUNK)
                count = min(rows, CHUNK - offset)
                targets = []
                for h in range(2):
                    target = 2 * CHUNK * chunk + CHUNK * h + offset
                    targets.append((pl.ds(OWN * h, OWN), out_ref.at[pl.ds(target, count)]))
            else:
                ref, start = (in_ref, 4 * CHUNK) if row < 20 * CHUNK else (down_ref, 20 * CHUNK)
                count = min(rows, start + 16 * CHUNK - row)
                targets = [(slice(None), ref.at[pl.ds(row - start, count)])]
            pairs.append((source.at[pl.ds(first, count)], count, targets))
            row, first, rows = row + count, first + count, rows - count

    for z in range(4):
        for s in range(4):
            pairs = []
            for slot, (number, sides) in zip(shape, held, strict=True):
                piece = PIECES[number][z]
                for side in sides if piece else ():
                    base = 3 * CHUNK * (4 * (piece - 1) + (side ^ s))
                    for array, first, rows, place in slot[side]:
                        part(pairs, refs[array], first, rows, base + place)

            @pl.when((plane == z) & (spot == s))
            def _():
                loads, stores, row = [], [], 0
                for i, (source, count, targets) in enumerate(pairs):
                    spot_rows = pl.ds(row, count)
                    loads.append(
                        pltpu.make_async_copy(source, stage_ref.at[spot_rows], load_sems.at[i])
                    )
                    stores.append([])
                    for columns, target in targets:
                        stores[-1].append(
                            pltpu.make_async_copy(
                                stage_ref.at[spot_rows, columns],
                                target,
                                store_sems.at[2 * i + len(stores[-1])],
                            )
                        )
                    row += count
                for load in loads:
                    load.start()
                for load, store in zip(loads, stores, strict=True):
                    load.wait()
                    for copy in store:
                        copy.start()
                for store in stores:
                    for copy in store:
                        copy.wait()


def place_rest(me, slots, held, state):
    arrays, shape = slot_arrays(
        [[slots[i][side] if side in sides else None for side in range(4)] for i, sides in held]
    )
    units = jax.ShapeDtypeStruct((UNITS, D), bf16)
    anywhere = pl.BlockSpec(memory_space=pl.ANY)
    return pl.pallas_call(
        functools.partial(place_rest_kernel, shape, held),
        in_specs=[pl.BlockSpec(memory_space=pltpu.SMEM)] + [anywhere] * (len(arrays) + len(state)),
        out_specs=[anywhere] * 3,
        out_shape=[jax.ShapeDtypeStruct((D, OWN), bf16), units, units],
        input_output_aliases={1 + len(arrays) + i: i for i in range(len(state))},
        scratch_shapes=[
            pltpu.VMEM((24 * CHUNK, D), bf16),
            pltpu.SemaphoreType.DMA((32,)),
            pltpu.SemaphoreType.DMA((64,)),
        ],
        compiler_params=params(),
        cost_estimate=cost(1),
        name="place_rest",
    )(me, *arrays, *state)


def plus(*values):
    total = values[0].astype(f32)
    for value in values[1:]:
        total = total + value.astype(f32)
    return total.astype(bf16)


def cross(sides):
    return send(sides[3], SIDE_Y), send(sides[4], SIDE_X)


def merge_kernel(x_ref, y_ref, upper_ref, lower_ref, x_out, y_out):
    x_out[:HALF] = (x_ref[:HALF].astype(f32) + upper_ref[...].astype(f32)).astype(bf16)
    x_out[HALF:] = x_ref[HALF:]
    y_out[:HALF] = y_ref[:HALF]
    y_out[HALF:] = (y_ref[HALF:].astype(f32) + lower_ref[...].astype(f32)).astype(bf16)


def across(sides, crossed):
    over_x, over_y = pl.pallas_call(
        merge_kernel,
        out_shape=[jax.ShapeDtypeStruct((3 * CHUNK, D), bf16)] * 2,
        compiler_params=params(),
        cost_estimate=cost(1),
        name="merge",
    )(sides[1], sides[2], *crossed)
    return send(over_x, SIDE_X), send(over_y, SIDE_Y)


def gather_vectors(low_vectors, ranks):
    count, width = low_vectors.shape
    block = jnp.pad(low_vectors, ((0, 16 - count), (0, 128 - width)))
    blocks = lax.all_to_all(jnp.broadcast_to(block, (ranks, 16, 128)), "dp", 0, 0, tiled=True)
    return blocks[:, :count, :width].transpose(1, 0, 2).reshape(count, ranks * width).astype(f32)


def scatter_vectors(rows, ranks, count):
    width = D // ranks
    blocks = rows.reshape(16, ranks, width).transpose(1, 0, 2)
    blocks = jnp.pad(blocks, ((0, 0), (0, 0), (0, 128 - width)))
    blocks = lax.all_to_all(blocks, "dp", 0, 0, tiled=True)
    return jnp.sum(blocks, axis=0)[:count, :width]


def selection(span, kind, source, half_len):
    chosen = span == 1
    masked = chosen & (kind < 8)
    swapped = chosen & (kind == 8)
    here = lax.broadcasted_iota(jnp.int32, (1, half_len), 1)
    origin = jnp.where(masked, -1, jnp.where(swapped, source, here))
    rows = lax.broadcasted_iota(jnp.int32, (half_len, half_len), 0)
    one_hot = (rows == origin).astype(f32).astype(bf16)
    first = lax.broadcasted_iota(jnp.int32, (16, half_len), 0) == 0
    mask_rows = jnp.where(first & masked, 1.0, 0.0).astype(bf16)
    return one_hot, mask_rows


def corrupt_kernel(span_ref, kind_ref, from_ref, hidden_ref, mask_ref, out_ref):
    seqs, half_len = span_ref.shape
    for s in range(seqs):
        rows = slice(s, s + 1)
        one_hot, mask_rows = selection(
            span_ref[rows, :], kind_ref[rows, :], from_ref[rows, :], half_len
        )
        picked = dot(one_hot, hidden_ref[s], TN) + dot(mask_rows, mask_ref[...], TN)
        out_ref[s] = picked.astype(bf16)


def corrupt(span, kind, source, hidden, mask_row):
    mask = jnp.broadcast_to(mask_row.astype(bf16)[None], (16, D))
    return pl.pallas_call(
        corrupt_kernel,
        out_shape=jax.ShapeDtypeStruct(hidden.shape, bf16),
        compiler_params=params(),
        name="corrupt",
    )(span, kind, source, hidden, mask)


def corrupt_back_kernel(
    span_ref, kind_ref, from_ref, grad_ref, own_ref, partial_ref, out_ref, mask_ref
):
    seqs, half_len = span_ref.shape
    mask_sum = jnp.zeros((16, D), f32)
    for s in range(seqs):
        rows = slice(s, s + 1)
        block = pl.ds(s * half_len, half_len)
        one_hot, mask_rows = selection(
            span_ref[rows, :], kind_ref[rows, :], from_ref[rows, :], half_len
        )
        grad = grad_ref[block] + own_ref[block] + partial_ref[block].astype(f32)
        high = grad.astype(bf16)
        low = (grad - high.astype(f32)).astype(bf16)
        out_ref[s] = dot(one_hot, high, NN) + dot(one_hot, low, NN)
        mask_sum = mask_sum + dot(mask_rows, high, NN) + dot(mask_rows, low, NN)
    mask_ref[...] = mask_sum


def corrupt_back(span, kind, source, grad, own, partial):
    seqs, half_len = span.shape
    return pl.pallas_call(
        corrupt_back_kernel,
        out_shape=[
            jax.ShapeDtypeStruct((seqs, half_len, D), f32),
            jax.ShapeDtypeStruct((16, D), f32),
        ],
        compiler_params=params(),
        cost_estimate=cost(1),
        name="corrupt_back",
    )(span, kind, source, grad, own, partial)


def attend_kernel(
    me_ref, own_ref, other_ref, mine_ref, theirs_ref, vals_ref, w_ref, qkv_ref, low_ref, wide_ref, lse_ref
):
    half_len = own_ref.shape[1]
    core = me_ref[1]

    @pl.when(pl.program_id(0) == 0)
    def _():
        for j in range(6):
            for ref, which in ((mine_ref, core), (theirs_ref, 1 - core)):
                where = pl.ds(pl.multiple_of((2 * j + which) * CHUNK, 16), CHUNK)
                w_ref[where] = ref[j]

    rows = jnp.concatenate([own_ref[0], other_ref[0]], axis=0)
    columns = pl.ds(pl.multiple_of(core * OWN, 128), OWN)
    bias = jnp.concatenate(
        [vals_ref[0:1, columns], jnp.zeros((1, OWN), f32), vals_ref[1:2, columns]], axis=-1
    )
    projected = (dot(rows, w_ref[...], NT) + bias).astype(bf16)
    qkv_ref[:, 0] = projected.reshape(2, half_len, 3 * OWN)
    wide, totals = [], []
    for h in range(OWN // HEAD_DIM):
        columns = slice(h * HEAD_DIM, (h + 1) * HEAD_DIM)
        query = projected[:, :OWN][:, columns] * bf16(HEAD_DIM**-0.5)
        key = projected[:, OWN : 2 * OWN][:, columns]
        value = projected[:, 2 * OWN :][:, columns]
        scores = dot(query, key, NT)
        highest = jnp.max(scores, axis=-1, keepdims=True)
        exponents = jnp.exp(scores - highest)
        total = jnp.sum(exponents, axis=-1, keepdims=True)
        probabilities = (exponents / total).astype(bf16)
        wide.append(dot(probabilities, value, NN))
        totals.append(highest + jnp.log(total))
    attended = jnp.concatenate(wide, axis=-1)
    wide_ref[:, 0] = attended.reshape(2, half_len, OWN)
    low_ref[:, 0] = attended.astype(bf16).reshape(2, half_len, OWN)
    fill = jnp.zeros((2 * half_len, 128 - len(totals)), f32)
    lse_ref[0] = jnp.concatenate(totals + [fill], axis=-1).T[:8]


def whole(*shape):
    return pl.BlockSpec(shape, lambda *_: (0,) * len(shape))


def attend(me, u_own, u_other, mine, theirs, vals):
    seqs, half_len, _ = u_own.shape
    block = lambda width: pl.BlockSpec((2, 1, half_len, width), lambda s: (0, s, 0, 0))
    token = pl.BlockSpec((1, half_len, D), lambda s: (s, 0, 0))
    return pl.pallas_call(
        attend_kernel,
        grid=(seqs,),
        in_specs=[
            pl.BlockSpec(memory_space=pltpu.SMEM),
            token,
            token,
            whole(6, CHUNK, D),
            whole(6, CHUNK, D),
            whole(*vals.shape),
        ],
        out_specs=[
            whole(3 * OWN, D),
            block(3 * OWN),
            block(OWN),
            block(OWN),
            pl.BlockSpec((1, 8, 2 * half_len), lambda s: (s, 0, 0)),
        ],
        out_shape=[
            jax.ShapeDtypeStruct((3 * OWN, D), bf16),
            jax.ShapeDtypeStruct((2, seqs, half_len, 3 * OWN), bf16),
            jax.ShapeDtypeStruct((2, seqs, half_len, OWN), bf16),
            jax.ShapeDtypeStruct((2, seqs, half_len, OWN), f32),
            jax.ShapeDtypeStruct((seqs, 8, 2 * half_len), f32),
        ],
        cost_estimate=cost(3),
        compiler_params=params(),
        name="attend",
    )(me, u_own, u_other, mine, theirs, vals)


def attend_back_kernel(
    skip, qkv_ref, own_ref, other_ref, wo_ref, wide_ref, lse_ref, *refs
):
    out_ref, sums_ref = refs[skip:]
    half_len = qkv_ref.shape[2]
    length = 2 * half_len
    projected = qkv_ref[:, 0].reshape(length, 3 * OWN)
    rows = jnp.concatenate([own_ref[0], other_ref[0]], axis=0)
    grad = dot(rows, wo_ref[...], NN).astype(bf16)
    product = grad.astype(f32) * wide_ref[:, 0].reshape(length, OWN)
    heads = OWN // HEAD_DIM
    deltas = [
        jnp.sum(product[:, h * HEAD_DIM : (h + 1) * HEAD_DIM], axis=-1, keepdims=True)
        for h in range(heads)
    ]
    fill = jnp.zeros((length, 128 - heads), f32)
    delta_rows = jnp.concatenate(deltas + [fill], axis=-1).T
    parts = [[], [], []]
    for h in range(heads):
        columns = slice(h * HEAD_DIM, (h + 1) * HEAD_DIM)
        query = projected[:, :OWN][:, columns] * bf16(HEAD_DIM**-0.5)
        key = projected[:, OWN : 2 * OWN][:, columns]
        value = projected[:, 2 * OWN :][:, columns]
        grad_head = grad[:, columns]
        weights = jnp.exp(dot(key, query, NT) - lse_ref[0, h : h + 1, :])
        grad_weights = dot(value, grad_head, NT)
        grad_scores = (weights * (grad_weights - delta_rows[h : h + 1, :])).astype(bf16)
        parts[0].append(dot(grad_scores, key, TN) * HEAD_DIM**-0.5)
        parts[1].append(dot(grad_scores, query, NN))
        parts[2].append(dot(weights.astype(bf16), grad_head, NN))
    result = jnp.concatenate(parts[0] + parts[1] + parts[2], axis=-1).astype(bf16)
    out_ref[:, 0] = result.reshape(2, half_len, 3 * OWN)
    sums = jnp.sum(result.astype(f32), axis=0, keepdims=True)

    @pl.when(pl.program_id(0) == 0)
    def _():
        sums_ref[...] = refs[1][...] if skip else jnp.zeros_like(sums_ref)

    sums_ref[...] += sums


def attend_back(qkv, own, other, wo_own, wide, lse, first, count, state):
    _, seqs, half_len, _ = qkv.shape
    block = lambda width: pl.BlockSpec((2, 1, half_len, width), lambda s: (0, s + first, 0, 0))
    token = pl.BlockSpec((1, half_len, D), lambda s: (s + first, 0, 0))
    return pl.pallas_call(
        functools.partial(attend_back_kernel, len(state)),
        grid=(count,),
        in_specs=[
            block(3 * OWN),
            token,
            token,
            whole(D, OWN),
            block(OWN),
            pl.BlockSpec((1, 8, 2 * half_len), lambda s: (s + first, 0, 0)),
        ]
        + ([pl.BlockSpec(memory_space=pl.ANY), whole(1, 3 * OWN)] if state else []),
        out_specs=[block(3 * OWN), whole(1, 3 * OWN)],
        input_output_aliases={6: 0} if state else {},
        out_shape=[
            jax.ShapeDtypeStruct((2, seqs, half_len, 3 * OWN), bf16),
            jax.ShapeDtypeStruct((1, 3 * OWN), f32),
        ],
        cost_estimate=cost(2 * count),
        compiler_params=params(),
        name="attend_back",
    )(qkv, own, other, wo_own, wide, lse, *state)


def norm(values):
    center = values - jnp.mean(values, axis=-1, keepdims=True)
    inv_std = lax.rsqrt(jnp.mean(center * center, axis=-1, keepdims=True) + ln_eps)
    return center * inv_std, inv_std


def norm_backward(upstream, normed, inv_std, gain):
    scaled = upstream * gain
    return inv_std * (
        scaled
        - jnp.mean(scaled, axis=-1, keepdims=True)
        - normed * jnp.mean(scaled * normed, axis=-1, keepdims=True)
    )


def row(ref, i):
    return ref[i : i + 1, :]


def branch_kernel(own_ref, other_ref, u_ref, wo_ref, wo_other_ref, vals_ref, normed_ref, inv_ref, low_ref):
    branch = dot(own_ref[0, 0], wo_ref[...], NT) + dot(other_ref[0], wo_other_ref[...], NT)
    normed, inv = norm(u_ref[0].astype(f32) + branch + row(vals_ref, 2))
    normed_ref[...] = normed
    inv_ref[...] = jnp.broadcast_to(inv, inv_ref.shape)
    low_ref[...] = (normed * row(vals_ref, 3) + row(vals_ref, 4)).astype(bf16)


def attention_branch(attended, from_other, u_own, wo_own, wo_other, vals):
    seqs, half_len, _ = u_own.shape
    rows = pl.BlockSpec((half_len, D), lambda s: (s, 0))
    return pl.pallas_call(
        branch_kernel,
        grid=(seqs,),
        in_specs=[
            pl.BlockSpec((1, 1, half_len, OWN), lambda s: (0, s, 0, 0)),
            pl.BlockSpec((1, half_len, OWN), lambda s: (s, 0, 0)),
            pl.BlockSpec((1, half_len, D), lambda s: (s, 0, 0)),
            whole(D, OWN),
            whole(D, OWN),
            whole(*vals.shape),
        ],
        out_specs=[rows, pl.BlockSpec((half_len, 128), lambda s: (s, 0)), rows],
        out_shape=[
            jax.ShapeDtypeStruct((seqs * half_len, D), f32),
            jax.ShapeDtypeStruct((seqs * half_len, 128), f32),
            jax.ShapeDtypeStruct((seqs * half_len, D), bf16),
        ],
        cost_estimate=cost(1),
        compiler_params=params(),
        name="attention_branch",
    )(attended, from_other, u_own, wo_own, wo_other, vals)


def hidden_kernel(own_ref, other_ref, w_ref, bias_ref, gelu_ref, slope_ref):
    for half, ref in enumerate((own_ref, other_ref)):
        points = dot(ref[...], w_ref[...], NT) + bias_ref[...]
        below = 0.5 * (1.0 + lax.erf(points * 2**-0.5))
        density = jnp.exp(-0.5 * points * points) * 0.3989422804014327
        gelu_ref[half] = (points * below).astype(bf16)
        slope_ref[half] = (below + points * density).astype(bf16)


def hidden_units(h_own, h_other, w_in, bias):
    rows = h_own.shape[0]
    width = 256
    block = pl.BlockSpec((2, rows, width), lambda i: (0, 0, i))
    return pl.pallas_call(
        hidden_kernel,
        grid=(UNITS // width,),
        in_specs=[
            whole(rows, D),
            whole(rows, D),
            pl.BlockSpec((width, D), lambda i: (i, 0)),
            pl.BlockSpec((1, width), lambda i: (0, i)),
        ],
        out_specs=[block, block],
        out_shape=[jax.ShapeDtypeStruct((2, rows, UNITS), bf16)] * 2,
        cost_estimate=cost(3),
        compiler_params=params(),
        name="hidden_units",
    )(h_own, h_other, w_in, bias)


def rows_kernel(left_ref, right_ref, out_ref):
    out_ref[...] = dot(left_ref[0], right_ref[...], NN).astype(out_ref.dtype)


def rows_times(left, half, right, dtype, name):
    _, rows, depth = left.shape
    tile = rows // 3
    return pl.pallas_call(
        rows_kernel,
        grid=(3,),
        in_specs=[pl.BlockSpec((1, tile, depth), lambda i: (half, i, 0)), whole(*right.shape)],
        out_specs=pl.BlockSpec((tile, D), lambda i: (i, 0)),
        out_shape=jax.ShapeDtypeStruct((rows, D), dtype),
        cost_estimate=cost(1),
        compiler_params=params(),
        name=name,
    )(left, right)


def add_sums(sums_ref, *values):
    @pl.when(pl.program_id(0) == 0)
    def _():
        sums_ref[...] = jnp.zeros_like(sums_ref)

    for i, value in enumerate(values):
        sums_ref[i : i + 1, :] += jnp.sum(value, axis=0, keepdims=True)


def finish_kernel(own_ref, other_ref, normed_ref, grad_ref, vals_ref, out_ref, wide_ref, low_ref, sums_ref):
    hidden_one = normed_ref[...] * row(vals_ref, 3) + row(vals_ref, 4)
    feed = own_ref[...] + other_ref[...].astype(f32) + row(vals_ref, 5)
    normed, inv = norm(hidden_one + feed)
    out_ref[...] = normed * row(vals_ref, 6) + row(vals_ref, 7)
    grad = grad_ref[...].astype(f32)
    wide = norm_backward(grad, normed, inv, row(vals_ref, 6))
    low = wide.astype(bf16)
    wide_ref[...] = wide
    low_ref[...] = low
    add_sums(sums_ref, low.astype(f32), grad * normed, grad)


def finish(own, other, normed, grad, vals):
    rows = own.shape[0]
    tile = rows // 3
    block = pl.BlockSpec((tile, D), lambda i: (i, 0))
    return pl.pallas_call(
        finish_kernel,
        grid=(3,),
        in_specs=[block] * 4 + [whole(*vals.shape)],
        out_specs=[block] * 3 + [whole(8, D)],
        out_shape=[
            jax.ShapeDtypeStruct((rows, D), f32),
            jax.ShapeDtypeStruct((rows, D), f32),
            jax.ShapeDtypeStruct((rows, D), bf16),
            jax.ShapeDtypeStruct((8, D), f32),
        ],
        cost_estimate=cost(1),
        compiler_params=params(),
        name="finish",
    )(own, other, normed, grad, vals)


def norm_one_kernel(two_ref, own_ref, other_ref, normed_ref, inv_ref, vals_ref, wide_ref, low_ref, sums_ref):
    grad = two_ref[...] + own_ref[...] + other_ref[...].astype(f32)
    normed = normed_ref[...]
    wide = norm_backward(grad, normed, inv_ref[:, 0:1], row(vals_ref, 3))
    low = wide.astype(bf16)
    wide_ref[...] = wide
    low_ref[...] = low
    add_sums(sums_ref, low.astype(f32), grad * normed, grad)


def norm_one_back(two, own, other, normed, inv, vals):
    rows = own.shape[0]
    tile = rows // 3
    block = pl.BlockSpec((tile, D), lambda i: (i, 0))
    return pl.pallas_call(
        norm_one_kernel,
        grid=(3,),
        in_specs=[block] * 4 + [pl.BlockSpec((tile, 128), lambda i: (i, 0)), whole(*vals.shape)],
        out_specs=[block] * 2 + [whole(8, D)],
        out_shape=[
            jax.ShapeDtypeStruct((rows, D), f32),
            jax.ShapeDtypeStruct((rows, D), bf16),
            jax.ShapeDtypeStruct((8, D), f32),
        ],
        cost_estimate=cost(1),
        compiler_params=params(),
        name="norm_one_back",
    )(two, own, other, normed, inv, vals)


def slope_kernel(grad_ref, w_ref, slope_ref, out_ref, sums_ref):
    low = (dot(grad_ref[...], w_ref[...], NT) * slope_ref[0].astype(f32)).astype(bf16)
    out_ref[0] = low
    sums_ref[...] = jnp.sum(low.astype(f32), axis=0, keepdims=True)


def before_gelu(grad, w_down, slope, half):
    rows = grad.shape[0]
    width = 384
    return pl.pallas_call(
        slope_kernel,
        grid=(UNITS // width,),
        in_specs=[
            whole(rows, D),
            pl.BlockSpec((width, D), lambda i: (i, 0)),
            pl.BlockSpec((1, rows, width), lambda i: (half, 0, i)),
        ],
        out_specs=[
            pl.BlockSpec((1, rows, width), lambda i: (0, 0, i)),
            pl.BlockSpec((1, width), lambda i: (0, i)),
        ],
        out_shape=[
            jax.ShapeDtypeStruct((1, rows, UNITS), bf16),
            jax.ShapeDtypeStruct((1, UNITS), f32),
        ],
        cost_estimate=cost(1),
        compiler_params=params(),
        name="before_gelu",
    )(grad, w_down, slope)


def rows_of(count):
    return jax.ShapeDtypeStruct((count, D), bf16)


CROSS = ((0, 0, 288), (1, 0, 288), (2, 0, 288), (3, 0, 144), (3, 144, 144))


def side_rows(spot, side, first, rows):
    start = 3 * CHUNK * (side + spot - 2 * (side & spot)) + first
    return pl.ds(pl.multiple_of(start, 16), rows)


def write_sides(spot, piece_ref, outs):
    for out, (side, first, rows) in zip(outs, CROSS, strict=True):
        out[...] = piece_ref[side_rows(spot, side, first, rows)]


def rows_at(step):
    return pl.ds(pl.multiple_of(step * OWN, 16), OWN)


def two_halves(left, left_other, right, right_other):
    return dot(left, right, TN) + dot(left_other, right_other, TN)


def grads3_kernel(me_ref, g_ref, d_ref, d_other_ref, *refs):
    piece_ref = refs[-1]
    step = pl.program_id(0)
    piece_ref[rows_at(step)] = two_halves(
        g_ref[0], g_ref[1], d_ref[...], d_other_ref[...]
    ).astype(bf16)

    @pl.when(step == 2)
    def _():
        write_sides(me_ref[0], piece_ref, refs[:-1])


def grads2_kernel(me_ref, z_ref, z_other_ref, h_ref, h_other_ref, g_ref, d_ref, d_other_ref, *refs):
    piece_ref = refs[-1]
    step = pl.program_id(0)

    @pl.when(step < 2)
    def _():
        piece_ref[rows_at(step)] = two_halves(
            z_ref[0], z_other_ref[0], h_ref[...], h_other_ref[...]
        ).astype(bf16)

    @pl.when(step == 2)
    def _():
        piece_ref[rows_at(step)] = two_halves(
            g_ref[0], g_ref[1], d_ref[...], d_other_ref[...]
        ).astype(bf16)
        write_sides(me_ref[0], piece_ref, refs[:-1])


def grads1_kernel(me_ref, z_ref, z_other_ref, h_ref, h_other_ref, a_ref, a_other_ref, att_ref, *refs):
    piece_ref = refs[-1]
    step = pl.program_id(0)

    @pl.when(step < 2)
    def _():
        piece_ref[rows_at(step + 1)] = two_halves(
            z_ref[0], z_other_ref[0], h_ref[...], h_other_ref[...]
        ).astype(bf16)

    @pl.when(step == 2)
    def _():
        wo = two_halves(a_ref[...], a_other_ref[...], att_ref[0], att_ref[1]).astype(bf16)
        for j in range(4):
            upper = wo[2 * CHUNK * j : 2 * CHUNK * j + CHUNK]
            lower = wo[2 * CHUNK * j + CHUNK : 2 * CHUNK * (j + 1)]
            piece_ref[CHUNK * j : CHUNK * (j + 1)] = jnp.concatenate([upper, lower], axis=-1)
        write_sides(me_ref[0], piece_ref, refs[:-1])


def grads_call(kernel, specs, arrays, name):
    return pl.pallas_call(
        kernel,
        grid=(3,),
        in_specs=[pl.BlockSpec(memory_space=pltpu.SMEM)] + specs,
        out_specs=[whole(count, D) for _, _, count in CROSS],
        out_shape=[rows_of(count) for _, _, count in CROSS],
        scratch_shapes=[pltpu.VMEM((12 * CHUNK, D), bf16)],
        cost_estimate=cost(2),
        compiler_params=params(),
        name=name,
    )(*arrays)


def grads0_kernel(me_ref, g_ref, u_ref, u_other_ref, keep_ref, give_ref, piece_ref):
    core = me_ref[1]
    step = pl.program_id(0)
    piece_ref[rows_at(step)] = two_halves(
        g_ref[0], g_ref[1], u_ref[...], u_other_ref[...]
    ).astype(bf16)

    @pl.when(step == 2)
    def _():
        for j in range(6):
            for ref, which in ((keep_ref, core), (give_ref, 1 - core)):
                where = pl.ds(pl.multiple_of((2 * j + which) * CHUNK, 16), CHUNK)
                ref[j] = piece_ref[where]


def grads0(me, grad, u_own, u_other):
    rows = grad.shape[1]
    half = jax.ShapeDtypeStruct((6, CHUNK, D), bf16)
    return pl.pallas_call(
        grads0_kernel,
        grid=(3,),
        in_specs=[
            pl.BlockSpec(memory_space=pltpu.SMEM),
            pl.BlockSpec((2, rows, OWN), lambda i: (0, 0, i)),
            whole(rows, D),
            whole(rows, D),
        ],
        out_specs=[whole(6, CHUNK, D)] * 2,
        out_shape=[half, half],
        scratch_shapes=[pltpu.VMEM((12 * CHUNK, D), bf16)],
        cost_estimate=cost(2),
        compiler_params=params(),
        name="grads0",
    )(me, grad, u_own, u_other)


def regroup_kernel(me_ref, keep_ref, take_ref, *refs):
    piece_ref = refs[-1]
    core = me_ref[1]
    for ref, who in ((keep_ref, core), (take_ref, 1 - core)):
        for j in range(6):
            chunk = 4 * (j // 2) + 2 * who + j % 2
            piece_ref[pl.ds(pl.multiple_of(chunk * CHUNK, 16), CHUNK)] = ref[j]
    write_sides(me_ref[0], piece_ref, refs[:-1])


def regroup(me, keep, take):
    return pl.pallas_call(
        regroup_kernel,
        in_specs=[pl.BlockSpec(memory_space=pltpu.SMEM)]
        + [pl.BlockSpec(memory_space=pltpu.VMEM)] * 2,
        out_shape=[rows_of(count) for _, _, count in CROSS],
        scratch_shapes=[pltpu.VMEM((12 * CHUNK, D), bf16)],
        cost_estimate=cost(1),
        compiler_params=params(),
        name="regroup",
    )(me, keep, take)


def vector_kernel(me_ref, qkv_ref, one_ref, two_ref, mask_ref, bias_ref, out_ref):
    out_ref[...] = jnp.zeros_like(out_ref)
    columns = pl.ds(pl.multiple_of(me_ref[1] * OWN, 128), OWN)
    out_ref[0:1, columns] = qkv_ref[:, :OWN]
    out_ref[1:2, columns] = qkv_ref[:, 2 * OWN :]
    out_ref[2:5, :] = one_ref[0:3, :]
    out_ref[5:8, :] = two_ref[0:3, :]
    out_ref[8:9, :] = mask_ref[0:1, :]
    out_ref[9:13, :] = bias_ref[...]


def vector_rows(me, qkv_sums, one_sums, two_sums, mask_sums, bias_sums):
    return pl.pallas_call(
        vector_kernel,
        in_specs=[pl.BlockSpec(memory_space=pltpu.SMEM)]
        + [pl.BlockSpec(memory_space=pltpu.VMEM)] * 5,
        out_shape=jax.ShapeDtypeStruct((16, D), f32),
        cost_estimate=cost(1),
        name="vector_rows",
    )(me, qkv_sums, one_sums, two_sums, mask_sums, bias_sums)


def adam_step(master, first_old, second, gradient, decay_on, step_rate):
    first_new = beta_one * first_old + (1.0 - beta_one) * gradient
    second_new = beta_two * second + (1.0 - beta_two) * gradient * gradient
    fix_one = 1.0 - beta_one**STEP
    fix_two = 1.0 - beta_two**STEP
    update = first_new / fix_one / (jnp.sqrt(second_new / fix_two) + adam_eps)
    return (master - step_rate * (update + decay_on * master), first_new, second_new)


def update_kernel(sums_ref, grad_ref, *refs):
    norm_value = jnp.sqrt(jnp.sum(sums_ref[...], axis=0))[0:1, 0:1]
    clip = 1.0 / jnp.maximum(norm_value, 1.0)
    master, first, second = (ref[...] for ref in refs[:3])
    gradient = grad_ref[...].astype(f32) * clip
    master, first, second = adam_step(master, first, second, gradient, decay_rate, learn_rate)
    for ref, value in zip(refs[3:], (master, first, second, master.astype(bf16)), strict=True):
        ref[...] = value


def update_weights(sums, grad, master, first, second):
    rows = grad.shape[0]
    tile = 144 if rows % 144 == 0 else rows
    block = pl.BlockSpec((tile, D), lambda i: (i, 0))
    return pl.pallas_call(
        update_kernel,
        grid=(rows // tile,),
        in_specs=[whole(*sums.shape)] + [block] * 4,
        out_specs=[block] * 4,
        out_shape=[jax.ShapeDtypeStruct((rows, D), f32)] * 3
        + [jax.ShapeDtypeStruct((rows, D), bf16)],
        cost_estimate=cost(1),
        compiler_params=params(),
        name="update_weights",
    )(sums, grad, master, first, second)


def shards(
    ranks,
    hidden,
    span_mask,
    replace_kind,
    replace_from,
    weights,
    vectors,
    weight_first,
    weight_second,
    vector_first,
    vector_second,
    cotangent,
):
    seqs, half_len, _ = hidden.shape
    rows = seqs * half_len
    index = lax.axis_index("dp")
    core = lax.axis_index("seq")
    staged = ranks == 16
    plane = index // 4
    spot = index % 4 if staged else jnp.zeros_like(index)
    me = jnp.stack([spot, core, plane]).astype(jnp.int32)
    low_weights = weights.astype(bf16)
    slots, grads, result = [], {}, []
    if staged:
        gather = Steps(gather_steps(pack(low_weights, index), slots))
    else:
        gather = Steps(None)
        stacked = pack(lax.all_gather(low_weights, "dp", axis=0, tiled=True), 0)

    gather()
    gather()
    vals = gather_vectors(vectors.astype(bf16), ranks)
    every, rest = (0, 1, 2, 3), ()
    if staged:
        rest = place_rest(me, slots, ((0, every),), ())
    vals, *rest = gather(vals, *rest)
    u_own = corrupt(span_mask, replace_kind, replace_from, hidden, vals[8])
    bias_in = lax.dynamic_index_in_dim(
        vals[9:].reshape(FF // (2 * CHUNK), 2, CHUNK), core, 1, keepdims=False
    ).reshape(1, UNITS)
    if staged:
        rest = place_rest(me, slots, ((1, every),), rest)
    u_own, vals, bias_in, *rest = gather(u_own, vals, bias_in, *rest)
    u_other = swap(u_own)

    if staged:
        mine, give = place_heads(me, slots)
    else:
        halves = stacked[: 12 * CHUNK].reshape(3, 2, 2, CHUNK, D)
        mine = lax.dynamic_index_in_dim(halves, core, 1, keepdims=False).reshape(6, CHUNK, D)
        give = lax.dynamic_index_in_dim(halves, 1 - core, 1, keepdims=False).reshape(6, CHUNK, D)
    w_qkv, qkv, attended, attended_wide, lse = attend(
        me, u_own, u_other, mine, swap(give), vals
    )
    w_qkv, qkv, attended, attended_wide, lse, *rest = gather(
        w_qkv, qkv, attended, attended_wide, lse, *rest
    )
    from_other = swap(attended[1])
    if staged:
        rest = place_rest(me, slots, ((2, every), (3, (0, 1, 2))), rest)
    attended, from_other, *rest = gather(attended, from_other, *rest)

    if staged:
        wo_own, w_in, w_down = place_rest(me, slots, ((3, (3,)),), rest)
    else:
        rest = stacked[12 * CHUNK :]
        wo_own = (
            rest[: 4 * CHUNK].reshape(4, CHUNK, 2, OWN).transpose(0, 2, 1, 3).reshape(D, OWN)
        )
        w_in, w_down = rest[4 * CHUNK : 20 * CHUNK], rest[20 * CHUNK :]
    normed_one, inv_one, h_own = attention_branch(
        attended, from_other, u_own, wo_own, swap(wo_own), vals
    )
    h_other = swap(h_own)
    gelu, slope = hidden_units(h_own, h_other, w_in, bias_in)
    feed_other = swap(rows_times(gelu, 1, w_down, bf16, "feed_other"))
    feed_own = rows_times(gelu, 0, w_down, f32, "feed_own")
    layer_out, grad_two, d_own, two_sums = finish(
        feed_own, feed_other, normed_one, cotangent.reshape(rows, D), vals
    )

    d_other = swap(d_own)
    z_own, z_sums = before_gelu(d_own, w_down, slope, 0)
    d_other, z_own, z_sums = barrier(d_other, z_own, z_sums)
    unit = lambda first: pl.BlockSpec((2, rows, OWN), lambda i: (0, 0, i + first))
    one_unit = lambda first: pl.BlockSpec((1, rows, OWN), lambda i: (0, 0, jnp.minimum(i, 1) + first))
    tokens = whole(rows, D)
    grads[3] = grads_call(
        grads3_kernel, [unit(1), tokens, tokens], (me, gelu, d_own, d_other), "grads3"
    )
    *grads[3], d_other = barrier(*grads[3], d_other)
    reduce = Steps(reduce_steps(grads, plane, result) if staged else None)
    z_other, z_other_sums = before_gelu(d_other, w_down, slope, 1)
    hidden_other = rows_times(z_other, 0, w_in, bf16, "hidden_other")
    z_other, z_other_sums, hidden_other, z_own = reduce(
        z_other, z_other_sums, hidden_other, z_own
    )
    sent_hidden = swap(hidden_other)
    hidden_own = rows_times(z_own, 0, w_in, f32, "hidden_own")
    grad_one, a_own, one_sums = norm_one_back(
        grad_two, hidden_own, sent_hidden, normed_one, inv_one, vals
    )
    first_unit = pl.BlockSpec((2, rows, OWN), lambda i: (0, 0, 0))
    grads[2] = grads_call(
        grads2_kernel,
        [one_unit(2), one_unit(2), tokens, tokens, first_unit, tokens, tokens],
        (me, z_own, z_other, h_own, h_other, gelu, d_own, d_other),
        "grads2",
    )
    *grads[2], grad_one, a_own, one_sums = reduce(*grads[2], grad_one, a_own, one_sums)
    a_other = swap(a_own)
    a_own, a_other, qkv = reduce(a_own, a_other, qkv)
    back = (
        a_own.reshape(seqs, half_len, D),
        a_other.reshape(seqs, half_len, D),
        wo_own,
        attended_wide,
        lse,
    )
    state = attend_back(qkv, *back, 0, 1, ())
    grads[1] = grads_call(
        grads1_kernel,
        [one_unit(0), one_unit(0), tokens, tokens, tokens, tokens, whole(2, rows, OWN)],
        (me, z_own, z_other, h_own, h_other, a_own, a_other, attended.reshape(2, rows, OWN)),
        "grads1",
    )
    *grads[1], a, b, qkv = reduce(*grads[1], *state, qkv)
    state = attend_back(qkv, *back, 1, 1, (a, b))
    a, b, qkv = reduce(*state, qkv)
    grad_qkv, qkv_sums = attend_back(qkv, *back, 2, seqs - 2, (a, b))
    grad_rows = grad_qkv.reshape(2, rows, 3 * OWN)
    keep, give = grads0(me, grad_rows, u_own.reshape(rows, D), u_other.reshape(rows, D))
    keep, give, grad_rows = reduce(keep, give, grad_rows)
    take = swap(give)
    inputs_other = rows_times(grad_rows, 1, w_qkv, bf16, "inputs_other")
    grads[0] = regroup(me, keep, take)
    *grads[0], grad_rows, inputs_other = reduce(*grads[0], grad_rows, inputs_other)
    sent_inputs = swap(inputs_other)
    inputs_own = rows_times(grad_rows, 0, w_qkv, f32, "inputs_own")
    sent_inputs, inputs_own, z_sums = reduce(sent_inputs, inputs_own, z_sums)
    input_grad, mask_sums = corrupt_back(
        span_mask, replace_kind, replace_from, grad_one, inputs_own, sent_inputs
    )
    bias_sums = jnp.zeros((FF // (2 * CHUNK), 2, CHUNK), f32)
    bias_sums = lax.dynamic_update_slice(
        bias_sums,
        (z_sums + z_other_sums).reshape(FF // (2 * CHUNK), 1, CHUNK),
        (0, core, 0),
    ).reshape(FF // D, D)
    vector_part = vector_rows(me, qkv_sums, one_sums, two_sums, mask_sums, bias_sums)
    input_grad, vector_part = reduce(input_grad, vector_part)
    vector_part = vector_part + swap(vector_part)
    (vector_part,) = reduce(vector_part)
    shard_v = scatter_vectors(vector_part, ranks, vectors.shape[0])
    (shard_v,) = reduce(shard_v)

    if staged:
        shard_half = result[0]
        shard_w = unpack(shard_half, swap(shard_half), index)
    else:
        core_rows = [block for i in range(4) for block in grads[i]]
        core_rows = jnp.concatenate(core_rows, axis=0)
        stacked = unpack(core_rows, swap(core_rows), 0).astype(f32)
        shard_w = lax.psum_scatter(stacked, "dp", scatter_dimension=0, tiled=True)
        shard_half = lax.dynamic_slice_in_dim(shard_w, core * OWN, OWN, axis=1)

    half32 = shard_half.astype(f32)
    squares = jnp.sum(half32 * half32) + 0.5 * jnp.sum(shard_v * shard_v)
    blocks = lax.all_to_all(
        jnp.full((2 * ranks, 8, 128), squares), ("dp", "seq"), 0, 0, tiled=True
    )
    grad_norm = jnp.sqrt(jnp.sum(blocks[:, 0, 0]))
    clip = 1.0 / jnp.maximum(grad_norm, 1.0)
    weights_new, weight_first_new, weight_second_new, weights_low = update_weights(
        blocks, shard_w, weights, weight_first, weight_second
    )
    vectors_new, vector_first_new, vector_second_new = adam_step(
        vectors, vector_first, vector_second, shard_v * clip, 0.0, vector_rate
    )
    return (
        layer_out.reshape(seqs, half_len, D),
        input_grad,
        grad_norm,
        weights_new,
        weight_first_new,
        weight_second_new,
        vectors_new,
        vector_first_new,
        vector_second_new,
        weights_low,
        vectors_new.astype(bf16),
    )


def solution(mesh):
    token = P("dp", "seq", None)
    by_row = P("dp", None)
    by_column = P(None, "dp")
    position = P("dp", "seq")
    in_specs = (
        (token,) + (position,) * 3 + (by_row, by_column, by_row, by_row, by_column, by_column, token)
    )
    out_specs = (token, token, P()) + (by_row,) * 3 + (by_column,) * 3 + (by_row, by_column)
    return jax.shard_map(
        functools.partial(shards, mesh.shape["dp"]),
        mesh=mesh,
        in_specs=in_specs,
        out_specs=out_specs,
        check_vma=False,
    )
```

```python
import functools

import jax
import jax.numpy as jnp
from jax import lax
from jax.experimental import pallas as pl
from jax.experimental.pallas import tpu as pltpu
from jax.sharding import PartitionSpec as P

D = 768
HEAD_DIM = 64
FF = 3072
STEP = 10
CHUNK = 96
OWN = D // 2
UNITS = FF // 2

ln_eps = 1e-12
beta_one = 0.9
beta_two = 0.999
adam_eps = 1e-08
learn_rate = 0.05
vector_rate = 0.3
decay_rate = 0.01

bf16 = jnp.bfloat16
f32 = jnp.float32
SWAP = [(0, 1), (1, 0)]


def params(limit=14):
    return pltpu.CompilerParams(vmem_limit_bytes=limit * 2**20)


def cost(micros):
    return pl.CostEstimate(flops=int(micros), bytes_accessed=0, transcendentals=0)


def dot(left, right, over):
    return lax.dot_general(left, right, (over, ((), ())), preferred_element_type=f32)


NT = ((1,), (1,))
NN = ((1,), (0,))
TN = ((0,), (0,))


def swap(value):
    return lax.ppermute(value, "seq", SWAP)


def pack(rows, index):
    core = lax.axis_index("seq")
    chunks = rows.shape[0] // (2 * CHUNK)
    plain = lax.dynamic_index_in_dim(rows.reshape(chunks, 2, CHUNK, D), core, 1, keepdims=False)
    columns = lax.dynamic_slice_in_dim(rows, core * OWN, OWN, axis=1).reshape(chunks, 2, CHUNK, OWN)
    wide = jnp.concatenate([columns[:, 0], columns[:, 1]], axis=-1)
    where = index * chunks + jnp.arange(chunks)
    is_out = ((where >= 12) & (where < 16))[:, None, None]
    return jnp.where(is_out, wide, plain).reshape(chunks * CHUNK, D)


def unpack(mine, theirs, index):
    core = lax.axis_index("seq")
    chunks = mine.shape[0] // CHUNK
    first = jnp.where(core == 0, mine, theirs).reshape(chunks, CHUNK, D)
    second = jnp.where(core == 0, theirs, mine).reshape(chunks, CHUNK, D)
    plain = jnp.stack([first, second], axis=1)
    upper = jnp.concatenate([first[..., :OWN], second[..., :OWN]], axis=-1)
    lower = jnp.concatenate([first[..., OWN:], second[..., OWN:]], axis=-1)
    wide = jnp.stack([upper, lower], axis=1)
    where = index * chunks + jnp.arange(chunks)
    is_out = ((where >= 12) & (where < 16))[:, None, None, None]
    return jnp.where(is_out, wide, plain).reshape(chunks * 2 * CHUNK, D)


SIDE_X = [(i, i ^ 1) for i in range(16)]
SIDE_Y = [(i, i ^ 2) for i in range(16)]


def up(first, last):
    return [(i, i + 4) for i in range(16) if first <= i // 4 <= last]


def down(first, last):
    return [(i, i - 4) for i in range(16) if first <= i // 4 <= last]


def send(value, pairs):
    return lax.ppermute(value, "dp", pairs)


def pick(plane, *options):
    result = options[-1]
    for i in range(len(options) - 2, -1, -1):
        result = jnp.where(plane == i, options[i], result)
    return result


def barrier(*values):
    return lax.optimization_barrier(values)


HALF = 3 * CHUNK // 2


def top(block):
    return block[:HALF]


def bottom(block):
    return block[HALF:]


def join(first, second):
    return jnp.concatenate([first, second], axis=0)


def planes(step, *targets):
    pairs = [(i, i ^ (4 * step)) for i in range(16)]
    return [pair for pair in pairs if not targets or pair[1] // 4 in targets]


PIECES = ((0, 1, 2, 3), (1, 0, 3, 2), (2, 2, 0, 0), (3, 3, 1, 1))


def gather_steps(block, slots):
    odd = lax.axis_index("dp") // 4 % 2 == 1
    x0, y0 = send(block, SIDE_X), send(block, SIDE_Y)
    s1, far = send(block, planes(1)), send(block, planes(2))
    c0 = send(top(x0), SIDE_Y), send(bottom(y0), SIDE_X)
    x0, y0, s1, far, *c0 = yield x0, y0, s1, far, *c0

    x1, y1 = send(s1, SIDE_X), send(s1, SIDE_Y)
    opposite = send(far, planes(1))
    x1, y1, opposite = yield x1, y1, opposite
    slots.append(((block, 0), (x0, 0), (y0, 0), tuple(c0)))

    s2 = jnp.where(odd, opposite, far)
    s3 = jnp.where(odd, far, opposite)
    x2, y2 = send(s2, SIDE_X), send(s2, SIDE_Y)
    c1 = send(top(x1), SIDE_Y), send(bottom(y1), SIDE_X)
    x2, y2, *c1 = yield x2, y2, *c1
    slots.append(((s1, 0), (x1, 0), (y1, 0), tuple(c1)))

    c2 = send(top(x2), SIDE_Y), send(bottom(y2), SIDE_X)
    c2 = yield c2
    slots.append(((s2, 0), (x2, 0), (y2, 0), tuple(c2)))

    x3, y3 = send(s3, SIDE_X), send(s3, SIDE_Y)
    x3, y3 = yield x3, y3
    c3 = send(top(x3), SIDE_Y), send(bottom(y3), SIDE_X)
    slots.append(((s3, 0), (x3, 0), (y3, 0), None))
    c3 = yield c3
    slots[3] = (*slots[3][:3], tuple(c3))


def reduce_steps(grads, plane, result):
    odd = plane % 2 == 1
    got = yield cross(grads[3])
    x, y = yield across(grads[3], got)
    own3 = plus(grads[3][0], x, y)
    got = yield cross(grads[2])
    x, y = yield across(grads[2], got)
    own2 = plus(grads[2][0], x, y)
    got = yield cross(grads[1])
    high = send(jnp.where(odd, own2, own3), planes(1))
    x, y, high = yield *across(grads[1], got), high
    own1 = plus(grads[1][0], x, y)
    high = plus(jnp.where(odd, own3, own2), high)
    yield ()
    got = yield cross(grads[0])
    x, y, one = yield *across(grads[0], got), send(own1, up(0, 0) + down(3, 3))
    own0 = plus(grads[0][0], x, y)
    own1 = plus(own1, one)
    zero, one, two = yield (
        send(own0, down(1, 1) + down(3, 3)),
        send(own1, down(2, 2)),
        send(high, planes(2, 2)),
    )
    own0 = plus(own0, zero)
    zero, three = yield send(own0, planes(2, 0)), send(high, planes(2, 3))
    result.append(pick(plane, plus(own0, zero), plus(own1, one), plus(high, two), plus(high, three)))


class Steps:
    def __init__(self, steps):
        self.steps = steps
        self.arrays = next(steps) if steps else ()

    def __call__(self, *values):
        count = len(self.arrays)
        passed = barrier(*self.arrays, *values) if count or values else ()
        if self.steps:
            try:
                self.arrays = self.steps.send(passed[:count])
            except StopIteration:
                self.steps, self.arrays = None, ()
        return passed[count:]


def parts_of(side):
    if side is None:
        return []
    first, second = side
    if isinstance(second, int):
        rows = 3 * CHUNK
        return [(first, second * rows, rows, 0)]
    return [(first, 0, HALF, 0), (second, 0, HALF, HALF)]


def slot_arrays(slots):
    arrays, known = [], {}
    shape = []
    for slot in slots:
        sides = []
        for side in slot:
            parts = []
            for array, start, rows, place in parts_of(side):
                if id(array) not in known:
                    known[id(array)] = len(arrays)
                    arrays.append(array)
                parts.append((known[id(array)], start, rows, place))
            sides.append(tuple(parts))
        shape.append(tuple(sides))
    return arrays, tuple(shape)


def run_copies(pairs, sems):
    copies = [
        pltpu.make_async_copy(source, target, sems.at[i])
        for i, (source, target) in enumerate(pairs)
    ]
    for copy in copies:
        copy.start()
    for copy in copies:
        copy.wait()


def place_heads_kernel(shape, me_ref, *refs):
    mine_ref, give_ref, whole_ref, sems = refs[-4:]
    spot, core, plane = me_ref[0], me_ref[1], me_ref[2]
    for z in range(4):

        @pl.when(plane == z)
        def _():
            pairs = []
            for side in range(4):
                start = 3 * CHUNK * (side + spot - 2 * (side & spot))
                for number, first, rows, place in shape[min(z, 2)][side]:
                    where = pl.ds(pl.multiple_of(start + place, 16), rows)
                    pairs.append((refs[number].at[pl.ds(first, rows)], whole_ref.at[where]))
            run_copies(pairs, sems)

    for ref, who in ((mine_ref, core), (give_ref, 1 - core)):
        for j in range(6):
            chunk = 4 * (j // 2) + 2 * who + j % 2
            ref[j] = whole_ref[pl.ds(pl.multiple_of(chunk * CHUNK, 16), CHUNK)]


def place_heads(me, slots):
    arrays, shape = slot_arrays(slots)
    half = jax.ShapeDtypeStruct((6, CHUNK, D), bf16)
    return pl.pallas_call(
        functools.partial(place_heads_kernel, shape),
        in_specs=[pl.BlockSpec(memory_space=pltpu.SMEM)]
        + [pl.BlockSpec(memory_space=pl.ANY)] * len(arrays),
        out_shape=[half, half],
        scratch_shapes=[pltpu.VMEM((12 * CHUNK, D), bf16), pltpu.SemaphoreType.DMA((8,))],
        compiler_params=params(),
        cost_estimate=cost(1),
        name="place_heads",
    )(me, *arrays)


def place_rest_kernel(shape, held, me_ref, *refs):
    out_ref, in_ref, down_ref, stage_ref, load_sems, store_sems = refs[-6:]
    spot, plane = me_ref[0], me_ref[2]

    def part(pairs, source, first, rows, row):
        while rows:
            if row < 4 * CHUNK:
                chunk, offset = divmod(row, CHUNK)
                count = min(rows, CHUNK - offset)
                targets = []
                for h in range(2):
                    target = 2 * CHUNK * chunk + CHUNK * h + offset
                    targets.append((pl.ds(OWN * h, OWN), out_ref.at[pl.ds(target, count)]))
            else:
                ref, start = (in_ref, 4 * CHUNK) if row < 20 * CHUNK else (down_ref, 20 * CHUNK)
                count = min(rows, start + 16 * CHUNK - row)
                targets = [(slice(None), ref.at[pl.ds(row - start, count)])]
            pairs.append((source.at[pl.ds(first, count)], count, targets))
            row, first, rows = row + count, first + count, rows - count

    for z in range(4):
        for s in range(4):
            pairs = []
            for slot, (number, sides) in zip(shape, held, strict=True):
                piece = PIECES[number][z]
                for side in sides if piece else ():
                    base = 3 * CHUNK * (4 * (piece - 1) + (side ^ s))
                    for array, first, rows, place in slot[side]:
                        part(pairs, refs[array], first, rows, base + place)

            @pl.when((plane == z) & (spot == s))
            def _():
                loads, stores, row = [], [], 0
                for i, (source, count, targets) in enumerate(pairs):
                    spot_rows = pl.ds(row, count)
                    loads.append(
                        pltpu.make_async_copy(source, stage_ref.at[spot_rows], load_sems.at[i])
                    )
                    stores.append([])
                    for columns, target in targets:
                        stores[-1].append(
                            pltpu.make_async_copy(
                                stage_ref.at[spot_rows, columns],
                                target,
                                store_sems.at[2 * i + len(stores[-1])],
                            )
                        )
                    row += count
                for load in loads:
                    load.start()
                for load, store in zip(loads, stores, strict=True):
                    load.wait()
                    for copy in store:
                        copy.start()
                for store in stores:
                    for copy in store:
                        copy.wait()


def place_rest(me, slots, held, state):
    arrays, shape = slot_arrays(
        [[slots[i][side] if side in sides else None for side in range(4)] for i, sides in held]
    )
    units = jax.ShapeDtypeStruct((UNITS, D), bf16)
    anywhere = pl.BlockSpec(memory_space=pl.ANY)
    return pl.pallas_call(
        functools.partial(place_rest_kernel, shape, held),
        in_specs=[pl.BlockSpec(memory_space=pltpu.SMEM)] + [anywhere] * (len(arrays) + len(state)),
        out_specs=[anywhere] * 3,
        out_shape=[jax.ShapeDtypeStruct((D, OWN), bf16), units, units],
        input_output_aliases={1 + len(arrays) + i: i for i in range(len(state))},
        scratch_shapes=[
            pltpu.VMEM((24 * CHUNK, D), bf16),
            pltpu.SemaphoreType.DMA((32,)),
            pltpu.SemaphoreType.DMA((64,)),
        ],
        compiler_params=params(),
        cost_estimate=cost(1),
        name="place_rest",
    )(me, *arrays, *state)


def plus(*values):
    total = values[0].astype(f32)
    for value in values[1:]:
        total = total + value.astype(f32)
    return total.astype(bf16)


def cross(sides):
    return send(sides[3], SIDE_Y), send(sides[4], SIDE_X)


def merge_kernel(x_ref, y_ref, upper_ref, lower_ref, x_out, y_out):
    x_out[:HALF] = (x_ref[:HALF].astype(f32) + upper_ref[...].astype(f32)).astype(bf16)
    x_out[HALF:] = x_ref[HALF:]
    y_out[:HALF] = y_ref[:HALF]
    y_out[HALF:] = (y_ref[HALF:].astype(f32) + lower_ref[...].astype(f32)).astype(bf16)


def across(sides, crossed):
    over_x, over_y = pl.pallas_call(
        merge_kernel,
        out_shape=[jax.ShapeDtypeStruct((3 * CHUNK, D), bf16)] * 2,
        compiler_params=params(),
        cost_estimate=cost(1),
        name="merge",
    )(sides[1], sides[2], *crossed)
    return send(over_x, SIDE_X), send(over_y, SIDE_Y)


def gather_vectors(low_vectors, ranks):
    count, width = low_vectors.shape
    block = jnp.pad(low_vectors, ((0, 16 - count), (0, 128 - width)))
    blocks = lax.all_to_all(jnp.broadcast_to(block, (ranks, 16, 128)), "dp", 0, 0, tiled=True)
    return blocks[:, :count, :width].transpose(1, 0, 2).reshape(count, ranks * width).astype(f32)


def scatter_vectors(rows, ranks, count):
    width = D // ranks
    blocks = rows.reshape(16, ranks, width).transpose(1, 0, 2)
    blocks = jnp.pad(blocks, ((0, 0), (0, 0), (0, 128 - width)))
    blocks = lax.all_to_all(blocks, "dp", 0, 0, tiled=True)
    return jnp.sum(blocks, axis=0)[:count, :width]


def selection(span, kind, source, half_len):
    chosen = span == 1
    masked = chosen & (kind < 8)
    swapped = chosen & (kind == 8)
    here = lax.broadcasted_iota(jnp.int32, (1, half_len), 1)
    origin = jnp.where(masked, -1, jnp.where(swapped, source, here))
    rows = lax.broadcasted_iota(jnp.int32, (half_len, half_len), 0)
    one_hot = (rows == origin).astype(f32).astype(bf16)
    first = lax.broadcasted_iota(jnp.int32, (16, half_len), 0) == 0
    mask_rows = jnp.where(first & masked, 1.0, 0.0).astype(bf16)
    return one_hot, mask_rows


def corrupt_kernel(span_ref, kind_ref, from_ref, hidden_ref, mask_ref, out_ref):
    seqs, half_len = span_ref.shape
    for s in range(seqs):
        rows = slice(s, s + 1)
        one_hot, mask_rows = selection(
            span_ref[rows, :], kind_ref[rows, :], from_ref[rows, :], half_len
        )
        picked = dot(one_hot, hidden_ref[s], TN) + dot(mask_rows, mask_ref[...], TN)
        out_ref[s] = picked.astype(bf16)


def corrupt(span, kind, source, hidden, mask_row):
    mask = jnp.broadcast_to(mask_row.astype(bf16)[None], (16, D))
    return pl.pallas_call(
        corrupt_kernel,
        out_shape=jax.ShapeDtypeStruct(hidden.shape, bf16),
        compiler_params=params(),
        name="corrupt",
    )(span, kind, source, hidden, mask)


def corrupt_back_kernel(
    span_ref, kind_ref, from_ref, grad_ref, own_ref, partial_ref, out_ref, mask_ref
):
    seqs, half_len = span_ref.shape
    mask_sum = jnp.zeros((16, D), f32)
    for s in range(seqs):
        rows = slice(s, s + 1)
        block = pl.ds(s * half_len, half_len)
        one_hot, mask_rows = selection(
            span_ref[rows, :], kind_ref[rows, :], from_ref[rows, :], half_len
        )
        grad = grad_ref[block] + own_ref[block] + partial_ref[block].astype(f32)
        high = grad.astype(bf16)
        low = (grad - high.astype(f32)).astype(bf16)
        out_ref[s] = dot(one_hot, high, NN) + dot(one_hot, low, NN)
        mask_sum = mask_sum + dot(mask_rows, high, NN) + dot(mask_rows, low, NN)
    mask_ref[...] = mask_sum


def corrupt_back(span, kind, source, grad, own, partial):
    seqs, half_len = span.shape
    return pl.pallas_call(
        corrupt_back_kernel,
        out_shape=[
            jax.ShapeDtypeStruct((seqs, half_len, D), f32),
            jax.ShapeDtypeStruct((16, D), f32),
        ],
        compiler_params=params(),
        cost_estimate=cost(1),
        name="corrupt_back",
    )(span, kind, source, grad, own, partial)


def attend_kernel(
    me_ref, own_ref, other_ref, mine_ref, theirs_ref, vals_ref, w_ref, qkv_ref, low_ref, wide_ref, lse_ref
):
    half_len = own_ref.shape[1]
    core = me_ref[1]

    @pl.when(pl.program_id(0) == 0)
    def _():
        for j in range(6):
            for ref, which in ((mine_ref, core), (theirs_ref, 1 - core)):
                where = pl.ds(pl.multiple_of((2 * j + which) * CHUNK, 16), CHUNK)
                w_ref[where] = ref[j]

    rows = jnp.concatenate([own_ref[0], other_ref[0]], axis=0)
    columns = pl.ds(pl.multiple_of(core * OWN, 128), OWN)
    bias = jnp.concatenate(
        [vals_ref[0:1, columns], jnp.zeros((1, OWN), f32), vals_ref[1:2, columns]], axis=-1
    )
    projected = (dot(rows, w_ref[...], NT) + bias).astype(bf16)
    qkv_ref[:, 0] = projected.reshape(2, half_len, 3 * OWN)
    wide, totals = [], []

    def score(h):
        columns = slice(h * HEAD_DIM, (h + 1) * HEAD_DIM)
        query = projected[:, :OWN][:, columns] * bf16(HEAD_DIM**-0.5)
        return dot(query, projected[:, OWN : 2 * OWN][:, columns], NT)

    heads = OWN // HEAD_DIM
    ahead = [score(0), score(1)]
    for h in range(heads):
        if h + 2 < heads:
            ahead.append(score(h + 2))
        scores = ahead.pop(0)
        value = projected[:, 2 * OWN :][:, h * HEAD_DIM : (h + 1) * HEAD_DIM]
        highest = jnp.max(scores, axis=-1, keepdims=True)
        exponents = jnp.exp(scores - highest)
        total = jnp.sum(exponents, axis=-1, keepdims=True)
        probabilities = (exponents / total).astype(bf16)
        wide.append(dot(probabilities, value, NN))
        totals.append(highest + jnp.log(total))
    attended = jnp.concatenate(wide, axis=-1)
    wide_ref[:, 0] = attended.reshape(2, half_len, OWN)
    low_ref[:, 0] = attended.astype(bf16).reshape(2, half_len, OWN)
    fill = jnp.zeros((2 * half_len, 128 - len(totals)), f32)
    lse_ref[0] = jnp.concatenate(totals + [fill], axis=-1).T[:8]


def whole(*shape):
    return pl.BlockSpec(shape, lambda *_: (0,) * len(shape))


def attend(me, u_own, u_other, mine, theirs, vals):
    seqs, half_len, _ = u_own.shape
    block = lambda width: pl.BlockSpec((2, 1, half_len, width), lambda s: (0, s, 0, 0))
    token = pl.BlockSpec((1, half_len, D), lambda s: (s, 0, 0))
    return pl.pallas_call(
        attend_kernel,
        grid=(seqs,),
        in_specs=[
            pl.BlockSpec(memory_space=pltpu.SMEM),
            token,
            token,
            whole(6, CHUNK, D),
            whole(6, CHUNK, D),
            whole(*vals.shape),
        ],
        out_specs=[
            whole(3 * OWN, D),
            block(3 * OWN),
            block(OWN),
            block(OWN),
            pl.BlockSpec((1, 8, 2 * half_len), lambda s: (s, 0, 0)),
        ],
        out_shape=[
            jax.ShapeDtypeStruct((3 * OWN, D), bf16),
            jax.ShapeDtypeStruct((2, seqs, half_len, 3 * OWN), bf16),
            jax.ShapeDtypeStruct((2, seqs, half_len, OWN), bf16),
            jax.ShapeDtypeStruct((2, seqs, half_len, OWN), f32),
            jax.ShapeDtypeStruct((seqs, 8, 2 * half_len), f32),
        ],
        cost_estimate=cost(3),
        compiler_params=params(),
        name="attend",
    )(me, u_own, u_other, mine, theirs, vals)


def attend_back_kernel(
    skip, qkv_ref, own_ref, other_ref, wo_ref, wide_ref, lse_ref, *refs
):
    out_ref, sums_ref = refs[skip:]
    half_len = qkv_ref.shape[2]
    length = 2 * half_len
    projected = qkv_ref[:, 0].reshape(length, 3 * OWN)
    rows = jnp.concatenate([own_ref[0], other_ref[0]], axis=0)
    grad = dot(rows, wo_ref[...], NN).astype(bf16)
    product = grad.astype(f32) * wide_ref[:, 0].reshape(length, OWN)
    heads = OWN // HEAD_DIM
    deltas = [
        jnp.sum(product[:, h * HEAD_DIM : (h + 1) * HEAD_DIM], axis=-1, keepdims=True)
        for h in range(heads)
    ]
    fill = jnp.zeros((length, 128 - heads), f32)
    delta_rows = jnp.concatenate(deltas + [fill], axis=-1).T
    parts = [[], [], []]

    def head(h):
        columns = slice(h * HEAD_DIM, (h + 1) * HEAD_DIM)
        query = projected[:, :OWN][:, columns] * bf16(HEAD_DIM**-0.5)
        key = projected[:, OWN : 2 * OWN][:, columns]
        value = projected[:, 2 * OWN :][:, columns]
        return query, key, value, grad[:, columns]

    def products(h):
        query, key, value, grad_head = head(h)
        return dot(key, query, NT), dot(value, grad_head, NT)

    ahead = [products(0)]
    for h in range(heads):
        if h + 1 < heads:
            ahead.append(products(h + 1))
        scores, grad_weights = ahead.pop(0)
        query, key, value, grad_head = head(h)
        weights = jnp.exp(scores - lse_ref[0, h : h + 1, :])
        grad_scores = (weights * (grad_weights - delta_rows[h : h + 1, :])).astype(bf16)
        parts[0].append(dot(grad_scores, key, TN) * HEAD_DIM**-0.5)
        parts[1].append(dot(grad_scores, query, NN))
        parts[2].append(dot(weights.astype(bf16), grad_head, NN))
    result = jnp.concatenate(parts[0] + parts[1] + parts[2], axis=-1).astype(bf16)
    out_ref[:, 0] = result.reshape(2, half_len, 3 * OWN)
    sums = jnp.sum(result.astype(f32), axis=0, keepdims=True)

    @pl.when(pl.program_id(0) == 0)
    def _():
        sums_ref[...] = refs[1][...] if skip else jnp.zeros_like(sums_ref)

    sums_ref[...] += sums


def attend_back(qkv, own, other, wo_own, wide, lse, first, count, state):
    _, seqs, half_len, _ = qkv.shape
    block = lambda width: pl.BlockSpec((2, 1, half_len, width), lambda s: (0, s + first, 0, 0))
    token = pl.BlockSpec((1, half_len, D), lambda s: (s + first, 0, 0))
    return pl.pallas_call(
        functools.partial(attend_back_kernel, len(state)),
        grid=(count,),
        in_specs=[
            block(3 * OWN),
            token,
            token,
            whole(D, OWN),
            block(OWN),
            pl.BlockSpec((1, 8, 2 * half_len), lambda s: (s + first, 0, 0)),
        ]
        + ([pl.BlockSpec(memory_space=pl.ANY), whole(1, 3 * OWN)] if state else []),
        out_specs=[block(3 * OWN), whole(1, 3 * OWN)],
        input_output_aliases={6: 0} if state else {},
        out_shape=[
            jax.ShapeDtypeStruct((2, seqs, half_len, 3 * OWN), bf16),
            jax.ShapeDtypeStruct((1, 3 * OWN), f32),
        ],
        cost_estimate=cost(2 * count),
        compiler_params=params(),
        name="attend_back",
    )(qkv, own, other, wo_own, wide, lse, *state)


def norm(values):
    center = values - jnp.mean(values, axis=-1, keepdims=True)
    inv_std = lax.rsqrt(jnp.mean(center * center, axis=-1, keepdims=True) + ln_eps)
    return center * inv_std, inv_std


def norm_backward(upstream, normed, inv_std, gain):
    scaled = upstream * gain
    return inv_std * (
        scaled
        - jnp.mean(scaled, axis=-1, keepdims=True)
        - normed * jnp.mean(scaled * normed, axis=-1, keepdims=True)
    )


def row(ref, i):
    return ref[i : i + 1, :]


def branch_kernel(own_ref, other_ref, u_ref, wo_ref, wo_other_ref, vals_ref, normed_ref, inv_ref, low_ref):
    branch = dot(own_ref[0, 0], wo_ref[...], NT) + dot(other_ref[0], wo_other_ref[...], NT)
    normed, inv = norm(u_ref[0].astype(f32) + branch + row(vals_ref, 2))
    normed_ref[...] = normed
    inv_ref[...] = jnp.broadcast_to(inv, inv_ref.shape)
    low_ref[...] = (normed * row(vals_ref, 3) + row(vals_ref, 4)).astype(bf16)


def attention_branch(attended, from_other, u_own, wo_own, wo_other, vals):
    seqs, half_len, _ = u_own.shape
    rows = pl.BlockSpec((half_len, D), lambda s: (s, 0))
    return pl.pallas_call(
        branch_kernel,
        grid=(seqs,),
        in_specs=[
            pl.BlockSpec((1, 1, half_len, OWN), lambda s: (0, s, 0, 0)),
            pl.BlockSpec((1, half_len, OWN), lambda s: (s, 0, 0)),
            pl.BlockSpec((1, half_len, D), lambda s: (s, 0, 0)),
            whole(D, OWN),
            whole(D, OWN),
            whole(*vals.shape),
        ],
        out_specs=[rows, pl.BlockSpec((half_len, 128), lambda s: (s, 0)), rows],
        out_shape=[
            jax.ShapeDtypeStruct((seqs * half_len, D), f32),
            jax.ShapeDtypeStruct((seqs * half_len, 128), f32),
            jax.ShapeDtypeStruct((seqs * half_len, D), bf16),
        ],
        cost_estimate=cost(1),
        compiler_params=params(),
        name="attention_branch",
    )(attended, from_other, u_own, wo_own, wo_other, vals)


def hidden_kernel(own_ref, other_ref, w_ref, bias_ref, gelu_ref, slope_ref):
    tile = own_ref.shape[0] // 3
    jobs = [
        (half, ref, slice(i * tile, (i + 1) * tile))
        for half, ref in enumerate((own_ref, other_ref))
        for i in range(3)
    ]

    def project(job):
        _, ref, rows = jobs[job]
        return dot(ref[rows], w_ref[...], NT) + bias_ref[...]

    ahead = project(0)
    for i, (half, _, rows) in enumerate(jobs):
        points = ahead
        if i + 1 < len(jobs):
            ahead = project(i + 1)
        below = 0.5 * (1.0 + lax.erf(points * 2**-0.5))
        density = jnp.exp(-0.5 * points * points) * 0.3989422804014327
        gelu_ref[half, rows] = (points * below).astype(bf16)
        slope_ref[half, rows] = (below + points * density).astype(bf16)


def hidden_units(h_own, h_other, w_in, bias):
    rows = h_own.shape[0]
    width = 384
    block = pl.BlockSpec((2, rows, width), lambda i: (0, 0, i))
    return pl.pallas_call(
        hidden_kernel,
        grid=(UNITS // width,),
        in_specs=[
            whole(rows, D),
            whole(rows, D),
            pl.BlockSpec((width, D), lambda i: (i, 0)),
            pl.BlockSpec((1, width), lambda i: (0, i)),
        ],
        out_specs=[block, block],
        out_shape=[jax.ShapeDtypeStruct((2, rows, UNITS), bf16)] * 2,
        cost_estimate=cost(3),
        compiler_params=params(),
        name="hidden_units",
    )(h_own, h_other, w_in, bias)


def rows_kernel(left_ref, right_ref, out_ref):
    out_ref[...] = dot(left_ref[0], right_ref[...], NN).astype(out_ref.dtype)


def rows_times(left, half, right, dtype, name):
    _, rows, depth = left.shape
    tile = rows // 3
    return pl.pallas_call(
        rows_kernel,
        grid=(3,),
        in_specs=[pl.BlockSpec((1, tile, depth), lambda i: (half, i, 0)), whole(*right.shape)],
        out_specs=pl.BlockSpec((tile, D), lambda i: (i, 0)),
        out_shape=jax.ShapeDtypeStruct((rows, D), dtype),
        cost_estimate=cost(1),
        compiler_params=params(),
        name=name,
    )(left, right)


def add_sums(sums_ref, *values):
    @pl.when(pl.program_id(0) == 0)
    def _():
        sums_ref[...] = jnp.zeros_like(sums_ref)

    for i, value in enumerate(values):
        sums_ref[i : i + 1, :] += jnp.sum(value, axis=0, keepdims=True)


def finish_kernel(own_ref, other_ref, normed_ref, grad_ref, vals_ref, out_ref, wide_ref, low_ref, sums_ref):
    hidden_one = normed_ref[...] * row(vals_ref, 3) + row(vals_ref, 4)
    feed = own_ref[...] + other_ref[...].astype(f32) + row(vals_ref, 5)
    normed, inv = norm(hidden_one + feed)
    out_ref[...] = normed * row(vals_ref, 6) + row(vals_ref, 7)
    grad = grad_ref[...].astype(f32)
    wide = norm_backward(grad, normed, inv, row(vals_ref, 6))
    low = wide.astype(bf16)
    wide_ref[...] = wide
    low_ref[...] = low
    add_sums(sums_ref, low.astype(f32), grad * normed, grad)


def finish(own, other, normed, grad, vals):
    rows = own.shape[0]
    tile = rows // 3
    block = pl.BlockSpec((tile, D), lambda i: (i, 0))
    return pl.pallas_call(
        finish_kernel,
        grid=(3,),
        in_specs=[block] * 4 + [whole(*vals.shape)],
        out_specs=[block] * 3 + [whole(8, D)],
        out_shape=[
            jax.ShapeDtypeStruct((rows, D), f32),
            jax.ShapeDtypeStruct((rows, D), f32),
            jax.ShapeDtypeStruct((rows, D), bf16),
            jax.ShapeDtypeStruct((8, D), f32),
        ],
        cost_estimate=cost(1),
        compiler_params=params(),
        name="finish",
    )(own, other, normed, grad, vals)


def norm_one_kernel(two_ref, own_ref, other_ref, normed_ref, inv_ref, vals_ref, wide_ref, low_ref, sums_ref):
    grad = two_ref[...] + own_ref[...] + other_ref[...].astype(f32)
    normed = normed_ref[...]
    wide = norm_backward(grad, normed, inv_ref[:, 0:1], row(vals_ref, 3))
    low = wide.astype(bf16)
    wide_ref[...] = wide
    low_ref[...] = low
    add_sums(sums_ref, low.astype(f32), grad * normed, grad)


def norm_one_back(two, own, other, normed, inv, vals):
    rows = own.shape[0]
    tile = rows // 3
    block = pl.BlockSpec((tile, D), lambda i: (i, 0))
    return pl.pallas_call(
        norm_one_kernel,
        grid=(3,),
        in_specs=[block] * 4 + [pl.BlockSpec((tile, 128), lambda i: (i, 0)), whole(*vals.shape)],
        out_specs=[block] * 2 + [whole(8, D)],
        out_shape=[
            jax.ShapeDtypeStruct((rows, D), f32),
            jax.ShapeDtypeStruct((rows, D), bf16),
            jax.ShapeDtypeStruct((8, D), f32),
        ],
        cost_estimate=cost(1),
        compiler_params=params(),
        name="norm_one_back",
    )(two, own, other, normed, inv, vals)


def slope_kernel(grad_ref, w_ref, slope_ref, out_ref, sums_ref):
    low = (dot(grad_ref[...], w_ref[...], NT) * slope_ref[0].astype(f32)).astype(bf16)
    out_ref[0] = low
    sums_ref[...] = jnp.sum(low.astype(f32), axis=0, keepdims=True)


def before_gelu(grad, w_down, slope, half):
    rows = grad.shape[0]
    width = 384
    return pl.pallas_call(
        slope_kernel,
        grid=(UNITS // width,),
        in_specs=[
            whole(rows, D),
            pl.BlockSpec((width, D), lambda i: (i, 0)),
            pl.BlockSpec((1, rows, width), lambda i: (half, 0, i)),
        ],
        out_specs=[
            pl.BlockSpec((1, rows, width), lambda i: (0, 0, i)),
            pl.BlockSpec((1, width), lambda i: (0, i)),
        ],
        out_shape=[
            jax.ShapeDtypeStruct((1, rows, UNITS), bf16),
            jax.ShapeDtypeStruct((1, UNITS), f32),
        ],
        cost_estimate=cost(1),
        compiler_params=params(),
        name="before_gelu",
    )(grad, w_down, slope)


def rows_of(count):
    return jax.ShapeDtypeStruct((count, D), bf16)


CROSS = ((0, 0, 288), (1, 0, 288), (2, 0, 288), (3, 0, 144), (3, 144, 144))


def side_rows(spot, side, first, rows):
    start = 3 * CHUNK * (side + spot - 2 * (side & spot)) + first
    return pl.ds(pl.multiple_of(start, 16), rows)


def write_sides(spot, piece_ref, outs):
    for out, (side, first, rows) in zip(outs, CROSS, strict=True):
        out[...] = piece_ref[side_rows(spot, side, first, rows)]


def rows_at(step):
    return pl.ds(pl.multiple_of(step * OWN, 16), OWN)


def two_halves(left, left_other, right, right_other):
    return dot(left, right, TN) + dot(left_other, right_other, TN)


def grads3_kernel(me_ref, g_ref, d_ref, d_other_ref, *refs):
    piece_ref = refs[-1]
    step = pl.program_id(0)
    piece_ref[rows_at(step)] = two_halves(
        g_ref[0], g_ref[1], d_ref[...], d_other_ref[...]
    ).astype(bf16)

    @pl.when(step == 2)
    def _():
        write_sides(me_ref[0], piece_ref, refs[:-1])


def grads2_kernel(me_ref, z_ref, z_other_ref, h_ref, h_other_ref, g_ref, d_ref, d_other_ref, *refs):
    piece_ref = refs[-1]
    step = pl.program_id(0)

    @pl.when(step < 2)
    def _():
        piece_ref[rows_at(step)] = two_halves(
            z_ref[0], z_other_ref[0], h_ref[...], h_other_ref[...]
        ).astype(bf16)

    @pl.when(step == 2)
    def _():
        piece_ref[rows_at(step)] = two_halves(
            g_ref[0], g_ref[1], d_ref[...], d_other_ref[...]
        ).astype(bf16)
        write_sides(me_ref[0], piece_ref, refs[:-1])


def grads1_kernel(me_ref, z_ref, z_other_ref, h_ref, h_other_ref, a_ref, a_other_ref, att_ref, *refs):
    piece_ref = refs[-1]
    step = pl.program_id(0)

    @pl.when(step < 2)
    def _():
        piece_ref[rows_at(step + 1)] = two_halves(
            z_ref[0], z_other_ref[0], h_ref[...], h_other_ref[...]
        ).astype(bf16)

    @pl.when(step == 2)
    def _():
        wo = two_halves(a_ref[...], a_other_ref[...], att_ref[0], att_ref[1]).astype(bf16)
        for j in range(4):
            upper = wo[2 * CHUNK * j : 2 * CHUNK * j + CHUNK]
            lower = wo[2 * CHUNK * j + CHUNK : 2 * CHUNK * (j + 1)]
            piece_ref[CHUNK * j : CHUNK * (j + 1)] = jnp.concatenate([upper, lower], axis=-1)
        write_sides(me_ref[0], piece_ref, refs[:-1])


def grads_call(kernel, specs, arrays, name):
    return pl.pallas_call(
        kernel,
        grid=(3,),
        in_specs=[pl.BlockSpec(memory_space=pltpu.SMEM)] + specs,
        out_specs=[whole(count, D) for _, _, count in CROSS],
        out_shape=[rows_of(count) for _, _, count in CROSS],
        scratch_shapes=[pltpu.VMEM((12 * CHUNK, D), bf16)],
        cost_estimate=cost(2),
        compiler_params=params(),
        name=name,
    )(*arrays)


def grads0_kernel(me_ref, g_ref, u_ref, u_other_ref, keep_ref, give_ref, piece_ref):
    core = me_ref[1]
    step = pl.program_id(0)
    piece_ref[rows_at(step)] = two_halves(
        g_ref[0], g_ref[1], u_ref[...], u_other_ref[...]
    ).astype(bf16)

    @pl.when(step == 2)
    def _():
        for j in range(6):
            for ref, which in ((keep_ref, core), (give_ref, 1 - core)):
                where = pl.ds(pl.multiple_of((2 * j + which) * CHUNK, 16), CHUNK)
                ref[j] = piece_ref[where]


def grads0(me, grad, u_own, u_other):
    rows = grad.shape[1]
    half = jax.ShapeDtypeStruct((6, CHUNK, D), bf16)
    return pl.pallas_call(
        grads0_kernel,
        grid=(3,),
        in_specs=[
            pl.BlockSpec(memory_space=pltpu.SMEM),
            pl.BlockSpec((2, rows, OWN), lambda i: (0, 0, i)),
            whole(rows, D),
            whole(rows, D),
        ],
        out_specs=[whole(6, CHUNK, D)] * 2,
        out_shape=[half, half],
        scratch_shapes=[pltpu.VMEM((12 * CHUNK, D), bf16)],
        cost_estimate=cost(2),
        compiler_params=params(),
        name="grads0",
    )(me, grad, u_own, u_other)


def regroup_kernel(me_ref, keep_ref, take_ref, *refs):
    piece_ref = refs[-1]
    core = me_ref[1]
    for ref, who in ((keep_ref, core), (take_ref, 1 - core)):
        for j in range(6):
            chunk = 4 * (j // 2) + 2 * who + j % 2
            piece_ref[pl.ds(pl.multiple_of(chunk * CHUNK, 16), CHUNK)] = ref[j]
    write_sides(me_ref[0], piece_ref, refs[:-1])


def regroup(me, keep, take):
    return pl.pallas_call(
        regroup_kernel,
        in_specs=[pl.BlockSpec(memory_space=pltpu.SMEM)]
        + [pl.BlockSpec(memory_space=pltpu.VMEM)] * 2,
        out_shape=[rows_of(count) for _, _, count in CROSS],
        scratch_shapes=[pltpu.VMEM((12 * CHUNK, D), bf16)],
        cost_estimate=cost(1),
        compiler_params=params(),
        name="regroup",
    )(me, keep, take)


def vector_kernel(me_ref, qkv_ref, one_ref, two_ref, mask_ref, bias_ref, out_ref):
    out_ref[...] = jnp.zeros_like(out_ref)
    columns = pl.ds(pl.multiple_of(me_ref[1] * OWN, 128), OWN)
    out_ref[0:1, columns] = qkv_ref[:, :OWN]
    out_ref[1:2, columns] = qkv_ref[:, 2 * OWN :]
    out_ref[2:5, :] = one_ref[0:3, :]
    out_ref[5:8, :] = two_ref[0:3, :]
    out_ref[8:9, :] = mask_ref[0:1, :]
    out_ref[9:13, :] = bias_ref[...]


def vector_rows(me, qkv_sums, one_sums, two_sums, mask_sums, bias_sums):
    return pl.pallas_call(
        vector_kernel,
        in_specs=[pl.BlockSpec(memory_space=pltpu.SMEM)]
        + [pl.BlockSpec(memory_space=pltpu.VMEM)] * 5,
        out_shape=jax.ShapeDtypeStruct((16, D), f32),
        cost_estimate=cost(1),
        name="vector_rows",
    )(me, qkv_sums, one_sums, two_sums, mask_sums, bias_sums)


def adam_step(master, first_old, second, gradient, decay_on, step_rate):
    first_new = beta_one * first_old + (1.0 - beta_one) * gradient
    second_new = beta_two * second + (1.0 - beta_two) * gradient * gradient
    fix_one = 1.0 - beta_one**STEP
    fix_two = 1.0 - beta_two**STEP
    update = first_new / fix_one / (jnp.sqrt(second_new / fix_two) + adam_eps)
    return (master - step_rate * (update + decay_on * master), first_new, second_new)


def update_kernel(sums_ref, grad_ref, *refs):
    norm_value = jnp.sqrt(jnp.sum(sums_ref[...], axis=0))[0:1, 0:1]
    clip = 1.0 / jnp.maximum(norm_value, 1.0)
    master, first, second = (ref[...] for ref in refs[:3])
    gradient = grad_ref[...].astype(f32) * clip
    master, first, second = adam_step(master, first, second, gradient, decay_rate, learn_rate)
    for ref, value in zip(refs[3:], (master, first, second, master.astype(bf16)), strict=True):
        ref[...] = value


def update_weights(sums, grad, master, first, second):
    rows = grad.shape[0]
    tile = 144 if rows % 144 == 0 else rows
    block = pl.BlockSpec((tile, D), lambda i: (i, 0))
    return pl.pallas_call(
        update_kernel,
        grid=(rows // tile,),
        in_specs=[whole(*sums.shape)] + [block] * 4,
        out_specs=[block] * 4,
        out_shape=[jax.ShapeDtypeStruct((rows, D), f32)] * 3
        + [jax.ShapeDtypeStruct((rows, D), bf16)],
        cost_estimate=cost(1),
        compiler_params=params(),
        name="update_weights",
    )(sums, grad, master, first, second)


def shards(
    ranks,
    hidden,
    span_mask,
    replace_kind,
    replace_from,
    weights,
    vectors,
    weight_first,
    weight_second,
    vector_first,
    vector_second,
    cotangent,
):
    seqs, half_len, _ = hidden.shape
    rows = seqs * half_len
    index = lax.axis_index("dp")
    core = lax.axis_index("seq")
    staged = ranks == 16
    plane = index // 4
    spot = index % 4 if staged else jnp.zeros_like(index)
    me = jnp.stack([spot, core, plane]).astype(jnp.int32)
    low_weights = weights.astype(bf16)
    slots, grads, result = [], {}, []
    if staged:
        gather = Steps(gather_steps(pack(low_weights, index), slots))
    else:
        gather = Steps(None)
        stacked = pack(lax.all_gather(low_weights, "dp", axis=0, tiled=True), 0)

    gather()
    gather()
    vals = gather_vectors(vectors.astype(bf16), ranks)
    every, rest = (0, 1, 2, 3), ()
    if staged:
        rest = place_rest(me, slots, ((0, every),), ())
    vals, *rest = gather(vals, *rest)
    u_own = corrupt(span_mask, replace_kind, replace_from, hidden, vals[8])
    bias_in = lax.dynamic_index_in_dim(
        vals[9:].reshape(FF // (2 * CHUNK), 2, CHUNK), core, 1, keepdims=False
    ).reshape(1, UNITS)
    if staged:
        rest = place_rest(me, slots, ((1, every),), rest)
    u_own, vals, bias_in, *rest = gather(u_own, vals, bias_in, *rest)
    u_other = swap(u_own)

    if staged:
        mine, give = place_heads(me, slots)
    else:
        halves = stacked[: 12 * CHUNK].reshape(3, 2, 2, CHUNK, D)
        mine = lax.dynamic_index_in_dim(halves, core, 1, keepdims=False).reshape(6, CHUNK, D)
        give = lax.dynamic_index_in_dim(halves, 1 - core, 1, keepdims=False).reshape(6, CHUNK, D)
    w_qkv, qkv, attended, attended_wide, lse = attend(
        me, u_own, u_other, mine, swap(give), vals
    )
    w_qkv, qkv, attended, attended_wide, lse, *rest = gather(
        w_qkv, qkv, attended, attended_wide, lse, *rest
    )
    from_other = swap(attended[1])
    if staged:
        rest = place_rest(me, slots, ((2, every), (3, (0, 1, 2))), rest)
    attended, from_other, *rest = gather(attended, from_other, *rest)

    if staged:
        wo_own, w_in, w_down = place_rest(me, slots, ((3, (3,)),), rest)
    else:
        rest = stacked[12 * CHUNK :]
        wo_own = (
            rest[: 4 * CHUNK].reshape(4, CHUNK, 2, OWN).transpose(0, 2, 1, 3).reshape(D, OWN)
        )
        w_in, w_down = rest[4 * CHUNK : 20 * CHUNK], rest[20 * CHUNK :]
    normed_one, inv_one, h_own = attention_branch(
        attended, from_other, u_own, wo_own, swap(wo_own), vals
    )
    h_other = swap(h_own)
    gelu, slope = hidden_units(h_own, h_other, w_in, bias_in)
    feed_other = swap(rows_times(gelu, 1, w_down, bf16, "feed_other"))
    feed_own = rows_times(gelu, 0, w_down, f32, "feed_own")
    layer_out, grad_two, d_own, two_sums = finish(
        feed_own, feed_other, normed_one, cotangent.reshape(rows, D), vals
    )

    d_other = swap(d_own)
    z_own, z_sums = before_gelu(d_own, w_down, slope, 0)
    d_other, z_own, z_sums = barrier(d_other, z_own, z_sums)
    unit = lambda first: pl.BlockSpec((2, rows, OWN), lambda i: (0, 0, i + first))
    one_unit = lambda first: pl.BlockSpec((1, rows, OWN), lambda i: (0, 0, jnp.minimum(i, 1) + first))
    tokens = whole(rows, D)
    grads[3] = grads_call(
        grads3_kernel, [unit(1), tokens, tokens], (me, gelu, d_own, d_other), "grads3"
    )
    *grads[3], d_other = barrier(*grads[3], d_other)
    reduce = Steps(reduce_steps(grads, plane, result) if staged else None)
    z_other, z_other_sums = before_gelu(d_other, w_down, slope, 1)
    hidden_other = rows_times(z_other, 0, w_in, bf16, "hidden_other")
    z_other, z_other_sums, hidden_other, z_own = reduce(
        z_other, z_other_sums, hidden_other, z_own
    )
    sent_hidden = swap(hidden_other)
    hidden_own = rows_times(z_own, 0, w_in, f32, "hidden_own")
    grad_one, a_own, one_sums = norm_one_back(
        grad_two, hidden_own, sent_hidden, normed_one, inv_one, vals
    )
    first_unit = pl.BlockSpec((2, rows, OWN), lambda i: (0, 0, 0))
    grads[2] = grads_call(
        grads2_kernel,
        [one_unit(2), one_unit(2), tokens, tokens, first_unit, tokens, tokens],
        (me, z_own, z_other, h_own, h_other, gelu, d_own, d_other),
        "grads2",
    )
    *grads[2], grad_one, a_own, one_sums = reduce(*grads[2], grad_one, a_own, one_sums)
    a_other = swap(a_own)
    a_own, a_other, qkv = reduce(a_own, a_other, qkv)
    back = (
        a_own.reshape(seqs, half_len, D),
        a_other.reshape(seqs, half_len, D),
        wo_own,
        attended_wide,
        lse,
    )
    state = attend_back(qkv, *back, 0, 1, ())
    grads[1] = grads_call(
        grads1_kernel,
        [one_unit(0), one_unit(0), tokens, tokens, tokens, tokens, whole(2, rows, OWN)],
        (me, z_own, z_other, h_own, h_other, a_own, a_other, attended.reshape(2, rows, OWN)),
        "grads1",
    )
    *grads[1], a, b, qkv = reduce(*grads[1], *state, qkv)
    state = attend_back(qkv, *back, 1, 1, (a, b))
    a, b, qkv = reduce(*state, qkv)
    grad_qkv, qkv_sums = attend_back(qkv, *back, 2, seqs - 2, (a, b))
    grad_rows = grad_qkv.reshape(2, rows, 3 * OWN)
    keep, give = grads0(me, grad_rows, u_own.reshape(rows, D), u_other.reshape(rows, D))
    keep, give, grad_rows = reduce(keep, give, grad_rows)
    take = swap(give)
    inputs_other = rows_times(grad_rows, 1, w_qkv, bf16, "inputs_other")
    grads[0] = regroup(me, keep, take)
    *grads[0], grad_rows, inputs_other = reduce(*grads[0], grad_rows, inputs_other)
    sent_inputs = swap(inputs_other)
    inputs_own = rows_times(grad_rows, 0, w_qkv, f32, "inputs_own")
    sent_inputs, inputs_own, z_sums = reduce(sent_inputs, inputs_own, z_sums)
    input_grad, mask_sums = corrupt_back(
        span_mask, replace_kind, replace_from, grad_one, inputs_own, sent_inputs
    )
    bias_sums = jnp.zeros((FF // (2 * CHUNK), 2, CHUNK), f32)
    bias_sums = lax.dynamic_update_slice(
        bias_sums,
        (z_sums + z_other_sums).reshape(FF // (2 * CHUNK), 1, CHUNK),
        (0, core, 0),
    ).reshape(FF // D, D)
    vector_part = vector_rows(me, qkv_sums, one_sums, two_sums, mask_sums, bias_sums)
    input_grad, vector_part = reduce(input_grad, vector_part)
    vector_part = vector_part + swap(vector_part)
    (vector_part,) = reduce(vector_part)
    shard_v = scatter_vectors(vector_part, ranks, vectors.shape[0])
    (shard_v,) = reduce(shard_v)

    if staged:
        shard_half = result[0]
        shard_w = unpack(shard_half, swap(shard_half), index)
    else:
        core_rows = [block for i in range(4) for block in grads[i]]
        core_rows = jnp.concatenate(core_rows, axis=0)
        stacked = unpack(core_rows, swap(core_rows), 0).astype(f32)
        shard_w = lax.psum_scatter(stacked, "dp", scatter_dimension=0, tiled=True)
        shard_half = lax.dynamic_slice_in_dim(shard_w, core * OWN, OWN, axis=1)

    half32 = shard_half.astype(f32)
    squares = jnp.sum(half32 * half32) + 0.5 * jnp.sum(shard_v * shard_v)
    blocks = lax.all_to_all(
        jnp.full((2 * ranks, 8, 128), squares), ("dp", "seq"), 0, 0, tiled=True
    )
    grad_norm = jnp.sqrt(jnp.sum(blocks[:, 0, 0]))
    clip = 1.0 / jnp.maximum(grad_norm, 1.0)
    weights_new, weight_first_new, weight_second_new, weights_low = update_weights(
        blocks, shard_w, weights, weight_first, weight_second
    )
    vectors_new, vector_first_new, vector_second_new = adam_step(
        vectors, vector_first, vector_second, shard_v * clip, 0.0, vector_rate
    )
    return (
        layer_out.reshape(seqs, half_len, D),
        input_grad,
        grad_norm,
        weights_new,
        weight_first_new,
        weight_second_new,
        vectors_new,
        vector_first_new,
        vector_second_new,
        weights_low,
        vectors_new.astype(bf16),
    )


def solution(mesh):
    token = P("dp", "seq", None)
    by_row = P("dp", None)
    by_column = P(None, "dp")
    position = P("dp", "seq")
    in_specs = (
        (token,) + (position,) * 3 + (by_row, by_column, by_row, by_row, by_column, by_column, token)
    )
    out_specs = (token, token, P()) + (by_row,) * 3 + (by_column,) * 3 + (by_row, by_column)
    return jax.shard_map(
        functools.partial(shards, mesh.shape["dp"]),
        mesh=mesh,
        in_specs=in_specs,
        out_specs=out_specs,
        check_vma=False,
    )
```

```python
import functools

import jax
import jax.numpy as jnp
from jax import lax
from jax.experimental import pallas as pl
from jax.experimental.pallas import tpu as pltpu
from jax.sharding import PartitionSpec as P

D = 768
HEAD_DIM = 64
FF = 3072
STEP = 10
CHUNK = 96
OWN = D // 2
UNITS = FF // 2

ln_eps = 1e-12
beta_one = 0.9
beta_two = 0.999
adam_eps = 1e-08
learn_rate = 0.05
vector_rate = 0.3
decay_rate = 0.01

bf16 = jnp.bfloat16
f32 = jnp.float32
SWAP = [(0, 1), (1, 0)]


def params(limit=14):
    return pltpu.CompilerParams(vmem_limit_bytes=limit * 2**20)


def cost(micros):
    return pl.CostEstimate(flops=int(micros), bytes_accessed=0, transcendentals=0)


def dot(left, right, over):
    return lax.dot_general(left, right, (over, ((), ())), preferred_element_type=f32)


NT = ((1,), (1,))
NN = ((1,), (0,))
TN = ((0,), (0,))


def swap(value):
    return lax.ppermute(value, "seq", SWAP)


def pack(rows, index):
    core = lax.axis_index("seq")
    chunks = rows.shape[0] // (2 * CHUNK)
    plain = lax.dynamic_index_in_dim(rows.reshape(chunks, 2, CHUNK, D), core, 1, keepdims=False)
    columns = lax.dynamic_slice_in_dim(rows, core * OWN, OWN, axis=1).reshape(chunks, 2, CHUNK, OWN)
    wide = jnp.concatenate([columns[:, 0], columns[:, 1]], axis=-1)
    where = index * chunks + jnp.arange(chunks)
    is_out = ((where >= 12) & (where < 16))[:, None, None]
    return jnp.where(is_out, wide, plain).reshape(chunks * CHUNK, D)


def unpack(mine, theirs, index):
    core = lax.axis_index("seq")
    chunks = mine.shape[0] // CHUNK
    first = jnp.where(core == 0, mine, theirs).reshape(chunks, CHUNK, D)
    second = jnp.where(core == 0, theirs, mine).reshape(chunks, CHUNK, D)
    plain = jnp.stack([first, second], axis=1)
    upper = jnp.concatenate([first[..., :OWN], second[..., :OWN]], axis=-1)
    lower = jnp.concatenate([first[..., OWN:], second[..., OWN:]], axis=-1)
    wide = jnp.stack([upper, lower], axis=1)
    where = index * chunks + jnp.arange(chunks)
    is_out = ((where >= 12) & (where < 16))[:, None, None, None]
    return jnp.where(is_out, wide, plain).reshape(chunks * 2 * CHUNK, D)


SIDE_X = [(i, i ^ 1) for i in range(16)]
SIDE_Y = [(i, i ^ 2) for i in range(16)]


def up(first, last):
    return [(i, i + 4) for i in range(16) if first <= i // 4 <= last]


def down(first, last):
    return [(i, i - 4) for i in range(16) if first <= i // 4 <= last]


def send(value, pairs):
    return lax.ppermute(value, "dp", pairs)


def pick(plane, *options):
    result = options[-1]
    for i in range(len(options) - 2, -1, -1):
        result = jnp.where(plane == i, options[i], result)
    return result


def barrier(*values):
    return lax.optimization_barrier(values)


HALF = 3 * CHUNK // 2


def top(block):
    return block[:HALF]


def bottom(block):
    return block[HALF:]


def join(first, second):
    return jnp.concatenate([first, second], axis=0)


def add_both_kernel(a_ref, b_ref, c_ref, d_ref, e_ref, first_ref, second_ref):
    total = a_ref[...].astype(f32) + b_ref[...].astype(f32) + c_ref[...].astype(f32)
    first_ref[...] = total.astype(bf16)
    second_ref[...] = (d_ref[...].astype(f32) + e_ref[...].astype(f32)).astype(bf16)


def add_both(*blocks):
    return pl.pallas_call(
        add_both_kernel,
        out_shape=[jax.ShapeDtypeStruct((3 * CHUNK, D), bf16)] * 2,
        compiler_params=params(),
        cost_estimate=cost(1),
        name="add_both",
    )(*blocks)


def planes(step, *targets):
    pairs = [(i, i ^ (4 * step)) for i in range(16)]
    return [pair for pair in pairs if not targets or pair[1] // 4 in targets]


PIECES = ((0, 1, 2, 3), (1, 0, 3, 2), (2, 2, 0, 0), (3, 3, 1, 1))


def gather_steps(block, slots):
    odd = lax.axis_index("dp") // 4 % 2 == 1
    x0, y0 = send(block, SIDE_X), send(block, SIDE_Y)
    s1, far = send(block, planes(1)), send(block, planes(2))
    c0 = send(top(x0), SIDE_Y), send(bottom(y0), SIDE_X)
    x0, y0, s1, far, *c0 = yield x0, y0, s1, far, *c0

    x1, y1 = send(s1, SIDE_X), send(s1, SIDE_Y)
    opposite = send(far, planes(1))
    x1, y1, opposite = yield x1, y1, opposite
    slots.append(((block, 0), (x0, 0), (y0, 0), tuple(c0)))

    s2 = jnp.where(odd, opposite, far)
    s3 = jnp.where(odd, far, opposite)
    x2, y2 = send(s2, SIDE_X), send(s2, SIDE_Y)
    c1 = send(top(x1), SIDE_Y), send(bottom(y1), SIDE_X)
    x2, y2, *c1 = yield x2, y2, *c1
    slots.append(((s1, 0), (x1, 0), (y1, 0), tuple(c1)))

    c2 = send(top(x2), SIDE_Y), send(bottom(y2), SIDE_X)
    c2 = yield c2
    slots.append(((s2, 0), (x2, 0), (y2, 0), tuple(c2)))

    x3, y3 = send(s3, SIDE_X), send(s3, SIDE_Y)
    x3, y3 = yield x3, y3
    c3 = send(top(x3), SIDE_Y), send(bottom(y3), SIDE_X)
    slots.append(((s3, 0), (x3, 0), (y3, 0), None))
    c3 = yield c3
    slots[3] = (*slots[3][:3], tuple(c3))


def reduce_steps(grads, plane, result):
    odd = plane % 2 == 1
    got = yield cross(grads[3])
    x, y = yield across(grads[3], got)
    own3 = plus(grads[3][0], x, y)
    got = yield cross(grads[2])
    x, y = yield across(grads[2], got)
    own2 = plus(grads[2][0], x, y)
    got = yield cross(grads[1])
    high = send(jnp.where(odd, own2, own3), planes(1))
    x, y, high = yield *across(grads[1], got), high
    own1 = plus(grads[1][0], x, y)
    high = plus(jnp.where(odd, own3, own2), high)
    yield ()
    got = yield cross(grads[0])
    x, y, one = yield *across(grads[0], got), send(own1, up(0, 0) + down(3, 3))
    own0, own1 = add_both(grads[0][0], x, y, own1, one)
    zero, one, two = yield (
        send(own0, down(1, 1) + down(3, 3)),
        send(own1, down(2, 2)),
        send(high, planes(2, 2)),
    )
    own0 = plus(own0, zero)
    zero, three = yield send(own0, planes(2, 0)), send(high, planes(2, 3))
    result.append(pick(plane, plus(own0, zero), plus(own1, one), plus(high, two), plus(high, three)))


class Steps:
    def __init__(self, steps):
        self.steps = steps
        self.arrays = next(steps) if steps else ()

    def __call__(self, *values):
        count = len(self.arrays)
        passed = barrier(*self.arrays, *values) if count or values else ()
        if self.steps:
            try:
                self.arrays = self.steps.send(passed[:count])
            except StopIteration:
                self.steps, self.arrays = None, ()
        return passed[count:]


def parts_of(side):
    if side is None:
        return []
    first, second = side
    if isinstance(second, int):
        rows = 3 * CHUNK
        return [(first, second * rows, rows, 0)]
    return [(first, 0, HALF, 0), (second, 0, HALF, HALF)]


def slot_arrays(slots):
    arrays, known = [], {}
    shape = []
    for slot in slots:
        sides = []
        for side in slot:
            parts = []
            for array, start, rows, place in parts_of(side):
                if id(array) not in known:
                    known[id(array)] = len(arrays)
                    arrays.append(array)
                parts.append((known[id(array)], start, rows, place))
            sides.append(tuple(parts))
        shape.append(tuple(sides))
    return arrays, tuple(shape)


def run_copies(pairs, sems):
    copies = [
        pltpu.make_async_copy(source, target, sems.at[i])
        for i, (source, target) in enumerate(pairs)
    ]
    for copy in copies:
        copy.start()
    for copy in copies:
        copy.wait()


def place_heads_kernel(shape, me_ref, *refs):
    mine_ref, give_ref, whole_ref, sems = refs[-4:]
    spot, core, plane = me_ref[0], me_ref[1], me_ref[2]
    for z in range(4):

        @pl.when(plane == z)
        def _():
            pairs = []
            for side in range(4):
                start = 3 * CHUNK * (side + spot - 2 * (side & spot))
                for number, first, rows, place in shape[min(z, 2)][side]:
                    where = pl.ds(pl.multiple_of(start + place, 16), rows)
                    pairs.append((refs[number].at[pl.ds(first, rows)], whole_ref.at[where]))
            run_copies(pairs, sems)

    for ref, who in ((mine_ref, core), (give_ref, 1 - core)):
        for j in range(6):
            chunk = 4 * (j // 2) + 2 * who + j % 2
            ref[j] = whole_ref[pl.ds(pl.multiple_of(chunk * CHUNK, 16), CHUNK)]


def place_heads(me, slots):
    arrays, shape = slot_arrays(slots)
    half = jax.ShapeDtypeStruct((6, CHUNK, D), bf16)
    return pl.pallas_call(
        functools.partial(place_heads_kernel, shape),
        in_specs=[pl.BlockSpec(memory_space=pltpu.SMEM)]
        + [pl.BlockSpec(memory_space=pl.ANY)] * len(arrays),
        out_shape=[half, half],
        scratch_shapes=[pltpu.VMEM((12 * CHUNK, D), bf16), pltpu.SemaphoreType.DMA((8,))],
        compiler_params=params(),
        cost_estimate=cost(1),
        name="place_heads",
    )(me, *arrays)


def place_rest_kernel(shape, held, me_ref, *refs):
    out_ref, in_ref, down_ref, stage_ref, load_sems, store_sems = refs[-6:]
    spot, plane = me_ref[0], me_ref[2]

    def part(pairs, source, first, rows, row):
        while rows:
            if row < 4 * CHUNK:
                chunk, offset = divmod(row, CHUNK)
                count = min(rows, CHUNK - offset)
                targets = []
                for h in range(2):
                    target = 2 * CHUNK * chunk + CHUNK * h + offset
                    targets.append((pl.ds(OWN * h, OWN), out_ref.at[pl.ds(target, count)]))
            else:
                ref, start = (in_ref, 4 * CHUNK) if row < 20 * CHUNK else (down_ref, 20 * CHUNK)
                count = min(rows, start + 16 * CHUNK - row)
                targets = [(slice(None), ref.at[pl.ds(row - start, count)])]
            pairs.append((source.at[pl.ds(first, count)], count, targets))
            row, first, rows = row + count, first + count, rows - count

    for z in range(4):
        for s in range(4):
            pairs = []
            for slot, (number, sides) in zip(shape, held, strict=True):
                piece = PIECES[number][z]
                for side in sides if piece else ():
                    base = 3 * CHUNK * (4 * (piece - 1) + (side ^ s))
                    for array, first, rows, place in slot[side]:
                        part(pairs, refs[array], first, rows, base + place)

            @pl.when((plane == z) & (spot == s))
            def _():
                loads, stores, row = [], [], 0
                for i, (source, count, targets) in enumerate(pairs):
                    spot_rows = pl.ds(row, count)
                    loads.append(
                        pltpu.make_async_copy(source, stage_ref.at[spot_rows], load_sems.at[i])
                    )
                    stores.append([])
                    for columns, target in targets:
                        stores[-1].append(
                            pltpu.make_async_copy(
                                stage_ref.at[spot_rows, columns],
                                target,
                                store_sems.at[2 * i + len(stores[-1])],
                            )
                        )
                    row += count
                for load in loads:
                    load.start()
                for load, store in zip(loads, stores, strict=True):
                    load.wait()
                    for copy in store:
                        copy.start()
                for store in stores:
                    for copy in store:
                        copy.wait()


def place_rest(me, slots, held, state):
    arrays, shape = slot_arrays(
        [[slots[i][side] if side in sides else None for side in range(4)] for i, sides in held]
    )
    units = jax.ShapeDtypeStruct((UNITS, D), bf16)
    anywhere = pl.BlockSpec(memory_space=pl.ANY)
    return pl.pallas_call(
        functools.partial(place_rest_kernel, shape, held),
        in_specs=[pl.BlockSpec(memory_space=pltpu.SMEM)] + [anywhere] * (len(arrays) + len(state)),
        out_specs=[anywhere] * 3,
        out_shape=[jax.ShapeDtypeStruct((D, OWN), bf16), units, units],
        input_output_aliases={1 + len(arrays) + i: i for i in range(len(state))},
        scratch_shapes=[
            pltpu.VMEM((24 * CHUNK, D), bf16),
            pltpu.SemaphoreType.DMA((32,)),
            pltpu.SemaphoreType.DMA((64,)),
        ],
        compiler_params=params(),
        cost_estimate=cost(1),
        name="place_rest",
    )(me, *arrays, *state)


def plus(*values):
    total = values[0].astype(f32)
    for value in values[1:]:
        total = total + value.astype(f32)
    return total.astype(bf16)


def cross(sides):
    return send(sides[3], SIDE_Y), send(sides[4], SIDE_X)


def merge_kernel(x_ref, y_ref, upper_ref, lower_ref, x_out, y_out):
    x_out[:HALF] = (x_ref[:HALF].astype(f32) + upper_ref[...].astype(f32)).astype(bf16)
    x_out[HALF:] = x_ref[HALF:]
    y_out[:HALF] = y_ref[:HALF]
    y_out[HALF:] = (y_ref[HALF:].astype(f32) + lower_ref[...].astype(f32)).astype(bf16)


def across(sides, crossed):
    over_x, over_y = pl.pallas_call(
        merge_kernel,
        out_shape=[jax.ShapeDtypeStruct((3 * CHUNK, D), bf16)] * 2,
        compiler_params=params(),
        cost_estimate=cost(1),
        name="merge",
    )(sides[1], sides[2], *crossed)
    return send(over_x, SIDE_X), send(over_y, SIDE_Y)


def gather_vectors(low_vectors, ranks):
    count, width = low_vectors.shape
    block = jnp.pad(low_vectors, ((0, 16 - count), (0, 128 - width)))
    blocks = lax.all_to_all(jnp.broadcast_to(block, (ranks, 16, 128)), "dp", 0, 0, tiled=True)
    return blocks[:, :count, :width].transpose(1, 0, 2).reshape(count, ranks * width).astype(f32)


def vector_blocks(rows, ranks):
    blocks = rows.reshape(16, ranks, D // ranks).transpose(1, 0, 2)
    return jnp.pad(blocks, ((0, 0), (0, 0), (0, 128 - D // ranks)))


def selection(span, kind, source, half_len):
    chosen = span == 1
    masked = chosen & (kind < 8)
    swapped = chosen & (kind == 8)
    here = lax.broadcasted_iota(jnp.int32, (1, half_len), 1)
    origin = jnp.where(masked, -1, jnp.where(swapped, source, here))
    rows = lax.broadcasted_iota(jnp.int32, (half_len, half_len), 0)
    one_hot = (rows == origin).astype(f32).astype(bf16)
    first = lax.broadcasted_iota(jnp.int32, (16, half_len), 0) == 0
    mask_rows = jnp.where(first & masked, 1.0, 0.0).astype(bf16)
    return one_hot, mask_rows


def corrupt_kernel(span_ref, kind_ref, from_ref, hidden_ref, mask_ref, out_ref):
    seqs, half_len = span_ref.shape
    for s in range(seqs):
        rows = slice(s, s + 1)
        one_hot, mask_rows = selection(
            span_ref[rows, :], kind_ref[rows, :], from_ref[rows, :], half_len
        )
        picked = dot(one_hot, hidden_ref[s], TN) + dot(mask_rows, mask_ref[...], TN)
        out_ref[s] = picked.astype(bf16)


def corrupt(span, kind, source, hidden, mask_row):
    mask = jnp.broadcast_to(mask_row.astype(bf16)[None], (16, D))
    return pl.pallas_call(
        corrupt_kernel,
        out_shape=jax.ShapeDtypeStruct(hidden.shape, bf16),
        compiler_params=params(),
        name="corrupt",
    )(span, kind, source, hidden, mask)


def corrupt_back_kernel(
    span_ref, kind_ref, from_ref, grad_ref, own_ref, partial_ref, out_ref, mask_ref
):
    seqs, half_len = span_ref.shape
    mask_sum = jnp.zeros((16, D), f32)
    for s in range(seqs):
        rows = slice(s, s + 1)
        block = pl.ds(s * half_len, half_len)
        one_hot, mask_rows = selection(
            span_ref[rows, :], kind_ref[rows, :], from_ref[rows, :], half_len
        )
        grad = grad_ref[block] + own_ref[block] + partial_ref[block].astype(f32)
        high = grad.astype(bf16)
        low = (grad - high.astype(f32)).astype(bf16)
        out_ref[s] = dot(one_hot, high, NN) + dot(one_hot, low, NN)
        mask_sum = mask_sum + dot(mask_rows, high, NN) + dot(mask_rows, low, NN)
    mask_ref[...] = mask_sum


def corrupt_back(span, kind, source, grad, own, partial):
    seqs, half_len = span.shape
    return pl.pallas_call(
        corrupt_back_kernel,
        out_shape=[
            jax.ShapeDtypeStruct((seqs, half_len, D), f32),
            jax.ShapeDtypeStruct((16, D), f32),
        ],
        compiler_params=params(),
        cost_estimate=cost(1),
        name="corrupt_back",
    )(span, kind, source, grad, own, partial)


def attend_kernel(
    me_ref, own_ref, other_ref, mine_ref, theirs_ref, vals_ref, w_ref, qkv_ref, low_ref, wide_ref, lse_ref
):
    half_len = own_ref.shape[1]
    core = me_ref[1]

    @pl.when(pl.program_id(0) == 0)
    def _():
        for j in range(6):
            for ref, which in ((mine_ref, core), (theirs_ref, 1 - core)):
                where = pl.ds(pl.multiple_of((2 * j + which) * CHUNK, 16), CHUNK)
                w_ref[where] = ref[j]

    rows = jnp.concatenate([own_ref[0], other_ref[0]], axis=0)
    columns = pl.ds(pl.multiple_of(core * OWN, 128), OWN)
    bias = jnp.concatenate(
        [vals_ref[0:1, columns], jnp.zeros((1, OWN), f32), vals_ref[1:2, columns]], axis=-1
    )
    projected = (dot(rows, w_ref[...], NT) + bias).astype(bf16)
    qkv_ref[:, 0] = projected.reshape(2, half_len, 3 * OWN)
    wide, totals = [], []

    def score(h):
        columns = slice(h * HEAD_DIM, (h + 1) * HEAD_DIM)
        query = projected[:, :OWN][:, columns] * bf16(HEAD_DIM**-0.5)
        return dot(query, projected[:, OWN : 2 * OWN][:, columns], NT)

    heads = OWN // HEAD_DIM
    ahead = [score(0), score(1)]
    for h in range(heads):
        if h + 2 < heads:
            ahead.append(score(h + 2))
        scores = ahead.pop(0)
        value = projected[:, 2 * OWN :][:, h * HEAD_DIM : (h + 1) * HEAD_DIM]
        highest = jnp.max(scores, axis=-1, keepdims=True)
        exponents = jnp.exp(scores - highest)
        total = jnp.sum(exponents, axis=-1, keepdims=True)
        probabilities = (exponents * (1.0 / total)).astype(bf16)
        wide.append(dot(probabilities, value, NN))
        totals.append(highest + jnp.log(total))
    attended = jnp.concatenate(wide, axis=-1)
    wide_ref[:, 0] = attended.reshape(2, half_len, OWN)
    low_ref[:, 0] = attended.astype(bf16).reshape(2, half_len, OWN)
    fill = jnp.zeros((2 * half_len, 128 - len(totals)), f32)
    lse_ref[0] = jnp.concatenate(totals + [fill], axis=-1).T[:8]


def whole(*shape):
    return pl.BlockSpec(shape, lambda *_: (0,) * len(shape))


def attend(me, u_own, u_other, mine, theirs, vals):
    seqs, half_len, _ = u_own.shape
    block = lambda width: pl.BlockSpec((2, 1, half_len, width), lambda s: (0, s, 0, 0))
    token = pl.BlockSpec((1, half_len, D), lambda s: (s, 0, 0))
    return pl.pallas_call(
        attend_kernel,
        grid=(seqs,),
        in_specs=[
            pl.BlockSpec(memory_space=pltpu.SMEM),
            token,
            token,
            whole(6, CHUNK, D),
            whole(6, CHUNK, D),
            whole(*vals.shape),
        ],
        out_specs=[
            whole(3 * OWN, D),
            block(3 * OWN),
            block(OWN),
            block(OWN),
            pl.BlockSpec((1, 8, 2 * half_len), lambda s: (s, 0, 0)),
        ],
        out_shape=[
            jax.ShapeDtypeStruct((3 * OWN, D), bf16),
            jax.ShapeDtypeStruct((2, seqs, half_len, 3 * OWN), bf16),
            jax.ShapeDtypeStruct((2, seqs, half_len, OWN), bf16),
            jax.ShapeDtypeStruct((2, seqs, half_len, OWN), f32),
            jax.ShapeDtypeStruct((seqs, 8, 2 * half_len), f32),
        ],
        cost_estimate=cost(3),
        compiler_params=params(),
        name="attend",
    )(me, u_own, u_other, mine, theirs, vals)


def attend_back_kernel(
    skip, qkv_ref, own_ref, other_ref, wo_ref, wide_ref, lse_ref, *refs
):
    out_ref, sums_ref = refs[skip:]
    half_len = qkv_ref.shape[2]
    length = 2 * half_len
    projected = qkv_ref[:, 0].reshape(length, 3 * OWN)
    rows = jnp.concatenate([own_ref[0], other_ref[0]], axis=0)
    grad = dot(rows, wo_ref[...], NN).astype(bf16)
    product = grad.astype(f32) * wide_ref[:, 0].reshape(length, OWN)
    heads = OWN // HEAD_DIM
    deltas = [
        jnp.sum(product[:, h * HEAD_DIM : (h + 1) * HEAD_DIM], axis=-1, keepdims=True)
        for h in range(heads)
    ]
    fill = jnp.zeros((length, 128 - heads), f32)
    delta_rows = jnp.concatenate(deltas + [fill], axis=-1).T
    parts = [[], [], []]

    def head(h):
        columns = slice(h * HEAD_DIM, (h + 1) * HEAD_DIM)
        query = projected[:, :OWN][:, columns] * bf16(HEAD_DIM**-0.5)
        key = projected[:, OWN : 2 * OWN][:, columns]
        value = projected[:, 2 * OWN :][:, columns]
        return query, key, value, grad[:, columns]

    def products(h):
        query, key, value, grad_head = head(h)
        return dot(key, query, NT), dot(value, grad_head, NT)

    ahead = [products(0)]
    for h in range(heads):
        if h + 1 < heads:
            ahead.append(products(h + 1))
        scores, grad_weights = ahead.pop(0)
        query, key, value, grad_head = head(h)
        weights = jnp.exp(scores - lse_ref[0, h : h + 1, :])
        grad_scores = (weights * (grad_weights - delta_rows[h : h + 1, :])).astype(bf16)
        parts[0].append(dot(grad_scores, key, TN) * HEAD_DIM**-0.5)
        parts[1].append(dot(grad_scores, query, NN))
        parts[2].append(dot(weights.astype(bf16), grad_head, NN))
    result = jnp.concatenate(parts[0] + parts[1] + parts[2], axis=-1).astype(bf16)
    out_ref[:, 0] = result.reshape(2, half_len, 3 * OWN)
    sums = jnp.sum(result.astype(f32), axis=0, keepdims=True)

    @pl.when(pl.program_id(0) == 0)
    def _():
        sums_ref[...] = refs[1][...] if skip else jnp.zeros_like(sums_ref)

    sums_ref[...] += sums


def attend_back(qkv, own, other, wo_own, wide, lse, first, count, state):
    _, seqs, half_len, _ = qkv.shape
    block = lambda width: pl.BlockSpec((2, 1, half_len, width), lambda s: (0, s + first, 0, 0))
    token = pl.BlockSpec((1, half_len, D), lambda s: (s + first, 0, 0))
    return pl.pallas_call(
        functools.partial(attend_back_kernel, len(state)),
        grid=(count,),
        in_specs=[
            block(3 * OWN),
            token,
            token,
            whole(D, OWN),
            block(OWN),
            pl.BlockSpec((1, 8, 2 * half_len), lambda s: (s + first, 0, 0)),
        ]
        + ([pl.BlockSpec(memory_space=pl.ANY), whole(1, 3 * OWN)] if state else []),
        out_specs=[block(3 * OWN), whole(1, 3 * OWN)],
        input_output_aliases={6: 0} if state else {},
        out_shape=[
            jax.ShapeDtypeStruct((2, seqs, half_len, 3 * OWN), bf16),
            jax.ShapeDtypeStruct((1, 3 * OWN), f32),
        ],
        cost_estimate=cost(2 * count),
        compiler_params=params(),
        name="attend_back",
    )(qkv, own, other, wo_own, wide, lse, *state)


def norm(values):
    center = values - jnp.mean(values, axis=-1, keepdims=True)
    inv_std = lax.rsqrt(jnp.mean(center * center, axis=-1, keepdims=True) + ln_eps)
    return center * inv_std, inv_std


def norm_backward(upstream, normed, inv_std, gain):
    scaled = upstream * gain
    return inv_std * (
        scaled
        - jnp.mean(scaled, axis=-1, keepdims=True)
        - normed * jnp.mean(scaled * normed, axis=-1, keepdims=True)
    )


def row(ref, i):
    return ref[i : i + 1, :]


def branch_kernel(own_ref, other_ref, u_ref, wo_ref, wo_other_ref, vals_ref, normed_ref, inv_ref, low_ref):
    branch = dot(own_ref[0, 0], wo_ref[...], NT) + dot(other_ref[0], wo_other_ref[...], NT)
    normed, inv = norm(u_ref[0].astype(f32) + branch + row(vals_ref, 2))
    normed_ref[...] = normed
    inv_ref[...] = jnp.broadcast_to(inv, inv_ref.shape)
    low_ref[...] = (normed * row(vals_ref, 3) + row(vals_ref, 4)).astype(bf16)


def attention_branch(attended, from_other, u_own, wo_own, wo_other, vals):
    seqs, half_len, _ = u_own.shape
    rows = pl.BlockSpec((half_len, D), lambda s: (s, 0))
    return pl.pallas_call(
        branch_kernel,
        grid=(seqs,),
        in_specs=[
            pl.BlockSpec((1, 1, half_len, OWN), lambda s: (0, s, 0, 0)),
            pl.BlockSpec((1, half_len, OWN), lambda s: (s, 0, 0)),
            pl.BlockSpec((1, half_len, D), lambda s: (s, 0, 0)),
            whole(D, OWN),
            whole(D, OWN),
            whole(*vals.shape),
        ],
        out_specs=[rows, pl.BlockSpec((half_len, 128), lambda s: (s, 0)), rows],
        out_shape=[
            jax.ShapeDtypeStruct((seqs * half_len, D), f32),
            jax.ShapeDtypeStruct((seqs * half_len, 128), f32),
            jax.ShapeDtypeStruct((seqs * half_len, D), bf16),
        ],
        cost_estimate=cost(1),
        compiler_params=params(),
        name="attention_branch",
    )(attended, from_other, u_own, wo_own, wo_other, vals)


def hidden_kernel(own_ref, other_ref, w_ref, bias_ref, gelu_ref, slope_ref):
    tile = own_ref.shape[0] // 3
    jobs = [
        (half, ref, slice(i * tile, (i + 1) * tile))
        for half, ref in enumerate((own_ref, other_ref))
        for i in range(3)
    ]

    def project(job):
        _, ref, rows = jobs[job]
        return dot(ref[rows], w_ref[...], NT) + bias_ref[...]

    ahead = project(0)
    for i, (half, _, rows) in enumerate(jobs):
        points = ahead
        if i + 1 < len(jobs):
            ahead = project(i + 1)
        below = 0.5 * (1.0 + lax.erf(points * 2**-0.5))
        density = jnp.exp(-0.5 * points * points) * 0.3989422804014327
        gelu_ref[half, rows] = (points * below).astype(bf16)
        slope_ref[half, rows] = (below + points * density).astype(bf16)


def hidden_units(h_own, h_other, w_in, bias):
    rows = h_own.shape[0]
    width = 384
    block = pl.BlockSpec((2, rows, width), lambda i: (0, 0, i))
    return pl.pallas_call(
        hidden_kernel,
        grid=(UNITS // width,),
        in_specs=[
            whole(rows, D),
            whole(rows, D),
            pl.BlockSpec((width, D), lambda i: (i, 0)),
            pl.BlockSpec((1, width), lambda i: (0, i)),
        ],
        out_specs=[block, block],
        out_shape=[jax.ShapeDtypeStruct((2, rows, UNITS), bf16)] * 2,
        cost_estimate=cost(3),
        compiler_params=params(),
        name="hidden_units",
    )(h_own, h_other, w_in, bias)


def rows_kernel(left_ref, right_ref, out_ref):
    out_ref[...] = dot(left_ref[0], right_ref[...], NN).astype(out_ref.dtype)


def rows_times(left, half, right, dtype, name):
    _, rows, depth = left.shape
    tile = rows // 3
    return pl.pallas_call(
        rows_kernel,
        grid=(3,),
        in_specs=[pl.BlockSpec((1, tile, depth), lambda i: (half, i, 0)), whole(*right.shape)],
        out_specs=pl.BlockSpec((tile, D), lambda i: (i, 0)),
        out_shape=jax.ShapeDtypeStruct((rows, D), dtype),
        cost_estimate=cost(1),
        compiler_params=params(),
        name=name,
    )(left, right)


def add_sums(sums_ref, *values):
    @pl.when(pl.program_id(0) == 0)
    def _():
        sums_ref[...] = jnp.zeros_like(sums_ref)

    for i, value in enumerate(values):
        sums_ref[i : i + 1, :] += jnp.sum(value, axis=0, keepdims=True)


def finish_kernel(own_ref, other_ref, normed_ref, grad_ref, vals_ref, out_ref, wide_ref, low_ref, sums_ref):
    hidden_one = normed_ref[...] * row(vals_ref, 3) + row(vals_ref, 4)
    feed = own_ref[...] + other_ref[...].astype(f32) + row(vals_ref, 5)
    normed, inv = norm(hidden_one + feed)
    out_ref[...] = normed * row(vals_ref, 6) + row(vals_ref, 7)
    grad = grad_ref[...].astype(f32)
    wide = norm_backward(grad, normed, inv, row(vals_ref, 6))
    low = wide.astype(bf16)
    wide_ref[...] = wide
    low_ref[...] = low
    add_sums(sums_ref, low.astype(f32), grad * normed, grad)


def finish(own, other, normed, grad, vals):
    rows = own.shape[0]
    tile = rows // 3
    block = pl.BlockSpec((tile, D), lambda i: (i, 0))
    return pl.pallas_call(
        finish_kernel,
        grid=(3,),
        in_specs=[block] * 4 + [whole(*vals.shape)],
        out_specs=[block] * 3 + [whole(8, D)],
        out_shape=[
            jax.ShapeDtypeStruct((rows, D), f32),
            jax.ShapeDtypeStruct((rows, D), f32),
            jax.ShapeDtypeStruct((rows, D), bf16),
            jax.ShapeDtypeStruct((8, D), f32),
        ],
        cost_estimate=cost(1),
        compiler_params=params(),
        name="finish",
    )(own, other, normed, grad, vals)


def norm_one_kernel(two_ref, own_ref, other_ref, normed_ref, inv_ref, vals_ref, wide_ref, low_ref, sums_ref):
    grad = two_ref[...] + own_ref[...] + other_ref[...].astype(f32)
    normed = normed_ref[...]
    wide = norm_backward(grad, normed, inv_ref[:, 0:1], row(vals_ref, 3))
    low = wide.astype(bf16)
    wide_ref[...] = wide
    low_ref[...] = low
    add_sums(sums_ref, low.astype(f32), grad * normed, grad)


def norm_one_back(two, own, other, normed, inv, vals):
    rows = own.shape[0]
    tile = rows // 3
    block = pl.BlockSpec((tile, D), lambda i: (i, 0))
    return pl.pallas_call(
        norm_one_kernel,
        grid=(3,),
        in_specs=[block] * 4 + [pl.BlockSpec((tile, 128), lambda i: (i, 0)), whole(*vals.shape)],
        out_specs=[block] * 2 + [whole(8, D)],
        out_shape=[
            jax.ShapeDtypeStruct((rows, D), f32),
            jax.ShapeDtypeStruct((rows, D), bf16),
            jax.ShapeDtypeStruct((8, D), f32),
        ],
        cost_estimate=cost(1),
        compiler_params=params(),
        name="norm_one_back",
    )(two, own, other, normed, inv, vals)


def slope_kernel(grad_ref, w_ref, slope_ref, out_ref, sums_ref):
    low = (dot(grad_ref[...], w_ref[...], NT) * slope_ref[0].astype(f32)).astype(bf16)
    out_ref[0] = low
    sums_ref[...] = jnp.sum(low.astype(f32), axis=0, keepdims=True)


def before_gelu(grad, w_down, slope, half):
    rows = grad.shape[0]
    width = 384
    return pl.pallas_call(
        slope_kernel,
        grid=(UNITS // width,),
        in_specs=[
            whole(rows, D),
            pl.BlockSpec((width, D), lambda i: (i, 0)),
            pl.BlockSpec((1, rows, width), lambda i: (half, 0, i)),
        ],
        out_specs=[
            pl.BlockSpec((1, rows, width), lambda i: (0, 0, i)),
            pl.BlockSpec((1, width), lambda i: (0, i)),
        ],
        out_shape=[
            jax.ShapeDtypeStruct((1, rows, UNITS), bf16),
            jax.ShapeDtypeStruct((1, UNITS), f32),
        ],
        cost_estimate=cost(1),
        compiler_params=params(),
        name="before_gelu",
    )(grad, w_down, slope)


def rows_of(count):
    return jax.ShapeDtypeStruct((count, D), bf16)


CROSS = ((0, 0, 288), (1, 0, 288), (2, 0, 288), (3, 0, 144), (3, 144, 144))


def side_rows(spot, side, first, rows):
    start = 3 * CHUNK * (side + spot - 2 * (side & spot)) + first
    return pl.ds(pl.multiple_of(start, 16), rows)


def write_sides(spot, piece_ref, outs):
    for out, (side, first, rows) in zip(outs, CROSS, strict=True):
        out[...] = piece_ref[side_rows(spot, side, first, rows)]


def rows_at(step):
    return pl.ds(pl.multiple_of(step * OWN, 16), OWN)


def two_halves(left, left_other, right, right_other):
    return dot(left, right, TN) + dot(left_other, right_other, TN)


def grads3_kernel(me_ref, g_ref, d_ref, d_other_ref, *refs):
    piece_ref = refs[-1]
    step = pl.program_id(0)
    piece_ref[rows_at(step)] = two_halves(
        g_ref[0], g_ref[1], d_ref[...], d_other_ref[...]
    ).astype(bf16)

    @pl.when(step == 2)
    def _():
        write_sides(me_ref[0], piece_ref, refs[:-1])


def grads2_kernel(me_ref, z_ref, z_other_ref, h_ref, h_other_ref, g_ref, d_ref, d_other_ref, *refs):
    piece_ref = refs[-1]
    step = pl.program_id(0)

    @pl.when(step < 2)
    def _():
        piece_ref[rows_at(step)] = two_halves(
            z_ref[0], z_other_ref[0], h_ref[...], h_other_ref[...]
        ).astype(bf16)

    @pl.when(step == 2)
    def _():
        piece_ref[rows_at(step)] = two_halves(
            g_ref[0], g_ref[1], d_ref[...], d_other_ref[...]
        ).astype(bf16)
        write_sides(me_ref[0], piece_ref, refs[:-1])


def grads1_kernel(me_ref, z_ref, z_other_ref, h_ref, h_other_ref, a_ref, a_other_ref, att_ref, *refs):
    piece_ref = refs[-1]
    step = pl.program_id(0)

    @pl.when(step < 2)
    def _():
        piece_ref[rows_at(step + 1)] = two_halves(
            z_ref[0], z_other_ref[0], h_ref[...], h_other_ref[...]
        ).astype(bf16)

    @pl.when(step == 2)
    def _():
        wo = two_halves(a_ref[...], a_other_ref[...], att_ref[0], att_ref[1]).astype(bf16)
        for j in range(4):
            upper = wo[2 * CHUNK * j : 2 * CHUNK * j + CHUNK]
            lower = wo[2 * CHUNK * j + CHUNK : 2 * CHUNK * (j + 1)]
            piece_ref[CHUNK * j : CHUNK * (j + 1)] = jnp.concatenate([upper, lower], axis=-1)
        write_sides(me_ref[0], piece_ref, refs[:-1])


def grads_call(kernel, specs, arrays, name):
    return pl.pallas_call(
        kernel,
        grid=(3,),
        in_specs=[pl.BlockSpec(memory_space=pltpu.SMEM)] + specs,
        out_specs=[whole(count, D) for _, _, count in CROSS],
        out_shape=[rows_of(count) for _, _, count in CROSS],
        scratch_shapes=[pltpu.VMEM((12 * CHUNK, D), bf16)],
        cost_estimate=cost(2),
        compiler_params=params(),
        name=name,
    )(*arrays)


def grads0_kernel(me_ref, g_ref, u_ref, u_other_ref, keep_ref, give_ref, piece_ref):
    core = me_ref[1]
    step = pl.program_id(0)
    piece_ref[rows_at(step)] = two_halves(
        g_ref[0], g_ref[1], u_ref[...], u_other_ref[...]
    ).astype(bf16)

    @pl.when(step == 2)
    def _():
        for j in range(6):
            for ref, which in ((keep_ref, core), (give_ref, 1 - core)):
                where = pl.ds(pl.multiple_of((2 * j + which) * CHUNK, 16), CHUNK)
                ref[j] = piece_ref[where]


def grads0(me, grad, u_own, u_other):
    rows = grad.shape[1]
    half = jax.ShapeDtypeStruct((6, CHUNK, D), bf16)
    return pl.pallas_call(
        grads0_kernel,
        grid=(3,),
        in_specs=[
            pl.BlockSpec(memory_space=pltpu.SMEM),
            pl.BlockSpec((2, rows, OWN), lambda i: (0, 0, i)),
            whole(rows, D),
            whole(rows, D),
        ],
        out_specs=[whole(6, CHUNK, D)] * 2,
        out_shape=[half, half],
        scratch_shapes=[pltpu.VMEM((12 * CHUNK, D), bf16)],
        cost_estimate=cost(2),
        compiler_params=params(),
        name="grads0",
    )(me, grad, u_own, u_other)


def regroup_kernel(me_ref, keep_ref, take_ref, *refs):
    piece_ref = refs[-1]
    core = me_ref[1]
    for ref, who in ((keep_ref, core), (take_ref, 1 - core)):
        for j in range(6):
            chunk = 4 * (j // 2) + 2 * who + j % 2
            piece_ref[pl.ds(pl.multiple_of(chunk * CHUNK, 16), CHUNK)] = ref[j]
    write_sides(me_ref[0], piece_ref, refs[:-1])


def regroup(me, keep, take):
    return pl.pallas_call(
        regroup_kernel,
        in_specs=[pl.BlockSpec(memory_space=pltpu.SMEM)]
        + [pl.BlockSpec(memory_space=pltpu.VMEM)] * 2,
        out_shape=[rows_of(count) for _, _, count in CROSS],
        scratch_shapes=[pltpu.VMEM((12 * CHUNK, D), bf16)],
        cost_estimate=cost(1),
        compiler_params=params(),
        name="regroup",
    )(me, keep, take)


def vector_kernel(me_ref, qkv_ref, one_ref, two_ref, mask_ref, bias_ref, out_ref):
    out_ref[...] = jnp.zeros_like(out_ref)
    columns = pl.ds(pl.multiple_of(me_ref[1] * OWN, 128), OWN)
    out_ref[0:1, columns] = qkv_ref[:, :OWN]
    out_ref[1:2, columns] = qkv_ref[:, 2 * OWN :]
    out_ref[2:5, :] = one_ref[0:3, :]
    out_ref[5:8, :] = two_ref[0:3, :]
    out_ref[8:9, :] = mask_ref[0:1, :]
    out_ref[9:13, :] = bias_ref[...]


def vector_rows(me, qkv_sums, one_sums, two_sums, mask_sums, bias_sums):
    return pl.pallas_call(
        vector_kernel,
        in_specs=[pl.BlockSpec(memory_space=pltpu.SMEM)]
        + [pl.BlockSpec(memory_space=pltpu.VMEM)] * 5,
        out_shape=jax.ShapeDtypeStruct((16, D), f32),
        cost_estimate=cost(1),
        name="vector_rows",
    )(me, qkv_sums, one_sums, two_sums, mask_sums, bias_sums)


def adam_step(master, first_old, second, gradient, decay_on, step_rate):
    first_new = beta_one * first_old + (1.0 - beta_one) * gradient
    second_new = beta_two * second + (1.0 - beta_two) * gradient * gradient
    fix_one = 1.0 / (1.0 - beta_one**STEP)
    fix_two = 1.0 / (1.0 - beta_two**STEP)
    update = first_new * fix_one / (jnp.sqrt(second_new * fix_two) + adam_eps)
    return (master - step_rate * (update + decay_on * master), first_new, second_new)


def update_kernel(sums_ref, grad_ref, *refs):
    norm_value = jnp.sqrt(jnp.sum(sums_ref[...], axis=0))[0:1, 0:1]
    clip = 1.0 / jnp.maximum(norm_value, 1.0)
    master, first, second = (ref[...] for ref in refs[:3])
    gradient = grad_ref[...].astype(f32) * clip
    master, first, second = adam_step(master, first, second, gradient, decay_rate, learn_rate)
    for ref, value in zip(refs[3:], (master, first, second, master.astype(bf16)), strict=True):
        ref[...] = value


def update_weights(sums, grad, master, first, second):
    rows = grad.shape[0]
    tile = 144 if rows % 144 == 0 else rows
    block = pl.BlockSpec((tile, D), lambda i: (i, 0))
    return pl.pallas_call(
        update_kernel,
        grid=(rows // tile,),
        in_specs=[whole(*sums.shape)] + [block] * 4,
        out_specs=[block] * 4,
        out_shape=[jax.ShapeDtypeStruct((rows, D), f32)] * 3
        + [jax.ShapeDtypeStruct((rows, D), bf16)],
        cost_estimate=cost(1),
        compiler_params=params(),
        name="update_weights",
    )(sums, grad, master, first, second)


def shards(
    ranks,
    hidden,
    span_mask,
    replace_kind,
    replace_from,
    weights,
    vectors,
    weight_first,
    weight_second,
    vector_first,
    vector_second,
    cotangent,
):
    seqs, half_len, _ = hidden.shape
    rows = seqs * half_len
    index = lax.axis_index("dp")
    core = lax.axis_index("seq")
    staged = ranks == 16
    plane = index // 4
    spot = index % 4 if staged else jnp.zeros_like(index)
    me = jnp.stack([spot, core, plane]).astype(jnp.int32)
    low_weights = weights.astype(bf16)
    slots, grads, result = [], {}, []
    if staged:
        gather = Steps(gather_steps(pack(low_weights, index), slots))
    else:
        gather = Steps(None)
        stacked = pack(lax.all_gather(low_weights, "dp", axis=0, tiled=True), 0)

    gather()
    gather()
    vals = gather_vectors(vectors.astype(bf16), ranks)
    every, rest = (0, 1, 2, 3), ()
    if staged:
        rest = place_rest(me, slots, ((0, every),), ())
    vals, *rest = gather(vals, *rest)
    u_own = corrupt(span_mask, replace_kind, replace_from, hidden, vals[8])
    bias_in = lax.dynamic_index_in_dim(
        vals[9:].reshape(FF // (2 * CHUNK), 2, CHUNK), core, 1, keepdims=False
    ).reshape(1, UNITS)
    if staged:
        rest = place_rest(me, slots, ((1, every),), rest)
    u_own, vals, bias_in, *rest = gather(u_own, vals, bias_in, *rest)
    u_other = swap(u_own)

    if staged:
        mine, give = place_heads(me, slots)
    else:
        halves = stacked[: 12 * CHUNK].reshape(3, 2, 2, CHUNK, D)
        mine = lax.dynamic_index_in_dim(halves, core, 1, keepdims=False).reshape(6, CHUNK, D)
        give = lax.dynamic_index_in_dim(halves, 1 - core, 1, keepdims=False).reshape(6, CHUNK, D)
    w_qkv, qkv, attended, attended_wide, lse = attend(
        me, u_own, u_other, mine, swap(give), vals
    )
    w_qkv, qkv, attended, attended_wide, lse, *rest = gather(
        w_qkv, qkv, attended, attended_wide, lse, *rest
    )
    from_other = swap(attended[1])
    if staged:
        rest = place_rest(me, slots, ((2, every), (3, (0, 1, 2))), rest)
    attended, from_other, *rest = gather(attended, from_other, *rest)

    if staged:
        wo_own, w_in, w_down = place_rest(me, slots, ((3, (3,)),), rest)
    else:
        rest = stacked[12 * CHUNK :]
        wo_own = (
            rest[: 4 * CHUNK].reshape(4, CHUNK, 2, OWN).transpose(0, 2, 1, 3).reshape(D, OWN)
        )
        w_in, w_down = rest[4 * CHUNK : 20 * CHUNK], rest[20 * CHUNK :]
    normed_one, inv_one, h_own = attention_branch(
        attended, from_other, u_own, wo_own, swap(wo_own), vals
    )
    h_other = swap(h_own)
    gelu, slope = hidden_units(h_own, h_other, w_in, bias_in)
    feed_other = swap(rows_times(gelu, 1, w_down, bf16, "feed_other"))
    feed_own = rows_times(gelu, 0, w_down, f32, "feed_own")
    layer_out, grad_two, d_own, two_sums = finish(
        feed_own, feed_other, normed_one, cotangent.reshape(rows, D), vals
    )

    d_other = swap(d_own)
    z_own, z_sums = before_gelu(d_own, w_down, slope, 0)
    d_other, z_own, z_sums = barrier(d_other, z_own, z_sums)
    unit = lambda first: pl.BlockSpec((2, rows, OWN), lambda i: (0, 0, i + first))
    one_unit = lambda first: pl.BlockSpec((1, rows, OWN), lambda i: (0, 0, jnp.minimum(i, 1) + first))
    tokens = whole(rows, D)
    grads[3] = grads_call(
        grads3_kernel, [unit(1), tokens, tokens], (me, gelu, d_own, d_other), "grads3"
    )
    *grads[3], d_other = barrier(*grads[3], d_other)
    reduce = Steps(reduce_steps(grads, plane, result) if staged else None)
    z_other, z_other_sums = before_gelu(d_other, w_down, slope, 1)
    hidden_other = rows_times(z_other, 0, w_in, bf16, "hidden_other")
    z_other, z_other_sums, hidden_other, z_own = reduce(
        z_other, z_other_sums, hidden_other, z_own
    )
    sent_hidden = swap(hidden_other)
    hidden_own = rows_times(z_own, 0, w_in, f32, "hidden_own")
    grad_one, a_own, one_sums = norm_one_back(
        grad_two, hidden_own, sent_hidden, normed_one, inv_one, vals
    )
    first_unit = pl.BlockSpec((2, rows, OWN), lambda i: (0, 0, 0))
    grads[2] = grads_call(
        grads2_kernel,
        [one_unit(2), one_unit(2), tokens, tokens, first_unit, tokens, tokens],
        (me, z_own, z_other, h_own, h_other, gelu, d_own, d_other),
        "grads2",
    )
    *grads[2], grad_one, a_own, one_sums = reduce(*grads[2], grad_one, a_own, one_sums)
    a_other = swap(a_own)
    a_own, a_other, qkv = reduce(a_own, a_other, qkv)
    back = (
        a_own.reshape(seqs, half_len, D),
        a_other.reshape(seqs, half_len, D),
        wo_own,
        attended_wide,
        lse,
    )
    state = attend_back(qkv, *back, 0, 1, ())
    grads[1] = grads_call(
        grads1_kernel,
        [one_unit(0), one_unit(0), tokens, tokens, tokens, tokens, whole(2, rows, OWN)],
        (me, z_own, z_other, h_own, h_other, a_own, a_other, attended.reshape(2, rows, OWN)),
        "grads1",
    )
    *grads[1], a, b, qkv = reduce(*grads[1], *state, qkv)
    state = attend_back(qkv, *back, 1, 1, (a, b))
    a, b, qkv = reduce(*state, qkv)
    grad_qkv, qkv_sums = attend_back(qkv, *back, 2, seqs - 2, (a, b))
    grad_rows = grad_qkv.reshape(2, rows, 3 * OWN)
    keep, give = grads0(me, grad_rows, u_own.reshape(rows, D), u_other.reshape(rows, D))
    keep, give, grad_rows = reduce(keep, give, grad_rows)
    take = swap(give)
    inputs_other = rows_times(grad_rows, 1, w_qkv, bf16, "inputs_other")
    grads[0] = regroup(me, keep, take)
    *grads[0], grad_rows, inputs_other = reduce(*grads[0], grad_rows, inputs_other)
    sent_inputs = swap(inputs_other)
    inputs_own = rows_times(grad_rows, 0, w_qkv, f32, "inputs_own")
    sent_inputs, inputs_own, z_sums = reduce(sent_inputs, inputs_own, z_sums)
    input_grad, mask_sums = corrupt_back(
        span_mask, replace_kind, replace_from, grad_one, inputs_own, sent_inputs
    )
    bias_sums = jnp.zeros((FF // (2 * CHUNK), 2, CHUNK), f32)
    bias_sums = lax.dynamic_update_slice(
        bias_sums,
        (z_sums + z_other_sums).reshape(FF // (2 * CHUNK), 1, CHUNK),
        (0, core, 0),
    ).reshape(FF // D, D)
    vector_part = vector_rows(me, qkv_sums, one_sums, two_sums, mask_sums, bias_sums)
    input_grad, vector_part = reduce(input_grad, vector_part)
    blocks = vector_blocks(vector_part + swap(vector_part), ranks)
    (blocks,) = reduce(blocks)
    blocks = lax.all_to_all(blocks, "dp", 0, 0, tiled=True)
    (blocks,) = reduce(blocks)
    count, width = vectors.shape
    shard_v = jnp.sum(blocks, axis=0)[:count, :width]

    if staged:
        shard_half = result[0]
        shard_w = unpack(shard_half, swap(shard_half), index)
    else:
        core_rows = [block for i in range(4) for block in grads[i]]
        core_rows = jnp.concatenate(core_rows, axis=0)
        stacked = unpack(core_rows, swap(core_rows), 0).astype(f32)
        shard_w = lax.psum_scatter(stacked, "dp", scatter_dimension=0, tiled=True)
        shard_half = lax.dynamic_slice_in_dim(shard_w, core * OWN, OWN, axis=1)

    half32 = shard_half.astype(f32)
    squares = jnp.sum(half32 * half32) + 0.5 * jnp.sum(shard_v * shard_v)
    blocks = lax.all_to_all(
        jnp.full((2 * ranks, 8, 128), squares), ("dp", "seq"), 0, 0, tiled=True
    )
    grad_norm = jnp.sqrt(jnp.sum(blocks[:, 0, 0]))
    clip = 1.0 / jnp.maximum(grad_norm, 1.0)
    weights_new, weight_first_new, weight_second_new, weights_low = update_weights(
        blocks, shard_w, weights, weight_first, weight_second
    )
    vectors_new, vector_first_new, vector_second_new = adam_step(
        vectors, vector_first, vector_second, shard_v * clip, 0.0, vector_rate
    )
    return (
        layer_out.reshape(seqs, half_len, D),
        input_grad,
        grad_norm,
        weights_new,
        weight_first_new,
        weight_second_new,
        vectors_new,
        vector_first_new,
        vector_second_new,
        weights_low,
        vectors_new.astype(bf16),
    )


def solution(mesh):
    token = P("dp", "seq", None)
    by_row = P("dp", None)
    by_column = P(None, "dp")
    position = P("dp", "seq")
    in_specs = (
        (token,) + (position,) * 3 + (by_row, by_column, by_row, by_row, by_column, by_column, token)
    )
    out_specs = (token, token, P()) + (by_row,) * 3 + (by_column,) * 3 + (by_row, by_column)
    return jax.shard_map(
        functools.partial(shards, mesh.shape["dp"]),
        mesh=mesh,
        in_specs=in_specs,
        out_specs=out_specs,
        check_vma=False,
    )
```

```python
import functools

import jax
import jax.numpy as jnp
from jax import lax
from jax.experimental import pallas as pl
from jax.experimental.pallas import tpu as pltpu
from jax.sharding import PartitionSpec as P

D = 768
HEAD_DIM = 64
FF = 3072
STEP = 10
CHUNK = 96
OWN = D // 2
UNITS = FF // 2

ln_eps = 1e-12
beta_one = 0.9
beta_two = 0.999
adam_eps = 1e-08
learn_rate = 0.05
vector_rate = 0.3
decay_rate = 0.01

bf16 = jnp.bfloat16
f32 = jnp.float32
SWAP = [(0, 1), (1, 0)]


def params(limit=14):
    return pltpu.CompilerParams(vmem_limit_bytes=limit * 2**20)


def cost(micros):
    return pl.CostEstimate(flops=int(micros), bytes_accessed=0, transcendentals=0)


def dot(left, right, over):
    return lax.dot_general(left, right, (over, ((), ())), preferred_element_type=f32)


NT = ((1,), (1,))
NN = ((1,), (0,))
TN = ((0,), (0,))


def swap(value):
    return lax.ppermute(value, "seq", SWAP)


def pack(rows, index):
    core = lax.axis_index("seq")
    chunks = rows.shape[0] // (2 * CHUNK)
    plain = lax.dynamic_index_in_dim(rows.reshape(chunks, 2, CHUNK, D), core, 1, keepdims=False)
    columns = lax.dynamic_slice_in_dim(rows, core * OWN, OWN, axis=1).reshape(chunks, 2, CHUNK, OWN)
    wide = jnp.concatenate([columns[:, 0], columns[:, 1]], axis=-1)
    where = index * chunks + jnp.arange(chunks)
    is_out = ((where >= 12) & (where < 16))[:, None, None]
    return jnp.where(is_out, wide, plain).reshape(chunks * CHUNK, D)


def unpack(mine, theirs, index):
    core = lax.axis_index("seq")
    chunks = mine.shape[0] // CHUNK
    first = jnp.where(core == 0, mine, theirs).reshape(chunks, CHUNK, D)
    second = jnp.where(core == 0, theirs, mine).reshape(chunks, CHUNK, D)
    plain = jnp.stack([first, second], axis=1)
    upper = jnp.concatenate([first[..., :OWN], second[..., :OWN]], axis=-1)
    lower = jnp.concatenate([first[..., OWN:], second[..., OWN:]], axis=-1)
    wide = jnp.stack([upper, lower], axis=1)
    where = index * chunks + jnp.arange(chunks)
    is_out = ((where >= 12) & (where < 16))[:, None, None, None]
    return jnp.where(is_out, wide, plain).reshape(chunks * 2 * CHUNK, D)


SIDE_X = [(i, i ^ 1) for i in range(16)]
SIDE_Y = [(i, i ^ 2) for i in range(16)]


def up(first, last):
    return [(i, i + 4) for i in range(16) if first <= i // 4 <= last]


def down(first, last):
    return [(i, i - 4) for i in range(16) if first <= i // 4 <= last]


def send(value, pairs):
    return lax.ppermute(value, "dp", pairs)


def pick(plane, *options):
    result = options[-1]
    for i in range(len(options) - 2, -1, -1):
        result = jnp.where(plane == i, options[i], result)
    return result


def barrier(*values):
    return lax.optimization_barrier(values)


HALF = 3 * CHUNK // 2


def top(block):
    return block[:HALF]


def bottom(block):
    return block[HALF:]


def join(first, second):
    return jnp.concatenate([first, second], axis=0)


def add_both_kernel(a_ref, b_ref, c_ref, d_ref, e_ref, first_ref, second_ref):
    total = a_ref[...].astype(f32) + b_ref[...].astype(f32) + c_ref[...].astype(f32)
    first_ref[...] = total.astype(bf16)
    second_ref[...] = (d_ref[...].astype(f32) + e_ref[...].astype(f32)).astype(bf16)


def add_both(*blocks):
    return pl.pallas_call(
        add_both_kernel,
        out_shape=[jax.ShapeDtypeStruct((3 * CHUNK, D), bf16)] * 2,
        compiler_params=params(),
        cost_estimate=cost(1),
        name="add_both",
    )(*blocks)


def planes(step, *targets):
    pairs = [(i, i ^ (4 * step)) for i in range(16)]
    return [pair for pair in pairs if not targets or pair[1] // 4 in targets]


PIECES = ((0, 1, 2, 3), (1, 0, 3, 2), (2, 2, 0, 0), (3, 3, 1, 1))


def gather_steps(block, slots):
    odd = lax.axis_index("dp") // 4 % 2 == 1
    x0, y0 = send(block, SIDE_X), send(block, SIDE_Y)
    s1, far = send(block, planes(1)), send(block, planes(2))
    c0 = send(top(x0), SIDE_Y), send(bottom(y0), SIDE_X)
    x0, y0, s1, far, *c0 = yield x0, y0, s1, far, *c0

    x1, y1 = send(s1, SIDE_X), send(s1, SIDE_Y)
    opposite = send(far, planes(1))
    x1, y1, opposite = yield x1, y1, opposite
    slots.append(((block, 0), (x0, 0), (y0, 0), tuple(c0)))

    s2 = jnp.where(odd, opposite, far)
    s3 = jnp.where(odd, far, opposite)
    x2, y2 = send(s2, SIDE_X), send(s2, SIDE_Y)
    c1 = send(top(x1), SIDE_Y), send(bottom(y1), SIDE_X)
    x2, y2, *c1 = yield x2, y2, *c1
    slots.append(((s1, 0), (x1, 0), (y1, 0), tuple(c1)))

    c2 = send(top(x2), SIDE_Y), send(bottom(y2), SIDE_X)
    c2 = yield c2
    slots.append(((s2, 0), (x2, 0), (y2, 0), tuple(c2)))

    x3, y3 = send(s3, SIDE_X), send(s3, SIDE_Y)
    x3, y3 = yield x3, y3
    c3 = send(top(x3), SIDE_Y), send(bottom(y3), SIDE_X)
    slots.append(((s3, 0), (x3, 0), (y3, 0), None))
    c3 = yield c3
    slots[3] = (*slots[3][:3], tuple(c3))


def reduce_steps(grads, plane, result):
    odd = plane % 2 == 1
    got = yield cross(grads[3])
    x, y = yield across(grads[3], got)
    own3 = plus(grads[3][0], x, y)
    got = yield cross(grads[2])
    x, y = yield across(grads[2], got)
    own2 = plus(grads[2][0], x, y)
    got = yield cross(grads[1])
    high = send(jnp.where(odd, own2, own3), planes(1))
    x, y, high = yield *across(grads[1], got), high
    own1 = plus(grads[1][0], x, y)
    high = plus(jnp.where(odd, own3, own2), high)
    yield ()
    got = yield cross(grads[0])
    x, y, one = yield *across(grads[0], got), send(own1, up(0, 0) + down(3, 3))
    own0, own1 = add_both(grads[0][0], x, y, own1, one)
    zero, one, two = yield (
        send(own0, down(1, 1) + down(3, 3)),
        send(own1, down(2, 2)),
        send(high, planes(2, 2)),
    )
    own0 = plus(own0, zero)
    zero, three = yield send(own0, planes(2, 0)), send(high, planes(2, 3))
    result.append(pick(plane, plus(own0, zero), plus(own1, one), plus(high, two), plus(high, three)))


class Steps:
    def __init__(self, steps):
        self.steps = steps
        self.arrays = next(steps) if steps else ()

    def __call__(self, *values):
        count = len(self.arrays)
        passed = barrier(*self.arrays, *values) if count or values else ()
        if self.steps:
            try:
                self.arrays = self.steps.send(passed[:count])
            except StopIteration:
                self.steps, self.arrays = None, ()
        return passed[count:]


def parts_of(side):
    if side is None:
        return []
    first, second = side
    if isinstance(second, int):
        rows = 3 * CHUNK
        return [(first, second * rows, rows, 0)]
    return [(first, 0, HALF, 0), (second, 0, HALF, HALF)]


def slot_arrays(slots):
    arrays, known = [], {}
    shape = []
    for slot in slots:
        sides = []
        for side in slot:
            parts = []
            for array, start, rows, place in parts_of(side):
                if id(array) not in known:
                    known[id(array)] = len(arrays)
                    arrays.append(array)
                parts.append((known[id(array)], start, rows, place))
            sides.append(tuple(parts))
        shape.append(tuple(sides))
    return arrays, tuple(shape)


def run_copies(pairs, sems):
    copies = [
        pltpu.make_async_copy(source, target, sems.at[i])
        for i, (source, target) in enumerate(pairs)
    ]
    for copy in copies:
        copy.start()
    for copy in copies:
        copy.wait()


def place_heads_kernel(shape, me_ref, *refs):
    mine_ref, give_ref, whole_ref, sems = refs[-4:]
    spot, core, plane = me_ref[0], me_ref[1], me_ref[2]
    for z in range(4):

        @pl.when(plane == z)
        def _():
            pairs = []
            for side in range(4):
                start = 3 * CHUNK * (side + spot - 2 * (side & spot))
                for number, first, rows, place in shape[min(z, 2)][side]:
                    where = pl.ds(pl.multiple_of(start + place, 16), rows)
                    pairs.append((refs[number].at[pl.ds(first, rows)], whole_ref.at[where]))
            run_copies(pairs, sems)

    for ref, who in ((mine_ref, core), (give_ref, 1 - core)):
        for j in range(6):
            chunk = 4 * (j // 2) + 2 * who + j % 2
            ref[j] = whole_ref[pl.ds(pl.multiple_of(chunk * CHUNK, 16), CHUNK)]


def place_heads(me, slots):
    arrays, shape = slot_arrays(slots)
    half = jax.ShapeDtypeStruct((6, CHUNK, D), bf16)
    return pl.pallas_call(
        functools.partial(place_heads_kernel, shape),
        in_specs=[pl.BlockSpec(memory_space=pltpu.SMEM)]
        + [pl.BlockSpec(memory_space=pl.ANY)] * len(arrays),
        out_shape=[half, half],
        scratch_shapes=[pltpu.VMEM((12 * CHUNK, D), bf16), pltpu.SemaphoreType.DMA((8,))],
        compiler_params=params(),
        cost_estimate=cost(1),
        name="place_heads",
    )(me, *arrays)


def place_rest_kernel(shape, held, me_ref, *refs):
    out_ref, in_ref, down_ref, stage_ref, load_sems, store_sems = refs[-6:]
    spot, plane = me_ref[0], me_ref[2]

    def part(pairs, source, first, rows, row):
        while rows:
            if row < 4 * CHUNK:
                chunk, offset = divmod(row, CHUNK)
                count = min(rows, CHUNK - offset)
                targets = []
                for h in range(2):
                    target = 2 * CHUNK * chunk + CHUNK * h + offset
                    targets.append((pl.ds(OWN * h, OWN), out_ref.at[pl.ds(target, count)]))
            else:
                ref, start = (in_ref, 4 * CHUNK) if row < 20 * CHUNK else (down_ref, 20 * CHUNK)
                count = min(rows, start + 16 * CHUNK - row)
                targets = [(slice(None), ref.at[pl.ds(row - start, count)])]
            pairs.append((source.at[pl.ds(first, count)], count, targets))
            row, first, rows = row + count, first + count, rows - count

    for z in range(4):
        for s in range(4):
            pairs = []
            for slot, (number, sides) in zip(shape, held, strict=True):
                piece = PIECES[number][z]
                for side in sides if piece else ():
                    base = 3 * CHUNK * (4 * (piece - 1) + (side ^ s))
                    for array, first, rows, place in slot[side]:
                        part(pairs, refs[array], first, rows, base + place)

            @pl.when((plane == z) & (spot == s))
            def _():
                loads, stores, row = [], [], 0
                for i, (source, count, targets) in enumerate(pairs):
                    spot_rows = pl.ds(row, count)
                    loads.append(
                        pltpu.make_async_copy(source, stage_ref.at[spot_rows], load_sems.at[i])
                    )
                    stores.append([])
                    for columns, target in targets:
                        stores[-1].append(
                            pltpu.make_async_copy(
                                stage_ref.at[spot_rows, columns],
                                target,
                                store_sems.at[2 * i + len(stores[-1])],
                            )
                        )
                    row += count
                for load in loads:
                    load.start()
                for load, store in zip(loads, stores, strict=True):
                    load.wait()
                    for copy in store:
                        copy.start()
                for store in stores:
                    for copy in store:
                        copy.wait()


def place_rest(me, slots, held, state):
    arrays, shape = slot_arrays(
        [[slots[i][side] if side in sides else None for side in range(4)] for i, sides in held]
    )
    units = jax.ShapeDtypeStruct((UNITS, D), bf16)
    anywhere = pl.BlockSpec(memory_space=pl.ANY)
    return pl.pallas_call(
        functools.partial(place_rest_kernel, shape, held),
        in_specs=[pl.BlockSpec(memory_space=pltpu.SMEM)] + [anywhere] * (len(arrays) + len(state)),
        out_specs=[anywhere] * 3,
        out_shape=[jax.ShapeDtypeStruct((D, OWN), bf16), units, units],
        input_output_aliases={1 + len(arrays) + i: i for i in range(len(state))},
        scratch_shapes=[
            pltpu.VMEM((24 * CHUNK, D), bf16),
            pltpu.SemaphoreType.DMA((32,)),
            pltpu.SemaphoreType.DMA((64,)),
        ],
        compiler_params=params(),
        cost_estimate=cost(1),
        name="place_rest",
    )(me, *arrays, *state)


def plus(*values):
    total = values[0].astype(f32)
    for value in values[1:]:
        total = total + value.astype(f32)
    return total.astype(bf16)


def cross(sides):
    return send(sides[3], SIDE_Y), send(sides[4], SIDE_X)


def merge_kernel(x_ref, y_ref, upper_ref, lower_ref, x_out, y_out):
    x_out[:HALF] = (x_ref[:HALF].astype(f32) + upper_ref[...].astype(f32)).astype(bf16)
    x_out[HALF:] = x_ref[HALF:]
    y_out[:HALF] = y_ref[:HALF]
    y_out[HALF:] = (y_ref[HALF:].astype(f32) + lower_ref[...].astype(f32)).astype(bf16)


def across(sides, crossed):
    over_x, over_y = pl.pallas_call(
        merge_kernel,
        out_shape=[jax.ShapeDtypeStruct((3 * CHUNK, D), bf16)] * 2,
        compiler_params=params(),
        cost_estimate=cost(1),
        name="merge",
    )(sides[1], sides[2], *crossed)
    return send(over_x, SIDE_X), send(over_y, SIDE_Y)


def gather_vectors(low_vectors, ranks):
    count, width = low_vectors.shape
    block = jnp.pad(low_vectors, ((0, 16 - count), (0, 128 - width)))
    blocks = lax.all_to_all(jnp.broadcast_to(block, (ranks, 16, 128)), "dp", 0, 0, tiled=True)
    return blocks[:, :count, :width].transpose(1, 0, 2).reshape(count, ranks * width).astype(f32)


def vector_blocks(rows, ranks):
    blocks = rows.reshape(16, ranks, D // ranks).transpose(1, 0, 2)
    return jnp.pad(blocks, ((0, 0), (0, 0), (0, 128 - D // ranks)))


def selection(span, kind, source, half_len):
    chosen = span == 1
    masked = chosen & (kind < 8)
    swapped = chosen & (kind == 8)
    here = lax.broadcasted_iota(jnp.int32, (1, half_len), 1)
    origin = jnp.where(masked, -1, jnp.where(swapped, source, here))
    rows = lax.broadcasted_iota(jnp.int32, (half_len, half_len), 0)
    one_hot = (rows == origin).astype(f32).astype(bf16)
    first = lax.broadcasted_iota(jnp.int32, (16, half_len), 0) == 0
    mask_rows = jnp.where(first & masked, 1.0, 0.0).astype(bf16)
    return one_hot, mask_rows


def corrupt_kernel(span_ref, kind_ref, from_ref, hidden_ref, mask_ref, out_ref):
    seqs, half_len = span_ref.shape
    for s in range(seqs):
        rows = slice(s, s + 1)
        one_hot, mask_rows = selection(
            span_ref[rows, :], kind_ref[rows, :], from_ref[rows, :], half_len
        )
        picked = dot(one_hot, hidden_ref[s], TN) + dot(mask_rows, mask_ref[...], TN)
        out_ref[s] = picked.astype(bf16)


def corrupt(span, kind, source, hidden, mask_row):
    mask = jnp.broadcast_to(mask_row.astype(bf16)[None], (16, D))
    return pl.pallas_call(
        corrupt_kernel,
        out_shape=jax.ShapeDtypeStruct(hidden.shape, bf16),
        compiler_params=params(),
        name="corrupt",
    )(span, kind, source, hidden, mask)


def corrupt_back_kernel(
    span_ref, kind_ref, from_ref, grad_ref, own_ref, partial_ref, out_ref, mask_ref
):
    seqs, half_len = span_ref.shape
    mask_sum = jnp.zeros((16, D), f32)
    for s in range(seqs):
        rows = slice(s, s + 1)
        block = pl.ds(s * half_len, half_len)
        one_hot, mask_rows = selection(
            span_ref[rows, :], kind_ref[rows, :], from_ref[rows, :], half_len
        )
        grad = grad_ref[block] + own_ref[block] + partial_ref[block].astype(f32)
        high = grad.astype(bf16)
        low = (grad - high.astype(f32)).astype(bf16)
        out_ref[s] = dot(one_hot, high, NN) + dot(one_hot, low, NN)
        mask_sum = mask_sum + dot(mask_rows, high, NN) + dot(mask_rows, low, NN)
    mask_ref[...] = mask_sum


def corrupt_back(span, kind, source, grad, own, partial):
    seqs, half_len = span.shape
    return pl.pallas_call(
        corrupt_back_kernel,
        out_shape=[
            jax.ShapeDtypeStruct((seqs, half_len, D), f32),
            jax.ShapeDtypeStruct((16, D), f32),
        ],
        compiler_params=params(),
        cost_estimate=cost(1),
        name="corrupt_back",
    )(span, kind, source, grad, own, partial)


def attend_kernel(
    me_ref, own_ref, other_ref, mine_ref, theirs_ref, vals_ref, w_ref, qkv_ref, low_ref, wide_ref, lse_ref
):
    half_len = own_ref.shape[1]
    core = me_ref[1]

    @pl.when(pl.program_id(0) == 0)
    def _():
        for j in range(6):
            for ref, which in ((mine_ref, core), (theirs_ref, 1 - core)):
                where = pl.ds(pl.multiple_of((2 * j + which) * CHUNK, 16), CHUNK)
                w_ref[where] = ref[j]

    rows = jnp.concatenate([own_ref[0], other_ref[0]], axis=0)
    columns = pl.ds(pl.multiple_of(core * OWN, 128), OWN)
    bias = jnp.concatenate(
        [vals_ref[0:1, columns], jnp.zeros((1, OWN), f32), vals_ref[1:2, columns]], axis=-1
    )
    projected = (dot(rows, w_ref[...], NT) + bias).astype(bf16)
    qkv_ref[:, 0] = projected.reshape(2, half_len, 3 * OWN)
    wide, totals = [], []

    def score(h):
        columns = slice(h * HEAD_DIM, (h + 1) * HEAD_DIM)
        query = projected[:, :OWN][:, columns] * bf16(HEAD_DIM**-0.5)
        return dot(query, projected[:, OWN : 2 * OWN][:, columns], NT)

    heads = OWN // HEAD_DIM
    ahead = [score(0), score(1)]
    for h in range(heads):
        if h + 2 < heads:
            ahead.append(score(h + 2))
        scores = ahead.pop(0)
        value = projected[:, 2 * OWN :][:, h * HEAD_DIM : (h + 1) * HEAD_DIM]
        highest = jnp.max(scores, axis=-1, keepdims=True)
        exponents = jnp.exp(scores - highest)
        total = jnp.sum(exponents, axis=-1, keepdims=True)
        probabilities = (exponents * (1.0 / total)).astype(bf16)
        wide.append(dot(probabilities, value, NN))
        totals.append(highest + jnp.log(total))
    attended = jnp.concatenate(wide, axis=-1)
    wide_ref[:, 0] = attended.reshape(2, half_len, OWN)
    low_ref[:, 0] = attended.astype(bf16).reshape(2, half_len, OWN)
    fill = jnp.zeros((2 * half_len, 128 - len(totals)), f32)
    lse_ref[0] = jnp.concatenate(totals + [fill], axis=-1).T[:8]


def whole(*shape):
    return pl.BlockSpec(shape, lambda *_: (0,) * len(shape))


def attend(me, u_own, u_other, mine, theirs, vals):
    seqs, half_len, _ = u_own.shape
    block = lambda width: pl.BlockSpec((2, 1, half_len, width), lambda s: (0, s, 0, 0))
    token = pl.BlockSpec((1, half_len, D), lambda s: (s, 0, 0))
    return pl.pallas_call(
        attend_kernel,
        grid=(seqs,),
        in_specs=[
            pl.BlockSpec(memory_space=pltpu.SMEM),
            token,
            token,
            whole(6, CHUNK, D),
            whole(6, CHUNK, D),
            whole(*vals.shape),
        ],
        out_specs=[
            whole(3 * OWN, D),
            block(3 * OWN),
            block(OWN),
            block(OWN),
            pl.BlockSpec((1, 8, 2 * half_len), lambda s: (s, 0, 0)),
        ],
        out_shape=[
            jax.ShapeDtypeStruct((3 * OWN, D), bf16),
            jax.ShapeDtypeStruct((2, seqs, half_len, 3 * OWN), bf16),
            jax.ShapeDtypeStruct((2, seqs, half_len, OWN), bf16),
            jax.ShapeDtypeStruct((2, seqs, half_len, OWN), f32),
            jax.ShapeDtypeStruct((seqs, 8, 2 * half_len), f32),
        ],
        cost_estimate=cost(3),
        compiler_params=params(),
        name="attend",
    )(me, u_own, u_other, mine, theirs, vals)


def attend_back_kernel(
    skip, qkv_ref, own_ref, other_ref, wo_ref, wide_ref, lse_ref, *refs
):
    out_ref, sums_ref = refs[skip:]
    half_len = qkv_ref.shape[2]
    length = 2 * half_len
    projected = qkv_ref[:, 0].reshape(length, 3 * OWN)
    rows = jnp.concatenate([own_ref[0], other_ref[0]], axis=0)
    grad = dot(rows, wo_ref[...], NN).astype(bf16)
    product = grad.astype(f32) * wide_ref[:, 0].reshape(length, OWN)
    heads = OWN // HEAD_DIM
    deltas = [
        jnp.sum(product[:, h * HEAD_DIM : (h + 1) * HEAD_DIM], axis=-1, keepdims=True)
        for h in range(heads)
    ]
    fill = jnp.zeros((length, 128 - heads), f32)
    delta_rows = jnp.concatenate(deltas + [fill], axis=-1).T
    parts = [[], [], []]

    def head(h):
        columns = slice(h * HEAD_DIM, (h + 1) * HEAD_DIM)
        query = projected[:, :OWN][:, columns] * bf16(HEAD_DIM**-0.5)
        key = projected[:, OWN : 2 * OWN][:, columns]
        value = projected[:, 2 * OWN :][:, columns]
        return query, key, value, grad[:, columns]

    def products(h):
        query, key, value, grad_head = head(h)
        return dot(key, query, NT), dot(value, grad_head, NT)

    ahead = [products(0)]
    for h in range(heads):
        if h + 1 < heads:
            ahead.append(products(h + 1))
        scores, grad_weights = ahead.pop(0)
        query, key, value, grad_head = head(h)
        weights = jnp.exp(scores - lse_ref[0, h : h + 1, :])
        grad_scores = (weights * (grad_weights - delta_rows[h : h + 1, :])).astype(bf16)
        parts[0].append(dot(grad_scores, key, TN) * HEAD_DIM**-0.5)
        parts[1].append(dot(grad_scores, query, NN))
        parts[2].append(dot(weights.astype(bf16), grad_head, NN))
    result = jnp.concatenate(parts[0] + parts[1] + parts[2], axis=-1).astype(bf16)
    out_ref[:, 0] = result.reshape(2, half_len, 3 * OWN)
    sums = jnp.sum(result.astype(f32), axis=0, keepdims=True)

    @pl.when(pl.program_id(0) == 0)
    def _():
        sums_ref[...] = refs[1][...] if skip else jnp.zeros_like(sums_ref)

    sums_ref[...] += sums


def attend_back(qkv, own, other, wo_own, wide, lse, first, count, state):
    _, seqs, half_len, _ = qkv.shape
    block = lambda width: pl.BlockSpec((2, 1, half_len, width), lambda s: (0, s + first, 0, 0))
    token = pl.BlockSpec((1, half_len, D), lambda s: (s + first, 0, 0))
    return pl.pallas_call(
        functools.partial(attend_back_kernel, len(state)),
        grid=(count,),
        in_specs=[
            block(3 * OWN),
            token,
            token,
            whole(D, OWN),
            block(OWN),
            pl.BlockSpec((1, 8, 2 * half_len), lambda s: (s + first, 0, 0)),
        ]
        + ([pl.BlockSpec(memory_space=pl.ANY), whole(1, 3 * OWN)] if state else []),
        out_specs=[block(3 * OWN), whole(1, 3 * OWN)],
        input_output_aliases={6: 0} if state else {},
        out_shape=[
            jax.ShapeDtypeStruct((2, seqs, half_len, 3 * OWN), bf16),
            jax.ShapeDtypeStruct((1, 3 * OWN), f32),
        ],
        cost_estimate=cost(2 * count),
        compiler_params=params(),
        name="attend_back",
    )(qkv, own, other, wo_own, wide, lse, *state)


def norm(values):
    center = values - jnp.mean(values, axis=-1, keepdims=True)
    inv_std = lax.rsqrt(jnp.mean(center * center, axis=-1, keepdims=True) + ln_eps)
    return center * inv_std, inv_std


def norm_backward(upstream, normed, inv_std, gain):
    scaled = upstream * gain
    return inv_std * (
        scaled
        - jnp.mean(scaled, axis=-1, keepdims=True)
        - normed * jnp.mean(scaled * normed, axis=-1, keepdims=True)
    )


def row(ref, i):
    return ref[i : i + 1, :]


def branch_kernel(own_ref, other_ref, u_ref, wo_ref, wo_other_ref, vals_ref, normed_ref, inv_ref, low_ref):
    branch = dot(own_ref[0, 0], wo_ref[...], NT) + dot(other_ref[0], wo_other_ref[...], NT)
    normed, inv = norm(u_ref[0].astype(f32) + branch + row(vals_ref, 2))
    normed_ref[...] = normed
    inv_ref[...] = jnp.broadcast_to(inv, inv_ref.shape)
    low_ref[...] = (normed * row(vals_ref, 3) + row(vals_ref, 4)).astype(bf16)


def attention_branch(attended, from_other, u_own, wo_own, wo_other, vals):
    seqs, half_len, _ = u_own.shape
    rows = pl.BlockSpec((half_len, D), lambda s: (s, 0))
    return pl.pallas_call(
        branch_kernel,
        grid=(seqs,),
        in_specs=[
            pl.BlockSpec((1, 1, half_len, OWN), lambda s: (0, s, 0, 0)),
            pl.BlockSpec((1, half_len, OWN), lambda s: (s, 0, 0)),
            pl.BlockSpec((1, half_len, D), lambda s: (s, 0, 0)),
            whole(D, OWN),
            whole(D, OWN),
            whole(*vals.shape),
        ],
        out_specs=[rows, pl.BlockSpec((half_len, 128), lambda s: (s, 0)), rows],
        out_shape=[
            jax.ShapeDtypeStruct((seqs * half_len, D), f32),
            jax.ShapeDtypeStruct((seqs * half_len, 128), f32),
            jax.ShapeDtypeStruct((seqs * half_len, D), bf16),
        ],
        cost_estimate=cost(1),
        compiler_params=params(),
        name="attention_branch",
    )(attended, from_other, u_own, wo_own, wo_other, vals)


def hidden_kernel(own_ref, other_ref, w_ref, bias_ref, gelu_ref, slope_ref):
    tile = own_ref.shape[0] // 3
    jobs = [
        (half, ref, slice(i * tile, (i + 1) * tile))
        for half, ref in enumerate((own_ref, other_ref))
        for i in range(3)
    ]

    def project(job):
        _, ref, rows = jobs[job]
        return dot(ref[rows], w_ref[...], NT) + bias_ref[...]

    ahead = project(0)
    for i, (half, _, rows) in enumerate(jobs):
        points = ahead
        if i + 1 < len(jobs):
            ahead = project(i + 1)
        below = 0.5 * (1.0 + lax.erf(points * 2**-0.5))
        density = jnp.exp(-0.5 * points * points) * 0.3989422804014327
        gelu_ref[half, rows] = (points * below).astype(bf16)
        slope_ref[half, rows] = (below + points * density).astype(bf16)


def hidden_units(h_own, h_other, w_in, bias):
    rows = h_own.shape[0]
    width = 384
    block = pl.BlockSpec((2, rows, width), lambda i: (0, 0, i))
    return pl.pallas_call(
        hidden_kernel,
        grid=(UNITS // width,),
        in_specs=[
            whole(rows, D),
            whole(rows, D),
            pl.BlockSpec((width, D), lambda i: (i, 0)),
            pl.BlockSpec((1, width), lambda i: (0, i)),
        ],
        out_specs=[block, block],
        out_shape=[jax.ShapeDtypeStruct((2, rows, UNITS), bf16)] * 2,
        cost_estimate=cost(3),
        compiler_params=params(),
        name="hidden_units",
    )(h_own, h_other, w_in, bias)


def rows_kernel(left_ref, right_ref, out_ref):
    out_ref[...] = dot(left_ref[0], right_ref[...], NN).astype(out_ref.dtype)


def rows_times(left, half, right, dtype, name):
    _, rows, depth = left.shape
    tile = rows // 3
    return pl.pallas_call(
        rows_kernel,
        grid=(3,),
        in_specs=[pl.BlockSpec((1, tile, depth), lambda i: (half, i, 0)), whole(*right.shape)],
        out_specs=pl.BlockSpec((tile, D), lambda i: (i, 0)),
        out_shape=jax.ShapeDtypeStruct((rows, D), dtype),
        cost_estimate=cost(1),
        compiler_params=params(),
        name=name,
    )(left, right)


def add_sums(sums_ref, *values):
    @pl.when(pl.program_id(0) == 0)
    def _():
        sums_ref[...] = jnp.zeros_like(sums_ref)

    for i, value in enumerate(values):
        sums_ref[i : i + 1, :] += jnp.sum(value, axis=0, keepdims=True)


def finish_kernel(own_ref, other_ref, normed_ref, grad_ref, vals_ref, out_ref, wide_ref, low_ref, sums_ref):
    hidden_one = normed_ref[...] * row(vals_ref, 3) + row(vals_ref, 4)
    feed = own_ref[...] + other_ref[...].astype(f32) + row(vals_ref, 5)
    normed, inv = norm(hidden_one + feed)
    out_ref[...] = normed * row(vals_ref, 6) + row(vals_ref, 7)
    grad = grad_ref[...].astype(f32)
    wide = norm_backward(grad, normed, inv, row(vals_ref, 6))
    low = wide.astype(bf16)
    wide_ref[...] = wide
    low_ref[...] = low
    add_sums(sums_ref, low.astype(f32), grad * normed, grad)


def finish(own, other, normed, grad, vals):
    rows = own.shape[0]
    tile = rows // 3
    block = pl.BlockSpec((tile, D), lambda i: (i, 0))
    return pl.pallas_call(
        finish_kernel,
        grid=(3,),
        in_specs=[block] * 4 + [whole(*vals.shape)],
        out_specs=[block] * 3 + [whole(8, D)],
        out_shape=[
            jax.ShapeDtypeStruct((rows, D), f32),
            jax.ShapeDtypeStruct((rows, D), f32),
            jax.ShapeDtypeStruct((rows, D), bf16),
            jax.ShapeDtypeStruct((8, D), f32),
        ],
        cost_estimate=cost(1),
        compiler_params=params(),
        name="finish",
    )(own, other, normed, grad, vals)


def norm_one_kernel(two_ref, own_ref, other_ref, normed_ref, inv_ref, vals_ref, wide_ref, low_ref, sums_ref):
    grad = two_ref[...] + own_ref[...] + other_ref[...].astype(f32)
    normed = normed_ref[...]
    wide = norm_backward(grad, normed, inv_ref[:, 0:1], row(vals_ref, 3))
    low = wide.astype(bf16)
    wide_ref[...] = wide
    low_ref[...] = low
    add_sums(sums_ref, low.astype(f32), grad * normed, grad)


def norm_one_back(two, own, other, normed, inv, vals):
    rows = own.shape[0]
    tile = rows // 3
    block = pl.BlockSpec((tile, D), lambda i: (i, 0))
    return pl.pallas_call(
        norm_one_kernel,
        grid=(3,),
        in_specs=[block] * 4 + [pl.BlockSpec((tile, 128), lambda i: (i, 0)), whole(*vals.shape)],
        out_specs=[block] * 2 + [whole(8, D)],
        out_shape=[
            jax.ShapeDtypeStruct((rows, D), f32),
            jax.ShapeDtypeStruct((rows, D), bf16),
            jax.ShapeDtypeStruct((8, D), f32),
        ],
        cost_estimate=cost(1),
        compiler_params=params(),
        name="norm_one_back",
    )(two, own, other, normed, inv, vals)


def slope_kernel(grad_ref, w_ref, slope_ref, out_ref, sums_ref):
    low = (dot(grad_ref[...], w_ref[...], NT) * slope_ref[0].astype(f32)).astype(bf16)
    out_ref[0] = low
    sums_ref[...] = jnp.sum(low.astype(f32), axis=0, keepdims=True)


def before_gelu(grad, w_down, slope, half):
    rows = grad.shape[0]
    width = 384
    return pl.pallas_call(
        slope_kernel,
        grid=(UNITS // width,),
        in_specs=[
            whole(rows, D),
            pl.BlockSpec((width, D), lambda i: (i, 0)),
            pl.BlockSpec((1, rows, width), lambda i: (half, 0, i)),
        ],
        out_specs=[
            pl.BlockSpec((1, rows, width), lambda i: (0, 0, i)),
            pl.BlockSpec((1, width), lambda i: (0, i)),
        ],
        out_shape=[
            jax.ShapeDtypeStruct((1, rows, UNITS), bf16),
            jax.ShapeDtypeStruct((1, UNITS), f32),
        ],
        cost_estimate=cost(1),
        compiler_params=params(),
        name="before_gelu",
    )(grad, w_down, slope)


def rows_of(count):
    return jax.ShapeDtypeStruct((count, D), bf16)


CROSS = ((0, 0, 288), (1, 0, 288), (2, 0, 288), (3, 0, 144), (3, 144, 144))


def side_rows(spot, side, first, rows):
    start = 3 * CHUNK * (side + spot - 2 * (side & spot)) + first
    return pl.ds(pl.multiple_of(start, 16), rows)


def write_sides(spot, piece_ref, outs):
    for out, (side, first, rows) in zip(outs, CROSS, strict=True):
        out[...] = piece_ref[side_rows(spot, side, first, rows)]


def rows_at(step):
    return pl.ds(pl.multiple_of(step * OWN, 16), OWN)


def two_halves(left, left_other, right, right_other):
    return dot(left, right, TN) + dot(left_other, right_other, TN)


def grads3_kernel(me_ref, g_ref, d_ref, d_other_ref, *refs):
    piece_ref = refs[-1]
    step = pl.program_id(0)
    piece_ref[rows_at(step)] = two_halves(
        g_ref[0], g_ref[1], d_ref[...], d_other_ref[...]
    ).astype(bf16)

    @pl.when(step == 2)
    def _():
        write_sides(me_ref[0], piece_ref, refs[:-1])


def grads2_kernel(me_ref, z_ref, z_other_ref, h_ref, h_other_ref, g_ref, d_ref, d_other_ref, *refs):
    piece_ref = refs[-1]
    step = pl.program_id(0)

    @pl.when(step < 2)
    def _():
        piece_ref[rows_at(step)] = two_halves(
            z_ref[0], z_other_ref[0], h_ref[...], h_other_ref[...]
        ).astype(bf16)

    @pl.when(step == 2)
    def _():
        piece_ref[rows_at(step)] = two_halves(
            g_ref[0], g_ref[1], d_ref[...], d_other_ref[...]
        ).astype(bf16)
        write_sides(me_ref[0], piece_ref, refs[:-1])


def grads1_kernel(me_ref, z_ref, z_other_ref, h_ref, h_other_ref, a_ref, a_other_ref, att_ref, *refs):
    piece_ref = refs[-1]
    step = pl.program_id(0)

    @pl.when(step < 2)
    def _():
        piece_ref[rows_at(step + 1)] = two_halves(
            z_ref[0], z_other_ref[0], h_ref[...], h_other_ref[...]
        ).astype(bf16)

    @pl.when(step == 2)
    def _():
        wo = two_halves(a_ref[...], a_other_ref[...], att_ref[0], att_ref[1]).astype(bf16)
        for j in range(4):
            upper = wo[2 * CHUNK * j : 2 * CHUNK * j + CHUNK]
            lower = wo[2 * CHUNK * j + CHUNK : 2 * CHUNK * (j + 1)]
            piece_ref[CHUNK * j : CHUNK * (j + 1)] = jnp.concatenate([upper, lower], axis=-1)
        write_sides(me_ref[0], piece_ref, refs[:-1])


def grads_call(kernel, specs, arrays, name):
    return pl.pallas_call(
        kernel,
        grid=(3,),
        in_specs=[pl.BlockSpec(memory_space=pltpu.SMEM)] + specs,
        out_specs=[whole(count, D) for _, _, count in CROSS],
        out_shape=[rows_of(count) for _, _, count in CROSS],
        scratch_shapes=[pltpu.VMEM((12 * CHUNK, D), bf16)],
        cost_estimate=cost(2),
        compiler_params=params(),
        name=name,
    )(*arrays)


def grads0_kernel(me_ref, g_ref, u_ref, u_other_ref, keep_ref, give_ref, piece_ref):
    core = me_ref[1]
    step = pl.program_id(0)
    piece_ref[rows_at(step)] = two_halves(
        g_ref[0], g_ref[1], u_ref[...], u_other_ref[...]
    ).astype(bf16)

    @pl.when(step == 2)
    def _():
        for j in range(6):
            for ref, which in ((keep_ref, core), (give_ref, 1 - core)):
                where = pl.ds(pl.multiple_of((2 * j + which) * CHUNK, 16), CHUNK)
                ref[j] = piece_ref[where]


def grads0(me, grad, u_own, u_other):
    rows = grad.shape[1]
    half = jax.ShapeDtypeStruct((6, CHUNK, D), bf16)
    return pl.pallas_call(
        grads0_kernel,
        grid=(3,),
        in_specs=[
            pl.BlockSpec(memory_space=pltpu.SMEM),
            pl.BlockSpec((2, rows, OWN), lambda i: (0, 0, i)),
            whole(rows, D),
            whole(rows, D),
        ],
        out_specs=[whole(6, CHUNK, D)] * 2,
        out_shape=[half, half],
        scratch_shapes=[pltpu.VMEM((12 * CHUNK, D), bf16)],
        cost_estimate=cost(2),
        compiler_params=params(),
        name="grads0",
    )(me, grad, u_own, u_other)


def regroup_kernel(me_ref, keep_ref, take_ref, *refs):
    piece_ref = refs[-1]
    core = me_ref[1]
    for ref, who in ((keep_ref, core), (take_ref, 1 - core)):
        for j in range(6):
            chunk = 4 * (j // 2) + 2 * who + j % 2
            piece_ref[pl.ds(pl.multiple_of(chunk * CHUNK, 16), CHUNK)] = ref[j]
    write_sides(me_ref[0], piece_ref, refs[:-1])


def regroup(me, keep, take):
    return pl.pallas_call(
        regroup_kernel,
        in_specs=[pl.BlockSpec(memory_space=pltpu.SMEM)]
        + [pl.BlockSpec(memory_space=pltpu.VMEM)] * 2,
        out_shape=[rows_of(count) for _, _, count in CROSS],
        scratch_shapes=[pltpu.VMEM((12 * CHUNK, D), bf16)],
        cost_estimate=cost(1),
        compiler_params=params(),
        name="regroup",
    )(me, keep, take)


def vector_kernel(me_ref, qkv_ref, one_ref, two_ref, mask_ref, bias_ref, out_ref):
    out_ref[...] = jnp.zeros_like(out_ref)
    columns = pl.ds(pl.multiple_of(me_ref[1] * OWN, 128), OWN)
    out_ref[0:1, columns] = qkv_ref[:, :OWN]
    out_ref[1:2, columns] = qkv_ref[:, 2 * OWN :]
    out_ref[2:5, :] = one_ref[0:3, :]
    out_ref[5:8, :] = two_ref[0:3, :]
    out_ref[8:9, :] = mask_ref[0:1, :]
    out_ref[9:13, :] = bias_ref[...]


def vector_rows(me, qkv_sums, one_sums, two_sums, mask_sums, bias_sums):
    return pl.pallas_call(
        vector_kernel,
        in_specs=[pl.BlockSpec(memory_space=pltpu.SMEM)]
        + [pl.BlockSpec(memory_space=pltpu.VMEM)] * 5,
        out_shape=jax.ShapeDtypeStruct((16, D), f32),
        cost_estimate=cost(1),
        name="vector_rows",
    )(me, qkv_sums, one_sums, two_sums, mask_sums, bias_sums)


def adam_step(master, first_old, second, gradient, decay_on, step_rate):
    first_new = beta_one * first_old + (1.0 - beta_one) * gradient
    second_new = beta_two * second + (1.0 - beta_two) * gradient * gradient
    fix_one = 1.0 / (1.0 - beta_one**STEP)
    fix_two = 1.0 / (1.0 - beta_two**STEP)
    update = first_new * fix_one / (jnp.sqrt(second_new * fix_two) + adam_eps)
    return (master - step_rate * (update + decay_on * master), first_new, second_new)


def update_kernel(sums_ref, grad_ref, *refs):
    norm_value = jnp.sqrt(jnp.sum(sums_ref[...], axis=0))[0:1, 0:1]
    clip = 1.0 / jnp.maximum(norm_value, 1.0)
    inputs, outs = refs[:7], refs[7:]
    master, first, second = (ref[...] for ref in inputs[:3])
    gradient = grad_ref[...].astype(f32) * clip
    master, first, second = adam_step(master, first, second, gradient, decay_rate, learn_rate)
    for ref, value in zip(outs[:4], (master, first, second, master.astype(bf16)), strict=True):
        ref[...] = value

    @pl.when(pl.program_id(0) == 0)
    def _():
        gradient, master, first, second = (ref[...] for ref in inputs[3:])
        values = adam_step(master, first, second, gradient * clip, 0.0, vector_rate)
        for ref, value in zip(outs[4:7], values, strict=True):
            ref[...] = value
        outs[7][...] = values[0].astype(bf16)
        outs[8][...] = norm_value


def update(sums, grad, weights, shard_v, vectors):
    rows = grad.shape[0]
    tile = 144 if rows % 144 == 0 else rows
    block = pl.BlockSpec((tile, D), lambda i: (i, 0))
    small = whole(*shard_v.shape)
    return pl.pallas_call(
        update_kernel,
        grid=(rows // tile,),
        in_specs=[whole(*sums.shape)] + [block] * 4 + [small] * 4,
        out_specs=[block] * 4 + [small] * 4 + [whole(1, 1)],
        out_shape=[jax.ShapeDtypeStruct((rows, D), f32)] * 3
        + [jax.ShapeDtypeStruct((rows, D), bf16)]
        + [jax.ShapeDtypeStruct(shard_v.shape, f32)] * 3
        + [jax.ShapeDtypeStruct(shard_v.shape, bf16), jax.ShapeDtypeStruct((1, 1), f32)],
        cost_estimate=cost(1),
        compiler_params=params(),
        name="update",
    )(sums, grad, *weights, shard_v, *vectors)


def shards(
    ranks,
    hidden,
    span_mask,
    replace_kind,
    replace_from,
    weights,
    vectors,
    weight_first,
    weight_second,
    vector_first,
    vector_second,
    cotangent,
):
    seqs, half_len, _ = hidden.shape
    rows = seqs * half_len
    index = lax.axis_index("dp")
    core = lax.axis_index("seq")
    staged = ranks == 16
    plane = index // 4
    spot = index % 4 if staged else jnp.zeros_like(index)
    me = jnp.stack([spot, core, plane]).astype(jnp.int32)
    low_weights = weights.astype(bf16)
    slots, grads, result = [], {}, []
    if staged:
        gather = Steps(gather_steps(pack(low_weights, index), slots))
    else:
        gather = Steps(None)
        stacked = pack(lax.all_gather(low_weights, "dp", axis=0, tiled=True), 0)

    gather()
    gather()
    vals = gather_vectors(vectors.astype(bf16), ranks)
    every, rest = (0, 1, 2, 3), ()
    if staged:
        rest = place_rest(me, slots, ((0, every),), ())
    vals, *rest = gather(vals, *rest)
    u_own = corrupt(span_mask, replace_kind, replace_from, hidden, vals[8])
    bias_in = lax.dynamic_index_in_dim(
        vals[9:].reshape(FF // (2 * CHUNK), 2, CHUNK), core, 1, keepdims=False
    ).reshape(1, UNITS)
    if staged:
        rest = place_rest(me, slots, ((1, every),), rest)
    u_own, vals, bias_in, *rest = gather(u_own, vals, bias_in, *rest)
    u_other = swap(u_own)

    if staged:
        mine, give = place_heads(me, slots)
    else:
        halves = stacked[: 12 * CHUNK].reshape(3, 2, 2, CHUNK, D)
        mine = lax.dynamic_index_in_dim(halves, core, 1, keepdims=False).reshape(6, CHUNK, D)
        give = lax.dynamic_index_in_dim(halves, 1 - core, 1, keepdims=False).reshape(6, CHUNK, D)
    w_qkv, qkv, attended, attended_wide, lse = attend(
        me, u_own, u_other, mine, swap(give), vals
    )
    w_qkv, qkv, attended, attended_wide, lse, *rest = gather(
        w_qkv, qkv, attended, attended_wide, lse, *rest
    )
    from_other = swap(attended[1])
    if staged:
        rest = place_rest(me, slots, ((2, every), (3, (0, 1, 2))), rest)
    attended, from_other, *rest = gather(attended, from_other, *rest)

    if staged:
        wo_own, w_in, w_down = place_rest(me, slots, ((3, (3,)),), rest)
    else:
        rest = stacked[12 * CHUNK :]
        wo_own = (
            rest[: 4 * CHUNK].reshape(4, CHUNK, 2, OWN).transpose(0, 2, 1, 3).reshape(D, OWN)
        )
        w_in, w_down = rest[4 * CHUNK : 20 * CHUNK], rest[20 * CHUNK :]
    normed_one, inv_one, h_own = attention_branch(
        attended, from_other, u_own, wo_own, swap(wo_own), vals
    )
    h_other = swap(h_own)
    gelu, slope = hidden_units(h_own, h_other, w_in, bias_in)
    feed_other = swap(rows_times(gelu, 1, w_down, bf16, "feed_other"))
    feed_own = rows_times(gelu, 0, w_down, f32, "feed_own")
    layer_out, grad_two, d_own, two_sums = finish(
        feed_own, feed_other, normed_one, cotangent.reshape(rows, D), vals
    )

    d_other = swap(d_own)
    z_own, z_sums = before_gelu(d_own, w_down, slope, 0)
    d_other, z_own, z_sums = barrier(d_other, z_own, z_sums)
    unit = lambda first: pl.BlockSpec((2, rows, OWN), lambda i: (0, 0, i + first))
    one_unit = lambda first: pl.BlockSpec((1, rows, OWN), lambda i: (0, 0, jnp.minimum(i, 1) + first))
    tokens = whole(rows, D)
    grads[3] = grads_call(
        grads3_kernel, [unit(1), tokens, tokens], (me, gelu, d_own, d_other), "grads3"
    )
    *grads[3], d_other = barrier(*grads[3], d_other)
    reduce = Steps(reduce_steps(grads, plane, result) if staged else None)
    z_other, z_other_sums = before_gelu(d_other, w_down, slope, 1)
    hidden_other = rows_times(z_other, 0, w_in, bf16, "hidden_other")
    z_other, z_other_sums, hidden_other, z_own = reduce(
        z_other, z_other_sums, hidden_other, z_own
    )
    sent_hidden = swap(hidden_other)
    hidden_own = rows_times(z_own, 0, w_in, f32, "hidden_own")
    grad_one, a_own, one_sums = norm_one_back(
        grad_two, hidden_own, sent_hidden, normed_one, inv_one, vals
    )
    first_unit = pl.BlockSpec((2, rows, OWN), lambda i: (0, 0, 0))
    grads[2] = grads_call(
        grads2_kernel,
        [one_unit(2), one_unit(2), tokens, tokens, first_unit, tokens, tokens],
        (me, z_own, z_other, h_own, h_other, gelu, d_own, d_other),
        "grads2",
    )
    *grads[2], grad_one, a_own, one_sums = reduce(*grads[2], grad_one, a_own, one_sums)
    a_other = swap(a_own)
    a_own, a_other, qkv = reduce(a_own, a_other, qkv)
    back = (
        a_own.reshape(seqs, half_len, D),
        a_other.reshape(seqs, half_len, D),
        wo_own,
        attended_wide,
        lse,
    )
    state = attend_back(qkv, *back, 0, 1, ())
    grads[1] = grads_call(
        grads1_kernel,
        [one_unit(0), one_unit(0), tokens, tokens, tokens, tokens, whole(2, rows, OWN)],
        (me, z_own, z_other, h_own, h_other, a_own, a_other, attended.reshape(2, rows, OWN)),
        "grads1",
    )
    *grads[1], a, b, qkv = reduce(*grads[1], *state, qkv)
    state = attend_back(qkv, *back, 1, 1, (a, b))
    a, b, qkv = reduce(*state, qkv)
    grad_qkv, qkv_sums = attend_back(qkv, *back, 2, seqs - 2, (a, b))
    grad_rows = grad_qkv.reshape(2, rows, 3 * OWN)
    keep, give = grads0(me, grad_rows, u_own.reshape(rows, D), u_other.reshape(rows, D))
    keep, give, grad_rows = reduce(keep, give, grad_rows)
    take = swap(give)
    inputs_other = rows_times(grad_rows, 1, w_qkv, bf16, "inputs_other")
    grads[0] = regroup(me, keep, take)
    *grads[0], grad_rows, inputs_other = reduce(*grads[0], grad_rows, inputs_other)
    sent_inputs = swap(inputs_other)
    inputs_own = rows_times(grad_rows, 0, w_qkv, f32, "inputs_own")
    sent_inputs, inputs_own, z_sums = reduce(sent_inputs, inputs_own, z_sums)
    input_grad, mask_sums = corrupt_back(
        span_mask, replace_kind, replace_from, grad_one, inputs_own, sent_inputs
    )
    bias_sums = jnp.zeros((FF // (2 * CHUNK), 2, CHUNK), f32)
    bias_sums = lax.dynamic_update_slice(
        bias_sums,
        (z_sums + z_other_sums).reshape(FF // (2 * CHUNK), 1, CHUNK),
        (0, core, 0),
    ).reshape(FF // D, D)
    vector_part = vector_rows(me, qkv_sums, one_sums, two_sums, mask_sums, bias_sums)
    input_grad, vector_part = reduce(input_grad, vector_part)
    blocks = vector_blocks(vector_part + swap(vector_part), ranks)
    (blocks,) = reduce(blocks)
    blocks = lax.all_to_all(blocks, "dp", 0, 0, tiled=True)
    (blocks,) = reduce(blocks)
    count, width = vectors.shape
    shard_v = jnp.sum(blocks, axis=0)[:count, :width]

    if staged:
        shard_half = result[0]
        shard_w = unpack(shard_half, swap(shard_half), index)
    else:
        core_rows = [block for i in range(4) for block in grads[i]]
        core_rows = jnp.concatenate(core_rows, axis=0)
        stacked = unpack(core_rows, swap(core_rows), 0).astype(f32)
        shard_w = lax.psum_scatter(stacked, "dp", scatter_dimension=0, tiled=True)
        shard_half = lax.dynamic_slice_in_dim(shard_w, core * OWN, OWN, axis=1)

    half32 = shard_half.astype(f32)
    squares = jnp.sum(half32 * half32) + 0.5 * jnp.sum(shard_v * shard_v)
    blocks = lax.all_to_all(
        jnp.full((2 * ranks, 8, 128), squares), ("dp", "seq"), 0, 0, tiled=True
    )
    (
        weights_new,
        weight_first_new,
        weight_second_new,
        weights_low,
        vectors_new,
        vector_first_new,
        vector_second_new,
        vectors_low,
        norm_value,
    ) = update(
        blocks,
        shard_w,
        (weights, weight_first, weight_second),
        shard_v,
        (vectors, vector_first, vector_second),
    )
    grad_norm = norm_value[0, 0]
    return (
        layer_out.reshape(seqs, half_len, D),
        input_grad,
        grad_norm,
        weights_new,
        weight_first_new,
        weight_second_new,
        vectors_new,
        vector_first_new,
        vector_second_new,
        weights_low,
        vectors_low,
    )


def solution(mesh):
    token = P("dp", "seq", None)
    by_row = P("dp", None)
    by_column = P(None, "dp")
    position = P("dp", "seq")
    in_specs = (
        (token,) + (position,) * 3 + (by_row, by_column, by_row, by_row, by_column, by_column, token)
    )
    out_specs = (token, token, P()) + (by_row,) * 3 + (by_column,) * 3 + (by_row, by_column)
    return jax.shard_map(
        functools.partial(shards, mesh.shape["dp"]),
        mesh=mesh,
        in_specs=in_specs,
        out_specs=out_specs,
        check_vma=False,
    )
```

```python
import functools

import jax
import jax.numpy as jnp
from jax import lax
from jax.experimental import pallas as pl
from jax.experimental.pallas import tpu as pltpu
from jax.sharding import PartitionSpec as P

D = 768
HEAD_DIM = 64
FF = 3072
STEP = 10
CHUNK = 96
OWN = D // 2
UNITS = FF // 2

ln_eps = 1e-12
beta_one = 0.9
beta_two = 0.999
adam_eps = 1e-08
learn_rate = 0.05
vector_rate = 0.3
decay_rate = 0.01

bf16 = jnp.bfloat16
f32 = jnp.float32
SWAP = [(0, 1), (1, 0)]


def params(limit=14):
    return pltpu.CompilerParams(vmem_limit_bytes=limit * 2**20)


def cost(micros):
    return pl.CostEstimate(flops=int(micros), bytes_accessed=0, transcendentals=0)


def dot(left, right, over):
    return lax.dot_general(left, right, (over, ((), ())), preferred_element_type=f32)


NT = ((1,), (1,))
NN = ((1,), (0,))
TN = ((0,), (0,))


def swap(value):
    return lax.ppermute(value, "seq", SWAP)


def pack(rows, index):
    core = lax.axis_index("seq")
    chunks = rows.shape[0] // (2 * CHUNK)
    plain = lax.dynamic_index_in_dim(rows.reshape(chunks, 2, CHUNK, D), core, 1, keepdims=False)
    columns = lax.dynamic_slice_in_dim(rows, core * OWN, OWN, axis=1).reshape(chunks, 2, CHUNK, OWN)
    wide = jnp.concatenate([columns[:, 0], columns[:, 1]], axis=-1)
    where = index * chunks + jnp.arange(chunks)
    is_out = ((where >= 12) & (where < 16))[:, None, None]
    return jnp.where(is_out, wide, plain).reshape(chunks * CHUNK, D)


def unpack(mine, theirs, index):
    core = lax.axis_index("seq")
    chunks = mine.shape[0] // CHUNK
    first = jnp.where(core == 0, mine, theirs).reshape(chunks, CHUNK, D)
    second = jnp.where(core == 0, theirs, mine).reshape(chunks, CHUNK, D)
    plain = jnp.stack([first, second], axis=1)
    upper = jnp.concatenate([first[..., :OWN], second[..., :OWN]], axis=-1)
    lower = jnp.concatenate([first[..., OWN:], second[..., OWN:]], axis=-1)
    wide = jnp.stack([upper, lower], axis=1)
    where = index * chunks + jnp.arange(chunks)
    is_out = ((where >= 12) & (where < 16))[:, None, None, None]
    return jnp.where(is_out, wide, plain).reshape(chunks * 2 * CHUNK, D)


SIDE_X = [(i, i ^ 1) for i in range(16)]
SIDE_Y = [(i, i ^ 2) for i in range(16)]


def up(first, last):
    return [(i, i + 4) for i in range(16) if first <= i // 4 <= last]


def down(first, last):
    return [(i, i - 4) for i in range(16) if first <= i // 4 <= last]


def send(value, pairs):
    return lax.ppermute(value, "dp", pairs)


def pick(plane, *options):
    result = options[-1]
    for i in range(len(options) - 2, -1, -1):
        result = jnp.where(plane == i, options[i], result)
    return result


def barrier(*values):
    return lax.optimization_barrier(values)


HALF = 3 * CHUNK // 2


def top(block):
    return block[:HALF]


def bottom(block):
    return block[HALF:]


def join(first, second):
    return jnp.concatenate([first, second], axis=0)


def add_both_kernel(a_ref, b_ref, c_ref, d_ref, e_ref, first_ref, second_ref):
    total = a_ref[...].astype(f32) + b_ref[...].astype(f32) + c_ref[...].astype(f32)
    first_ref[...] = total.astype(bf16)
    second_ref[...] = (d_ref[...].astype(f32) + e_ref[...].astype(f32)).astype(bf16)


def add_both(*blocks):
    return pl.pallas_call(
        add_both_kernel,
        out_shape=[jax.ShapeDtypeStruct((3 * CHUNK, D), bf16)] * 2,
        compiler_params=params(),
        cost_estimate=cost(1),
        name="add_both",
    )(*blocks)


def planes(step, *targets):
    pairs = [(i, i ^ (4 * step)) for i in range(16)]
    return [pair for pair in pairs if not targets or pair[1] // 4 in targets]


PIECES = ((0, 1, 2, 3), (1, 0, 3, 2), (2, 2, 0, 0), (3, 3, 1, 1))


def gather_steps(block, slots):
    odd = lax.axis_index("dp") // 4 % 2 == 1
    x0, y0 = send(block, SIDE_X), send(block, SIDE_Y)
    s1, far = send(block, planes(1)), send(block, planes(2))
    c0 = send(top(x0), SIDE_Y), send(bottom(y0), SIDE_X)
    x0, y0, s1, far, *c0 = yield x0, y0, s1, far, *c0

    x1, y1 = send(s1, SIDE_X), send(s1, SIDE_Y)
    opposite = send(far, planes(1))
    x1, y1, opposite = yield x1, y1, opposite
    slots.append(((block, 0), (x0, 0), (y0, 0), tuple(c0)))

    s2 = jnp.where(odd, opposite, far)
    s3 = jnp.where(odd, far, opposite)
    x2, y2 = send(s2, SIDE_X), send(s2, SIDE_Y)
    c1 = send(top(x1), SIDE_Y), send(bottom(y1), SIDE_X)
    x2, y2, *c1 = yield x2, y2, *c1
    slots.append(((s1, 0), (x1, 0), (y1, 0), tuple(c1)))

    c2 = send(top(x2), SIDE_Y), send(bottom(y2), SIDE_X)
    c2 = yield c2
    slots.append(((s2, 0), (x2, 0), (y2, 0), tuple(c2)))

    x3, y3 = send(s3, SIDE_X), send(s3, SIDE_Y)
    x3, y3 = yield x3, y3
    c3 = send(top(x3), SIDE_Y), send(bottom(y3), SIDE_X)
    slots.append(((s3, 0), (x3, 0), (y3, 0), None))
    c3 = yield c3
    slots[3] = (*slots[3][:3], tuple(c3))


def reduce_steps(grads, plane, result):
    odd = plane % 2 == 1
    got = yield cross(grads[3])
    x, y = yield across(grads[3], got)
    own3 = plus(grads[3][0], x, y)
    got = yield cross(grads[2])
    x, y = yield across(grads[2], got)
    own2 = plus(grads[2][0], x, y)
    got = yield cross(grads[1])
    high = send(jnp.where(odd, own2, own3), planes(1))
    x, y, high = yield *across(grads[1], got), high
    own1 = plus(grads[1][0], x, y)
    high = plus(jnp.where(odd, own3, own2), high)
    yield ()
    got = yield cross(grads[0])
    x, y, one = yield *across(grads[0], got), send(own1, up(0, 0) + down(3, 3))
    own0, own1 = add_both(grads[0][0], x, y, own1, one)
    zero, one, two = yield (
        send(own0, down(1, 1) + down(3, 3)),
        send(own1, down(2, 2)),
        send(high, planes(2, 2)),
    )
    own0 = plus(own0, zero)
    zero, three = yield send(own0, planes(2, 0)), send(high, planes(2, 3))
    result.append(pick(plane, plus(own0, zero), plus(own1, one), plus(high, two), plus(high, three)))


class Steps:
    def __init__(self, steps):
        self.steps = steps
        self.arrays = next(steps) if steps else ()

    def __call__(self, *values):
        count = len(self.arrays)
        passed = barrier(*self.arrays, *values) if count or values else ()
        if self.steps:
            try:
                self.arrays = self.steps.send(passed[:count])
            except StopIteration:
                self.steps, self.arrays = None, ()
        return passed[count:]


def parts_of(side):
    if side is None:
        return []
    first, second = side
    if isinstance(second, int):
        rows = 3 * CHUNK
        return [(first, second * rows, rows, 0)]
    return [(first, 0, HALF, 0), (second, 0, HALF, HALF)]


def slot_arrays(slots):
    arrays, known = [], {}
    shape = []
    for slot in slots:
        sides = []
        for side in slot:
            parts = []
            for array, start, rows, place in parts_of(side):
                if id(array) not in known:
                    known[id(array)] = len(arrays)
                    arrays.append(array)
                parts.append((known[id(array)], start, rows, place))
            sides.append(tuple(parts))
        shape.append(tuple(sides))
    return arrays, tuple(shape)


def run_copies(pairs, sems):
    copies = [
        pltpu.make_async_copy(source, target, sems.at[i])
        for i, (source, target) in enumerate(pairs)
    ]
    for copy in copies:
        copy.start()
    for copy in copies:
        copy.wait()


def place_heads_kernel(shape, me_ref, *refs):
    mine_ref, give_ref, whole_ref, sems = refs[-4:]
    spot, core, plane = me_ref[0], me_ref[1], me_ref[2]
    for z in range(4):

        @pl.when(plane == z)
        def _():
            pairs = []
            for side in range(4):
                start = 3 * CHUNK * (side + spot - 2 * (side & spot))
                for number, first, rows, place in shape[min(z, 2)][side]:
                    where = pl.ds(pl.multiple_of(start + place, 16), rows)
                    pairs.append((refs[number].at[pl.ds(first, rows)], whole_ref.at[where]))
            run_copies(pairs, sems)

    for ref, who in ((mine_ref, core), (give_ref, 1 - core)):
        for j in range(6):
            chunk = 4 * (j // 2) + 2 * who + j % 2
            ref[j] = whole_ref[pl.ds(pl.multiple_of(chunk * CHUNK, 16), CHUNK)]


def place_heads(me, slots):
    arrays, shape = slot_arrays(slots)
    half = jax.ShapeDtypeStruct((6, CHUNK, D), bf16)
    return pl.pallas_call(
        functools.partial(place_heads_kernel, shape),
        in_specs=[pl.BlockSpec(memory_space=pltpu.SMEM)]
        + [pl.BlockSpec(memory_space=pl.ANY)] * len(arrays),
        out_shape=[half, half],
        scratch_shapes=[pltpu.VMEM((12 * CHUNK, D), bf16), pltpu.SemaphoreType.DMA((8,))],
        compiler_params=params(),
        cost_estimate=cost(1),
        name="place_heads",
    )(me, *arrays)


def place_rest_kernel(shape, held, me_ref, *refs):
    out_ref, in_ref, down_ref, stage_ref, load_sems, store_sems = refs[-6:]
    spot, plane = me_ref[0], me_ref[2]

    def part(pairs, source, first, rows, row):
        while rows:
            if row < 4 * CHUNK:
                chunk, offset = divmod(row, CHUNK)
                count = min(rows, CHUNK - offset)
                targets = []
                for h in range(2):
                    target = 2 * CHUNK * chunk + CHUNK * h + offset
                    targets.append((pl.ds(OWN * h, OWN), out_ref.at[pl.ds(target, count)]))
            else:
                ref, start = (in_ref, 4 * CHUNK) if row < 20 * CHUNK else (down_ref, 20 * CHUNK)
                count = min(rows, start + 16 * CHUNK - row)
                targets = [(slice(None), ref.at[pl.ds(row - start, count)])]
            pairs.append((source.at[pl.ds(first, count)], count, targets))
            row, first, rows = row + count, first + count, rows - count

    for z in range(4):
        for s in range(4):
            pairs = []
            for slot, (number, sides) in zip(shape, held, strict=True):
                piece = PIECES[number][z]
                for side in sides if piece else ():
                    base = 3 * CHUNK * (4 * (piece - 1) + (side ^ s))
                    for array, first, rows, place in slot[side]:
                        part(pairs, refs[array], first, rows, base + place)

            @pl.when((plane == z) & (spot == s))
            def _():
                loads, stores, row = [], [], 0
                for i, (source, count, targets) in enumerate(pairs):
                    spot_rows = pl.ds(row, count)
                    loads.append(
                        pltpu.make_async_copy(source, stage_ref.at[spot_rows], load_sems.at[i])
                    )
                    stores.append([])
                    for columns, target in targets:
                        stores[-1].append(
                            pltpu.make_async_copy(
                                stage_ref.at[spot_rows, columns],
                                target,
                                store_sems.at[2 * i + len(stores[-1])],
                            )
                        )
                    row += count
                for load in loads:
                    load.start()
                for load, store in zip(loads, stores, strict=True):
                    load.wait()
                    for copy in store:
                        copy.start()
                for store in stores:
                    for copy in store:
                        copy.wait()


def place_rest(me, slots, held, state):
    arrays, shape = slot_arrays(
        [[slots[i][side] if side in sides else None for side in range(4)] for i, sides in held]
    )
    units = jax.ShapeDtypeStruct((UNITS, D), bf16)
    anywhere = pl.BlockSpec(memory_space=pl.ANY)
    return pl.pallas_call(
        functools.partial(place_rest_kernel, shape, held),
        in_specs=[pl.BlockSpec(memory_space=pltpu.SMEM)] + [anywhere] * (len(arrays) + len(state)),
        out_specs=[anywhere] * 3,
        out_shape=[jax.ShapeDtypeStruct((D, OWN), bf16), units, units],
        input_output_aliases={1 + len(arrays) + i: i for i in range(len(state))},
        scratch_shapes=[
            pltpu.VMEM((24 * CHUNK, D), bf16),
            pltpu.SemaphoreType.DMA((32,)),
            pltpu.SemaphoreType.DMA((64,)),
        ],
        compiler_params=params(),
        cost_estimate=cost(1),
        name="place_rest",
    )(me, *arrays, *state)


def plus(*values):
    total = values[0].astype(f32)
    for value in values[1:]:
        total = total + value.astype(f32)
    return total.astype(bf16)


def cross(sides):
    return send(sides[3], SIDE_Y), send(sides[4], SIDE_X)


def merge_kernel(x_ref, y_ref, upper_ref, lower_ref, x_out, y_out):
    x_out[:HALF] = (x_ref[:HALF].astype(f32) + upper_ref[...].astype(f32)).astype(bf16)
    x_out[HALF:] = x_ref[HALF:]
    y_out[:HALF] = y_ref[:HALF]
    y_out[HALF:] = (y_ref[HALF:].astype(f32) + lower_ref[...].astype(f32)).astype(bf16)


def across(sides, crossed):
    over_x, over_y = pl.pallas_call(
        merge_kernel,
        out_shape=[jax.ShapeDtypeStruct((3 * CHUNK, D), bf16)] * 2,
        compiler_params=params(),
        cost_estimate=cost(1),
        name="merge",
    )(sides[1], sides[2], *crossed)
    return send(over_x, SIDE_X), send(over_y, SIDE_Y)


def gather_vectors(low_vectors, ranks):
    count, width = low_vectors.shape
    block = jnp.pad(low_vectors, ((0, 16 - count), (0, 128 - width)))
    blocks = lax.all_to_all(jnp.broadcast_to(block, (ranks, 16, 128)), "dp", 0, 0, tiled=True)
    return blocks[:, :count, :width].transpose(1, 0, 2).reshape(count, ranks * width).astype(f32)


def vector_blocks(rows, ranks):
    blocks = rows.reshape(16, ranks, D // ranks).transpose(1, 0, 2)
    return jnp.pad(blocks, ((0, 0), (0, 0), (0, 128 - D // ranks)))


def selection(span, kind, source, half_len):
    chosen = span == 1
    masked = chosen & (kind < 8)
    swapped = chosen & (kind == 8)
    here = lax.broadcasted_iota(jnp.int32, (1, half_len), 1)
    origin = jnp.where(masked, -1, jnp.where(swapped, source, here))
    rows = lax.broadcasted_iota(jnp.int32, (half_len, half_len), 0)
    one_hot = (rows == origin).astype(f32).astype(bf16)
    first = lax.broadcasted_iota(jnp.int32, (16, half_len), 0) == 0
    mask_rows = jnp.where(first & masked, 1.0, 0.0).astype(bf16)
    return one_hot, mask_rows


def corrupt_kernel(span_ref, kind_ref, from_ref, hidden_ref, mask_ref, out_ref):
    seqs, half_len = span_ref.shape
    for s in range(seqs):
        rows = slice(s, s + 1)
        one_hot, mask_rows = selection(
            span_ref[rows, :], kind_ref[rows, :], from_ref[rows, :], half_len
        )
        picked = dot(one_hot, hidden_ref[s], TN) + dot(mask_rows, mask_ref[...], TN)
        out_ref[s] = picked.astype(bf16)


def corrupt(span, kind, source, hidden, mask_row):
    mask = jnp.broadcast_to(mask_row.astype(bf16)[None], (16, D))
    return pl.pallas_call(
        corrupt_kernel,
        out_shape=jax.ShapeDtypeStruct(hidden.shape, bf16),
        compiler_params=params(),
        name="corrupt",
    )(span, kind, source, hidden, mask)


def corrupt_back_kernel(
    span_ref, kind_ref, from_ref, grad_ref, own_ref, partial_ref, out_ref, mask_ref
):
    seqs, half_len = span_ref.shape
    mask_sum = jnp.zeros((16, D), f32)
    for s in range(seqs):
        rows = slice(s, s + 1)
        block = pl.ds(s * half_len, half_len)
        one_hot, mask_rows = selection(
            span_ref[rows, :], kind_ref[rows, :], from_ref[rows, :], half_len
        )
        grad = grad_ref[block] + own_ref[block] + partial_ref[block].astype(f32)
        high = grad.astype(bf16)
        low = (grad - high.astype(f32)).astype(bf16)
        out_ref[s] = dot(one_hot, high, NN) + dot(one_hot, low, NN)
        mask_sum = mask_sum + dot(mask_rows, high, NN) + dot(mask_rows, low, NN)
    mask_ref[...] = mask_sum


def corrupt_back(span, kind, source, grad, own, partial):
    seqs, half_len = span.shape
    return pl.pallas_call(
        corrupt_back_kernel,
        out_shape=[
            jax.ShapeDtypeStruct((seqs, half_len, D), f32),
            jax.ShapeDtypeStruct((16, D), f32),
        ],
        compiler_params=params(),
        cost_estimate=cost(1),
        name="corrupt_back",
    )(span, kind, source, grad, own, partial)


def attend_kernel(
    me_ref, own_ref, other_ref, mine_ref, theirs_ref, vals_ref, w_ref, qkv_ref, low_ref, wide_ref, lse_ref
):
    half_len = own_ref.shape[1]
    core = me_ref[1]

    @pl.when(pl.program_id(0) == 0)
    def _():
        for j in range(6):
            for ref, which in ((mine_ref, core), (theirs_ref, 1 - core)):
                where = pl.ds(pl.multiple_of((2 * j + which) * CHUNK, 16), CHUNK)
                w_ref[where] = ref[j]

    rows = jnp.concatenate([own_ref[0], other_ref[0]], axis=0)
    columns = pl.ds(pl.multiple_of(core * OWN, 128), OWN)
    bias = jnp.concatenate(
        [vals_ref[0:1, columns], jnp.zeros((1, OWN), f32), vals_ref[1:2, columns]], axis=-1
    )
    projected = (dot(rows, w_ref[...], NT) + bias).astype(bf16)
    qkv_ref[:, 0] = projected.reshape(2, half_len, 3 * OWN)
    wide, totals = [], []

    def score(h):
        columns = slice(h * HEAD_DIM, (h + 1) * HEAD_DIM)
        query = projected[:, :OWN][:, columns] * bf16(HEAD_DIM**-0.5)
        return dot(query, projected[:, OWN : 2 * OWN][:, columns], NT)

    heads = OWN // HEAD_DIM
    ahead = [score(0), score(1)]
    for h in range(heads):
        if h + 2 < heads:
            ahead.append(score(h + 2))
        scores = ahead.pop(0)
        value = projected[:, 2 * OWN :][:, h * HEAD_DIM : (h + 1) * HEAD_DIM]
        highest = jnp.max(scores, axis=-1, keepdims=True)
        exponents = jnp.exp(scores - highest)
        total = jnp.sum(exponents, axis=-1, keepdims=True)
        probabilities = (exponents * (1.0 / total)).astype(bf16)
        wide.append(dot(probabilities, value, NN))
        totals.append(highest + jnp.log(total))
    attended = jnp.concatenate(wide, axis=-1)
    wide_ref[:, 0] = attended.reshape(2, half_len, OWN)
    low_ref[:, 0] = attended.astype(bf16).reshape(2, half_len, OWN)
    fill = jnp.zeros((2 * half_len, 128 - len(totals)), f32)
    lse_ref[0] = jnp.concatenate(totals + [fill], axis=-1).T[:8]


def whole(*shape):
    return pl.BlockSpec(shape, lambda *_: (0,) * len(shape))


def attend(me, u_own, u_other, mine, theirs, vals):
    seqs, half_len, _ = u_own.shape
    block = lambda width: pl.BlockSpec((2, 1, half_len, width), lambda s: (0, s, 0, 0))
    token = pl.BlockSpec((1, half_len, D), lambda s: (s, 0, 0))
    return pl.pallas_call(
        attend_kernel,
        grid=(seqs,),
        in_specs=[
            pl.BlockSpec(memory_space=pltpu.SMEM),
            token,
            token,
            whole(6, CHUNK, D),
            whole(6, CHUNK, D),
            whole(*vals.shape),
        ],
        out_specs=[
            whole(3 * OWN, D),
            block(3 * OWN),
            block(OWN),
            block(OWN),
            pl.BlockSpec((1, 8, 2 * half_len), lambda s: (s, 0, 0)),
        ],
        out_shape=[
            jax.ShapeDtypeStruct((3 * OWN, D), bf16),
            jax.ShapeDtypeStruct((2, seqs, half_len, 3 * OWN), bf16),
            jax.ShapeDtypeStruct((2, seqs, half_len, OWN), bf16),
            jax.ShapeDtypeStruct((2, seqs, half_len, OWN), f32),
            jax.ShapeDtypeStruct((seqs, 8, 2 * half_len), f32),
        ],
        cost_estimate=cost(3),
        compiler_params=params(),
        name="attend",
    )(me, u_own, u_other, mine, theirs, vals)


def attend_back_kernel(
    skip, qkv_ref, own_ref, other_ref, wo_ref, wide_ref, lse_ref, *refs
):
    out_ref, sums_ref = refs[skip:]
    half_len = qkv_ref.shape[2]
    length = 2 * half_len
    projected = qkv_ref[:, 0].reshape(length, 3 * OWN)
    rows = jnp.concatenate([own_ref[0], other_ref[0]], axis=0)
    grad = dot(rows, wo_ref[...], NN).astype(bf16)
    product = grad.astype(f32) * wide_ref[:, 0].reshape(length, OWN)
    heads = OWN // HEAD_DIM
    deltas = [
        jnp.sum(product[:, h * HEAD_DIM : (h + 1) * HEAD_DIM], axis=-1, keepdims=True)
        for h in range(heads)
    ]
    fill = jnp.zeros((length, 128 - heads), f32)
    delta_rows = jnp.concatenate(deltas + [fill], axis=-1).T
    parts = [[], [], []]

    def head(h):
        columns = slice(h * HEAD_DIM, (h + 1) * HEAD_DIM)
        query = projected[:, :OWN][:, columns] * bf16(HEAD_DIM**-0.5)
        key = projected[:, OWN : 2 * OWN][:, columns]
        value = projected[:, 2 * OWN :][:, columns]
        return query, key, value, grad[:, columns]

    def products(h):
        query, key, value, grad_head = head(h)
        return dot(key, query, NT), dot(value, grad_head, NT)

    ahead = [products(0)]
    for h in range(heads):
        if h + 1 < heads:
            ahead.append(products(h + 1))
        scores, grad_weights = ahead.pop(0)
        query, key, value, grad_head = head(h)
        weights = jnp.exp(scores - lse_ref[0, h : h + 1, :])
        grad_scores = (weights * (grad_weights - delta_rows[h : h + 1, :])).astype(bf16)
        parts[0].append(dot(grad_scores, key, TN) * HEAD_DIM**-0.5)
        parts[1].append(dot(grad_scores, query, NN))
        parts[2].append(dot(weights.astype(bf16), grad_head, NN))
    result = jnp.concatenate(parts[0] + parts[1] + parts[2], axis=-1).astype(bf16)
    out_ref[:, 0] = result.reshape(2, half_len, 3 * OWN)
    sums = jnp.sum(result.astype(f32), axis=0, keepdims=True)

    @pl.when(pl.program_id(0) == 0)
    def _():
        sums_ref[...] = refs[1][...] if skip else jnp.zeros_like(sums_ref)

    sums_ref[...] += sums


def attend_back(qkv, own, other, wo_own, wide, lse, first, count, state):
    _, seqs, half_len, _ = qkv.shape
    block = lambda width: pl.BlockSpec((2, 1, half_len, width), lambda s: (0, s + first, 0, 0))
    token = pl.BlockSpec((1, half_len, D), lambda s: (s + first, 0, 0))
    return pl.pallas_call(
        functools.partial(attend_back_kernel, len(state)),
        grid=(count,),
        in_specs=[
            block(3 * OWN),
            token,
            token,
            whole(D, OWN),
            block(OWN),
            pl.BlockSpec((1, 8, 2 * half_len), lambda s: (s + first, 0, 0)),
        ]
        + ([pl.BlockSpec(memory_space=pl.ANY), whole(1, 3 * OWN)] if state else []),
        out_specs=[block(3 * OWN), whole(1, 3 * OWN)],
        input_output_aliases={6: 0} if state else {},
        out_shape=[
            jax.ShapeDtypeStruct((2, seqs, half_len, 3 * OWN), bf16),
            jax.ShapeDtypeStruct((1, 3 * OWN), f32),
        ],
        cost_estimate=cost(2 * count),
        compiler_params=params(),
        name="attend_back",
    )(qkv, own, other, wo_own, wide, lse, *state)


def norm(values):
    center = values - jnp.mean(values, axis=-1, keepdims=True)
    inv_std = lax.rsqrt(jnp.mean(center * center, axis=-1, keepdims=True) + ln_eps)
    return center * inv_std, inv_std


def norm_backward(upstream, normed, inv_std, gain):
    scaled = upstream * gain
    return inv_std * (
        scaled
        - jnp.mean(scaled, axis=-1, keepdims=True)
        - normed * jnp.mean(scaled * normed, axis=-1, keepdims=True)
    )


def row(ref, i):
    return ref[i : i + 1, :]


def branch_kernel(own_ref, other_ref, u_ref, wo_ref, wo_other_ref, vals_ref, normed_ref, inv_ref, low_ref):
    branch = dot(own_ref[0, 0], wo_ref[...], NT) + dot(other_ref[0], wo_other_ref[...], NT)
    normed, inv = norm(u_ref[0].astype(f32) + branch + row(vals_ref, 2))
    normed_ref[...] = normed
    inv_ref[...] = jnp.broadcast_to(inv, inv_ref.shape)
    low_ref[...] = (normed * row(vals_ref, 3) + row(vals_ref, 4)).astype(bf16)


def attention_branch(attended, from_other, u_own, wo_own, wo_other, vals):
    seqs, half_len, _ = u_own.shape
    rows = pl.BlockSpec((half_len, D), lambda s: (s, 0))
    return pl.pallas_call(
        branch_kernel,
        grid=(seqs,),
        in_specs=[
            pl.BlockSpec((1, 1, half_len, OWN), lambda s: (0, s, 0, 0)),
            pl.BlockSpec((1, half_len, OWN), lambda s: (s, 0, 0)),
            pl.BlockSpec((1, half_len, D), lambda s: (s, 0, 0)),
            whole(D, OWN),
            whole(D, OWN),
            whole(*vals.shape),
        ],
        out_specs=[rows, pl.BlockSpec((half_len, 128), lambda s: (s, 0)), rows],
        out_shape=[
            jax.ShapeDtypeStruct((seqs * half_len, D), f32),
            jax.ShapeDtypeStruct((seqs * half_len, 128), f32),
            jax.ShapeDtypeStruct((seqs * half_len, D), bf16),
        ],
        cost_estimate=cost(1),
        compiler_params=params(),
        name="attention_branch",
    )(attended, from_other, u_own, wo_own, wo_other, vals)


def hidden_kernel(own_ref, other_ref, w_ref, bias_ref, gelu_ref, slope_ref):
    tile = own_ref.shape[0] // 3
    jobs = [
        (half, ref, slice(i * tile, (i + 1) * tile))
        for half, ref in enumerate((own_ref, other_ref))
        for i in range(3)
    ]

    def project(job):
        _, ref, rows = jobs[job]
        return dot(ref[rows], w_ref[...], NT) + bias_ref[...]

    ahead = project(0)
    for i, (half, _, rows) in enumerate(jobs):
        points = ahead
        if i + 1 < len(jobs):
            ahead = project(i + 1)
        below = 0.5 * (1.0 + lax.erf(points * 2**-0.5))
        density = jnp.exp(-0.5 * points * points) * 0.3989422804014327
        gelu_ref[half, rows] = (points * below).astype(bf16)
        slope_ref[half, rows] = (below + points * density).astype(bf16)


def hidden_units(h_own, h_other, w_in, bias):
    rows = h_own.shape[0]
    width = 384
    block = pl.BlockSpec((2, rows, width), lambda i: (0, 0, i))
    return pl.pallas_call(
        hidden_kernel,
        grid=(UNITS // width,),
        in_specs=[
            whole(rows, D),
            whole(rows, D),
            pl.BlockSpec((width, D), lambda i: (i, 0)),
            pl.BlockSpec((1, width), lambda i: (0, i)),
        ],
        out_specs=[block, block],
        out_shape=[jax.ShapeDtypeStruct((2, rows, UNITS), bf16)] * 2,
        cost_estimate=cost(3),
        compiler_params=params(),
        name="hidden_units",
    )(h_own, h_other, w_in, bias)


def rows_kernel(left_ref, right_ref, out_ref):
    out_ref[...] = dot(left_ref[0], right_ref[...], NN).astype(out_ref.dtype)


def rows_times(left, half, right, dtype, name):
    _, rows, depth = left.shape
    tile = rows // 3
    return pl.pallas_call(
        rows_kernel,
        grid=(3,),
        in_specs=[pl.BlockSpec((1, tile, depth), lambda i: (half, i, 0)), whole(*right.shape)],
        out_specs=pl.BlockSpec((tile, D), lambda i: (i, 0)),
        out_shape=jax.ShapeDtypeStruct((rows, D), dtype),
        cost_estimate=cost(1),
        compiler_params=params(),
        name=name,
    )(left, right)


def add_sums(sums_ref, *values):
    @pl.when(pl.program_id(0) == 0)
    def _():
        sums_ref[...] = jnp.zeros_like(sums_ref)

    for i, value in enumerate(values):
        sums_ref[i : i + 1, :] += jnp.sum(value, axis=0, keepdims=True)


def finish_kernel(own_ref, other_ref, normed_ref, grad_ref, vals_ref, out_ref, wide_ref, low_ref, sums_ref):
    hidden_one = normed_ref[...] * row(vals_ref, 3) + row(vals_ref, 4)
    feed = own_ref[...] + other_ref[...].astype(f32) + row(vals_ref, 5)
    normed, inv = norm(hidden_one + feed)
    out_ref[...] = normed * row(vals_ref, 6) + row(vals_ref, 7)
    grad = grad_ref[...].astype(f32)
    wide = norm_backward(grad, normed, inv, row(vals_ref, 6))
    low = wide.astype(bf16)
    wide_ref[...] = wide
    low_ref[...] = low
    add_sums(sums_ref, low.astype(f32), grad * normed, grad)


def finish(own, other, normed, grad, vals):
    rows = own.shape[0]
    tile = rows // 6
    block = pl.BlockSpec((tile, D), lambda i: (i, 0))
    return pl.pallas_call(
        finish_kernel,
        grid=(6,),
        in_specs=[block] * 4 + [whole(*vals.shape)],
        out_specs=[block] * 3 + [whole(8, D)],
        out_shape=[
            jax.ShapeDtypeStruct((rows, D), f32),
            jax.ShapeDtypeStruct((rows, D), f32),
            jax.ShapeDtypeStruct((rows, D), bf16),
            jax.ShapeDtypeStruct((8, D), f32),
        ],
        cost_estimate=cost(1),
        compiler_params=params(),
        name="finish",
    )(own, other, normed, grad, vals)


def norm_one_kernel(two_ref, own_ref, other_ref, normed_ref, inv_ref, vals_ref, wide_ref, low_ref, sums_ref):
    grad = two_ref[...] + own_ref[...] + other_ref[...].astype(f32)
    normed = normed_ref[...]
    wide = norm_backward(grad, normed, inv_ref[:, 0:1], row(vals_ref, 3))
    low = wide.astype(bf16)
    wide_ref[...] = wide
    low_ref[...] = low
    add_sums(sums_ref, low.astype(f32), grad * normed, grad)


def norm_one_back(two, own, other, normed, inv, vals):
    rows = own.shape[0]
    tile = rows // 3
    block = pl.BlockSpec((tile, D), lambda i: (i, 0))
    return pl.pallas_call(
        norm_one_kernel,
        grid=(3,),
        in_specs=[block] * 4 + [pl.BlockSpec((tile, 128), lambda i: (i, 0)), whole(*vals.shape)],
        out_specs=[block] * 2 + [whole(8, D)],
        out_shape=[
            jax.ShapeDtypeStruct((rows, D), f32),
            jax.ShapeDtypeStruct((rows, D), bf16),
            jax.ShapeDtypeStruct((8, D), f32),
        ],
        cost_estimate=cost(1),
        compiler_params=params(),
        name="norm_one_back",
    )(two, own, other, normed, inv, vals)


def slope_kernel(grad_ref, w_ref, slope_ref, out_ref, sums_ref):
    low = (dot(grad_ref[...], w_ref[...], NT) * slope_ref[0].astype(f32)).astype(bf16)
    out_ref[0] = low
    sums_ref[...] = jnp.sum(low.astype(f32), axis=0, keepdims=True)


def before_gelu(grad, w_down, slope, half):
    rows = grad.shape[0]
    width = 384
    return pl.pallas_call(
        slope_kernel,
        grid=(UNITS // width,),
        in_specs=[
            whole(rows, D),
            pl.BlockSpec((width, D), lambda i: (i, 0)),
            pl.BlockSpec((1, rows, width), lambda i: (half, 0, i)),
        ],
        out_specs=[
            pl.BlockSpec((1, rows, width), lambda i: (0, 0, i)),
            pl.BlockSpec((1, width), lambda i: (0, i)),
        ],
        out_shape=[
            jax.ShapeDtypeStruct((1, rows, UNITS), bf16),
            jax.ShapeDtypeStruct((1, UNITS), f32),
        ],
        cost_estimate=cost(1),
        compiler_params=params(),
        name="before_gelu",
    )(grad, w_down, slope)


def rows_of(count):
    return jax.ShapeDtypeStruct((count, D), bf16)


CROSS = ((0, 0, 288), (1, 0, 288), (2, 0, 288), (3, 0, 144), (3, 144, 144))


def side_rows(spot, side, first, rows):
    start = 3 * CHUNK * (side + spot - 2 * (side & spot)) + first
    return pl.ds(pl.multiple_of(start, 16), rows)


def write_sides(spot, piece_ref, outs):
    for out, (side, first, rows) in zip(outs, CROSS, strict=True):
        out[...] = piece_ref[side_rows(spot, side, first, rows)]


def rows_at(step):
    return pl.ds(pl.multiple_of(step * OWN, 16), OWN)


def two_halves(left, left_other, right, right_other):
    return dot(left, right, TN) + dot(left_other, right_other, TN)


def grads3_kernel(me_ref, g_ref, d_ref, d_other_ref, *refs):
    piece_ref = refs[-1]
    step = pl.program_id(0)
    piece_ref[rows_at(step)] = two_halves(
        g_ref[0], g_ref[1], d_ref[...], d_other_ref[...]
    ).astype(bf16)

    @pl.when(step == 2)
    def _():
        write_sides(me_ref[0], piece_ref, refs[:-1])


def grads2_kernel(me_ref, z_ref, z_other_ref, h_ref, h_other_ref, g_ref, d_ref, d_other_ref, *refs):
    piece_ref = refs[-1]
    step = pl.program_id(0)

    @pl.when(step < 2)
    def _():
        piece_ref[rows_at(step)] = two_halves(
            z_ref[0], z_other_ref[0], h_ref[...], h_other_ref[...]
        ).astype(bf16)

    @pl.when(step == 2)
    def _():
        piece_ref[rows_at(step)] = two_halves(
            g_ref[0], g_ref[1], d_ref[...], d_other_ref[...]
        ).astype(bf16)
        write_sides(me_ref[0], piece_ref, refs[:-1])


def grads1_kernel(me_ref, z_ref, z_other_ref, h_ref, h_other_ref, a_ref, a_other_ref, att_ref, *refs):
    piece_ref = refs[-1]
    step = pl.program_id(0)

    @pl.when(step < 2)
    def _():
        piece_ref[rows_at(step + 1)] = two_halves(
            z_ref[0], z_other_ref[0], h_ref[...], h_other_ref[...]
        ).astype(bf16)

    @pl.when(step == 2)
    def _():
        wo = two_halves(a_ref[...], a_other_ref[...], att_ref[0], att_ref[1]).astype(bf16)
        for j in range(4):
            upper = wo[2 * CHUNK * j : 2 * CHUNK * j + CHUNK]
            lower = wo[2 * CHUNK * j + CHUNK : 2 * CHUNK * (j + 1)]
            piece_ref[CHUNK * j : CHUNK * (j + 1)] = jnp.concatenate([upper, lower], axis=-1)
        write_sides(me_ref[0], piece_ref, refs[:-1])


def grads_call(kernel, specs, arrays, name):
    return pl.pallas_call(
        kernel,
        grid=(3,),
        in_specs=[pl.BlockSpec(memory_space=pltpu.SMEM)] + specs,
        out_specs=[whole(count, D) for _, _, count in CROSS],
        out_shape=[rows_of(count) for _, _, count in CROSS],
        scratch_shapes=[pltpu.VMEM((12 * CHUNK, D), bf16)],
        cost_estimate=cost(2),
        compiler_params=params(),
        name=name,
    )(*arrays)


def grads0_kernel(me_ref, g_ref, u_ref, u_other_ref, keep_ref, give_ref, piece_ref):
    core = me_ref[1]
    step = pl.program_id(0)
    piece_ref[rows_at(step)] = two_halves(
        g_ref[0], g_ref[1], u_ref[...], u_other_ref[...]
    ).astype(bf16)

    @pl.when(step == 2)
    def _():
        for j in range(6):
            for ref, which in ((keep_ref, core), (give_ref, 1 - core)):
                where = pl.ds(pl.multiple_of((2 * j + which) * CHUNK, 16), CHUNK)
                ref[j] = piece_ref[where]


def grads0(me, grad, u_own, u_other):
    rows = grad.shape[1]
    half = jax.ShapeDtypeStruct((6, CHUNK, D), bf16)
    return pl.pallas_call(
        grads0_kernel,
        grid=(3,),
        in_specs=[
            pl.BlockSpec(memory_space=pltpu.SMEM),
            pl.BlockSpec((2, rows, OWN), lambda i: (0, 0, i)),
            whole(rows, D),
            whole(rows, D),
        ],
        out_specs=[whole(6, CHUNK, D)] * 2,
        out_shape=[half, half],
        scratch_shapes=[pltpu.VMEM((12 * CHUNK, D), bf16)],
        cost_estimate=cost(2),
        compiler_params=params(),
        name="grads0",
    )(me, grad, u_own, u_other)


def regroup_kernel(me_ref, keep_ref, take_ref, *refs):
    piece_ref = refs[-1]
    core = me_ref[1]
    for ref, who in ((keep_ref, core), (take_ref, 1 - core)):
        for j in range(6):
            chunk = 4 * (j // 2) + 2 * who + j % 2
            piece_ref[pl.ds(pl.multiple_of(chunk * CHUNK, 16), CHUNK)] = ref[j]
    write_sides(me_ref[0], piece_ref, refs[:-1])


def regroup(me, keep, take):
    return pl.pallas_call(
        regroup_kernel,
        in_specs=[pl.BlockSpec(memory_space=pltpu.SMEM)]
        + [pl.BlockSpec(memory_space=pltpu.VMEM)] * 2,
        out_shape=[rows_of(count) for _, _, count in CROSS],
        scratch_shapes=[pltpu.VMEM((12 * CHUNK, D), bf16)],
        cost_estimate=cost(1),
        compiler_params=params(),
        name="regroup",
    )(me, keep, take)


def vector_kernel(me_ref, qkv_ref, one_ref, two_ref, mask_ref, bias_ref, out_ref):
    out_ref[...] = jnp.zeros_like(out_ref)
    columns = pl.ds(pl.multiple_of(me_ref[1] * OWN, 128), OWN)
    out_ref[0:1, columns] = qkv_ref[:, :OWN]
    out_ref[1:2, columns] = qkv_ref[:, 2 * OWN :]
    out_ref[2:5, :] = one_ref[0:3, :]
    out_ref[5:8, :] = two_ref[0:3, :]
    out_ref[8:9, :] = mask_ref[0:1, :]
    out_ref[9:13, :] = bias_ref[...]


def vector_rows(me, qkv_sums, one_sums, two_sums, mask_sums, bias_sums):
    return pl.pallas_call(
        vector_kernel,
        in_specs=[pl.BlockSpec(memory_space=pltpu.SMEM)]
        + [pl.BlockSpec(memory_space=pltpu.VMEM)] * 5,
        out_shape=jax.ShapeDtypeStruct((16, D), f32),
        cost_estimate=cost(1),
        name="vector_rows",
    )(me, qkv_sums, one_sums, two_sums, mask_sums, bias_sums)


def adam_step(master, first_old, second, gradient, decay_on, step_rate):
    first_new = beta_one * first_old + (1.0 - beta_one) * gradient
    second_new = beta_two * second + (1.0 - beta_two) * gradient * gradient
    fix_one = 1.0 / (1.0 - beta_one**STEP)
    fix_two = 1.0 / (1.0 - beta_two**STEP)
    update = first_new * fix_one / (jnp.sqrt(second_new * fix_two) + adam_eps)
    return (master - step_rate * (update + decay_on * master), first_new, second_new)


def update_kernel(sums_ref, grad_ref, *refs):
    norm_value = jnp.sqrt(jnp.sum(sums_ref[...], axis=0))[0:1, 0:1]
    clip = 1.0 / jnp.maximum(norm_value, 1.0)
    inputs, outs = refs[:7], refs[7:]
    master, first, second = (ref[...] for ref in inputs[:3])
    gradient = grad_ref[...].astype(f32) * clip
    master, first, second = adam_step(master, first, second, gradient, decay_rate, learn_rate)
    for ref, value in zip(outs[:4], (master, first, second, master.astype(bf16)), strict=True):
        ref[...] = value

    @pl.when(pl.program_id(0) == 0)
    def _():
        gradient, master, first, second = (ref[...] for ref in inputs[3:])
        values = adam_step(master, first, second, gradient * clip, 0.0, vector_rate)
        for ref, value in zip(outs[4:7], values, strict=True):
            ref[...] = value
        outs[7][...] = values[0].astype(bf16)
        outs[8][...] = norm_value


def update(sums, grad, weights, shard_v, vectors):
    rows = grad.shape[0]
    tile = 144 if rows % 144 == 0 else rows
    block = pl.BlockSpec((tile, D), lambda i: (i, 0))
    small = whole(*shard_v.shape)
    return pl.pallas_call(
        update_kernel,
        grid=(rows // tile,),
        in_specs=[whole(*sums.shape)] + [block] * 4 + [small] * 4,
        out_specs=[block] * 4 + [small] * 4 + [whole(1, 1)],
        out_shape=[jax.ShapeDtypeStruct((rows, D), f32)] * 3
        + [jax.ShapeDtypeStruct((rows, D), bf16)]
        + [jax.ShapeDtypeStruct(shard_v.shape, f32)] * 3
        + [jax.ShapeDtypeStruct(shard_v.shape, bf16), jax.ShapeDtypeStruct((1, 1), f32)],
        cost_estimate=cost(1),
        compiler_params=params(),
        name="update",
    )(sums, grad, *weights, shard_v, *vectors)


def shards(
    ranks,
    hidden,
    span_mask,
    replace_kind,
    replace_from,
    weights,
    vectors,
    weight_first,
    weight_second,
    vector_first,
    vector_second,
    cotangent,
):
    seqs, half_len, _ = hidden.shape
    rows = seqs * half_len
    index = lax.axis_index("dp")
    core = lax.axis_index("seq")
    staged = ranks == 16
    plane = index // 4
    spot = index % 4 if staged else jnp.zeros_like(index)
    me = jnp.stack([spot, core, plane]).astype(jnp.int32)
    low_weights = weights.astype(bf16)
    slots, grads, result = [], {}, []
    if staged:
        gather = Steps(gather_steps(pack(low_weights, index), slots))
    else:
        gather = Steps(None)
        stacked = pack(lax.all_gather(low_weights, "dp", axis=0, tiled=True), 0)

    gather()
    gather()
    vals = gather_vectors(vectors.astype(bf16), ranks)
    every, rest = (0, 1, 2, 3), ()
    if staged:
        rest = place_rest(me, slots, ((0, every),), ())
    vals, *rest = gather(vals, *rest)
    u_own = corrupt(span_mask, replace_kind, replace_from, hidden, vals[8])
    bias_in = lax.dynamic_index_in_dim(
        vals[9:].reshape(FF // (2 * CHUNK), 2, CHUNK), core, 1, keepdims=False
    ).reshape(1, UNITS)
    if staged:
        rest = place_rest(me, slots, ((1, every),), rest)
    u_own, vals, bias_in, *rest = gather(u_own, vals, bias_in, *rest)
    u_other = swap(u_own)

    if staged:
        mine, give = place_heads(me, slots)
    else:
        halves = stacked[: 12 * CHUNK].reshape(3, 2, 2, CHUNK, D)
        mine = lax.dynamic_index_in_dim(halves, core, 1, keepdims=False).reshape(6, CHUNK, D)
        give = lax.dynamic_index_in_dim(halves, 1 - core, 1, keepdims=False).reshape(6, CHUNK, D)
    w_qkv, qkv, attended, attended_wide, lse = attend(
        me, u_own, u_other, mine, swap(give), vals
    )
    w_qkv, qkv, attended, attended_wide, lse, *rest = gather(
        w_qkv, qkv, attended, attended_wide, lse, *rest
    )
    from_other = swap(attended[1])
    if staged:
        rest = place_rest(me, slots, ((2, every), (3, (0, 1, 2))), rest)
    attended, from_other, *rest = gather(attended, from_other, *rest)

    if staged:
        wo_own, w_in, w_down = place_rest(me, slots, ((3, (3,)),), rest)
    else:
        rest = stacked[12 * CHUNK :]
        wo_own = (
            rest[: 4 * CHUNK].reshape(4, CHUNK, 2, OWN).transpose(0, 2, 1, 3).reshape(D, OWN)
        )
        w_in, w_down = rest[4 * CHUNK : 20 * CHUNK], rest[20 * CHUNK :]
    normed_one, inv_one, h_own = attention_branch(
        attended, from_other, u_own, wo_own, swap(wo_own), vals
    )
    h_other = swap(h_own)
    gelu, slope = hidden_units(h_own, h_other, w_in, bias_in)
    feed_other = swap(rows_times(gelu, 1, w_down, bf16, "feed_other"))
    feed_own = rows_times(gelu, 0, w_down, f32, "feed_own")
    layer_out, grad_two, d_own, two_sums = finish(
        feed_own, feed_other, normed_one, cotangent.reshape(rows, D), vals
    )

    d_other = swap(d_own)
    z_own, z_sums = before_gelu(d_own, w_down, slope, 0)
    d_other, z_own, z_sums = barrier(d_other, z_own, z_sums)
    unit = lambda first: pl.BlockSpec((2, rows, OWN), lambda i: (0, 0, i + first))
    one_unit = lambda first: pl.BlockSpec((1, rows, OWN), lambda i: (0, 0, jnp.minimum(i, 1) + first))
    tokens = whole(rows, D)
    grads[3] = grads_call(
        grads3_kernel, [unit(1), tokens, tokens], (me, gelu, d_own, d_other), "grads3"
    )
    *grads[3], d_other = barrier(*grads[3], d_other)
    reduce = Steps(reduce_steps(grads, plane, result) if staged else None)
    z_other, z_other_sums = before_gelu(d_other, w_down, slope, 1)
    hidden_other = rows_times(z_other, 0, w_in, bf16, "hidden_other")
    z_other, z_other_sums, hidden_other, z_own = reduce(
        z_other, z_other_sums, hidden_other, z_own
    )
    sent_hidden = swap(hidden_other)
    hidden_own = rows_times(z_own, 0, w_in, f32, "hidden_own")
    grad_one, a_own, one_sums = norm_one_back(
        grad_two, hidden_own, sent_hidden, normed_one, inv_one, vals
    )
    first_unit = pl.BlockSpec((2, rows, OWN), lambda i: (0, 0, 0))
    grads[2] = grads_call(
        grads2_kernel,
        [one_unit(2), one_unit(2), tokens, tokens, first_unit, tokens, tokens],
        (me, z_own, z_other, h_own, h_other, gelu, d_own, d_other),
        "grads2",
    )
    *grads[2], grad_one, a_own, one_sums = reduce(*grads[2], grad_one, a_own, one_sums)
    a_other = swap(a_own)
    a_own, a_other, qkv = reduce(a_own, a_other, qkv)
    back = (
        a_own.reshape(seqs, half_len, D),
        a_other.reshape(seqs, half_len, D),
        wo_own,
        attended_wide,
        lse,
    )
    state = attend_back(qkv, *back, 0, 1, ())
    grads[1] = grads_call(
        grads1_kernel,
        [one_unit(0), one_unit(0), tokens, tokens, tokens, tokens, whole(2, rows, OWN)],
        (me, z_own, z_other, h_own, h_other, a_own, a_other, attended.reshape(2, rows, OWN)),
        "grads1",
    )
    *grads[1], a, b, qkv = reduce(*grads[1], *state, qkv)
    state = attend_back(qkv, *back, 1, 1, (a, b))
    a, b, qkv = reduce(*state, qkv)
    grad_qkv, qkv_sums = attend_back(qkv, *back, 2, seqs - 2, (a, b))
    grad_rows = grad_qkv.reshape(2, rows, 3 * OWN)
    keep, give = grads0(me, grad_rows, u_own.reshape(rows, D), u_other.reshape(rows, D))
    keep, give, grad_rows = reduce(keep, give, grad_rows)
    take = swap(give)
    inputs_other = rows_times(grad_rows, 1, w_qkv, bf16, "inputs_other")
    grads[0] = regroup(me, keep, take)
    *grads[0], grad_rows, inputs_other = reduce(*grads[0], grad_rows, inputs_other)
    sent_inputs = swap(inputs_other)
    inputs_own = rows_times(grad_rows, 0, w_qkv, f32, "inputs_own")
    sent_inputs, inputs_own, z_sums = reduce(sent_inputs, inputs_own, z_sums)
    input_grad, mask_sums = corrupt_back(
        span_mask, replace_kind, replace_from, grad_one, inputs_own, sent_inputs
    )
    bias_sums = jnp.zeros((FF // (2 * CHUNK), 2, CHUNK), f32)
    bias_sums = lax.dynamic_update_slice(
        bias_sums,
        (z_sums + z_other_sums).reshape(FF // (2 * CHUNK), 1, CHUNK),
        (0, core, 0),
    ).reshape(FF // D, D)
    vector_part = vector_rows(me, qkv_sums, one_sums, two_sums, mask_sums, bias_sums)
    input_grad, vector_part = reduce(input_grad, vector_part)
    blocks = vector_blocks(vector_part + swap(vector_part), ranks)
    (blocks,) = reduce(blocks)
    blocks = lax.all_to_all(blocks, "dp", 0, 0, tiled=True)
    (blocks,) = reduce(blocks)
    count, width = vectors.shape
    shard_v = jnp.sum(blocks, axis=0)[:count, :width]

    if staged:
        shard_half = result[0]
        shard_w = unpack(shard_half, swap(shard_half), index)
    else:
        core_rows = [block for i in range(4) for block in grads[i]]
        core_rows = jnp.concatenate(core_rows, axis=0)
        stacked = unpack(core_rows, swap(core_rows), 0).astype(f32)
        shard_w = lax.psum_scatter(stacked, "dp", scatter_dimension=0, tiled=True)
        shard_half = lax.dynamic_slice_in_dim(shard_w, core * OWN, OWN, axis=1)

    half32 = shard_half.astype(f32)
    squares = jnp.sum(half32 * half32) + 0.5 * jnp.sum(shard_v * shard_v)
    blocks = lax.all_to_all(
        jnp.full((2 * ranks, 8, 128), squares), ("dp", "seq"), 0, 0, tiled=True
    )
    (
        weights_new,
        weight_first_new,
        weight_second_new,
        weights_low,
        vectors_new,
        vector_first_new,
        vector_second_new,
        vectors_low,
        norm_value,
    ) = update(
        blocks,
        shard_w,
        (weights, weight_first, weight_second),
        shard_v,
        (vectors, vector_first, vector_second),
    )
    grad_norm = norm_value[0, 0]
    return (
        layer_out.reshape(seqs, half_len, D),
        input_grad,
        grad_norm,
        weights_new,
        weight_first_new,
        weight_second_new,
        vectors_new,
        vector_first_new,
        vector_second_new,
        weights_low,
        vectors_low,
    )


def solution(mesh):
    token = P("dp", "seq", None)
    by_row = P("dp", None)
    by_column = P(None, "dp")
    position = P("dp", "seq")
    in_specs = (
        (token,) + (position,) * 3 + (by_row, by_column, by_row, by_row, by_column, by_column, token)
    )
    out_specs = (token, token, P()) + (by_row,) * 3 + (by_column,) * 3 + (by_row, by_column)
    return jax.shard_map(
        functools.partial(shards, mesh.shape["dp"]),
        mesh=mesh,
        in_specs=in_specs,
        out_specs=out_specs,
        check_vma=False,
    )
```
